32 devices in a mesh: head: 4 (over x, core), gx: 8 (over z, y).
Axes of the slice: x: 2, y: 2, z: 4, core: 2. Of those that a mesh axis runs over, the one named last changes fastest.
Arguments:
- level_set: float32 [72, 48, 8, 128], P('gx', 'head'), may hold values from -6 to 6
- wind_field: float32 [2, 72, 128], P(None, 'gx'), may hold values from -3 to 3
- target_mask: int32 [72, 128], P('gx'), may hold values 0 or 1
- target_depth: float32 [72, 128], P('gx'), may hold values from 0.2 to 2
Outputs:
- level_next: float32 [72, 48, 8, 128], P('gx', 'head')
The draws below stay inside these ranges and needn't reach their ends.
Inputs may be any that keep to these rules, and one draw needn't show every extreme that they name: `target_mask`: 1 marks a cell of the target set, 0 a cell outside it.
All inputs are finite; a program needn't handle non-finite values. No bound on the sum of `target_mask` on one device may be relied on, other than what follows from the above.
Results may differ from the reference program's by a relative error of at most 0.0003.
Values sent between devices are 32-bit elements; how exact they have to be, the bound alone decides.
No kernel may reach another device: no remote copies, remote signals or barrier semaphores. Data moves between devices by JAX's collectives and lax.ppermute only.
A program may use at most 64 MiB of HBM per device.

```python
import math
import jax
import jax.numpy as jnp
from jax import lax

NV = 8
NY = 128
NX = 72
NTH = 48


def with_ends(result, stream_key, low, high):
    spot = [jax.random.randint(jax.random.fold_in(stream_key, axis), (), 0, length) for axis, length in enumerate(result.shape)]
    widest = result.shape.index(max(result.shape))
    neighbour = spot[:widest] + [(spot[widest] + 1) % result.shape[widest]] + spot[widest + 1:]
    return result.at[tuple(spot)].set(low).at[tuple(neighbour)].set(high)


def block_scale(own_key, extent, cuts, low, top_value):
    gain, own = 1.0, jax.random.fold_in(own_key, 6)
    for dim, parts in cuts:
        steps = jnp.exp(jax.random.uniform(jax.random.fold_in(own, dim), (parts,), jnp.float32, low / len(cuts), top_value / len(cuts)))
        gain = gain * jnp.repeat(steps, extent[dim] // parts).reshape([-1 if axis == dim else 1 for axis in range(len(extent))])
    return gain


def centred(own_key, shape, deviation, bound, pieces=(), kind=jnp.bfloat16):
    gain = block_scale(own_key, shape, pieces, -0.22, 0.18) if pieces else 1.0
    drawn = jax.random.normal(own_key, shape, jnp.float32) * deviation * gain
    return jnp.minimum(jnp.maximum(drawn, -bound), bound).astype(kind)


def setup_inputs(seed: int = 0) -> dict:
    seeds = jax.random.split(jax.random.key(seed), 5)
    level_set = centred(seeds[0], (NX, NTH, NV, NY), 1.0, 6.0, ((0, 8), (1, 4)), jnp.float32)
    wind_field = centred(seeds[1], (2, NX, NY), 0.5, 3.0, ((1, 8),), jnp.float32)
    target_mask = with_ends((jax.random.randint(seeds[2], (NX, NY), 0, 3) < 1).astype(jnp.int32), jax.random.fold_in(seeds[2], 1), 0, 1)
    target_depth = jnp.clip(jnp.exp(math.log(2.0) - 2.3025851 * jax.random.uniform(seeds[3], (NX, NY), jnp.float32) ** block_scale(seeds[3], (NX, NY), ((0, 8),), -0.2, 0.2)), 0.2, 2.0)
    return {"level_set": level_set, "wind_field": wind_field, "target_mask": target_mask, "target_depth": target_depth}


epsilon = 1e-6
courant = 0.5
spacing = 0.05
turn_limit = 1.0
thrust_limit = 0.5
speed_low = 0.5
speed_high = 1.5


def weno_side(slope_a, slope_b, slope_c, slope_d, slope_e):
    guess_a = slope_a / 3.0 - 7.0 * slope_b / 6.0 + 11.0 * slope_c / 6.0
    guess_b = -slope_b / 6.0 + 5.0 * slope_c / 6.0 + slope_d / 3.0
    guess_c = slope_c / 3.0 + 5.0 * slope_d / 6.0 - slope_e / 6.0
    bend_a = slope_a - 2.0 * slope_b + slope_c
    tilt_a = slope_a - 4.0 * slope_b + 3.0 * slope_c
    bend_b = slope_b - 2.0 * slope_c + slope_d
    tilt_b = slope_b - slope_d
    bend_c = slope_c - 2.0 * slope_d + slope_e
    tilt_c = 3.0 * slope_c - 4.0 * slope_d + slope_e
    smooth_a = 13.0 / 12.0 * bend_a * bend_a + 0.25 * tilt_a * tilt_a + epsilon
    smooth_b = 13.0 / 12.0 * bend_b * bend_b + 0.25 * tilt_b * tilt_b + epsilon
    smooth_c = 13.0 / 12.0 * bend_c * bend_c + 0.25 * tilt_c * tilt_c + epsilon
    weight_a = 0.1 / (smooth_a * smooth_a)
    weight_b = 0.6 / (smooth_b * smooth_b)
    weight_c = 0.3 / (smooth_c * smooth_c)
    return (weight_a * guess_a + weight_b * guess_b + weight_c * guess_c) / (weight_a + weight_b + weight_c)


def weno_pair(padded, along, step_size):
    inner_count = padded.shape[along] - 6
    differences = jnp.diff(padded, axis=along) / step_size

    def window(offset):
        return lax.slice_in_dim(differences, offset, offset + inner_count, axis=along)

    minus_side = weno_side(window(0), window(1), window(2), window(3), window(4))
    plus_side = weno_side(window(5), window(4), window(3), window(2), window(1))
    return minus_side, plus_side


def hamilton(padded, heading_step, speed_step, speeds, cosines, sines, wind_x, wind_y, peak_x, peak_y):
    inner = padded[3:-3, 3:-3]
    minus_x, plus_x = weno_pair(padded[:, 3:-3], 0, spacing)
    minus_t, plus_t = weno_pair(padded[3:-3], 1, heading_step)
    minus_v, plus_v = weno_pair(jnp.pad(inner, ((0, 0), (0, 0), (3, 3), (0, 0)), mode="edge"), 2, speed_step)
    minus_y, plus_y = weno_pair(jnp.pad(inner, ((0, 0), (0, 0), (0, 0), (3, 3)), mode="edge"), 3, spacing)
    flow_x = speeds * cosines + wind_x
    flow_y = speeds * sines + wind_y
    slope_x = 0.5 * (minus_x + plus_x)
    slope_y = 0.5 * (minus_y + plus_y)
    slope_t = 0.5 * (minus_t + plus_t)
    slope_v = 0.5 * (minus_v + plus_v)
    drift = slope_x * flow_x + slope_y * flow_y - turn_limit * jnp.abs(slope_t) - thrust_limit * jnp.abs(slope_v)
    spread = peak_x * (plus_x - minus_x) + peak_y * (plus_y - minus_y) + turn_limit * (plus_t - minus_t) + thrust_limit * (plus_v - minus_v)
    return drift + 0.5 * spread


def reference(level_set, wind_field, target_mask, target_depth):
    heading_step = 2.0 * math.pi / NTH
    speed_step = (speed_high - speed_low) / (NV - 1)
    speed_row = speed_low + jnp.arange(NV, dtype=jnp.int32).astype(jnp.float32) * speed_step
    angles = jnp.arange(NTH, dtype=jnp.int32).astype(jnp.float32) * heading_step
    cosine_row = jnp.cos(angles)
    sine_row = jnp.sin(angles)
    wind_x = wind_field[0]
    wind_y = wind_field[1]
    target = jnp.where(target_mask == 1, -target_depth, target_depth)[:, None, None, :]
    products_x = cosine_row[:, None] * speed_row[None, :]
    products_y = sine_row[:, None] * speed_row[None, :]

    def plane_peak(plane_index):
        row_x = lax.dynamic_slice_in_dim(wind_x, plane_index, 1, 0)
        row_y = lax.dynamic_slice_in_dim(wind_y, plane_index, 1, 0)
        top_x = jnp.max(jnp.abs(products_x[None, :, :, None] + row_x[:, None, None, :]))
        top_y = jnp.max(jnp.abs(products_y[None, :, :, None] + row_y[:, None, None, :]))
        return jnp.stack([top_x, top_y])

    peaks = jnp.max(lax.map(plane_peak, jnp.arange(NX, dtype=jnp.int32)), axis=0)
    peak_x = peaks[0]
    peak_y = peaks[1]
    time_step = courant / (peak_x / spacing + peak_y / spacing + turn_limit / heading_step + thrust_limit / speed_step)
    speeds = speed_row.reshape(1, 1, NV, 1)
    cosines = cosine_row.reshape(1, NTH, 1, 1)
    sines = sine_row.reshape(1, NTH, 1, 1)

    def rate_all(values):
        padded = jnp.pad(values, ((0, 0), (3, 3), (0, 0), (0, 0)), mode="wrap")
        padded = jnp.pad(padded, ((3, 3), (0, 0), (0, 0), (0, 0)), mode="edge")

        def one_block(block_index):
            start = (block_index * 3).astype(jnp.int32)
            block = lax.dynamic_slice_in_dim(padded, start, 9, 0)
            row_x = lax.dynamic_slice_in_dim(wind_x, start, 3, 0)[:, None, None, :]
            row_y = lax.dynamic_slice_in_dim(wind_y, start, 3, 0)[:, None, None, :]
            return hamilton(block, heading_step, speed_step, speeds, cosines, sines, row_x, row_y, peak_x, peak_y)

        blocks = lax.map(one_block, jnp.arange(NX // 3, dtype=jnp.int32))
        return blocks.reshape(NX, NTH, NV, NY)

    section_one = jnp.minimum(level_set + time_step * rate_all(level_set), target)
    section_two = jnp.minimum(0.75 * level_set + 0.25 * (section_one + time_step * rate_all(section_one)), target)
    level_next = jnp.minimum((1.0 / 3.0) * level_set + (2.0 / 3.0) * (section_two + time_step * rate_all(section_two)), target)
    return level_next
```

```python
import functools
import math

import jax
import jax.numpy as jnp
import numpy as np
from jax import lax
from jax.experimental import pallas as pl
from jax.experimental.pallas import tpu as pltpu
from jax.sharding import PartitionSpec as P

epsilon = 1e-06
courant = 0.5
spacing = 0.05
turn_limit = 1.0
thrust_limit = 0.5
speed_low = 0.5
speed_high = 1.5
rim = 3


def inverse(value):
    return pl.reciprocal(value, approx=True)


def weights_of(e1, e2, turn, eps):
    level = turn * turn * (4.0 / 3.0) + eps
    ia = inverse(level + e2 * (e2 + turn))
    ib = inverse(level + e2 * e1)
    ic = inverse(level + e1 * (e1 - turn))
    return ia * ia, ib * ib * 6.0, ic * ic


def sides(fl, f0, fr, a2, a1, b1, b0, c0, c1):
    a3 = a1 * 3.0
    c3 = c0 * 3.0
    minus = ((fl + fl) * a2 + f0 * c3) * inverse(a2 + b1 + c3)
    plus = ((fr + fr) * c1 + f0 * a3) * inverse(c1 + b0 + a3)
    return minus, plus


def row_terms(cells, step):
    count = len(cells) - 2 * rim
    eps = epsilon * step * step
    slope = [cells[i + 1] - cells[i] for i in range(len(cells) - 1)]
    bend = {m: slope[m + 3] - slope[m + 2] for m in range(-2, count + 2)}
    turn = {m: bend[m + 1] - bend[m] for m in range(-2, count + 1)}
    jerk = {m: turn[m] - turn[m - 1] for m in range(-1, count + 1)}
    a, b, c = {}, {}, {}
    for m in turn:
        a[m], b[m], c[m] = weights_of(bend[m], bend[m + 1], turn[m], eps)
    out = []
    for i in range(count):
        base = (cells[i + 4] - cells[i + 2]) * 6.0 - (turn[i - 1] + turn[i])
        minus, plus = sides(
            jerk[i - 1], jerk[i], jerk[i + 1], a[i - 2], a[i - 1], b[i - 1], b[i], c[i], c[i + 1]
        )
        out.append((base + (plus - minus), (plus + minus) - jerk[i]))
    return out


def tile_terms(cell, axis, step):
    count = cell.shape[axis]
    eps = epsilon * step * step
    place = lax.broadcasted_iota(jnp.int32, cell.shape, axis)
    first = place == 0
    last = place == count - 1

    def after(value, by=1):
        return pltpu.roll(value, count - by, axis)

    def before(value):
        return pltpu.roll(value, 1, axis)

    ahead = jnp.where(last, 0.0, after(cell) - cell)
    behind = before(ahead)
    bend = ahead - behind
    wrapped = before(bend)
    turn_lo = bend - jnp.where(first, 0.0, wrapped)
    turn_hi = jnp.where(last, -bend, after(turn_lo))
    jerk = turn_hi - turn_lo
    jerk_l = jnp.where(first, bend, before(jerk))
    jerk_r = jnp.where(last, bend, after(jerk))
    bend_l = jnp.where(first, 0.0, wrapped)
    level = turn_lo * turn_lo * (4.0 / 3.0) + eps
    ia = inverse(level + bend * (bend + turn_lo))
    ib = inverse(level + bend * bend_l)
    turn_ring = jnp.where(first, -wrapped, turn_lo)
    level_ring = turn_ring * turn_ring * (4.0 / 3.0) + eps
    ic = inverse(level_ring + wrapped * (wrapped - turn_ring))
    ib_ring = jnp.where(first, inverse(level_ring), ib)
    a1 = ia * ia
    b1 = ib * ib * 6.0
    c_low = ic * ic
    b0 = after(ib_ring * ib_ring * 6.0)
    flat = 1.0 / (eps * eps)
    a2 = jnp.where(first, flat, before(a1))
    c0 = after(c_low)
    c1 = jnp.where(last, flat, after(c_low, 2))
    base = (ahead + behind) * 6.0 - (turn_lo + turn_hi)
    minus, plus = sides(jerk_l, jerk, jerk_r, a2, a1, b1, b0, c0, c1)
    return base + (plus - minus), (plus + minus) - jerk


def splat(row, like):
    return jnp.broadcast_to(row, like)


def inner_kernel(split, speed_step, s_ref, wind_ref, taby_ref, *rest):
    planes, headings = s_ref.shape[:2]
    tile = s_ref.shape[2:]
    gain = 1.0 / (12.0 * spacing)
    gain_v = thrust_limit / (12.0 * speed_step)
    if split:
        part_ref, extra_ref = rest
    else:
        pk_ref, part_ref = rest

    def plane(i, carry):
        wind = splat(wind_ref[1, pl.ds(i, 1), :] * gain, tile)

        def heading(j, inner):
            cell = s_ref[i, j]
            mean, gap = tile_terms(cell, 1, spacing)
            mean_v, gap_v = tile_terms(cell, 0, speed_step)
            part = mean * (taby_ref[j] + wind) + gain_v * (gap_v - jnp.abs(mean_v))
            if split:
                part_ref[i, j] = part
                extra_ref[i, j] = gap
            else:
                part_ref[i, j] = part + gap * splat(pk_ref[1:2, :] * gain, tile)
            return inner

        return lax.fori_loop(0, headings, heading, carry)

    lax.fori_loop(0, planes, plane, 0)


def peaks_into(pk_ref, gathered_ref, bounds, heading_step, speed_step):
    peaks = []
    for q in range(2):
        rows = [gathered_ref[g, q] for g in range(gathered_ref.shape[0])]
        top = jnp.max(functools.reduce(jnp.maximum, rows), axis=(0, 1), keepdims=True)
        low = jnp.min(functools.reduce(jnp.minimum, rows), axis=(0, 1), keepdims=True)
        peaks.append(jnp.maximum(top + bounds[q][1], -(low + bounds[q][0])))
    time_step = courant / (
        peaks[0] / spacing
        + peaks[1] / spacing
        + turn_limit / heading_step
        + thrust_limit / speed_step
    )
    width = pk_ref.shape[1]
    for row, value in enumerate(peaks + [time_step]):
        pk_ref[row : row + 1, :] = splat(value, (1, width))


def outer_kernel(
    section, bounds, heading_step, speed_step, ends_ref, *refs
):
    refs = list(refs)
    base_ref = None if section == 1 else refs.pop(0)
    s_ref, part_ref = refs.pop(0), refs.pop(0)
    extra_ref = refs.pop(0) if section == 1 else None
    xlo_ref, xhi_ref, tlo_ref, thi_ref = (refs.pop(0) for _ in range(4))
    wind_ref, tabx_ref, mask_ref, depth_ref = (refs.pop(0) for _ in range(4))
    if section == 1:
        gathered_ref = refs.pop(0)
    else:
        pk_ref = refs.pop(0)
    out_ref = refs.pop(0)
    if section < 3:
        edge_refs = [refs.pop(0) for _ in range(4)]
    if section == 1:
        pk_ref = refs.pop(0)
    acc_ref = refs.pop(0)
    planes, headings = s_ref.shape[:2]
    tile = s_ref.shape[2:]
    gain = 1.0 / (12.0 * spacing)
    gain_t = turn_limit / (12.0 * heading_step)
    if section == 1:
        peaks_into(pk_ref, gathered_ref, bounds, heading_step, speed_step)
    at_low = ends_ref[0] == 1
    at_high = ends_ref[1] == 1

    def along_x(j, carry):
        cells = [s_ref[i, j] for i in range(planes)]
        lows = [jnp.where(at_low, cells[0], xlo_ref[k, j]) for k in range(rim)]
        highs = [jnp.where(at_high, cells[-1], xhi_ref[k, j]) for k in range(rim)]
        peak = splat(pk_ref[0:1, :] * gain, tile)
        table = tabx_ref[j]
        for i, (mean, gap) in enumerate(row_terms(lows + cells + highs, spacing)):
            flow = table + splat(wind_ref[0, i : i + 1, :] * gain, tile)
            total = part_ref[i, j] + (mean * flow + gap * peak)
            if section == 1:
                total = total + extra_ref[i, j] * splat(pk_ref[1:2, :] * gain, tile)
            acc_ref[i, j] = total
        return carry

    lax.fori_loop(0, headings, along_x, 0)

    def along_t(i, carry):
        cells = (
            [tlo_ref[i, k] for k in range(rim)]
            + [s_ref[i, j] for j in range(headings)]
            + [thi_ref[i, k] for k in range(rim)]
        )
        step = splat(pk_ref[2:3, :], tile)
        depth = depth_ref[pl.ds(i, 1), :]
        target = splat(jnp.where(mask_ref[pl.ds(i, 1), :] == 1, -depth, depth), tile)
        for j, (mean, gap) in enumerate(row_terms(cells, heading_step)):
            rate = acc_ref[i, j] + gain_t * (gap - jnp.abs(mean))
            moved = cells[j + rim] + step * rate
            if section == 2:
                moved = 0.75 * base_ref[i, j] + 0.25 * moved
            if section == 3:
                moved = (1.0 / 3.0) * base_ref[i, j] + (2.0 / 3.0) * moved
            result = jnp.minimum(moved, target)
            out_ref[i, j] = result
            if section < 3 and j < rim:
                edge_refs[2][i, j] = result
            if section < 3 and j >= headings - rim:
                edge_refs[3][i, j - (headings - rim)] = result
        return carry

    lax.fori_loop(0, planes, along_t, 0)
    if section < 3:
        edge_refs[0][...] = out_ref[:rim]
        edge_refs[1][...] = out_ref[planes - rim :]


def swap(edges):
    size_x, size_t = lax.axis_size("gx"), lax.axis_size("head")
    x_up = [(i, i + 1) for i in range(size_x - 1)]
    x_down = [(j, i) for i, j in x_up]
    t_up = [(i, (i + 1) % size_t) for i in range(size_t)]
    t_down = [(j, i) for i, j in t_up]
    x_low, x_high, t_low, t_high = edges
    from_low = lax.ppermute(x_high, "gx", x_up)
    from_high = lax.ppermute(x_low, "gx", x_down)
    from_left = lax.ppermute(t_high, "head", t_up)
    from_right = lax.ppermute(t_low, "head", t_down)
    return from_low, from_high, from_left, from_right


def local(level_set, wind_field, target_mask, target_depth):
    planes, headings, speed_count, cross_count = level_set.shape
    heading_total = headings * lax.axis_size("head")
    heading_step = 2.0 * math.pi / heading_total
    speed_step = (speed_high - speed_low) / (speed_count - 1)
    gain = 1.0 / (12.0 * spacing)
    speed_row = np.float32(speed_low) + np.arange(speed_count, dtype=np.float32) * np.float32(
        speed_step
    )
    angles = np.arange(heading_total, dtype=np.float32) * np.float32(heading_step)
    bounds, tables = [], []
    for wave in (np.cos(angles), np.sin(angles)):
        product = wave[:, None] * speed_row[None, :]
        bounds.append((float(product.min()), float(product.max())))
        tables.append(product * np.float32(gain))
    first_heading = lax.axis_index("head") * headings
    position = lax.axis_index("gx")
    ends = jnp.stack([position == 0, position == lax.axis_size("gx") - 1]).astype(jnp.int32)
    tables = lax.dynamic_slice_in_dim(jnp.asarray(np.stack(tables)), first_heading, headings, 1)
    tables = jnp.broadcast_to(tables[..., None], (2, headings, speed_count, cross_count))
    gathered = lax.all_gather(wind_field, "gx")

    vmem = pl.BlockSpec(memory_space=pltpu.VMEM)
    smem = pl.BlockSpec(memory_space=pltpu.SMEM)
    field = jax.ShapeDtypeStruct(level_set.shape, jnp.float32)
    x_edge = jax.ShapeDtypeStruct((rim,) + level_set.shape[1:], jnp.float32)
    t_edge = jax.ShapeDtypeStruct((planes, rim, speed_count, cross_count), jnp.float32)
    pk_shape = jax.ShapeDtypeStruct((8, cross_count), jnp.float32)
    cells = math.prod(level_set.shape)

    def call(kernel, ins, outs, scratch, work, scalar_first):
        specs = [vmem] * len(ins)
        if scalar_first:
            specs[0] = smem
        return pl.pallas_call(
            kernel,
            out_shape=outs,
            in_specs=specs,
            out_specs=[vmem] * len(outs),
            scratch_shapes=scratch,
            compiler_params=pltpu.CompilerParams(vmem_limit_bytes=16 * 1024 * 1024),
            cost_estimate=pl.CostEstimate(
                flops=work * cells, bytes_accessed=12 * cells, transcendentals=0
            ),
        )(*ins)

    values, pk = level_set, None
    edges = (
        level_set[:rim],
        level_set[planes - rim :],
        level_set[:, :rim],
        level_set[:, headings - rim :],
    )
    for section in (1, 2, 3):
        ghosts = swap(edges)
        inner = functools.partial(inner_kernel, section == 1, speed_step)
        ins = [values, wind_field, tables[1]] + ([] if section == 1 else [pk])
        parts = call(inner, ins, [field] * (2 if section == 1 else 1), [], 120, False)
        outer = functools.partial(outer_kernel, section, bounds, heading_step, speed_step)
        ins = [ends] + ([] if section == 1 else [level_set]) + [values, *parts, *ghosts]
        ins += [wind_field, tables[0], target_mask, target_depth]
        ins += [gathered] if section == 1 else [pk]
        outs = [field]
        if section < 3:
            outs += [x_edge, x_edge, t_edge, t_edge]
        if section == 1:
            outs += [pk_shape]
        scratch = [pltpu.VMEM(level_set.shape, jnp.float32)]
        results = call(outer, ins, outs, scratch, 120, True)
        values = results[0]
        edges = results[1:5]
        if section == 1:
            pk = results[5]
    return values


def solution(mesh):
    return jax.shard_map(
        local,
        mesh=mesh,
        in_specs=(P("gx", "head", None, None), P(None, "gx", None), P("gx", None), P("gx", None)),
        out_specs=P("gx", "head", None, None),
        check_vma=False,
    )
```

```python
import functools
import math

import jax
import jax.numpy as jnp
import numpy as np
from jax import lax
from jax.experimental import pallas as pl
from jax.experimental.pallas import tpu as pltpu
from jax.sharding import PartitionSpec as P

epsilon = 1e-06
courant = 0.5
spacing = 0.05
turn_limit = 1.0
thrust_limit = 0.5
speed_low = 0.5
speed_high = 1.5
rim = 3


def inverse(value):
    return pl.reciprocal(value, approx=True)


def weights_of(e1, e2, turn, eps):
    level = turn * turn * (4.0 / 3.0) + eps
    ia = inverse(level + e2 * (e2 + turn))
    ib = inverse(level + e2 * e1)
    ic = inverse(level + e1 * (e1 - turn))
    return ia * ia, ib * ib * 6.0, ic * ic


def sides(fl, f0, fr, a2, a1, b1, b0, c0, c1):
    a3 = a1 * 3.0
    c3 = c0 * 3.0
    minus = ((fl + fl) * a2 + f0 * c3) * inverse(a2 + b1 + c3)
    plus = ((fr + fr) * c1 + f0 * a3) * inverse(c1 + b0 + a3)
    return minus, plus


def row_terms(cells, step):
    count = len(cells) - 2 * rim
    eps = epsilon * step * step
    slope = [cells[i + 1] - cells[i] for i in range(len(cells) - 1)]
    bend = {m: slope[m + 3] - slope[m + 2] for m in range(-2, count + 2)}
    turn = {m: bend[m + 1] - bend[m] for m in range(-2, count + 1)}
    jerk = {m: turn[m] - turn[m - 1] for m in range(-1, count + 1)}
    a, b, c = {}, {}, {}
    for m in turn:
        a[m], b[m], c[m] = weights_of(bend[m], bend[m + 1], turn[m], eps)
    out = []
    for i in range(count):
        base = (cells[i + 4] - cells[i + 2]) * 6.0 - (turn[i - 1] + turn[i])
        minus, plus = sides(
            jerk[i - 1], jerk[i], jerk[i + 1], a[i - 2], a[i - 1], b[i - 1], b[i], c[i], c[i + 1]
        )
        out.append((base + (plus - minus), (plus + minus) - jerk[i]))
    return out


def tile_terms(cell, step):
    count = cell.shape[1]
    eps = epsilon * step * step
    flat = 1.0 / (eps * eps)
    place = lax.broadcasted_iota(jnp.int32, cell.shape, 1)

    def after(value, by=1):
        return pltpu.roll(value, count - by, 1)

    def before(value, by=1):
        return pltpu.roll(value, by, 1)

    up1 = jnp.where(place == count - 1, cell, after(cell))
    up2 = jnp.where(place >= count - 2, up1, after(cell, 2))
    dn1 = jnp.where(place == 0, cell, before(cell))
    dn2 = jnp.where(place <= 1, dn1, before(cell, 2))
    ahead = up1 - cell
    behind = cell - dn1
    bend_l = behind - (dn1 - dn2)
    bend = ahead - behind
    bend_r = (up2 - up1) - ahead
    turn_l = bend - bend_l
    turn_r = bend_r - bend
    jerk = turn_r - turn_l
    level_l = turn_l * turn_l * (4.0 / 3.0) + eps
    level_r = turn_r * turn_r * (4.0 / 3.0) + eps
    ia = inverse(level_l + bend * (bend + turn_l))
    ib = inverse(level_l + bend * bend_l)
    jb = inverse(level_r + bend * bend_r)
    jc = inverse(level_r + bend * (bend - turn_r))
    a1 = ia * ia
    c0 = jc * jc
    a2 = jnp.where(place == 0, flat, before(a1))
    c1 = jnp.where(place == count - 1, flat, after(c0))
    jerk_l = jnp.where(place == 0, bend, before(jerk))
    jerk_r = jnp.where(place == count - 1, bend, after(jerk))
    base = (ahead + behind) * 6.0 - (turn_l + turn_r)
    minus, plus = sides(
        jerk_l, jerk, jerk_r, a2, a1, ib * ib * 6.0, jb * jb * 6.0, c0, c1
    )
    return base + (plus - minus), (plus + minus) - jerk


def splat(row, like):
    return jnp.broadcast_to(row, like)


def inner_kernel(split, speed_step, s_ref, wind_ref, tab_ref, *rest):
    planes, headings, speeds, width = s_ref.shape
    tile = (speeds, width)
    gain = 1.0 / (12.0 * spacing)
    gain_v = thrust_limit / (12.0 * speed_step)
    if split:
        part_ref, extra_ref = rest
    else:
        pk_ref, part_ref = rest
    cells = planes * headings
    group = 8
    s_rows = s_ref.reshape(cells * speeds, width)
    part_rows = part_ref.reshape(cells * speeds, width)

    def speed_group(g, carry):
        start = jnp.minimum(g * group, cells - group) * speeds
        lines = [
            s_rows[pl.ds(start + k, group, stride=speeds), :] for k in range(speeds)
        ]
        ends = [lines[0]] * rim + lines + [lines[-1]] * rim
        for k, (mean, gap) in enumerate(row_terms(ends, speed_step)):
            part_rows[pl.ds(start + k, group, stride=speeds), :] = gain_v * (
                gap - jnp.abs(mean)
            )
        return carry

    lax.fori_loop(0, -(-cells // group), speed_group, 0)

    def plane(i, carry):
        wind = splat(wind_ref[i, 1:2, :] * gain, tile)
        for j in range(headings):
            mean, gap = tile_terms(s_ref[i, j], spacing)
            part = part_ref[i, j] + mean * (tab_ref[1, j] + wind)
            if split:
                part_ref[i, j] = part
                extra_ref[i, j] = gap
            else:
                part_ref[i, j] = part + gap * splat(pk_ref[1:2, :] * gain, tile)
        return carry

    lax.fori_loop(0, planes, plane, 0)


def opening_kernel(level_ref, wind_in, mask_in, depth_in, *refs):
    edge_refs, (wind_ref, mask_ref, depth_ref, most_ref, sems) = refs[:4], refs[4:]
    planes, headings = level_ref.shape[:2]
    pairs = [
        (wind_in, wind_ref),
        (level_ref.at[:rim], edge_refs[0]),
        (level_ref.at[planes - rim :], edge_refs[1]),
        (level_ref.at[:, :rim], edge_refs[2]),
        (level_ref.at[:, headings - rim :], edge_refs[3]),
        (mask_in, mask_ref),
        (depth_in, depth_ref),
    ]
    copies = [
        pltpu.make_async_copy(src, dst, sems.at[k]) for k, (src, dst) in enumerate(pairs)
    ]
    for copy in copies:
        copy.start()
    copies[0].wait()
    rows = [wind_ref[i] for i in range(planes)]
    most_ref[...] = jnp.zeros_like(most_ref)
    most_ref[0:2, :] = functools.reduce(jnp.maximum, rows)
    most_ref[2:4, :] = -functools.reduce(jnp.minimum, rows)
    for copy in copies[1:]:
        copy.wait()


def peaks_into(pk_ref, most_ref, bounds, heading_step, speed_step):
    most = jnp.max(most_ref[...], axis=1, keepdims=True)
    peaks = [
        jnp.maximum(most[q : q + 1] + bounds[q][1], most[q + 2 : q + 3] - bounds[q][0])
        for q in range(2)
    ]
    time_step = courant / (
        peaks[0] / spacing
        + peaks[1] / spacing
        + turn_limit / heading_step
        + thrust_limit / speed_step
    )
    width = pk_ref.shape[1]
    for row, value in enumerate(peaks + [time_step]):
        pk_ref[row : row + 1, :] = splat(value, (1, width))


def outer_kernel(
    section, bounds, heading_step, speed_step, ends_ref, *refs
):
    refs = list(refs)
    base_ref = None if section == 1 else refs.pop(0)
    s_ref, part_ref = refs.pop(0), refs.pop(0)
    extra_ref = refs.pop(0) if section == 1 else None
    xlo_ref, xhi_ref, tlo_ref, thi_ref = (refs.pop(0) for _ in range(4))
    wind_ref, tab_ref, mask_ref, depth_ref = (refs.pop(0) for _ in range(4))
    if section == 1:
        most_ref = refs.pop(0)
    else:
        pk_ref = refs.pop(0)
    out_ref = refs.pop(0)
    if section < 3:
        edge_refs = [refs.pop(0) for _ in range(4)]
    if section == 1:
        pk_ref = refs.pop(0)
    acc_ref = refs.pop(0)
    planes, headings = s_ref.shape[:2]
    tile = s_ref.shape[2:]
    gain = 1.0 / (12.0 * spacing)
    gain_t = turn_limit / (12.0 * heading_step)
    if section == 1:
        peaks_into(pk_ref, most_ref, bounds, heading_step, speed_step)
    at_low = ends_ref[0] == 1
    at_high = ends_ref[1] == 1

    def along_x(j, carry):
        cells = [s_ref[i, j] for i in range(planes)]
        lows = [jnp.where(at_low, cells[0], xlo_ref[k, j]) for k in range(rim)]
        highs = [jnp.where(at_high, cells[-1], xhi_ref[k, j]) for k in range(rim)]
        peak = splat(pk_ref[0:1, :] * gain, tile)
        table = tab_ref[0, j]
        for i, (mean, gap) in enumerate(row_terms(lows + cells + highs, spacing)):
            flow = table + splat(wind_ref[i, 0:1, :] * gain, tile)
            total = part_ref[i, j] + (mean * flow + gap * peak)
            if section == 1:
                total = total + extra_ref[i, j] * splat(pk_ref[1:2, :] * gain, tile)
            acc_ref[i, j] = total
        return carry

    lax.fori_loop(0, headings, along_x, 0)

    def along_t(i, carry):
        cells = (
            [tlo_ref[i, k] for k in range(rim)]
            + [s_ref[i, j] for j in range(headings)]
            + [thi_ref[i, k] for k in range(rim)]
        )
        step = splat(pk_ref[2:3, :], tile)
        depth = depth_ref[pl.ds(i, 1), :]
        target = splat(jnp.where(mask_ref[pl.ds(i, 1), :] == 1, -depth, depth), tile)
        for j, (mean, gap) in enumerate(row_terms(cells, heading_step)):
            rate = acc_ref[i, j] + gain_t * (gap - jnp.abs(mean))
            moved = cells[j + rim] + step * rate
            if section == 2:
                moved = 0.75 * base_ref[i, j] + 0.25 * moved
            if section == 3:
                moved = (1.0 / 3.0) * base_ref[i, j] + (2.0 / 3.0) * moved
            result = jnp.minimum(moved, target)
            out_ref[i, j] = result
            if section < 3 and j < rim:
                edge_refs[2][i, j] = result
            if section < 3 and j >= headings - rim:
                edge_refs[3][i, j - (headings - rim)] = result
        return carry

    lax.fori_loop(0, planes, along_t, 0)
    if section < 3:
        edge_refs[0][...] = out_ref[:rim]
        edge_refs[1][...] = out_ref[planes - rim :]


def swap(edges):
    size_x, size_t = lax.axis_size("gx"), lax.axis_size("head")
    x_up = [(i, i + 1) for i in range(size_x - 1)]
    x_down = [(j, i) for i, j in x_up]
    t_up = [(i, (i + 1) % size_t) for i in range(size_t)]
    t_down = [(j, i) for i, j in t_up]
    x_low, x_high, t_low, t_high = edges
    from_low = lax.ppermute(x_high, "gx", x_up)
    from_high = lax.ppermute(x_low, "gx", x_down)
    from_left = lax.ppermute(t_high, "head", t_up)
    from_right = lax.ppermute(t_low, "head", t_down)
    return from_low, from_high, from_left, from_right


def most_of_all(most):
    size, reach = lax.axis_size("gx"), 1
    while reach < size:
        if size & (size - 1):
            pairs = [(i, (i + reach) % size) for i in range(size)]
        else:
            pairs = [(i, i ^ reach) for i in range(size)]
        most = jnp.maximum(most, lax.ppermute(most, "gx", pairs))
        reach *= 2
    return most


def local(level_set, wind_field, target_mask, target_depth):
    planes, headings, speed_count, cross_count = level_set.shape
    heading_total = headings * lax.axis_size("head")
    heading_step = 2.0 * math.pi / heading_total
    speed_step = (speed_high - speed_low) / (speed_count - 1)
    gain = 1.0 / (12.0 * spacing)
    speed_row = np.float32(speed_low) + np.arange(speed_count, dtype=np.float32) * np.float32(
        speed_step
    )
    angles = np.arange(heading_total, dtype=np.float32) * np.float32(heading_step)
    bounds, tables = [], []
    for wave in (np.cos(angles), np.sin(angles)):
        product = wave[:, None] * speed_row[None, :]
        bounds.append((float(product.min()), float(product.max())))
        tables.append(product * np.float32(gain))
    first_heading = lax.axis_index("head") * headings
    position = lax.axis_index("gx")
    ends = jnp.stack([position == 0, position == lax.axis_size("gx") - 1]).astype(jnp.int32)
    tables = np.stack(tables)[..., None] * np.ones(cross_count, np.float32)
    tables = lax.dynamic_slice_in_dim(jnp.asarray(tables), first_heading, headings, 1)

    vmem = pl.BlockSpec(memory_space=pltpu.VMEM)
    smem = pl.BlockSpec(memory_space=pltpu.SMEM)
    field = jax.ShapeDtypeStruct(level_set.shape, jnp.float32)
    x_edge = jax.ShapeDtypeStruct((rim,) + level_set.shape[1:], jnp.float32)
    t_edge = jax.ShapeDtypeStruct((planes, rim, speed_count, cross_count), jnp.float32)
    pk_shape = jax.ShapeDtypeStruct((8, cross_count), jnp.float32)
    cells = math.prod(level_set.shape)

    def call(kernel, ins, outs, scratch, work, scalar_first):
        specs = [vmem] * len(ins)
        if scalar_first:
            specs[0] = smem
        return pl.pallas_call(
            kernel,
            out_shape=outs,
            in_specs=specs,
            out_specs=[vmem] * len(outs),
            scratch_shapes=scratch,
            compiler_params=pltpu.CompilerParams(vmem_limit_bytes=16 * 1024 * 1024),
            cost_estimate=pl.CostEstimate(
                flops=work * cells, bytes_accessed=12 * cells, transcendentals=0
            ),
        )(*ins)

    hbm = pl.BlockSpec(memory_space=pltpu.HBM)
    *edges, wind, mask, depth, most = pl.pallas_call(
        opening_kernel,
        out_shape=[x_edge, x_edge, t_edge, t_edge]
        + [
            jax.ShapeDtypeStruct((planes, 2, cross_count), jnp.float32),
            jax.ShapeDtypeStruct(target_mask.shape, target_mask.dtype),
            jax.ShapeDtypeStruct(target_depth.shape, jnp.float32),
            pk_shape,
        ],
        in_specs=[hbm] * 4,
        out_specs=[vmem] * 8,
        scratch_shapes=[pltpu.SemaphoreType.DMA((7,))],
        cost_estimate=pl.CostEstimate(flops=0, bytes_accessed=8 * cells, transcendentals=0),
    )(level_set, jnp.transpose(wind_field, (1, 0, 2)), target_mask, target_depth)
    values, pk = level_set, None
    for section in (1, 2, 3):
        ghosts = swap(edges)
        if section == 1:
            most = most_of_all(most)
        inner = functools.partial(inner_kernel, section == 1, speed_step)
        ins = [values, wind, tables] + ([] if section == 1 else [pk])
        parts = call(inner, ins, [field] * (2 if section == 1 else 1), [], 120, False)
        outer = functools.partial(outer_kernel, section, bounds, heading_step, speed_step)
        ins = [ends] + ([] if section == 1 else [level_set]) + [values, *parts, *ghosts]
        ins += [wind, tables, mask, depth]
        ins += [most] if section == 1 else [pk]
        outs = [field]
        if section < 3:
            outs += [x_edge, x_edge, t_edge, t_edge]
        if section == 1:
            outs += [pk_shape]
        scratch = [pltpu.VMEM(level_set.shape, jnp.float32)]
        results = call(outer, ins, outs, scratch, 120, True)
        values = results[0]
        edges = results[1:5]
        if section == 1:
            pk = results[5]
    return values


def solution(mesh):
    return jax.shard_map(
        local,
        mesh=mesh,
        in_specs=(P("gx", "head", None, None), P(None, "gx", None), P("gx", None), P("gx", None)),
        out_specs=P("gx", "head", None, None),
        check_vma=False,
    )
```

```python
import functools
import math

import jax
import jax.numpy as jnp
import numpy as np
from jax import lax
from jax.experimental import pallas as pl
from jax.experimental.pallas import tpu as pltpu
from jax.sharding import PartitionSpec as P

epsilon = 1e-06
courant = 0.5
spacing = 0.05
turn_limit = 1.0
thrust_limit = 0.5
speed_low = 0.5
speed_high = 1.5
rim = 3
gain = 1.0 / (12.0 * spacing)


def inverse(value):
    return pltpu.reciprocal(value, approx=True)


def weights_of(e1, e2, turn, eps):
    level = turn * turn * (4.0 / 3.0) + eps
    ia = inverse(level + e2 * (e2 + turn))
    ib = inverse(level + e2 * e1)
    ic = inverse(level + e1 * (e1 - turn))
    return ia * ia, ib * ib * 6.0, ic * ic


def sides(fl, f0, fr, a2, a1, b1, b0, c0, c1):
    a3 = a1 * 3.0
    c3 = c0 * 3.0
    minus = ((fl + fl) * a2 + f0 * c3) * inverse(a2 + b1 + c3)
    plus = ((fr + fr) * c1 + f0 * a3) * inverse(c1 + b0 + a3)
    return minus, plus


def row_terms(cells, step):
    count = len(cells) - 2 * rim
    eps = epsilon * step * step
    slope = [cells[i + 1] - cells[i] for i in range(len(cells) - 1)]
    bend = {m: slope[m + 3] - slope[m + 2] for m in range(-2, count + 2)}
    turn = {m: bend[m + 1] - bend[m] for m in range(-2, count + 1)}
    jerk = {m: turn[m] - turn[m - 1] for m in range(-1, count + 1)}
    a, b, c = {}, {}, {}
    for m in turn:
        a[m], b[m], c[m] = weights_of(bend[m], bend[m + 1], turn[m], eps)
    out = []
    for i in range(count):
        base = (cells[i + 4] - cells[i + 2]) * 6.0 - (turn[i - 1] + turn[i])
        minus, plus = sides(
            jerk[i - 1], jerk[i], jerk[i + 1], a[i - 2], a[i - 1], b[i - 1], b[i], c[i], c[i + 1]
        )
        out.append((base + (plus - minus), (plus + minus) - jerk[i]))
    return out


def tile_terms(cell, step):
    count = cell.shape[1]
    eps = epsilon * step * step
    flat = 1.0 / (eps * eps)
    place = lax.broadcasted_iota(jnp.int32, cell.shape, 1)

    def after(value, by=1):
        return pltpu.roll(value, count - by, 1)

    def before(value, by=1):
        return pltpu.roll(value, by, 1)

    up1 = jnp.where(place == count - 1, cell, after(cell))
    up2 = jnp.where(place >= count - 2, up1, after(cell, 2))
    dn1 = jnp.where(place == 0, cell, before(cell))
    dn2 = jnp.where(place <= 1, dn1, before(cell, 2))
    ahead = up1 - cell
    behind = cell - dn1
    bend_l = behind - (dn1 - dn2)
    bend = ahead - behind
    bend_r = (up2 - up1) - ahead
    turn_l = bend - bend_l
    turn_r = bend_r - bend
    jerk = turn_r - turn_l
    level_l = turn_l * turn_l * (4.0 / 3.0) + eps
    level_r = turn_r * turn_r * (4.0 / 3.0) + eps
    ia = inverse(level_l + bend * (bend + turn_l))
    ib = inverse(level_l + bend * bend_l)
    jb = inverse(level_r + bend * bend_r)
    jc = inverse(level_r + bend * (bend - turn_r))
    a1 = ia * ia
    c0 = jc * jc
    a2 = jnp.where(place == 0, flat, before(a1))
    c1 = jnp.where(place == count - 1, flat, after(c0))
    jerk_l = jnp.where(place == 0, bend, before(jerk))
    jerk_r = jnp.where(place == count - 1, bend, after(jerk))
    base = (ahead + behind) * 6.0 - (turn_l + turn_r)
    minus, plus = sides(
        jerk_l, jerk, jerk_r, a2, a1, ib * ib * 6.0, jb * jb * 6.0, c0, c1
    )
    return base + (plus - minus), (plus + minus) - jerk


def batches(total, most):
    return max(k for k in range(1, most + 1) if total % k == 0)


def splat(row, tile):
    return jnp.broadcast_to(row, tile)


def speeds_of(tile, speed_step):
    place = lax.broadcasted_iota(jnp.int32, tile, 0).astype(jnp.float32)
    return speed_low + place * speed_step


def odd_place(axis):
    return lax.rem(lax.axis_index(axis), 2) == 1


def speed_kernel(speed_step, s_ref, part_ref):
    planes, headings, speeds, width = s_ref.shape
    gain_v = thrust_limit / (12.0 * speed_step)
    cells = planes * headings
    group = 8
    s_rows = s_ref.reshape(cells * speeds, width)
    part_rows = part_ref.reshape(cells * speeds, width)
    groups = -(-cells // group)
    wide = batches(groups, 2)

    def step(n, carry):
        for k in range(wide):
            start = jnp.minimum((n * wide + k) * group, cells - group) * speeds
            lines = [
                s_rows[pl.ds(start + v, group, stride=speeds), :] for v in range(speeds)
            ]
            ends = [lines[0]] * rim + lines + [lines[-1]] * rim
            for v, (mean, gap) in enumerate(row_terms(ends, speed_step)):
                part_rows[pl.ds(start + v, group, stride=speeds), :] = gain_v * (
                    gap - jnp.abs(mean)
                )
        return carry

    lax.fori_loop(0, groups // wide, step, 0)


def cross_kernel(split, speed_step, s_ref, part_ref, wind_ref, waves_ref, *rest):
    planes, headings, speeds, width = s_ref.shape
    tile = (speeds, width)
    if split:
        out_ref, extra_ref = rest
    else:
        pk_ref, out_ref = rest
        peak = splat(pk_ref[1:2, :] * gain, tile)
    pace = speeds_of(tile, speed_step) * gain
    first = lax.axis_index("head") * headings
    wide = batches(headings, 2)

    def step(n, carry):
        for k in range(wide):
            j = n * wide + k
            table = splat(waves_ref[1, pl.ds(first + j, 1), :], tile) * pace
            for i in range(planes):
                mean, gap = tile_terms(s_ref[i, j], spacing)
                flow = table + splat(wind_ref[i, 1:2, :] * gain, tile)
                part = part_ref[i, j] + mean * flow
                if split:
                    out_ref[i, j] = part
                    extra_ref[i, j] = gap
                else:
                    out_ref[i, j] = part + gap * peak
        return carry

    lax.fori_loop(0, headings // wide, step, 0)


def heading_kernel(heading_step, s_ref, part_ref, near_ref, far_ref, out_ref):
    planes, headings = s_ref.shape[:2]
    gain_t = turn_limit / (12.0 * heading_step)
    odd = odd_place("head")
    wide = batches(planes, 3)

    def step(n, carry):
        for w in range(wide):
            i = n * wide + w
            ghosts = [(near_ref[i, k], far_ref[i, k]) for k in range(rim)]
            lows = [jnp.where(odd, near, far) for near, far in ghosts]
            highs = [jnp.where(odd, far, near) for near, far in ghosts]
            cells = lows + [s_ref[i, j] for j in range(headings)] + highs
            for j, (mean, gap) in enumerate(row_terms(cells, heading_step)):
                out_ref[i, j] = part_ref[i, j] + gain_t * (gap - jnp.abs(mean))
        return carry

    lax.fori_loop(0, planes // wide, step, 0)


def peaks_into(pk_ref, most, bounds, heading_step, speed_step):
    most = jnp.max(most, axis=1, keepdims=True)
    peaks = [
        jnp.maximum(most[q : q + 1] + bounds[q][1], most[q + 2 : q + 3] - bounds[q][0])
        for q in range(2)
    ]
    time_step = courant / (
        peaks[0] / spacing
        + peaks[1] / spacing
        + turn_limit / heading_step
        + thrust_limit / speed_step
    )
    width = pk_ref.shape[1]
    for row, value in enumerate(peaks + [time_step]):
        pk_ref[row : row + 1, :] = splat(value, (1, width))


def cut_edges(field_ref, x_near, x_far, t_near, t_far):
    planes, headings = field_ref.shape[:2]
    x_low = jnp.where(odd_place("gx"), 0, planes - rim)
    t_low = jnp.where(odd_place("head"), 0, headings - rim)
    for k in range(rim):
        x_near[k * headings : (k + 1) * headings] = field_ref[x_low + k]
        x_far[k * headings : (k + 1) * headings] = field_ref[planes - rim - x_low + k]
        for i in range(planes):
            t_near[i, k] = field_ref[i, t_low + k]
            t_far[i, k] = field_ref[i, headings - rim - t_low + k]


def section_kernel(section, bounds, heading_step, speed_step, *refs):
    refs = list(refs)
    base_ref = None if section == 1 else refs.pop(0)
    s_ref, part_ref = refs.pop(0), refs.pop(0)
    extra_ref = refs.pop(0) if section == 1 else None
    near_ref, far_ref = refs.pop(0), refs.pop(0)
    wind_ref, waves_ref, mask_ref, depth_ref = (refs.pop(0) for _ in range(4))
    if section == 1:
        most_refs = [refs.pop(0), refs.pop(0)]
    else:
        pk_ref = refs.pop(0)
    out_ref = refs.pop(0)
    if section < 3:
        edge_refs = [refs.pop(0) for _ in range(4)]
    if section == 1:
        pk_ref = refs.pop(0)
    flow_ref, target_ref = refs
    planes, headings = s_ref.shape[:2]
    tile = s_ref.shape[2:]
    if section == 1:
        most = jnp.maximum(most_refs[0][...], most_refs[1][...])
        peaks_into(pk_ref, most, bounds, heading_step, speed_step)
    for i in range(planes):
        depth = depth_ref[i : i + 1, :]
        target_ref[i] = splat(jnp.where(mask_ref[i : i + 1, :] == 1, -depth, depth), tile)
        flow_ref[i] = splat(wind_ref[i, 0:1, :] * gain, tile)
    odd = odd_place("gx")
    at_low = lax.axis_index("gx") == 0
    at_high = lax.axis_index("gx") == lax.axis_size("gx") - 1
    peak_x = splat(pk_ref[0:1, :] * gain, tile)
    peak_y = splat(pk_ref[1:2, :] * gain, tile)
    time_step = splat(pk_ref[2:3, :], tile)
    pace = speeds_of(tile, speed_step) * gain
    first = lax.axis_index("head") * headings
    wide = batches(headings, 3)

    def step(n, carry):
        for w in range(wide):
            j = n * wide + w
            cells = [s_ref[i, j] for i in range(planes)]
            ghosts = [(near_ref[k * headings + j], far_ref[k * headings + j]) for k in range(rim)]
            lows = [jnp.where(at_low, cells[0], jnp.where(odd, near, far)) for near, far in ghosts]
            highs = [jnp.where(at_high, cells[-1], jnp.where(odd, far, near)) for near, far in ghosts]
            table = splat(waves_ref[0, pl.ds(first + j, 1), :], tile) * pace
            for i, (mean, gap) in enumerate(row_terms(lows + cells + highs, spacing)):
                rate = part_ref[i, j] + (mean * (table + flow_ref[i]) + gap * peak_x)
                if section == 1:
                    rate = rate + extra_ref[i, j] * peak_y
                moved = cells[i] + time_step * rate
                if section == 2:
                    moved = 0.75 * base_ref[i, j] + 0.25 * moved
                if section == 3:
                    moved = (1.0 / 3.0) * base_ref[i, j] + (2.0 / 3.0) * moved
                out_ref[i, j] = jnp.minimum(moved, target_ref[i])
        return carry

    lax.fori_loop(0, headings // wide, step, 0)
    if section < 3:
        cut_edges(out_ref, *edge_refs)


def opening_kernel(level_ref, wind_ref, *refs):
    edge_refs, (wind_in, sides_in, rims_in, sems) = refs[:4], refs[4:]
    planes, headings = level_ref.shape[:2]
    pairs = [
        (wind_ref, wind_in),
        (level_ref.at[:rim], sides_in.at[0]),
        (level_ref.at[planes - rim :], sides_in.at[1]),
        (level_ref.at[:, :rim], rims_in.at[0]),
        (level_ref.at[:, headings - rim :], rims_in.at[1]),
    ]
    copies = [
        pltpu.make_async_copy(src, dst, sems.at[k]) for k, (src, dst) in enumerate(pairs)
    ]
    for copy in copies:
        copy.start()
    x_near, x_far, t_near, t_far = edge_refs
    copies[0].wait()
    rows = [wind_in[i] for i in range(planes)]
    spot = rim * headings
    x_near[spot] = jnp.zeros_like(x_near[spot])
    x_near[spot, 0:2, :] = functools.reduce(jnp.maximum, rows)
    x_near[spot, 2:4, :] = -functools.reduce(jnp.minimum, rows)
    for copy in copies[1:]:
        copy.wait()
    x_side = jnp.where(odd_place("gx"), 0, 1)
    t_side = jnp.where(odd_place("head"), 0, 1)
    for k in range(rim):
        x_near[k * headings : (k + 1) * headings] = sides_in[x_side, k]
        x_far[k * headings : (k + 1) * headings] = sides_in[1 - x_side, k]
    t_near[...] = rims_in[t_side]
    t_far[...] = rims_in[1 - t_side]


def trade(value, axis, reach, wrap=False):
    size = lax.axis_size(axis)
    pairs = [(i, i + 1) for i in range(reach, size - 1, 2)]
    if wrap and reach and size % 2 == 0:
        pairs.append((size - 1, 0))
    return lax.ppermute(value, axis, pairs + [(j, i) for i, j in pairs])


def local(level_set, wind_field, target_mask, target_depth):
    planes, headings, speed_count, cross_count = level_set.shape
    heading_total = headings * lax.axis_size("head")
    heading_step = 2.0 * math.pi / heading_total
    speed_step = (speed_high - speed_low) / (speed_count - 1)
    speed_row = np.float32(speed_low) + np.arange(speed_count, dtype=np.float32) * np.float32(
        speed_step
    )
    angles = np.arange(heading_total, dtype=np.float32) * np.float32(heading_step)
    waves = [np.cos(angles), np.sin(angles)]
    bounds = []
    for wave in waves:
        product = wave[:, None] * speed_row[None, :]
        bounds.append((float(product.min()), float(product.max())))
    waves = jnp.asarray(np.stack(waves)[..., None] * np.ones(cross_count, np.float32))

    vmem = pl.BlockSpec(memory_space=pltpu.VMEM)
    hbm = pl.BlockSpec(memory_space=pltpu.HBM)
    tile = (speed_count, cross_count)

    def shape(*dims):
        return jax.ShapeDtypeStruct(dims + tile, jnp.float32)

    field = shape(planes, headings)
    t_edge = shape(planes, rim)
    cells = math.prod(level_set.shape)

    def call(kernel, ins, outs, scratch=(), work=50):
        return pl.pallas_call(
            kernel,
            out_shape=outs,
            in_specs=[vmem] * len(ins),
            out_specs=[vmem] * len(outs),
            scratch_shapes=list(scratch),
            compiler_params=pltpu.CompilerParams(vmem_limit_bytes=16 * 1024 * 1024),
            cost_estimate=pl.CostEstimate(
                flops=work * cells, bytes_accessed=12 * cells, transcendentals=0
            ),
        )(*ins)

    wind = jnp.transpose(wind_field, (1, 0, 2))
    edges = pl.pallas_call(
        opening_kernel,
        out_shape=[shape(rim * headings + 1), shape(rim * headings), t_edge, t_edge],
        in_specs=[hbm] * 2,
        out_specs=[vmem] * 4,
        scratch_shapes=[
            pltpu.VMEM(wind.shape, jnp.float32),
            pltpu.VMEM((2, rim, headings) + tile, jnp.float32),
            pltpu.VMEM((2, planes, rim) + tile, jnp.float32),
            pltpu.SemaphoreType.DMA((5,)),
        ],
        cost_estimate=pl.CostEstimate(flops=0, bytes_accessed=8 * cells, transcendentals=0),
    )(level_set, wind)

    values, pk = level_set, None
    for section in (1, 2, 3):
        x_out, x_last, t_out, t_last = edges
        x_near = trade(x_out, "gx", 0)
        t_near = trade(t_out, "head", 0)
        t_far = trade(t_last, "head", 1, True)
        (part,) = call(functools.partial(speed_kernel, speed_step), [values], [field])
        x_last, x_near, part = lax.optimization_barrier((x_last, x_near, part))
        if section == 1:
            most = [x_out[-1], x_near[-1]]
            reach = 2
            while reach < lax.axis_size("gx"):
                both = jnp.maximum(*most)
                size = lax.axis_size("gx")
                if size & (size - 1):
                    pairs = [(i, (i + reach) % size) for i in range(size)]
                else:
                    pairs = [(i, i ^ reach) for i in range(size)]
                most = [both, lax.ppermute(both, "gx", pairs)]
                reach *= 2
        x_far = trade(x_last, "gx", 1)
        split = section == 1
        turning = functools.partial(heading_kernel, heading_step)
        (part,) = call(turning, [values, part, t_near, t_far], [field])
        cross = functools.partial(cross_kernel, split, speed_step)
        ins = [values, part, wind, waves] + ([] if split else [pk])
        part, *extra = call(cross, ins, [field] * (2 if split else 1))
        last = functools.partial(section_kernel, section, bounds, heading_step, speed_step)
        ins = ([] if split else [level_set]) + [values, part, *extra, x_near, x_far]
        ins += [wind, waves, target_mask, target_depth]
        ins += most if split else [pk]
        outs = [field]
        if section < 3:
            outs += [shape(rim * headings)] * 2 + [t_edge] * 2
        if split:
            outs += [shape()]
        rows = pltpu.VMEM((planes,) + tile, jnp.float32)
        results = call(last, ins, outs, [rows, rows])
        values, edges = results[0], results[1:5]
        if split:
            pk = results[5]
    return values


def solution(mesh):
    return jax.shard_map(
        local,
        mesh=mesh,
        in_specs=(P("gx", "head", None, None), P(None, "gx", None), P("gx", None), P("gx", None)),
        out_specs=P("gx", "head", None, None),
        check_vma=False,
    )
```

```python
import functools
import math

import jax
import jax.numpy as jnp
import numpy as np
from jax import lax
from jax.experimental import pallas as pl
from jax.experimental.pallas import tpu as pltpu
from jax.sharding import PartitionSpec as P

epsilon = 1e-06
courant = 0.5
spacing = 0.05
turn_limit = 1.0
thrust_limit = 0.5
speed_low = 0.5
speed_high = 1.5
rim = 3
gain = 1.0 / (12.0 * spacing)


def inverse(value):
    return pltpu.reciprocal(value, approx=True)


def weights_of(e1, e2, turn, eps):
    level = turn * turn * (4.0 / 3.0) + eps
    ia = inverse(level + e2 * (e2 + turn))
    ib = inverse(level + e2 * e1)
    ic = inverse(level + e1 * (e1 - turn))
    return ia * ia, ib * ib * 6.0, ic * ic


def sides(fl, f0, fr, a2, a1, b1, b0, c0, c1):
    a3 = a1 * 3.0
    c3 = c0 * 3.0
    minus = ((fl + fl) * a2 + f0 * c3) * inverse(a2 + b1 + c3)
    plus = ((fr + fr) * c1 + f0 * a3) * inverse(c1 + b0 + a3)
    return minus, plus


def row_terms(cells, step):
    count = len(cells) - 2 * rim
    eps = epsilon * step * step
    slope = [cells[i + 1] - cells[i] for i in range(len(cells) - 1)]
    bend = {m: slope[m + 3] - slope[m + 2] for m in range(-2, count + 2)}
    turn = {m: bend[m + 1] - bend[m] for m in range(-2, count + 1)}
    jerk = {m: turn[m] - turn[m - 1] for m in range(-1, count + 1)}
    a, b, c = {}, {}, {}
    for m in turn:
        a[m], b[m], c[m] = weights_of(bend[m], bend[m + 1], turn[m], eps)
    out = []
    for i in range(count):
        base = (cells[i + 4] - cells[i + 2]) * 6.0 - (turn[i - 1] + turn[i])
        minus, plus = sides(
            jerk[i - 1], jerk[i], jerk[i + 1], a[i - 2], a[i - 1], b[i - 1], b[i], c[i], c[i + 1]
        )
        out.append((base + (plus - minus), (plus + minus) - jerk[i]))
    return out


def tile_terms(cell, step):
    count = cell.shape[1]
    eps = epsilon * step * step
    flat = 1.0 / (eps * eps)
    place = lax.broadcasted_iota(jnp.int32, cell.shape, 1)

    def after(value, by=1):
        return pltpu.roll(value, count - by, 1)

    def before(value, by=1):
        return pltpu.roll(value, by, 1)

    up1 = jnp.where(place == count - 1, cell, after(cell))
    up2 = jnp.where(place >= count - 2, up1, after(cell, 2))
    dn1 = jnp.where(place == 0, cell, before(cell))
    dn2 = jnp.where(place <= 1, dn1, before(cell, 2))
    ahead = up1 - cell
    behind = cell - dn1
    bend_l = behind - (dn1 - dn2)
    bend = ahead - behind
    bend_r = (up2 - up1) - ahead
    turn_l = bend - bend_l
    turn_r = bend_r - bend
    jerk = turn_r - turn_l
    level_l = turn_l * turn_l * (4.0 / 3.0) + eps
    level_r = turn_r * turn_r * (4.0 / 3.0) + eps
    ia = inverse(level_l + bend * (bend + turn_l))
    ib = inverse(level_l + bend * bend_l)
    jb = inverse(level_r + bend * bend_r)
    jc = inverse(level_r + bend * (bend - turn_r))
    a1 = ia * ia
    c0 = jc * jc
    a2 = jnp.where(place == 0, flat, before(a1))
    c1 = jnp.where(place == count - 1, flat, after(c0))
    jerk_l = jnp.where(place == 0, bend, before(jerk))
    jerk_r = jnp.where(place == count - 1, bend, after(jerk))
    base = (ahead + behind) * 6.0 - (turn_l + turn_r)
    minus, plus = sides(
        jerk_l, jerk, jerk_r, a2, a1, ib * ib * 6.0, jb * jb * 6.0, c0, c1
    )
    return base + (plus - minus), (plus + minus) - jerk


def batches(total, most):
    return max(k for k in range(1, most + 1) if total % k == 0)


def splat(row, tile):
    return jnp.broadcast_to(row, tile)


def speeds_of(tile, speed_step):
    place = lax.broadcasted_iota(jnp.int32, tile, 0).astype(jnp.float32)
    return speed_low + place * speed_step


def odd_place(axis):
    return lax.rem(lax.axis_index(axis), 2) == 1


def extremes_of(wind_ref):
    rows = [wind_ref[i] for i in range(wind_ref.shape[0])]
    return functools.reduce(jnp.maximum, rows), -functools.reduce(jnp.minimum, rows)


def opening_kernel(level_ref, wind_ref, *refs):
    most_ref = refs[-1]
    top, low = extremes_of(wind_ref)
    most_ref[...] = jnp.zeros_like(most_ref)
    most_ref[0:2, :] = top
    most_ref[2:4, :] = low
    cut_edges(level_ref, *refs[:-1])


def speed_kernel(speed_step, s_ref, *refs):
    if len(refs) == 1:
        part_ref = refs[0]
    else:
        wind_ref, other_ref, part_ref, most_ref = refs
        top, low = extremes_of(wind_ref)
        most_ref[...] = other_ref[...]
        most_ref[0:2, :] = jnp.maximum(top, other_ref[0:2, :])
        most_ref[2:4, :] = jnp.maximum(low, other_ref[2:4, :])
    planes, headings, speeds, width = s_ref.shape
    gain_v = thrust_limit / (12.0 * speed_step)
    cells = planes * headings
    group = 8
    s_rows = s_ref.reshape(cells * speeds, width)
    part_rows = part_ref.reshape(cells * speeds, width)
    groups = -(-cells // group)
    wide = batches(groups, 2)

    def step(n, carry):
        for k in range(wide):
            start = jnp.minimum((n * wide + k) * group, cells - group) * speeds
            lines = [
                s_rows[pl.ds(start + v, group, stride=speeds), :] for v in range(speeds)
            ]
            ends = [lines[0]] * rim + lines + [lines[-1]] * rim
            for v, (mean, gap) in enumerate(row_terms(ends, speed_step)):
                part_rows[pl.ds(start + v, group, stride=speeds), :] = gain_v * (
                    gap - jnp.abs(mean)
                )
        return carry

    lax.fori_loop(0, groups // wide, step, 0)


def cross_kernel(split, speed_step, s_ref, part_ref, wind_ref, waves_ref, *rest):
    planes, headings, speeds, width = s_ref.shape
    tile = (speeds, width)
    if split:
        out_ref, extra_ref = rest
    else:
        pk_ref, out_ref = rest
        peak = splat(pk_ref[1:2, :] * gain, tile)
    pace = speeds_of(tile, speed_step) * gain
    first = lax.axis_index("head") * headings
    wide = batches(headings, 2)

    def step(n, carry):
        for k in range(wide):
            j = n * wide + k
            table = splat(waves_ref[1, pl.ds(first + j, 1), :], tile) * pace
            for i in range(planes):
                mean, gap = tile_terms(s_ref[i, j], spacing)
                flow = table + splat(wind_ref[i, 1:2, :] * gain, tile)
                part = part_ref[i, j] + mean * flow
                if split:
                    out_ref[i, j] = part
                    extra_ref[i, j] = gap
                else:
                    out_ref[i, j] = part + gap * peak
        return carry

    lax.fori_loop(0, headings // wide, step, 0)


def heading_kernel(heading_step, s_ref, part_ref, near_ref, far_ref, out_ref):
    planes, headings = s_ref.shape[:2]
    gain_t = turn_limit / (12.0 * heading_step)
    odd = odd_place("head")
    wide = batches(planes, 3)

    def step(n, carry):
        for w in range(wide):
            i = n * wide + w
            ghosts = [(near_ref[i * rim + k], far_ref[i * rim + k]) for k in range(rim)]
            lows = [jnp.where(odd, near, far) for near, far in ghosts]
            highs = [jnp.where(odd, far, near) for near, far in ghosts]
            cells = lows + [s_ref[i, j] for j in range(headings)] + highs
            for j, (mean, gap) in enumerate(row_terms(cells, heading_step)):
                out_ref[i, j] = part_ref[i, j] + gain_t * (gap - jnp.abs(mean))
        return carry

    lax.fori_loop(0, planes // wide, step, 0)


def peaks_into(pk_ref, most, bounds, heading_step, speed_step):
    most = jnp.max(most, axis=1, keepdims=True)
    peaks = [
        jnp.maximum(most[q : q + 1] + bounds[q][1], most[q + 2 : q + 3] - bounds[q][0])
        for q in range(2)
    ]
    time_step = courant / (
        peaks[0] / spacing
        + peaks[1] / spacing
        + turn_limit / heading_step
        + thrust_limit / speed_step
    )
    width = pk_ref.shape[1]
    for row, value in enumerate(peaks + [time_step]):
        pk_ref[row : row + 1, :] = splat(value, (1, width))


def cut_edges(field_ref, x_near, x_far, t_near, t_far):
    planes, headings = field_ref.shape[:2]
    x_low = jnp.where(odd_place("gx"), 0, planes - rim)
    t_low = jnp.where(odd_place("head"), 0, headings - rim)
    for k in range(rim):
        x_near[k * headings : (k + 1) * headings] = field_ref[x_low + k]
        x_far[k * headings : (k + 1) * headings] = field_ref[planes - rim - x_low + k]
        for i in range(planes):
            t_near[i * rim + k] = field_ref[i, t_low + k]
            t_far[i * rim + k] = field_ref[i, headings - rim - t_low + k]


def section_kernel(section, bounds, heading_step, speed_step, *refs):
    refs = list(refs)
    base_ref = None if section == 1 else refs.pop(0)
    s_ref, part_ref = refs.pop(0), refs.pop(0)
    extra_ref = refs.pop(0) if section == 1 else None
    near_ref, far_ref = refs.pop(0), refs.pop(0)
    wind_ref, waves_ref, mask_ref, depth_ref = (refs.pop(0) for _ in range(4))
    if section == 1:
        most_refs = [refs.pop(0), refs.pop(0)]
    else:
        pk_ref = refs.pop(0)
    out_ref = refs.pop(0)
    if section < 3:
        edge_refs = [refs.pop(0) for _ in range(4)]
    if section == 1:
        pk_ref = refs.pop(0)
    flow_ref, target_ref = refs
    planes, headings = s_ref.shape[:2]
    tile = s_ref.shape[2:]
    if section == 1:
        most = jnp.maximum(most_refs[0][...], most_refs[1][...])
        peaks_into(pk_ref, most, bounds, heading_step, speed_step)
    for i in range(planes):
        depth = depth_ref[i : i + 1, :]
        target_ref[i] = splat(jnp.where(mask_ref[i : i + 1, :] == 1, -depth, depth), tile)
        flow_ref[i] = splat(wind_ref[i, 0:1, :] * gain, tile)
    odd = odd_place("gx")
    at_low = lax.axis_index("gx") == 0
    at_high = lax.axis_index("gx") == lax.axis_size("gx") - 1
    peak_x = splat(pk_ref[0:1, :] * gain, tile)
    peak_y = splat(pk_ref[1:2, :] * gain, tile)
    time_step = splat(pk_ref[2:3, :], tile)
    pace = speeds_of(tile, speed_step) * gain
    first = lax.axis_index("head") * headings
    wide = batches(headings, 3)

    def step(n, carry):
        for w in range(wide):
            j = n * wide + w
            cells = [s_ref[i, j] for i in range(planes)]
            ghosts = [(near_ref[k * headings + j], far_ref[k * headings + j]) for k in range(rim)]
            lows = [jnp.where(at_low, cells[0], jnp.where(odd, near, far)) for near, far in ghosts]
            highs = [jnp.where(at_high, cells[-1], jnp.where(odd, far, near)) for near, far in ghosts]
            table = splat(waves_ref[0, pl.ds(first + j, 1), :], tile) * pace
            for i, (mean, gap) in enumerate(row_terms(lows + cells + highs, spacing)):
                rate = part_ref[i, j] + (mean * (table + flow_ref[i]) + gap * peak_x)
                if section == 1:
                    rate = rate + extra_ref[i, j] * peak_y
                moved = cells[i] + time_step * rate
                if section == 2:
                    moved = 0.75 * base_ref[i, j] + 0.25 * moved
                if section == 3:
                    moved = (1.0 / 3.0) * base_ref[i, j] + (2.0 / 3.0) * moved
                out_ref[i, j] = jnp.minimum(moved, target_ref[i])
        return carry

    lax.fori_loop(0, headings // wide, step, 0)
    if section < 3:
        cut_edges(out_ref, *edge_refs)


def trade(value, axis, reach, wrap=False):
    size = lax.axis_size(axis)
    pairs = [(i, i + 1) for i in range(reach, size - 1, 2)]
    if wrap and reach and size % 2 == 0:
        pairs.append((size - 1, 0))
    return lax.ppermute(value, axis, pairs + [(j, i) for i, j in pairs])


def local(level_set, wind_field, target_mask, target_depth):
    planes, headings, speed_count, cross_count = level_set.shape
    heading_total = headings * lax.axis_size("head")
    heading_step = 2.0 * math.pi / heading_total
    speed_step = (speed_high - speed_low) / (speed_count - 1)
    speed_row = np.float32(speed_low) + np.arange(speed_count, dtype=np.float32) * np.float32(
        speed_step
    )
    angles = np.arange(heading_total, dtype=np.float32) * np.float32(heading_step)
    waves = [np.cos(angles), np.sin(angles)]
    bounds = []
    for wave in waves:
        product = wave[:, None] * speed_row[None, :]
        bounds.append((float(product.min()), float(product.max())))
    waves = jnp.asarray(np.stack(waves)[..., None] * np.ones(cross_count, np.float32))

    vmem = pl.BlockSpec(memory_space=pltpu.VMEM)
    tile = (speed_count, cross_count)

    def shape(*dims):
        return jax.ShapeDtypeStruct(dims + tile, jnp.float32)

    field = shape(planes, headings)
    short = rim * headings
    middle = max(short + 1, rim * planes)

    def edge_shapes(far_first):
        x_shapes = [shape(middle + 1), shape(short)]
        return x_shapes[:: -1 if far_first else 1] + [shape(middle)] * 2

    cells = math.prod(level_set.shape)

    def call(kernel, ins, outs, scratch=(), work=0):
        return pl.pallas_call(
            kernel,
            out_shape=outs,
            in_specs=[vmem] * len(ins),
            out_specs=[vmem] * len(outs),
            scratch_shapes=list(scratch),
            compiler_params=pltpu.CompilerParams(vmem_limit_bytes=16 * 1024 * 1024),
            cost_estimate=pl.CostEstimate(
                flops=work * cells, bytes_accessed=work * cells, transcendentals=0
            ),
        )(*ins)

    wind = jnp.transpose(wind_field, (1, 0, 2))
    values, pk = level_set, None
    size = lax.axis_size("gx")

    def spread(most, reach):
        if size & (size - 1):
            pairs = [(i, (i + reach) % size) for i in range(size)]
        else:
            pairs = [(i, i ^ reach) for i in range(size)]
        return lax.ppermute(most, "gx", pairs)

    for section in (1, 2, 3):
        opening = section == 1
        speed = functools.partial(speed_kernel, speed_step)
        if opening:
            *edges, most = call(opening_kernel, [values, wind], edge_shapes(True) + [shape()])
            other = spread(most, 1)
        x_out, x_last, t_out, t_last = edges
        if opening:
            x_far = trade(x_last, "gx", 1)
        else:
            x_near = trade(x_out, "gx", 0)
        t_near = trade(t_out, "head", 0)
        t_far = trade(t_last, "head", 1, True)
        if opening:
            part, most = call(speed, [values, wind, other], [field, shape()])
            other = spread(most, 2)
            x_out, most = lax.optimization_barrier((x_out, most))
            x_near = trade(x_out, "gx", 0)
        else:
            (part,) = call(speed, [values], [field])
            x_far = trade(x_last, "gx", 1)
        turning = functools.partial(heading_kernel, heading_step)
        (part,) = call(turning, [values, part, t_near, t_far], [field])
        if opening:
            reach = 4
            while reach < size:
                most = jnp.maximum(most, other)
                other = spread(most, reach)
                reach *= 2
            part, x_far = lax.optimization_barrier((part, x_far))
        else:
            part, x_near = lax.optimization_barrier((part, x_near))
        cross = functools.partial(cross_kernel, opening, speed_step)
        ins = [values, part, wind, waves] + ([] if opening else [pk])
        part, *extra = call(cross, ins, [field] * (2 if opening else 1), work=1000)
        last = functools.partial(section_kernel, section, bounds, heading_step, speed_step)
        ins = ([] if opening else [level_set]) + [values, part, *extra, x_near, x_far]
        ins += [wind, waves, target_mask, target_depth]
        ins += [most, other] if opening else [pk]
        outs = [field]
        if section < 3:
            outs += edge_shapes(False)
        if opening:
            outs += [shape()]
        rows = pltpu.VMEM((planes,) + tile, jnp.float32)
        results = call(last, ins, outs, [rows, rows])
        values, edges = results[0], results[1:5]
        if opening:
            pk = results[5]
    return values


def solution(mesh):
    return jax.shard_map(
        local,
        mesh=mesh,
        in_specs=(P("gx", "head", None, None), P(None, "gx", None), P("gx", None), P("gx", None)),
        out_specs=P("gx", "head", None, None),
        check_vma=False,
    )
```

```python
import functools
import math

import jax
import jax.numpy as jnp
import numpy as np
from jax import lax
from jax.experimental import pallas as pl
from jax.experimental.pallas import tpu as pltpu
from jax.sharding import PartitionSpec as P

epsilon = 1e-06
courant = 0.5
spacing = 0.05
turn_limit = 1.0
thrust_limit = 0.5
speed_low = 0.5
speed_high = 1.5
rim = 3
gain = 1.0 / (12.0 * spacing)


def inverse(value):
    return pltpu.reciprocal(value, approx=True)


def weights_of(e1, e2, turn, eps):
    level = turn * turn * (4.0 / 3.0) + eps
    ia = inverse(level + e2 * (e2 + turn))
    ib = inverse(level + e2 * e1)
    ic = inverse(level + e1 * (e1 - turn))
    return ia * ia, ib * ib * 6.0, ic * ic


def sides(fl, f0, fr, a2, a1, b1, b0, c0, c1):
    a3 = a1 * 3.0
    c3 = c0 * 3.0
    minus = ((fl + fl) * a2 + f0 * c3) * inverse(a2 + b1 + c3)
    plus = ((fr + fr) * c1 + f0 * a3) * inverse(c1 + b0 + a3)
    return minus, plus


def row_terms(cells, step):
    count = len(cells) - 2 * rim
    eps = epsilon * step * step
    slope = [cells[i + 1] - cells[i] for i in range(len(cells) - 1)]
    bend = {m: slope[m + 3] - slope[m + 2] for m in range(-2, count + 2)}
    turn = {m: bend[m + 1] - bend[m] for m in range(-2, count + 1)}
    jerk = {m: turn[m] - turn[m - 1] for m in range(-1, count + 1)}
    a, b, c = {}, {}, {}
    for m in turn:
        a[m], b[m], c[m] = weights_of(bend[m], bend[m + 1], turn[m], eps)
    out = []
    for i in range(count):
        base = (cells[i + 4] - cells[i + 2]) * 6.0 - (turn[i - 1] + turn[i])
        minus, plus = sides(
            jerk[i - 1], jerk[i], jerk[i + 1], a[i - 2], a[i - 1], b[i - 1], b[i], c[i], c[i + 1]
        )
        out.append((base + (plus - minus), (plus + minus) - jerk[i]))
    return out


def tile_terms(cell, step):
    count = cell.shape[1]
    eps = epsilon * step * step
    flat = 1.0 / (eps * eps)
    place = lax.broadcasted_iota(jnp.int32, cell.shape, 1)

    def after(value, by=1):
        return pltpu.roll(value, count - by, 1)

    def before(value, by=1):
        return pltpu.roll(value, by, 1)

    up1 = jnp.where(place == count - 1, cell, after(cell))
    up2 = jnp.where(place >= count - 2, up1, after(cell, 2))
    dn1 = jnp.where(place == 0, cell, before(cell))
    dn2 = jnp.where(place <= 1, dn1, before(cell, 2))
    ahead = up1 - cell
    behind = cell - dn1
    bend_l = behind - (dn1 - dn2)
    bend = ahead - behind
    bend_r = (up2 - up1) - ahead
    turn_l = bend - bend_l
    turn_r = bend_r - bend
    jerk = turn_r - turn_l
    level_l = turn_l * turn_l * (4.0 / 3.0) + eps
    level_r = turn_r * turn_r * (4.0 / 3.0) + eps
    ia = inverse(level_l + bend * (bend + turn_l))
    ib = inverse(level_l + bend * bend_l)
    jb = inverse(level_r + bend * bend_r)
    jc = inverse(level_r + bend * (bend - turn_r))
    a1 = ia * ia
    c0 = jc * jc
    a2 = jnp.where(place == 0, flat, before(a1))
    c1 = jnp.where(place == count - 1, flat, after(c0))
    jerk_l = jnp.where(place == 0, bend, before(jerk))
    jerk_r = jnp.where(place == count - 1, bend, after(jerk))
    base = (ahead + behind) * 6.0 - (turn_l + turn_r)
    minus, plus = sides(
        jerk_l, jerk, jerk_r, a2, a1, ib * ib * 6.0, jb * jb * 6.0, c0, c1
    )
    return base + (plus - minus), (plus + minus) - jerk


def batches(total, most):
    return max(k for k in range(1, most + 1) if total % k == 0)


def splat(row, tile):
    return jnp.broadcast_to(row, tile)


def speeds_of(tile, speed_step):
    place = lax.broadcasted_iota(jnp.int32, tile, 0).astype(jnp.float32)
    return speed_low + place * speed_step


def odd_place(axis):
    return lax.rem(lax.axis_index(axis), 2) == 1


def extremes_of(wind_ref):
    rows = [wind_ref[i] for i in range(wind_ref.shape[0])]
    return functools.reduce(jnp.maximum, rows), -functools.reduce(jnp.minimum, rows)


def put_extremes(wind_ref, most_ref):
    top, low = extremes_of(wind_ref)
    most_ref[...] = jnp.zeros_like(most_ref)
    most_ref[0:2, :] = top
    most_ref[2:4, :] = low


def opening_kernel(level_in, wind_in, level_ref, x_near, x_far, t_near, t_far, wind_ref, sems):
    planes, headings = level_ref.shape[:2]
    step = planes // batches(planes, 3)
    pairs = [(wind_in, wind_ref)] + [
        (level_in.at[pl.ds(i, step)], level_ref.at[pl.ds(i, step)])
        for i in range(0, planes, step)
    ]
    copies = [
        pltpu.make_async_copy(src, dst, sems.at[k]) for k, (src, dst) in enumerate(pairs)
    ]
    for copy in copies:
        copy.start()
    copies[0].wait()
    put_extremes(wind_ref, x_near.at[x_near.shape[0] - 2])
    for copy in copies[1:]:
        copy.wait()
    cut_edges(level_ref, x_near, x_far, t_near, t_far)


def meeting_kernel(wind_ref, x_near, most_ref):
    put_extremes(wind_ref, most_ref)
    most_ref[...] = jnp.maximum(most_ref[...], x_near[x_near.shape[0] - 2])


def speed_kernel(speed_step, s_ref, part_ref):
    planes, headings, speeds, width = s_ref.shape
    gain_v = thrust_limit / (12.0 * speed_step)
    cells = planes * headings
    group = 8
    s_rows = s_ref.reshape(cells * speeds, width)
    part_rows = part_ref.reshape(cells * speeds, width)
    groups = -(-cells // group)
    wide = batches(groups, 7)

    def step(n, carry):
        for k in range(wide):
            start = jnp.minimum((n * wide + k) * group, cells - group) * speeds
            lines = [
                s_rows[pl.ds(start + v, group, stride=speeds), :] for v in range(speeds)
            ]
            ends = [lines[0]] * rim + lines + [lines[-1]] * rim
            for v, (mean, gap) in enumerate(row_terms(ends, speed_step)):
                part_rows[pl.ds(start + v, group, stride=speeds), :] = gain_v * (
                    gap - jnp.abs(mean)
                )
        return carry

    lax.fori_loop(0, groups // wide, step, 0)


def cross_kernel(split, speed_step, s_ref, part_ref, wind_ref, waves_ref, *rest):
    planes, headings, speeds, width = s_ref.shape
    tile = (speeds, width)
    if split:
        out_ref, extra_ref = rest
    else:
        pk_ref, out_ref = rest
        peak = splat(pk_ref[1:2, :] * gain, tile)
    pace = speeds_of(tile, speed_step) * gain
    first = lax.axis_index("head") * headings
    wide = batches(headings, 4)

    def step(n, carry):
        for k in range(wide):
            j = n * wide + k
            table = splat(waves_ref[1, pl.ds(first + j, 1), :], tile) * pace
            for i in range(planes):
                mean, gap = tile_terms(s_ref[i, j], spacing)
                flow = table + splat(wind_ref[i, 1:2, :] * gain, tile)
                part = part_ref[i, j] + mean * flow
                if split:
                    out_ref[i, j] = part
                    extra_ref[i, j] = gap
                else:
                    out_ref[i, j] = part + gap * peak
        return carry

    lax.fori_loop(0, headings // wide, step, 0)


def heading_kernel(heading_step, s_ref, part_ref, near_ref, far_ref, out_ref):
    planes, headings = s_ref.shape[:2]
    gain_t = turn_limit / (12.0 * heading_step)
    odd = odd_place("head")
    wide = batches(planes, 3)

    def step(n, carry):
        for w in range(wide):
            i = n * wide + w
            ghosts = [(near_ref[i * rim + k], far_ref[i * rim + k]) for k in range(rim)]
            lows = [jnp.where(odd, near, far) for near, far in ghosts]
            highs = [jnp.where(odd, far, near) for near, far in ghosts]
            cells = lows + [s_ref[i, j] for j in range(headings)] + highs
            for j, (mean, gap) in enumerate(row_terms(cells, heading_step)):
                out_ref[i, j] = part_ref[i, j] + gain_t * (gap - jnp.abs(mean))
        return carry

    lax.fori_loop(0, planes // wide, step, 0)


def peaks_into(pk_ref, most, bounds, heading_step, speed_step):
    most = jnp.max(most, axis=1, keepdims=True)
    peaks = [
        jnp.maximum(most[q : q + 1] + bounds[q][1], most[q + 2 : q + 3] - bounds[q][0])
        for q in range(2)
    ]
    time_step = courant / (
        peaks[0] / spacing
        + peaks[1] / spacing
        + turn_limit / heading_step
        + thrust_limit / speed_step
    )
    width = pk_ref.shape[1]
    for row, value in enumerate(peaks + [time_step]):
        pk_ref[row : row + 1, :] = splat(value, (1, width))


def cut_edges(field_ref, x_near, x_far, t_near, t_far):
    planes, headings = field_ref.shape[:2]
    x_low = jnp.where(odd_place("gx"), 0, planes - rim)
    t_low = jnp.where(odd_place("head"), 0, headings - rim)
    for k in range(rim):
        x_near[k * headings : (k + 1) * headings] = field_ref[x_low + k]
        x_far[k * headings : (k + 1) * headings] = field_ref[planes - rim - x_low + k]
        for i in range(planes):
            t_near[i * rim + k] = field_ref[i, t_low + k]
            t_far[i * rim + k] = field_ref[i, headings - rim - t_low + k]


def section_kernel(section, bounds, heading_step, speed_step, *refs):
    refs = list(refs)
    base_ref = None if section == 1 else refs.pop(0)
    s_ref, part_ref = refs.pop(0), refs.pop(0)
    extra_ref = refs.pop(0) if section == 1 else None
    near_ref, far_ref = refs.pop(0), refs.pop(0)
    wind_ref, waves_ref, mask_ref, depth_ref = (refs.pop(0) for _ in range(4))
    if section == 1:
        most_refs = [refs.pop(0), refs.pop(0)]
    else:
        pk_ref = refs.pop(0)
    out_ref = refs.pop(0)
    if section < 3:
        edge_refs = [refs.pop(0) for _ in range(4)]
    if section == 1:
        pk_ref = refs.pop(0)
    flow_ref, target_ref = refs[:2]
    planes, headings = s_ref.shape[:2]
    tile = s_ref.shape[2:]
    if section == 1:
        most = jnp.maximum(most_refs[0][...], most_refs[1][...])
        peaks_into(pk_ref, most, bounds, heading_step, speed_step)
    for i in range(planes):
        depth = depth_ref[i : i + 1, :]
        target_ref[i] = splat(jnp.where(mask_ref[i : i + 1, :] == 1, -depth, depth), tile)
        flow_ref[i] = splat(wind_ref[i, 0:1, :] * gain, tile)
    odd = odd_place("gx")
    at_low = lax.axis_index("gx") == 0
    at_high = lax.axis_index("gx") == lax.axis_size("gx") - 1
    peak_x = splat(pk_ref[0:1, :] * gain, tile)
    peak_y = splat(pk_ref[1:2, :] * gain, tile)
    time_step = splat(pk_ref[2:3, :], tile)
    pace = speeds_of(tile, speed_step) * gain
    first = lax.axis_index("head") * headings
    wide = batches(headings, 6 if section < 3 else 3)
    result_ref = out_ref if section < 3 else refs[2]

    def leaving(n):
        part = (slice(None), pl.ds(n * wide, wide))
        return pltpu.make_async_copy(result_ref.at[part], out_ref.at[part], refs[3].at[n])

    def step(n, carry):
        for w in range(wide):
            j = n * wide + w
            cells = [s_ref[i, j] for i in range(planes)]
            ghosts = [(near_ref[k * headings + j], far_ref[k * headings + j]) for k in range(rim)]
            lows = [jnp.where(at_low, cells[0], jnp.where(odd, near, far)) for near, far in ghosts]
            highs = [jnp.where(at_high, cells[-1], jnp.where(odd, far, near)) for near, far in ghosts]
            table = splat(waves_ref[0, pl.ds(first + j, 1), :], tile) * pace
            for i, (mean, gap) in enumerate(row_terms(lows + cells + highs, spacing)):
                rate = part_ref[i, j] + (mean * (table + flow_ref[i]) + gap * peak_x)
                if section == 1:
                    rate = rate + extra_ref[i, j] * peak_y
                moved = cells[i] + time_step * rate
                if section == 2:
                    moved = 0.75 * base_ref[i, j] + 0.25 * moved
                if section == 3:
                    moved = (1.0 / 3.0) * base_ref[i, j] + (2.0 / 3.0) * moved
                result_ref[i, j] = jnp.minimum(moved, target_ref[i])
        if section == 3:
            leaving(n).start()
        return carry

    lax.fori_loop(0, headings // wide, step, 0)
    if section < 3:
        cut_edges(out_ref, *edge_refs)
    else:
        for n in range(headings // wide):
            leaving(n).wait()


def trade(value, axis, reach, wrap=False):
    size = lax.axis_size(axis)
    pairs = [(i, i + 1) for i in range(reach, size - 1, 2)]
    if wrap and reach and size % 2 == 0:
        pairs.append((size - 1, 0))
    return lax.ppermute(value, axis, pairs + [(j, i) for i, j in pairs])


def local(level_set, wind_field, target_mask, target_depth):
    planes, headings, speed_count, cross_count = level_set.shape
    heading_total = headings * lax.axis_size("head")
    heading_step = 2.0 * math.pi / heading_total
    speed_step = (speed_high - speed_low) / (speed_count - 1)
    speed_row = np.float32(speed_low) + np.arange(speed_count, dtype=np.float32) * np.float32(
        speed_step
    )
    angles = np.arange(heading_total, dtype=np.float32) * np.float32(heading_step)
    waves = [np.cos(angles), np.sin(angles)]
    bounds = []
    for wave in waves:
        product = wave[:, None] * speed_row[None, :]
        bounds.append((float(product.min()), float(product.max())))
    waves = jnp.asarray(np.stack(waves)[..., None] * np.ones(cross_count, np.float32))

    vmem = pl.BlockSpec(memory_space=pltpu.VMEM)
    tile = (speed_count, cross_count)

    def shape(*dims):
        return jax.ShapeDtypeStruct(dims + tile, jnp.float32)

    field = shape(planes, headings)
    short = rim * max(planes, headings)

    def edge_shapes():
        return [shape(short + 2), shape(short + 1)] + [shape(rim * planes)] * 2

    cells = math.prod(level_set.shape)

    def call(kernel, ins, outs, scratch=(), work=0, place=vmem):
        return pl.pallas_call(
            kernel,
            out_shape=outs,
            in_specs=[vmem] * len(ins),
            out_specs=[place] * len(outs),
            scratch_shapes=list(scratch),
            compiler_params=pltpu.CompilerParams(vmem_limit_bytes=16 * 1024 * 1024),
            cost_estimate=pl.CostEstimate(
                flops=work * cells, bytes_accessed=work * cells, transcendentals=0
            ),
        )(*ins)

    wind = jnp.transpose(wind_field, (1, 0, 2))
    size = lax.axis_size("gx")

    def spread(most, reach):
        if size & (size - 1):
            pairs = [(i, (i + reach) % size) for i in range(size)]
        else:
            pairs = [(i, i ^ reach) for i in range(size)]
        return lax.ppermute(most, "gx", pairs)

    hbm = pl.BlockSpec(memory_space=pltpu.HBM)
    level, *edges = pl.pallas_call(
        opening_kernel,
        out_shape=[field] + edge_shapes(),
        in_specs=[hbm] * 2,
        out_specs=[vmem] * 5,
        scratch_shapes=[pltpu.VMEM(wind.shape, jnp.float32), pltpu.SemaphoreType.DMA((planes + 1,))],
        cost_estimate=pl.CostEstimate(flops=0, bytes_accessed=0, transcendentals=0),
    )(level_set, wind)
    values, pk = level, None
    for section in (1, 2, 3):
        opening = section == 1
        x_out, x_last, t_out, t_last = edges
        x_near = trade(x_out, "gx", 0)
        x_far = trade(x_last, "gx", 1)
        t_near = trade(t_out, "head", 0)
        t_far = trade(t_last, "head", 1, True)
        (part,) = call(functools.partial(speed_kernel, speed_step), [values], [field])
        if opening:
            (most,) = call(meeting_kernel, [wind, x_near], [shape()])
            other = spread(most, 2)
        cross = functools.partial(cross_kernel, opening, speed_step)
        ins = [values, part, wind, waves] + ([] if opening else [pk])
        part, *extra = call(cross, ins, [field] * (2 if opening else 1), work=100)
        if opening:
            reach = 4
            while reach < size:
                most = jnp.maximum(most, other)
                most, part = lax.optimization_barrier((most, part))
                other = spread(most, reach)
                reach *= 2
        turning = functools.partial(heading_kernel, heading_step)
        (part,) = call(turning, [values, part, t_near, t_far], [field])
        last = functools.partial(section_kernel, section, bounds, heading_step, speed_step)
        ins = ([] if opening else [level]) + [values, part, *extra, x_near, x_far]
        ins += [wind, waves, target_mask, target_depth]
        ins += [most, other] if opening else [pk]
        outs = [field]
        if section < 3:
            outs += edge_shapes()
        if opening:
            outs += [shape()]
        rows = pltpu.VMEM((planes,) + tile, jnp.float32)
        scratch = [rows, rows]
        if section == 3:
            scratch += [
                pltpu.VMEM(level_set.shape, jnp.float32),
                pltpu.SemaphoreType.DMA((headings,)),
            ]
        results = call(last, ins, outs, scratch, place=vmem if section < 3 else hbm)
        values, edges = results[0], results[1:5]
        if opening:
            pk = results[5]
    return values


def solution(mesh):
    return jax.shard_map(
        local,
        mesh=mesh,
        in_specs=(P("gx", "head", None, None), P(None, "gx", None), P("gx", None), P("gx", None)),
        out_specs=P("gx", "head", None, None),
        check_vma=False,
    )
```

```python
import functools
import math

import jax
import jax.numpy as jnp
import numpy as np
from jax import lax
from jax.experimental import pallas as pl
from jax.experimental.pallas import tpu as pltpu
from jax.sharding import PartitionSpec as P

epsilon = 1e-06
courant = 0.5
spacing = 0.05
turn_limit = 1.0
thrust_limit = 0.5
speed_low = 0.5
speed_high = 1.5
rim = 3
gain = 1.0 / (12.0 * spacing)


def inverse(value):
    return pltpu.reciprocal(value, approx=True)


def weights_of(e1, e2, turn, eps):
    level = turn * turn * (4.0 / 3.0) + eps
    ia = inverse(level + e2 * (e2 + turn))
    ib = inverse(level + e2 * e1)
    ic = inverse(level + e1 * (e1 - turn))
    return ia * ia, ib * ib * 6.0, ic * ic


def sides(fl, f0, fr, a2, a1, b1, b0, c0, c1):
    a3 = a1 * 3.0
    c3 = c0 * 3.0
    minus = ((fl + fl) * a2 + f0 * c3) * inverse(a2 + b1 + c3)
    plus = ((fr + fr) * c1 + f0 * a3) * inverse(c1 + b0 + a3)
    return minus, plus


def row_terms(cells, step):
    count = len(cells) - 2 * rim
    eps = epsilon * step * step
    slope = [cells[i + 1] - cells[i] for i in range(len(cells) - 1)]
    bend = {m: slope[m + 3] - slope[m + 2] for m in range(-2, count + 2)}
    turn = {m: bend[m + 1] - bend[m] for m in range(-2, count + 1)}
    jerk = {m: turn[m] - turn[m - 1] for m in range(-1, count + 1)}
    a, b, c = {}, {}, {}
    for m in turn:
        a[m], b[m], c[m] = weights_of(bend[m], bend[m + 1], turn[m], eps)
    out = []
    for i in range(count):
        base = (cells[i + 4] - cells[i + 2]) * 6.0 - (turn[i - 1] + turn[i])
        minus, plus = sides(
            jerk[i - 1], jerk[i], jerk[i + 1], a[i - 2], a[i - 1], b[i - 1], b[i], c[i], c[i + 1]
        )
        out.append((base + (plus - minus), (plus + minus) - jerk[i]))
    return out


def tile_terms(cell, step):
    count = cell.shape[1]
    eps = epsilon * step * step
    flat = 1.0 / (eps * eps)
    place = lax.broadcasted_iota(jnp.int32, cell.shape, 1)

    def after(value, by=1):
        return pltpu.roll(value, count - by, 1)

    def before(value, by=1):
        return pltpu.roll(value, by, 1)

    up1 = jnp.where(place == count - 1, cell, after(cell))
    up2 = jnp.where(place >= count - 2, up1, after(cell, 2))
    dn1 = jnp.where(place == 0, cell, before(cell))
    dn2 = jnp.where(place <= 1, dn1, before(cell, 2))
    ahead = up1 - cell
    behind = cell - dn1
    bend_l = behind - (dn1 - dn2)
    bend = ahead - behind
    bend_r = (up2 - up1) - ahead
    turn_l = bend - bend_l
    turn_r = bend_r - bend
    jerk = turn_r - turn_l
    level_l = turn_l * turn_l * (4.0 / 3.0) + eps
    level_r = turn_r * turn_r * (4.0 / 3.0) + eps
    ia = inverse(level_l + bend * (bend + turn_l))
    ib = inverse(level_l + bend * bend_l)
    jb = inverse(level_r + bend * bend_r)
    jc = inverse(level_r + bend * (bend - turn_r))
    a1 = ia * ia
    c0 = jc * jc
    a2 = jnp.where(place == 0, flat, before(a1))
    c1 = jnp.where(place == count - 1, flat, after(c0))
    jerk_l = jnp.where(place == 0, bend, before(jerk))
    jerk_r = jnp.where(place == count - 1, bend, after(jerk))
    base = (ahead + behind) * 6.0 - (turn_l + turn_r)
    minus, plus = sides(
        jerk_l, jerk, jerk_r, a2, a1, ib * ib * 6.0, jb * jb * 6.0, c0, c1
    )
    return base + (plus - minus), (plus + minus) - jerk


def batches(total, most):
    return max(k for k in range(1, most + 1) if total % k == 0)


def splat(row, tile):
    return jnp.broadcast_to(row, tile)


def speeds_of(tile, speed_step):
    place = lax.broadcasted_iota(jnp.int32, tile, 0).astype(jnp.float32)
    return speed_low + place * speed_step


def odd_place(axis):
    return lax.rem(lax.axis_index(axis), 2) == 1


def extremes_of(wind_ref):
    rows = [wind_ref[i] for i in range(wind_ref.shape[0])]
    return functools.reduce(jnp.maximum, rows), -functools.reduce(jnp.minimum, rows)


def put_extremes(wind_ref, most_ref):
    top, low = extremes_of(wind_ref)
    most_ref[...] = jnp.zeros_like(most_ref)
    most_ref[0:2, :] = top
    most_ref[2:4, :] = low


def opening_kernel(level_ref, wind_ref, x_near, *others):
    put_extremes(wind_ref, x_near.at[x_near.shape[0] - 1])
    cut_edges(level_ref, x_near, *others)


def meeting_kernel(wind_ref, x_near, most_ref):
    put_extremes(wind_ref, most_ref)
    most_ref[...] = jnp.maximum(most_ref[...], x_near[x_near.shape[0] - 1])


def free_kernel(split, speed_step, s_ref, wind_ref, waves_ref, *rest):
    planes, headings, speeds, width = s_ref.shape
    tile = (speeds, width)
    if split:
        speed_ref, out_ref, extra_ref = rest
    else:
        pk_ref, speed_ref, out_ref = rest
        peak = splat(pk_ref[1:2, :] * gain, tile)
    pace = speeds_of(tile, speed_step) * gain
    gain_v = thrust_limit / (12.0 * speed_step)
    first = lax.axis_index("head") * headings
    cells = planes * headings
    s_rows = s_ref.reshape(cells * speeds, width)
    speed_rows = speed_ref.reshape(cells * speeds, width)
    wide = batches(headings, 2)
    group = 8

    def along_speed(start, count, stride):
        spots = [pl.ds(start * speeds + v, count, stride=stride * speeds) for v in range(speeds)]
        lines = [s_rows[spot, :] for spot in spots]
        ends = [lines[0]] * rim + lines + [lines[-1]] * rim
        for spot, (mean, gap) in zip(spots, row_terms(ends, speed_step)):
            speed_rows[spot, :] = gain_v * (gap - jnp.abs(mean))

    def step(n, carry):
        for k in range(wide):
            j = n * wide + k
            table = splat(waves_ref[1, pl.ds(first + j, 1), :], tile) * pace
            for i in range(planes):
                mean, gap = tile_terms(s_ref[i, j], spacing)
                flow = table + splat(wind_ref[i, 1:2, :] * gain, tile)
                if split:
                    out_ref[i, j] = mean * flow
                    extra_ref[i, j] = gap
                else:
                    out_ref[i, j] = mean * flow + gap * peak
            for i in range(0, planes - group + 1, group):
                along_speed(i * headings + j, group, headings)
        return carry

    lax.fori_loop(0, headings // wide, step, 0)
    count = min(group, headings)
    for i in range(planes // group * group, planes):
        for j in range(0, headings, count):
            along_speed(i * headings + min(j, headings - count), count, 1)


def heading_kernel(heading_step, s_ref, speed_ref, part_ref, near_ref, far_ref, out_ref):
    planes, headings = s_ref.shape[:2]
    gain_t = turn_limit / (12.0 * heading_step)
    odd = odd_place("head")
    wide = batches(planes, 3)

    def step(n, carry):
        for w in range(wide):
            i = n * wide + w
            ghosts = [(near_ref[i * rim + k], far_ref[i * rim + k]) for k in range(rim)]
            lows = [jnp.where(odd, near, far) for near, far in ghosts]
            highs = [jnp.where(odd, far, near) for near, far in ghosts]
            cells = lows + [s_ref[i, j] for j in range(headings)] + highs
            for j, (mean, gap) in enumerate(row_terms(cells, heading_step)):
                own = speed_ref[i, j] + part_ref[i, j]
                out_ref[i, j] = own + gain_t * (gap - jnp.abs(mean))
        return carry

    lax.fori_loop(0, planes // wide, step, 0)


def peaks_into(pk_ref, most, bounds, heading_step, speed_step):
    most = jnp.max(most, axis=1, keepdims=True)
    peaks = [
        jnp.maximum(most[q : q + 1] + bounds[q][1], most[q + 2 : q + 3] - bounds[q][0])
        for q in range(2)
    ]
    time_step = courant / (
        peaks[0] / spacing
        + peaks[1] / spacing
        + turn_limit / heading_step
        + thrust_limit / speed_step
    )
    width = pk_ref.shape[1]
    for row, value in enumerate(peaks + [time_step]):
        pk_ref[row : row + 1, :] = splat(value, (1, width))


def cut_edges(field_ref, x_near, x_far, t_near, t_far):
    planes, headings = field_ref.shape[:2]
    x_low = jnp.where(odd_place("gx"), 0, planes - rim)
    t_low = jnp.where(odd_place("head"), 0, headings - rim)
    for k in range(rim):
        x_near[k * headings : (k + 1) * headings] = field_ref[x_low + k]
        x_far[k * headings : (k + 1) * headings] = field_ref[planes - rim - x_low + k]
        for i in range(planes):
            t_near[i * rim + k] = field_ref[i, t_low + k]
            t_far[i * rim + k] = field_ref[i, headings - rim - t_low + k]


def section_kernel(section, bounds, heading_step, speed_step, *refs):
    refs = list(refs)
    base_ref = None if section == 1 else refs.pop(0)
    s_ref, part_ref = refs.pop(0), refs.pop(0)
    extra_ref = refs.pop(0) if section == 1 else None
    near_ref, far_ref = refs.pop(0), refs.pop(0)
    wind_ref, waves_ref, mask_ref, depth_ref = (refs.pop(0) for _ in range(4))
    if section == 1:
        most_refs = [refs.pop(0), refs.pop(0)]
    else:
        pk_ref = refs.pop(0)
    out_ref = refs.pop(0)
    if section < 3:
        edge_refs = [refs.pop(0) for _ in range(4)]
    if section == 1:
        pk_ref = refs.pop(0)
    flow_ref, target_ref = refs
    planes, headings = s_ref.shape[:2]
    tile = s_ref.shape[2:]
    if section == 1:
        most = jnp.maximum(most_refs[0][...], most_refs[1][...])
        peaks_into(pk_ref, most, bounds, heading_step, speed_step)
    for i in range(planes):
        depth = depth_ref[i : i + 1, :]
        target_ref[i] = splat(jnp.where(mask_ref[i : i + 1, :] == 1, -depth, depth), tile)
        flow_ref[i] = splat(wind_ref[i, 0:1, :] * gain, tile)
    odd = odd_place("gx")
    at_low = lax.axis_index("gx") == 0
    at_high = lax.axis_index("gx") == lax.axis_size("gx") - 1
    peak_x = splat(pk_ref[0:1, :] * gain, tile)
    peak_y = splat(pk_ref[1:2, :] * gain, tile)
    time_step = splat(pk_ref[2:3, :], tile)
    pace = speeds_of(tile, speed_step) * gain
    first = lax.axis_index("head") * headings
    wide = batches(headings, 6)

    def step(n, carry):
        for w in range(wide):
            j = n * wide + w
            cells = [s_ref[i, j] for i in range(planes)]
            ghosts = [(near_ref[k * headings + j], far_ref[k * headings + j]) for k in range(rim)]
            lows = [jnp.where(at_low, cells[0], jnp.where(odd, near, far)) for near, far in ghosts]
            highs = [jnp.where(at_high, cells[-1], jnp.where(odd, far, near)) for near, far in ghosts]
            table = splat(waves_ref[0, pl.ds(first + j, 1), :], tile) * pace
            for i, (mean, gap) in enumerate(row_terms(lows + cells + highs, spacing)):
                rate = part_ref[i, j] + (mean * (table + flow_ref[i]) + gap * peak_x)
                if section == 1:
                    rate = rate + extra_ref[i, j] * peak_y
                moved = cells[i] + time_step * rate
                if section == 2:
                    moved = 0.75 * base_ref[i, j] + 0.25 * moved
                if section == 3:
                    moved = (1.0 / 3.0) * base_ref[i, j] + (2.0 / 3.0) * moved
                out_ref[i, j] = jnp.minimum(moved, target_ref[i])
        return carry

    lax.fori_loop(0, headings // wide, step, 0)
    if section < 3:
        cut_edges(out_ref, *edge_refs)


def trade(value, axis, reach, wrap=False):
    size = lax.axis_size(axis)
    pairs = [(i, i + 1) for i in range(reach, size - 1, 2)]
    if wrap and reach and size % 2 == 0:
        pairs.append((size - 1, 0))
    return lax.ppermute(value, axis, pairs + [(j, i) for i, j in pairs])


def local(level_set, wind_field, target_mask, target_depth):
    planes, headings, speed_count, cross_count = level_set.shape
    heading_total = headings * lax.axis_size("head")
    heading_step = 2.0 * math.pi / heading_total
    speed_step = (speed_high - speed_low) / (speed_count - 1)
    speed_row = np.float32(speed_low) + np.arange(speed_count, dtype=np.float32) * np.float32(
        speed_step
    )
    angles = np.arange(heading_total, dtype=np.float32) * np.float32(heading_step)
    waves = [np.cos(angles), np.sin(angles)]
    bounds = []
    for wave in waves:
        product = wave[:, None] * speed_row[None, :]
        bounds.append((float(product.min()), float(product.max())))
    waves = jnp.asarray(np.stack(waves)[..., None] * np.ones(cross_count, np.float32))

    vmem = pl.BlockSpec(memory_space=pltpu.VMEM)
    tile = (speed_count, cross_count)

    def shape(*dims):
        return jax.ShapeDtypeStruct(dims + tile, jnp.float32)

    field = shape(planes, headings)
    short = rim * headings
    middle = max(short + 1, rim * planes)

    edge_shapes = [shape(middle + 1), shape(short)] + [shape(middle)] * 2
    cells = math.prod(level_set.shape)

    def call(kernel, ins, outs, scratch=(), work=0):
        return pl.pallas_call(
            kernel,
            out_shape=outs,
            in_specs=[vmem] * len(ins),
            out_specs=[vmem] * len(outs),
            scratch_shapes=list(scratch),
            compiler_params=pltpu.CompilerParams(vmem_limit_bytes=16 * 1024 * 1024),
            cost_estimate=pl.CostEstimate(
                flops=work * cells, bytes_accessed=work * cells, transcendentals=0
            ),
        )(*ins)

    wind = jnp.transpose(wind_field, (1, 0, 2))
    values, pk = level_set, None
    size = lax.axis_size("gx")

    def spread(most, reach):
        if size & (size - 1):
            pairs = [(i, (i + reach) % size) for i in range(size)]
        else:
            pairs = [(i, i ^ reach) for i in range(size)]
        return lax.ppermute(most, "gx", pairs)

    edges = call(opening_kernel, [values, wind], edge_shapes)
    for section in (1, 2, 3):
        opening = section == 1
        x_out, x_last, t_out, t_last = edges
        x_near = trade(x_out, "gx", 0)
        t_near = trade(t_out, "head", 0)
        t_far = trade(t_last, "head", 1, True)
        x_far = trade(x_last, "gx", 1)
        free = functools.partial(free_kernel, opening, speed_step)
        turning = functools.partial(heading_kernel, heading_step)
        if opening:
            (most,) = call(meeting_kernel, [wind, x_near], [shape()])
            other = spread(most, 2)
            spun, part, extra = call(free, [values, wind, waves], [field] * 3, work=300)
            reach = 4
            while reach < size:
                most = jnp.maximum(most, other)
                most, part = lax.optimization_barrier((most, part))
                other = spread(most, reach)
                reach *= 2
        else:
            spun, part = call(free, [values, wind, waves, pk], [field] * 2)
            part, x_near = lax.optimization_barrier((part, x_near))
        (part,) = call(turning, [values, spun, part, t_near, t_far], [field], work=1000)
        last = functools.partial(section_kernel, section, bounds, heading_step, speed_step)
        ins = [values, part, extra] if opening else [level_set, values, part]
        ins += [x_near, x_far]
        ins += [wind, waves, target_mask, target_depth]
        ins += [most, other] if opening else [pk]
        outs = [field]
        if section < 3:
            outs += edge_shapes
        if opening:
            outs += [shape()]
        rows = pltpu.VMEM((planes,) + tile, jnp.float32)
        results = call(last, ins, outs, [rows, rows])
        values, edges = results[0], results[1:5]
        if opening:
            pk = results[5]
    return values


def solution(mesh):
    return jax.shard_map(
        local,
        mesh=mesh,
        in_specs=(P("gx", "head", None, None), P(None, "gx", None), P("gx", None), P("gx", None)),
        out_specs=P("gx", "head", None, None),
        check_vma=False,
    )
```

```python
import functools
import math

import jax
import jax.numpy as jnp
import numpy as np
from jax import lax
from jax.experimental import pallas as pl
from jax.experimental.pallas import tpu as pltpu
from jax.sharding import PartitionSpec as P

epsilon = 1e-06
courant = 0.5
spacing = 0.05
turn_limit = 1.0
thrust_limit = 0.5
speed_low = 0.5
speed_high = 1.5
rim = 3
gain = 1.0 / (12.0 * spacing)


def inverse(value):
    return pltpu.reciprocal(value, approx=True)


def weights_of(e1, e2, turn, eps):
    level = turn * turn * (4.0 / 3.0) + eps
    ia = inverse(level + e2 * (e2 + turn))
    ib = inverse(level + e2 * e1)
    ic = inverse(level + e1 * (e1 - turn))
    return ia * ia, ib * ib * 6.0, ic * ic


def sides(fl, f0, fr, a2, a1, b1, b0, c0, c1):
    a3 = a1 * 3.0
    c3 = c0 * 3.0
    minus = ((fl + fl) * a2 + f0 * c3) * inverse(a2 + b1 + c3)
    plus = ((fr + fr) * c1 + f0 * a3) * inverse(c1 + b0 + a3)
    return minus, plus


def row_terms(cells, step):
    count = len(cells) - 2 * rim
    eps = epsilon * step * step
    slope = [cells[i + 1] - cells[i] for i in range(len(cells) - 1)]
    bend = {m: slope[m + 3] - slope[m + 2] for m in range(-2, count + 2)}
    turn = {m: bend[m + 1] - bend[m] for m in range(-2, count + 1)}
    jerk = {m: turn[m] - turn[m - 1] for m in range(-1, count + 1)}
    a, b, c = {}, {}, {}
    for m in turn:
        a[m], b[m], c[m] = weights_of(bend[m], bend[m + 1], turn[m], eps)
    out = []
    for i in range(count):
        base = (cells[i + 4] - cells[i + 2]) * 6.0 - (turn[i - 1] + turn[i])
        minus, plus = sides(
            jerk[i - 1], jerk[i], jerk[i + 1], a[i - 2], a[i - 1], b[i - 1], b[i], c[i], c[i + 1]
        )
        out.append((base + (plus - minus), (plus + minus) - jerk[i]))
    return out


def tile_terms(cell, step):
    count = cell.shape[1]
    eps = epsilon * step * step
    flat = 1.0 / (eps * eps)
    place = lax.broadcasted_iota(jnp.int32, cell.shape, 1)

    def after(value, by=1):
        return pltpu.roll(value, count - by, 1)

    def before(value, by=1):
        return pltpu.roll(value, by, 1)

    up1 = jnp.where(place == count - 1, cell, after(cell))
    up2 = jnp.where(place >= count - 2, up1, after(cell, 2))
    dn1 = jnp.where(place == 0, cell, before(cell))
    dn2 = jnp.where(place <= 1, dn1, before(cell, 2))
    ahead = up1 - cell
    behind = cell - dn1
    bend_l = behind - (dn1 - dn2)
    bend = ahead - behind
    bend_r = (up2 - up1) - ahead
    turn_l = bend - bend_l
    turn_r = bend_r - bend
    jerk = turn_r - turn_l
    level_l = turn_l * turn_l * (4.0 / 3.0) + eps
    level_r = turn_r * turn_r * (4.0 / 3.0) + eps
    ia = inverse(level_l + bend * (bend + turn_l))
    ib = inverse(level_l + bend * bend_l)
    jb = inverse(level_r + bend * bend_r)
    jc = inverse(level_r + bend * (bend - turn_r))
    a1 = ia * ia
    c0 = jc * jc
    a2 = jnp.where(place == 0, flat, before(a1))
    c1 = jnp.where(place == count - 1, flat, after(c0))
    jerk_l = jnp.where(place == 0, bend, before(jerk))
    jerk_r = jnp.where(place == count - 1, bend, after(jerk))
    base = (ahead + behind) * 6.0 - (turn_l + turn_r)
    minus, plus = sides(
        jerk_l, jerk, jerk_r, a2, a1, ib * ib * 6.0, jb * jb * 6.0, c0, c1
    )
    return base + (plus - minus), (plus + minus) - jerk


def batches(total, most):
    return max(k for k in range(1, most + 1) if total % k == 0)


def splat(row, tile):
    return jnp.broadcast_to(row, tile)


def speeds_of(tile, speed_step):
    place = lax.broadcasted_iota(jnp.int32, tile, 0).astype(jnp.float32)
    return speed_low + place * speed_step


def odd_place(axis):
    return lax.rem(lax.axis_index(axis), 2) == 1


def put_extremes(wind_ref, most_ref):
    rows = [wind_ref[i] for i in range(wind_ref.shape[0])]
    most_ref[...] = jnp.zeros_like(most_ref)
    most_ref[0:2, :] = functools.reduce(jnp.maximum, rows)
    most_ref[2:4, :] = -functools.reduce(jnp.minimum, rows)


def opening_kernel(level_ref, wind_ref, x_near, *others):
    put_extremes(wind_ref, x_near.at[x_near.shape[0] - 1])
    cut_edges(level_ref, x_near, *others)


def meeting_kernel(wind_ref, x_near, most_ref):
    put_extremes(wind_ref, most_ref)
    most_ref[...] = jnp.maximum(most_ref[...], x_near[x_near.shape[0] - 1])


def free_kernel(split, speed_step, s_ref, wind_ref, waves_ref, *rest):
    planes, headings, speeds, width = s_ref.shape
    tile = (speeds, width)
    if split:
        speed_ref, out_ref, extra_ref = rest
    else:
        pk_ref, speed_ref, out_ref = rest
        peak = splat(pk_ref[1:2, :] * gain, tile)
    pace = speeds_of(tile, speed_step) * gain
    gain_v = thrust_limit / (12.0 * speed_step)
    first = lax.axis_index("head") * headings
    cells = planes * headings
    s_rows = s_ref.reshape(cells * speeds, width)
    speed_rows = speed_ref.reshape(cells * speeds, width)
    wide = batches(headings, 2)
    group = 8

    def along_speed(start, count, stride):
        spots = [pl.ds(start * speeds + v, count, stride=stride * speeds) for v in range(speeds)]
        lines = [s_rows[spot, :] for spot in spots]
        ends = [lines[0]] * rim + lines + [lines[-1]] * rim
        for spot, (mean, gap) in zip(spots, row_terms(ends, speed_step)):
            speed_rows[spot, :] = gain_v * (gap - jnp.abs(mean))

    def step(n, carry):
        for k in range(wide):
            j = n * wide + k
            table = splat(waves_ref[1, pl.ds(first + j, 1), :], tile) * pace
            for i in range(planes):
                mean, gap = tile_terms(s_ref[i, j], spacing)
                flow = table + splat(wind_ref[i, 1:2, :] * gain, tile)
                if split:
                    out_ref[i, j] = mean * flow
                    extra_ref[i, j] = gap
                else:
                    out_ref[i, j] = mean * flow + gap * peak
            for i in range(0, planes - group + 1, group):
                along_speed(i * headings + j, group, headings)
        return carry

    lax.fori_loop(0, headings // wide, step, 0)
    count = min(group, headings)
    for i in range(planes // group * group, planes):
        for j in range(0, headings, count):
            along_speed(i * headings + min(j, headings - count), count, 1)


def heading_kernel(heading_step, s_ref, speed_ref, part_ref, near_ref, far_ref, out_ref):
    planes, headings = s_ref.shape[:2]
    gain_t = turn_limit / (12.0 * heading_step)
    odd = odd_place("head")
    wide = batches(planes, 3)

    def step(n, carry):
        for w in range(wide):
            i = n * wide + w
            ghosts = [(near_ref[i * rim + k], far_ref[i * rim + k]) for k in range(rim)]
            lows = [jnp.where(odd, near, far) for near, far in ghosts]
            highs = [jnp.where(odd, far, near) for near, far in ghosts]
            cells = lows + [s_ref[i, j] for j in range(headings)] + highs
            for j, (mean, gap) in enumerate(row_terms(cells, heading_step)):
                own = speed_ref[i, j] + part_ref[i, j]
                out_ref[i, j] = own + gain_t * (gap - jnp.abs(mean))
        return carry

    lax.fori_loop(0, planes // wide, step, 0)


def peaks_into(pk_ref, most, bounds, heading_step, speed_step):
    most = jnp.max(most, axis=1, keepdims=True)
    peaks = [
        jnp.maximum(most[q : q + 1] + bounds[q][1], most[q + 2 : q + 3] - bounds[q][0])
        for q in range(2)
    ]
    time_step = courant / (
        peaks[0] / spacing
        + peaks[1] / spacing
        + turn_limit / heading_step
        + thrust_limit / speed_step
    )
    width = pk_ref.shape[1]
    for row, value in enumerate(peaks + [time_step]):
        pk_ref[row : row + 1, :] = splat(value, (1, width))


def cut_edges(field_ref, x_near, x_far, t_near, t_far):
    planes, headings = field_ref.shape[:2]
    x_low = jnp.where(odd_place("gx"), 0, planes - rim)
    t_low = jnp.where(odd_place("head"), 0, headings - rim)
    for k in range(rim):
        x_near[k * headings : (k + 1) * headings] = field_ref[x_low + k]
        x_far[k * headings : (k + 1) * headings] = field_ref[planes - rim - x_low + k]
        for i in range(planes):
            t_near[i * rim + k] = field_ref[i, t_low + k]
            t_far[i * rim + k] = field_ref[i, headings - rim - t_low + k]


def splat_targets(mask_ref, depth_ref, target_ref):
    for i in range(target_ref.shape[0]):
        depth = depth_ref[i : i + 1, :]
        target = jnp.where(mask_ref[i : i + 1, :] == 1, -depth, depth)
        target_ref[i] = splat(target, target_ref.shape[1:])


def across_planes(wide, speed_step, s_ref, near_ref, far_ref, wind_ref, waves_ref, flow_ref, use):
    planes, headings = s_ref.shape[:2]
    tile = s_ref.shape[2:]
    for i in range(planes):
        flow_ref[i] = splat(wind_ref[i, 0:1, :] * gain, tile)
    odd = odd_place("gx")
    at_low = lax.axis_index("gx") == 0
    at_high = lax.axis_index("gx") == lax.axis_size("gx") - 1
    pace = speeds_of(tile, speed_step) * gain
    first = lax.axis_index("head") * headings

    def step(n, carry):
        for w in range(wide):
            j = n * wide + w
            cells = [s_ref[i, j] for i in range(planes)]
            ghosts = [(near_ref[k * headings + j], far_ref[k * headings + j]) for k in range(rim)]
            lows = [jnp.where(at_low, cells[0], jnp.where(odd, near, far)) for near, far in ghosts]
            highs = [jnp.where(at_high, cells[-1], jnp.where(odd, far, near)) for near, far in ghosts]
            table = splat(waves_ref[0, pl.ds(first + j, 1), :], tile) * pace
            for i, (mean, gap) in enumerate(row_terms(lows + cells + highs, spacing)):
                use(i, j, mean * (table + flow_ref[i]), gap, cells[i])
        return carry

    lax.fori_loop(0, headings // wide, step, 0)


def first_kernel(
    speed_step, s_ref, part_ref, near_ref, far_ref, wind_ref, waves_ref, out_ref, gap_ref, flow_ref
):
    def use(i, j, drift, gap, cell):
        out_ref[i, j] = part_ref[i, j] + drift
        gap_ref[i, j] = gap

    wide = batches(s_ref.shape[1], 6)
    across_planes(
        wide, speed_step, s_ref, near_ref, far_ref, wind_ref, waves_ref, flow_ref, use
    )


def closing_kernel(
    bounds, heading_step, speed_step, s_ref, part_ref, gap_x_ref, gap_y_ref, mask_ref, depth_ref,
    most_ref, other_ref, out_ref, x_near, x_far, t_near, t_far, pk_ref, target_ref
):
    planes, headings = s_ref.shape[:2]
    tile = s_ref.shape[2:]
    most = jnp.maximum(most_ref[...], other_ref[...])
    peaks_into(pk_ref, most, bounds, heading_step, speed_step)
    splat_targets(mask_ref, depth_ref, target_ref)
    peak_x = splat(pk_ref[0:1, :] * gain, tile)
    peak_y = splat(pk_ref[1:2, :] * gain, tile)
    time_step = splat(pk_ref[2:3, :], tile)

    def plane(i, carry):
        for j in range(headings):
            rate = part_ref[i, j] + (gap_x_ref[i, j] * peak_x + gap_y_ref[i, j] * peak_y)
            out_ref[i, j] = jnp.minimum(s_ref[i, j] + time_step * rate, target_ref[i])
        return carry

    lax.fori_loop(0, planes, plane, 0)
    cut_edges(out_ref, x_near, x_far, t_near, t_far)


def section_kernel(
    section, speed_step, base_ref, s_ref, part_ref, near_ref, far_ref, wind_ref, waves_ref,
    mask_ref, depth_ref, pk_ref, out_ref, *refs
):
    edge_refs, (flow_ref, target_ref) = refs[:-2], refs[-2:]
    tile = s_ref.shape[2:]
    splat_targets(mask_ref, depth_ref, target_ref)
    peak_x = splat(pk_ref[0:1, :] * gain, tile)
    time_step = splat(pk_ref[2:3, :], tile)
    base_share = 0.75 if section == 2 else 1.0 / 3.0
    own_share = 0.25 if section == 2 else 2.0 / 3.0

    def use(i, j, drift, gap, cell):
        rate = part_ref[i, j] + (drift + gap * peak_x)
        moved = base_share * base_ref[i, j] + own_share * (cell + time_step * rate)
        out_ref[i, j] = jnp.minimum(moved, target_ref[i])

    wide = batches(s_ref.shape[1], 6)
    across_planes(
        wide, speed_step, s_ref, near_ref, far_ref, wind_ref, waves_ref, flow_ref, use
    )
    if section == 2:
        cut_edges(out_ref, *edge_refs)


def trade(value, axis, reach, wrap=False):
    size = lax.axis_size(axis)
    pairs = [(i, i + 1) for i in range(reach, size - 1, 2)]
    if wrap and reach and size % 2 == 0:
        pairs.append((size - 1, 0))
    pairs += [(j, i) for i, j in pairs]
    pairs += [(i, i) for i in range(size) if i not in dict(pairs)]
    return lax.ppermute(value, axis, pairs)


def local(level_set, wind_field, target_mask, target_depth):
    planes, headings, speed_count, cross_count = level_set.shape
    heading_total = headings * lax.axis_size("head")
    heading_step = 2.0 * math.pi / heading_total
    speed_step = (speed_high - speed_low) / (speed_count - 1)
    speed_row = np.float32(speed_low) + np.arange(speed_count, dtype=np.float32) * np.float32(
        speed_step
    )
    angles = np.arange(heading_total, dtype=np.float32) * np.float32(heading_step)
    waves = [np.cos(angles), np.sin(angles)]
    bounds = []
    for wave in waves:
        product = wave[:, None] * speed_row[None, :]
        bounds.append((float(product.min()), float(product.max())))
    waves = jnp.asarray(np.stack(waves)[..., None] * np.ones(cross_count, np.float32))

    vmem = pl.BlockSpec(memory_space=pltpu.VMEM)
    tile = (speed_count, cross_count)

    def shape(*dims):
        return jax.ShapeDtypeStruct(dims + tile, jnp.float32)

    field = shape(planes, headings)
    short = rim * headings
    middle = max(short + 1, rim * planes)

    edge_shapes = [shape(middle + 1), shape(short)] + [shape(middle)] * 2
    rows = pltpu.VMEM((planes,) + tile, jnp.float32)
    cells = math.prod(level_set.shape)

    def call(kernel, ins, outs, scratch=(), work=0):
        return pl.pallas_call(
            kernel,
            out_shape=outs,
            in_specs=[vmem] * len(ins),
            out_specs=[vmem] * len(outs),
            scratch_shapes=list(scratch),
            compiler_params=pltpu.CompilerParams(vmem_limit_bytes=16 * 1024 * 1024),
            cost_estimate=pl.CostEstimate(
                flops=work * cells, bytes_accessed=work * cells, transcendentals=0
            ),
        )(*ins)

    wind = jnp.transpose(wind_field, (1, 0, 2))
    values, pk = level_set, None
    size = lax.axis_size("gx")

    def spread(most, reach):
        if size & (size - 1):
            pairs = [(i, (i + reach) % size) for i in range(size)]
        else:
            pairs = [(i, i ^ reach) for i in range(size)]
        return lax.ppermute(most, "gx", pairs)

    edges = call(opening_kernel, [values, wind], edge_shapes)
    for section in (1, 2, 3):
        opening = section == 1
        x_out, x_last, t_out, t_last = edges
        x_near = trade(x_out, "gx", 0)
        t_near = trade(t_out, "head", 0)
        t_far = trade(t_last, "head", 1, True)
        x_far = trade(x_last, "gx", 1)
        free = functools.partial(free_kernel, opening, speed_step)
        turning = functools.partial(heading_kernel, heading_step)
        if opening:
            (most,) = call(meeting_kernel, [wind, x_near], [shape()])
            other = spread(most, 2)
            spun, part, extra = call(free, [values, wind, waves], [field] * 3, work=300)
            reach = 4
            while reach < size:
                most = jnp.maximum(most, other)
                most, part = lax.optimization_barrier((most, part))
                other = spread(most, reach)
                reach *= 2
        else:
            spun, part = call(free, [values, wind, waves, pk], [field] * 2)
            part, x_near = lax.optimization_barrier((part, x_near))
        (part,) = call(turning, [values, spun, part, t_near, t_far], [field], work=1000)
        if opening:
            ins = [values, part, x_near, x_far, wind, waves]
            first = functools.partial(first_kernel, speed_step)
            part, gap = call(first, ins, [field] * 2, [rows])
            closing = functools.partial(closing_kernel, bounds, heading_step, speed_step)
            ins = [values, part, gap, extra, target_mask, target_depth, most, other]
            values, *edges, pk = call(closing, ins, [field, *edge_shapes, shape()], [rows])
        else:
            ins = [level_set, values, part, x_near, x_far, wind, waves]
            ins += [target_mask, target_depth, pk]
            outs = [field] + (edge_shapes if section == 2 else [])
            last = functools.partial(section_kernel, section, speed_step)
            values, *edges = call(last, ins, outs, [rows, rows])
    return values


def solution(mesh):
    return jax.shard_map(
        local,
        mesh=mesh,
        in_specs=(P("gx", "head", None, None), P(None, "gx", None), P("gx", None), P("gx", None)),
        out_specs=P("gx", "head", None, None),
        check_vma=False,
    )
```

```python
import functools
import math

import jax
import jax.numpy as jnp
import numpy as np
from jax import lax
from jax.experimental import pallas as pl
from jax.experimental.pallas import tpu as pltpu
from jax.sharding import PartitionSpec as P

epsilon = 1e-06
courant = 0.5
spacing = 0.05
turn_limit = 1.0
thrust_limit = 0.5
speed_low = 0.5
speed_high = 1.5
rim = 3
gain = 1.0 / (12.0 * spacing)


def inverse(value):
    return pltpu.reciprocal(value, approx=True)


def weights_of(e1, e2, turn, eps):
    level = turn * turn * (4.0 / 3.0) + eps
    ia = inverse(level + e2 * (e2 + turn))
    ib = inverse(level + e2 * e1)
    ic = inverse(level + e1 * (e1 - turn))
    return ia * ia, ib * ib * 6.0, ic * ic


def sides(fl, f0, fr, a2, a1, b1, b0, c0, c1):
    a3 = a1 * 3.0
    c3 = c0 * 3.0
    minus = ((fl + fl) * a2 + f0 * c3) * inverse(a2 + b1 + c3)
    plus = ((fr + fr) * c1 + f0 * a3) * inverse(c1 + b0 + a3)
    return minus, plus


def row_terms(cells, step):
    count = len(cells) - 2 * rim
    eps = epsilon * step * step
    slope = [cells[i + 1] - cells[i] for i in range(len(cells) - 1)]
    bend = {m: slope[m + 3] - slope[m + 2] for m in range(-2, count + 2)}
    turn = {m: bend[m + 1] - bend[m] for m in range(-2, count + 1)}
    jerk = {m: turn[m] - turn[m - 1] for m in range(-1, count + 1)}
    a, b, c = {}, {}, {}
    for m in turn:
        a[m], b[m], c[m] = weights_of(bend[m], bend[m + 1], turn[m], eps)
    out = []
    for i in range(count):
        base = (cells[i + 4] - cells[i + 2]) * 6.0 - (turn[i - 1] + turn[i])
        minus, plus = sides(
            jerk[i - 1], jerk[i], jerk[i + 1], a[i - 2], a[i - 1], b[i - 1], b[i], c[i], c[i + 1]
        )
        out.append((base + (plus - minus), (plus + minus) - jerk[i]))
    return out


def batches(total, most):
    return max(k for k in range(1, most + 1) if total % k == 0)


def splat(row, tile):
    return jnp.broadcast_to(row, tile)


def speeds_of(tile, speed_step):
    place = lax.broadcasted_iota(jnp.int32, tile, 0).astype(jnp.float32)
    return speed_low + place * speed_step


def odd_place(axis):
    return lax.rem(lax.axis_index(axis), 2) == 1


def put_extremes(wind_ref, most_ref):
    rows = [wind_ref[i] for i in range(wind_ref.shape[0])]
    most_ref[...] = jnp.zeros_like(most_ref)
    most_ref[0:2, :] = functools.reduce(jnp.maximum, rows)
    most_ref[2:4, :] = -functools.reduce(jnp.minimum, rows)


def opening_kernel(level_ref, wind_ref, x_near, *others):
    put_extremes(wind_ref, x_near.at[x_near.shape[0] - 1])
    cut_edges(level_ref, x_near, *others)


def meeting_kernel(wind_ref, x_near, most_ref):
    put_extremes(wind_ref, most_ref)
    most_ref[...] = jnp.maximum(most_ref[...], x_near[x_near.shape[0] - 1])


def free_kernel(split, speed_step, s_ref, wind_ref, waves_ref, *rest):
    planes, headings, speeds, width = s_ref.shape
    tile = (speeds, width)
    if split:
        speed_ref, out_ref, extra_ref, turned_ref, mean_ref, gap_ref, flow_ref = rest
    else:
        pk_ref, speed_ref, out_ref, turned_ref, mean_ref, gap_ref, flow_ref = rest
        peak = splat(pk_ref[1:2, :] * gain, tile)
    gain_v = thrust_limit / (12.0 * speed_step)
    first = lax.axis_index("head") * headings
    cells = planes * headings
    s_rows = s_ref.reshape(cells * speeds, width)
    speed_rows = speed_ref.reshape(cells * speeds, width)
    out_rows = out_ref.reshape(cells * speeds, width)
    flow_rows = flow_ref.reshape(cells * speeds, width)
    few, many = 8, turned_ref.shape[2] // speeds
    groups = turned_ref.shape[0]
    lanes = many * speeds
    high = 8
    lines = width // high

    def along_speed(n):
        start = jnp.minimum(n * few, cells - few) * speeds
        spots = [pl.ds(start + v, few, stride=speeds) for v in range(speeds)]
        rows = [s_rows[spot, :] for spot in spots]
        ends = [rows[0]] * rim + rows + [rows[-1]] * rim
        for spot, (mean, gap) in zip(spots, row_terms(ends, speed_step)):
            speed_rows[spot, :] = gain_v * (gap - jnp.abs(mean))

    def span(n):
        return pl.ds(pl.multiple_of(jnp.minimum(n * many, cells - many) * speeds, speeds), lanes)

    def turn_in(n, carry):
        along_speed(n)
        turned = s_rows[span(n), :].T
        turned_ref[n, rim : rim + width, :] = turned
        for k in range(rim):
            turned_ref[n, k : k + 1, :] = turned[:1]
            turned_ref[n, rim + width + k : rim + width + k + 1, :] = turned[-1:]
        return carry

    def along_y(n, carry):
        ends = [turned_ref[n, pl.ds(k, high, stride=lines), :] for k in range(lines + 2 * rim)]
        for k, (mean, gap) in enumerate(row_terms(ends, spacing)):
            mean_ref[n, pl.ds(k, high, stride=lines), :] = mean
            gap_ref[n, pl.ds(k, high, stride=lines), :] = gap
        return carry

    def turn_out(n, carry):
        along_speed(groups + n)
        mean = mean_ref[n].T
        gap = gap_ref[n].T
        drift = mean * flow_rows[span(n), :]
        if split:
            out_rows[span(n), :] = drift
            extra_ref.reshape(cells * speeds, width)[span(n), :] = gap
        else:
            out_rows[span(n), :] = drift + gap * splat(peak[:1], gap.shape)
        return carry

    pace = speeds_of(tile, speed_step) * gain
    tables = [
        splat(waves_ref[1, pl.ds(first + j, 1), :], tile) * pace for j in range(headings)
    ]
    for i in range(planes):
        wind = splat(wind_ref[i, 1:2, :] * gain, tile)
        for j in range(headings):
            flow_ref[i, j] = tables[j] + wind
    lax.fori_loop(0, groups, turn_in, 0)
    lax.fori_loop(0, groups, along_y, 0)
    lax.fori_loop(0, groups, turn_out, 0)


def heading_kernel(heading_step, s_ref, speed_ref, part_ref, near_ref, far_ref, out_ref):
    planes, headings = s_ref.shape[:2]
    gain_t = turn_limit / (12.0 * heading_step)
    odd = odd_place("head")
    wide = batches(planes, 3)

    def step(n, carry):
        for w in range(wide):
            i = n * wide + w
            ghosts = [(near_ref[i * rim + k], far_ref[i * rim + k]) for k in range(rim)]
            lows = [jnp.where(odd, near, far) for near, far in ghosts]
            highs = [jnp.where(odd, far, near) for near, far in ghosts]
            cells = lows + [s_ref[i, j] for j in range(headings)] + highs
            for j, (mean, gap) in enumerate(row_terms(cells, heading_step)):
                own = speed_ref[i, j] + part_ref[i, j]
                out_ref[i, j] = own + gain_t * (gap - jnp.abs(mean))
        return carry

    lax.fori_loop(0, planes // wide, step, 0)


def peaks_into(pk_ref, most, bounds, heading_step, speed_step):
    most = jnp.max(most, axis=1, keepdims=True)
    peaks = [
        jnp.maximum(most[q : q + 1] + bounds[q][1], most[q + 2 : q + 3] - bounds[q][0])
        for q in range(2)
    ]
    time_step = courant / (
        peaks[0] / spacing
        + peaks[1] / spacing
        + turn_limit / heading_step
        + thrust_limit / speed_step
    )
    width = pk_ref.shape[1]
    for row, value in enumerate(peaks + [time_step]):
        pk_ref[row : row + 1, :] = splat(value, (1, width))


def cut_edges(field_ref, x_near, x_far, t_near, t_far):
    planes, headings = field_ref.shape[:2]
    x_low = jnp.where(odd_place("gx"), 0, planes - rim)
    t_low = jnp.where(odd_place("head"), 0, headings - rim)
    for k in range(rim):
        x_near[k * headings : (k + 1) * headings] = field_ref[x_low + k]
        x_far[k * headings : (k + 1) * headings] = field_ref[planes - rim - x_low + k]
        for i in range(planes):
            t_near[i * rim + k] = field_ref[i, t_low + k]
            t_far[i * rim + k] = field_ref[i, headings - rim - t_low + k]


def splat_targets(mask_ref, depth_ref, target_ref):
    for i in range(target_ref.shape[0]):
        depth = depth_ref[i : i + 1, :]
        target = jnp.where(mask_ref[i : i + 1, :] == 1, -depth, depth)
        target_ref[i] = splat(target, target_ref.shape[1:])


def across_planes(wide, speed_step, s_ref, near_ref, far_ref, wind_ref, waves_ref, flow_ref, use):
    planes, headings = s_ref.shape[:2]
    tile = s_ref.shape[2:]
    for i in range(planes):
        flow_ref[i] = splat(wind_ref[i, 0:1, :] * gain, tile)
    odd = odd_place("gx")
    at_low = lax.axis_index("gx") == 0
    at_high = lax.axis_index("gx") == lax.axis_size("gx") - 1
    pace = speeds_of(tile, speed_step) * gain
    first = lax.axis_index("head") * headings

    def step(n, carry):
        for w in range(wide):
            j = n * wide + w
            cells = [s_ref[i, j] for i in range(planes)]
            ghosts = [(near_ref[k * headings + j], far_ref[k * headings + j]) for k in range(rim)]
            lows = [jnp.where(at_low, cells[0], jnp.where(odd, near, far)) for near, far in ghosts]
            highs = [jnp.where(at_high, cells[-1], jnp.where(odd, far, near)) for near, far in ghosts]
            table = splat(waves_ref[0, pl.ds(first + j, 1), :], tile) * pace
            for i, (mean, gap) in enumerate(row_terms(lows + cells + highs, spacing)):
                use(i, j, mean * (table + flow_ref[i]), gap, cells[i])
        return carry

    lax.fori_loop(0, headings // wide, step, 0)


def first_kernel(
    speed_step, s_ref, part_ref, near_ref, far_ref, wind_ref, waves_ref, out_ref, gap_ref, flow_ref
):
    def use(i, j, drift, gap, cell):
        out_ref[i, j] = part_ref[i, j] + drift
        gap_ref[i, j] = gap

    wide = batches(s_ref.shape[1], 6)
    across_planes(
        wide, speed_step, s_ref, near_ref, far_ref, wind_ref, waves_ref, flow_ref, use
    )


def closing_kernel(
    bounds, heading_step, speed_step, s_ref, part_ref, gap_x_ref, gap_y_ref, mask_ref, depth_ref,
    most_ref, other_ref, out_ref, x_near, x_far, t_near, t_far, pk_ref, target_ref
):
    planes, headings = s_ref.shape[:2]
    tile = s_ref.shape[2:]
    most = jnp.maximum(most_ref[...], other_ref[...])
    peaks_into(pk_ref, most, bounds, heading_step, speed_step)
    splat_targets(mask_ref, depth_ref, target_ref)
    peak_x = splat(pk_ref[0:1, :] * gain, tile)
    peak_y = splat(pk_ref[1:2, :] * gain, tile)
    time_step = splat(pk_ref[2:3, :], tile)

    def plane(i, carry):
        for j in range(headings):
            rate = part_ref[i, j] + (gap_x_ref[i, j] * peak_x + gap_y_ref[i, j] * peak_y)
            out_ref[i, j] = jnp.minimum(s_ref[i, j] + time_step * rate, target_ref[i])
        return carry

    lax.fori_loop(0, planes, plane, 0)
    cut_edges(out_ref, x_near, x_far, t_near, t_far)


def section_kernel(
    section, speed_step, base_ref, s_ref, part_ref, near_ref, far_ref, wind_ref, waves_ref,
    mask_ref, depth_ref, pk_ref, out_ref, *refs
):
    edge_refs, (flow_ref, target_ref) = refs[:-2], refs[-2:]
    tile = s_ref.shape[2:]
    splat_targets(mask_ref, depth_ref, target_ref)
    peak_x = splat(pk_ref[0:1, :] * gain, tile)
    time_step = splat(pk_ref[2:3, :], tile)
    base_share = 0.75 if section == 2 else 1.0 / 3.0
    own_share = 0.25 if section == 2 else 2.0 / 3.0

    def use(i, j, drift, gap, cell):
        rate = part_ref[i, j] + (drift + gap * peak_x)
        moved = base_share * base_ref[i, j] + own_share * (cell + time_step * rate)
        out_ref[i, j] = jnp.minimum(moved, target_ref[i])

    wide = batches(s_ref.shape[1], 6)
    across_planes(
        wide, speed_step, s_ref, near_ref, far_ref, wind_ref, waves_ref, flow_ref, use
    )
    if section == 2:
        cut_edges(out_ref, *edge_refs)


def trade(value, axis, reach, wrap=False):
    size = lax.axis_size(axis)
    pairs = [(i, i + 1) for i in range(reach, size - 1, 2)]
    if wrap and reach and size % 2 == 0:
        pairs.append((size - 1, 0))
    pairs += [(j, i) for i, j in pairs]
    pairs += [(i, i) for i in range(size) if i not in dict(pairs)]
    return lax.ppermute(value, axis, pairs)


def local(level_set, wind_field, target_mask, target_depth):
    planes, headings, speed_count, cross_count = level_set.shape
    heading_total = headings * lax.axis_size("head")
    heading_step = 2.0 * math.pi / heading_total
    speed_step = (speed_high - speed_low) / (speed_count - 1)
    speed_row = np.float32(speed_low) + np.arange(speed_count, dtype=np.float32) * np.float32(
        speed_step
    )
    angles = np.arange(heading_total, dtype=np.float32) * np.float32(heading_step)
    waves = [np.cos(angles), np.sin(angles)]
    bounds = []
    for wave in waves:
        product = wave[:, None] * speed_row[None, :]
        bounds.append((float(product.min()), float(product.max())))
    waves = jnp.asarray(np.stack(waves)[..., None] * np.ones(cross_count, np.float32))

    vmem = pl.BlockSpec(memory_space=pltpu.VMEM)
    tile = (speed_count, cross_count)

    def shape(*dims):
        return jax.ShapeDtypeStruct(dims + tile, jnp.float32)

    field = shape(planes, headings)
    short = rim * headings
    middle = max(short + 1, rim * planes)

    longest, t_shapes = middle + 1, [shape(middle)] * 2
    first_edges = [shape(longest), shape(short)] + t_shapes
    later_edges = [shape(short), shape(longest)] + t_shapes
    rows = pltpu.VMEM((planes,) + tile, jnp.float32)
    cells = math.prod(level_set.shape)

    def call(kernel, ins, outs, scratch=(), work=0):
        return pl.pallas_call(
            kernel,
            out_shape=outs,
            in_specs=[vmem] * len(ins),
            out_specs=[vmem] * len(outs),
            scratch_shapes=list(scratch),
            compiler_params=pltpu.CompilerParams(vmem_limit_bytes=16 * 1024 * 1024),
            cost_estimate=pl.CostEstimate(
                flops=work * cells, bytes_accessed=work * cells, transcendentals=0
            ),
        )(*ins)

    wind = jnp.transpose(wind_field, (1, 0, 2))
    many = 16
    groups, lanes = -(-planes * headings // many), many * speed_count
    room = [
        pltpu.VMEM((groups, cross_count + 8, lanes), jnp.float32),
        pltpu.VMEM((groups, cross_count, lanes), jnp.float32),
        pltpu.VMEM((groups, cross_count, lanes), jnp.float32),
        pltpu.VMEM(level_set.shape, jnp.float32),
    ]
    values, pk = level_set, None
    size = lax.axis_size("gx")

    def spread(most, reach):
        if size & (size - 1):
            pairs = [(i, (i + reach) % size) for i in range(size)]
        else:
            pairs = [(i, i ^ reach) for i in range(size)]
        return lax.ppermute(most, "gx", pairs)

    edges = call(opening_kernel, [values, wind], first_edges)
    for section in (1, 2, 3):
        opening = section == 1
        x_out, x_last, t_out, t_last = edges
        x_near = trade(x_out, "gx", 0)
        t_near = trade(t_out, "head", 0)
        t_far = trade(t_last, "head", 1, True)
        x_far = trade(x_last, "gx", 1)
        free = functools.partial(free_kernel, opening, speed_step)
        turning = functools.partial(heading_kernel, heading_step)
        if opening:
            (most,) = call(meeting_kernel, [wind, x_near], [shape()])
            other = spread(most, 2)
            ins = [values, wind, waves]
            spun, part, extra = call(free, ins, [field] * 3, room, work=300)
            reach = 4
            while reach < size:
                most = jnp.maximum(most, other)
                most, part = lax.optimization_barrier((most, part))
                other = spread(most, reach)
                reach *= 2
        else:
            spun, part = call(free, [values, wind, waves, pk], [field] * 2, room)
            part, x_far = lax.optimization_barrier((part, x_far))
        (part,) = call(turning, [values, spun, part, t_near, t_far], [field], work=1000)
        if opening:
            ins = [values, part, x_near, x_far, wind, waves]
            first = functools.partial(first_kernel, speed_step)
            part, gap = call(first, ins, [field] * 2, [rows])
            closing = functools.partial(closing_kernel, bounds, heading_step, speed_step)
            ins = [values, part, gap, extra, target_mask, target_depth, most, other]
            values, *edges, pk = call(closing, ins, [field, *later_edges, shape()], [rows])
        else:
            ins = [level_set, values, part, x_near, x_far, wind, waves]
            ins += [target_mask, target_depth, pk]
            outs = [field] + (later_edges if section == 2 else [])
            last = functools.partial(section_kernel, section, speed_step)
            values, *edges = call(last, ins, outs, [rows, rows])
    return values


def solution(mesh):
    return jax.shard_map(
        local,
        mesh=mesh,
        in_specs=(P("gx", "head", None, None), P(None, "gx", None), P("gx", None), P("gx", None)),
        out_specs=P("gx", "head", None, None),
        check_vma=False,
    )
```

```python
import functools
import math

import jax
import jax.numpy as jnp
import numpy as np
from jax import lax
from jax.experimental import pallas as pl
from jax.experimental.pallas import tpu as pltpu
from jax.sharding import PartitionSpec as P

epsilon = 1e-06
courant = 0.5
spacing = 0.05
turn_limit = 1.0
thrust_limit = 0.5
speed_low = 0.5
speed_high = 1.5
rim = 3
gain = 1.0 / (12.0 * spacing)


def inverse(value):
    return pltpu.reciprocal(value, approx=True)


def weights_of(e1, e2, turn, eps):
    level = turn * turn * (4.0 / 3.0) + eps
    ia = inverse(level + e2 * (e2 + turn))
    ib = inverse(level + e2 * e1)
    ic = inverse(level + e1 * (e1 - turn))
    return ia * ia, ib * ib * 6.0, ic * ic


def sides(fl, f0, fr, a2, a1, b1, b0, c0, c1):
    a3 = a1 * 3.0
    c3 = c0 * 3.0
    minus = ((fl + fl) * a2 + f0 * c3) * inverse(a2 + b1 + c3)
    plus = ((fr + fr) * c1 + f0 * a3) * inverse(c1 + b0 + a3)
    return minus, plus


def row_terms(cells, step):
    count = len(cells) - 2 * rim
    eps = epsilon * step * step
    slope = [cells[i + 1] - cells[i] for i in range(len(cells) - 1)]
    bend = {m: slope[m + 3] - slope[m + 2] for m in range(-2, count + 2)}
    turn = {m: bend[m + 1] - bend[m] for m in range(-2, count + 1)}
    jerk = {m: turn[m] - turn[m - 1] for m in range(-1, count + 1)}
    a, b, c = {}, {}, {}
    for m in turn:
        a[m], b[m], c[m] = weights_of(bend[m], bend[m + 1], turn[m], eps)
    out = []
    for i in range(count):
        base = (cells[i + 4] - cells[i + 2]) * 6.0 - (turn[i - 1] + turn[i])
        minus, plus = sides(
            jerk[i - 1], jerk[i], jerk[i + 1], a[i - 2], a[i - 1], b[i - 1], b[i], c[i], c[i + 1]
        )
        out.append((base + (plus - minus), (plus + minus) - jerk[i]))
    return out


def batches(total, most):
    return max(k for k in range(1, most + 1) if total % k == 0)


def splat(row, tile):
    return jnp.broadcast_to(row, tile)


def speeds_of(tile, speed_step):
    place = lax.broadcasted_iota(jnp.int32, tile, 0).astype(jnp.float32)
    return speed_low + place * speed_step


def odd_place(axis):
    return lax.rem(lax.axis_index(axis), 2) == 1


def put_extremes(wind_ref, most_ref):
    rows = [wind_ref[i] for i in range(wind_ref.shape[0])]
    most_ref[...] = jnp.zeros_like(most_ref)
    most_ref[0:2, :] = functools.reduce(jnp.maximum, rows)
    most_ref[2:4, :] = -functools.reduce(jnp.minimum, rows)


def near_kernel(level_ref, wind_ref, x_near):
    put_extremes(wind_ref, x_near.at[x_near.shape[0] - 1])
    cut_near(level_ref, x_near)


def far_kernel(level_ref, x_far, t_near, t_far):
    cut_far(level_ref, x_far)
    cut_headings(level_ref, t_near, t_far)


def meeting_kernel(wind_ref, x_near, most_ref):
    put_extremes(wind_ref, most_ref)
    most_ref[...] = jnp.maximum(most_ref[...], x_near[x_near.shape[0] - 1])


def free_kernel(split, speed_step, s_ref, wind_ref, waves_ref, *rest):
    planes, headings, speeds, width = s_ref.shape
    tile = (speeds, width)
    if split:
        speed_ref, out_ref, extra_ref, turned_ref, mean_ref, gap_ref, flow_ref = rest
    else:
        pk_ref, speed_ref, out_ref, turned_ref, mean_ref, gap_ref, flow_ref = rest
        peak = splat(pk_ref[1:2, :] * gain, tile)
    gain_v = thrust_limit / (12.0 * speed_step)
    first = lax.axis_index("head") * headings
    cells = planes * headings
    s_rows = s_ref.reshape(cells * speeds, width)
    speed_rows = speed_ref.reshape(cells * speeds, width)
    out_rows = out_ref.reshape(cells * speeds, width)
    flow_rows = flow_ref.reshape(cells * speeds, width)
    few, many = 8, turned_ref.shape[2] // speeds
    groups = turned_ref.shape[0]
    lanes = many * speeds
    high = 8
    lines = width // high

    def along_speed(n):
        start = jnp.minimum(n * few, cells - few) * speeds
        spots = [pl.ds(start + v, few, stride=speeds) for v in range(speeds)]
        rows = [s_rows[spot, :] for spot in spots]
        ends = [rows[0]] * rim + rows + [rows[-1]] * rim
        for spot, (mean, gap) in zip(spots, row_terms(ends, speed_step)):
            speed_rows[spot, :] = gain_v * (gap - jnp.abs(mean))

    def span(n):
        return pl.ds(pl.multiple_of(jnp.minimum(n * many, cells - many) * speeds, speeds), lanes)

    def turn_in(n, carry):
        along_speed(n)
        turned = s_rows[span(n), :].T
        turned_ref[n, rim : rim + width, :] = turned
        for k in range(rim):
            turned_ref[n, k : k + 1, :] = turned[:1]
            turned_ref[n, rim + width + k : rim + width + k + 1, :] = turned[-1:]
        return carry

    def along_y(n, carry):
        ends = [turned_ref[n, pl.ds(k, high, stride=lines), :] for k in range(lines + 2 * rim)]
        for k, (mean, gap) in enumerate(row_terms(ends, spacing)):
            mean_ref[n, pl.ds(k, high, stride=lines), :] = mean
            gap_ref[n, pl.ds(k, high, stride=lines), :] = gap
        return carry

    def turn_out(n, carry):
        along_speed(groups + n)
        mean = mean_ref[n].T
        gap = gap_ref[n].T
        drift = mean * flow_rows[span(n), :]
        if split:
            out_rows[span(n), :] = drift
            extra_ref.reshape(cells * speeds, width)[span(n), :] = gap
        else:
            out_rows[span(n), :] = drift + gap * splat(peak[:1], gap.shape)
        return carry

    pace = speeds_of(tile, speed_step) * gain
    tables = [
        splat(waves_ref[1, pl.ds(first + j, 1), :], tile) * pace for j in range(headings)
    ]
    for i in range(planes):
        wind = splat(wind_ref[i, 1:2, :] * gain, tile)
        for j in range(headings):
            flow_ref[i, j] = tables[j] + wind
    lax.fori_loop(0, groups, turn_in, 0)
    lax.fori_loop(0, groups, along_y, 0)
    lax.fori_loop(0, groups, turn_out, 0)


def heading_kernel(heading_step, s_ref, speed_ref, part_ref, near_ref, far_ref, out_ref):
    planes, headings = s_ref.shape[:2]
    gain_t = turn_limit / (12.0 * heading_step)
    odd = odd_place("head")
    wide = batches(planes, 3)

    def step(n, carry):
        for w in range(wide):
            i = n * wide + w
            ghosts = [(near_ref[i * rim + k], far_ref[i * rim + k]) for k in range(rim)]
            lows = [jnp.where(odd, near, far) for near, far in ghosts]
            highs = [jnp.where(odd, far, near) for near, far in ghosts]
            cells = lows + [s_ref[i, j] for j in range(headings)] + highs
            for j, (mean, gap) in enumerate(row_terms(cells, heading_step)):
                own = speed_ref[i, j] + part_ref[i, j]
                out_ref[i, j] = own + gain_t * (gap - jnp.abs(mean))
        return carry

    lax.fori_loop(0, planes // wide, step, 0)


def peaks_into(pk_ref, most, bounds, heading_step, speed_step):
    most = jnp.max(most, axis=1, keepdims=True)
    peaks = [
        jnp.maximum(most[q : q + 1] + bounds[q][1], most[q + 2 : q + 3] - bounds[q][0])
        for q in range(2)
    ]
    time_step = courant / (
        peaks[0] / spacing
        + peaks[1] / spacing
        + turn_limit / heading_step
        + thrust_limit / speed_step
    )
    width = pk_ref.shape[1]
    for row, value in enumerate(peaks + [time_step]):
        pk_ref[row : row + 1, :] = splat(value, (1, width))


def plane_at(i, planes):
    return jnp.where(odd_place("gx"), i, planes - 1 - i)


def alone(reach):
    place, size = lax.axis_index("gx"), lax.axis_size("gx")
    if reach == 0:
        return (place == size - 1) if size % 2 else place < 0
    return (place == 0) | (place == size - 1) if size % 2 == 0 else place == 0


def cut_near(field_ref, x_near):
    planes, headings = field_ref.shape[:2]
    for k in range(rim):
        i = jnp.where(alone(0), 0, k)
        x_near[k * headings : (k + 1) * headings] = field_ref[plane_at(i, planes)]


def cut_far(field_ref, x_far):
    planes, headings = field_ref.shape[:2]
    for k in range(rim):
        i = planes - 1 - jnp.where(alone(1), 0, k)
        x_far[k * headings : (k + 1) * headings] = field_ref[plane_at(i, planes)]


def cut_headings(field_ref, t_near, t_far):
    planes, headings = field_ref.shape[:2]
    t_low = jnp.where(odd_place("head"), 0, headings - rim)
    for k in range(rim):
        for i in range(planes):
            t_near[i * rim + k] = field_ref[i, t_low + k]
            t_far[i * rim + k] = field_ref[i, headings - rim - t_low + k]


def splat_targets(mask_ref, depth_ref, target_ref):
    for i in range(target_ref.shape[0]):
        depth = depth_ref[i : i + 1, :]
        target = jnp.where(mask_ref[i : i + 1, :] == 1, -depth, depth)
        target_ref[i] = splat(target, target_ref.shape[1:])


def across_planes(
    span, speed_step, s_ref, near_ref, far_ref, wind_ref, waves_ref, flow_ref, use
):
    planes, headings = s_ref.shape[:2]
    tile = s_ref.shape[2:]
    side = jnp.where(odd_place("gx"), gain, -gain).astype(jnp.float32)
    spots = [plane_at(i, planes) for i in range(planes)]
    for i in range(planes):
        flow_ref[i] = splat(wind_ref[i, 0:1, :] * side, tile)
    pace = speeds_of(tile, speed_step) * side
    first = lax.axis_index("head") * headings
    low, high = span
    wide = batches(headings, max(1, 54 // (high - low)))

    def line(i, j):
        if i < 0:
            return near_ref[(-1 - i) * headings + j]
        if i >= planes:
            return far_ref[(i - planes) * headings + j]
        return s_ref[spots[i], j]

    def step(n, carry):
        for w in range(wide):
            j = n * wide + w
            cells = [line(i, j) for i in range(low - rim, high + rim)]
            table = splat(waves_ref[0, pl.ds(first + j, 1), :], tile) * pace
            for k, (mean, gap) in enumerate(row_terms(cells, spacing)):
                spot = spots[low + k]
                use(spot, j, mean * (table + flow_ref[spot]), gap, cells[k + rim])
        return carry

    lax.fori_loop(0, headings // wide, step, 0)


def first_kernel(
    speed_step, s_ref, part_ref, near_ref, far_ref, wind_ref, waves_ref, out_ref, gap_ref, flow_ref
):
    def use(i, j, drift, gap, cell):
        out_ref[i, j] = part_ref[i, j] + drift
        gap_ref[i, j] = gap

    across_planes(
        (0, s_ref.shape[0]), speed_step, s_ref, near_ref, far_ref, wind_ref, waves_ref, flow_ref, use
    )


def closing_kernel(
    bounds, heading_step, speed_step, s_ref, part_ref, gap_x_ref, gap_y_ref, mask_ref, depth_ref,
    most_ref, other_ref, out_ref, x_near, x_far, t_near, t_far, pk_ref, target_ref
):
    planes, headings = s_ref.shape[:2]
    tile = s_ref.shape[2:]
    most = jnp.maximum(most_ref[...], other_ref[...])
    peaks_into(pk_ref, most, bounds, heading_step, speed_step)
    splat_targets(mask_ref, depth_ref, target_ref)
    peak_x = splat(pk_ref[0:1, :] * gain, tile)
    peak_y = splat(pk_ref[1:2, :] * gain, tile)
    time_step = splat(pk_ref[2:3, :], tile)

    def plane(i, carry):
        for j in range(headings):
            rate = part_ref[i, j] + (gap_x_ref[i, j] * peak_x + gap_y_ref[i, j] * peak_y)
            out_ref[i, j] = jnp.minimum(s_ref[i, j] + time_step * rate, target_ref[i])
        return carry

    lax.fori_loop(0, planes, plane, 0)
    cut_near(out_ref, x_near)
    cut_far(out_ref, x_far)
    cut_headings(out_ref, t_near, t_far)


def section_kernel(
    section, span, speed_step, base_ref, s_ref, part_ref, ghosts_ref, wind_ref, waves_ref,
    mask_ref, depth_ref, pk_ref, *refs
):
    planes = s_ref.shape[0]
    refs, (flow_ref, target_ref) = list(refs[:-2]), refs[-2:]
    early_ref = refs.pop(0) if span[0] > 0 else None
    out_ref = refs.pop(0)
    tile = s_ref.shape[2:]
    splat_targets(mask_ref, depth_ref, target_ref)
    peak_x = splat(pk_ref[0:1, :] * gain, tile)
    time_step = splat(pk_ref[2:3, :], tile)
    base_share = 0.75 if section == 2 else 1.0 / 3.0
    own_share = 0.25 if section == 2 else 2.0 / 3.0

    def use(i, j, drift, gap, cell):
        rate = part_ref[i, j] + (drift + gap * peak_x)
        moved = base_share * base_ref[i, j] + own_share * (cell + time_step * rate)
        out_ref[i, j] = jnp.minimum(moved, target_ref[i])

    near_ref, far_ref = (None, ghosts_ref) if span[0] > 0 else (ghosts_ref, None)
    across_planes(
        span, speed_step, s_ref, near_ref, far_ref, wind_ref, waves_ref, flow_ref, use
    )
    for i in range(span[0]):
        spot = plane_at(i, planes)
        out_ref[spot] = early_ref[spot]
    if section == 2 and span[0] == 0:
        cut_near(out_ref, *refs)
    elif section == 2:
        cut_far(out_ref, refs[0])
        cut_headings(out_ref, *refs[1:])


def trade(value, axis, reach, wrap=False):
    size = lax.axis_size(axis)
    pairs = [(i, i + 1) for i in range(reach, size - 1, 2)]
    if wrap and reach and size % 2 == 0:
        pairs.append((size - 1, 0))
    pairs += [(j, i) for i, j in pairs]
    pairs += [(i, i) for i in range(size) if i not in dict(pairs)]
    return lax.ppermute(value, axis, pairs)


def local(level_set, wind_field, target_mask, target_depth):
    planes, headings, speed_count, cross_count = level_set.shape
    heading_total = headings * lax.axis_size("head")
    heading_step = 2.0 * math.pi / heading_total
    speed_step = (speed_high - speed_low) / (speed_count - 1)
    speed_row = np.float32(speed_low) + np.arange(speed_count, dtype=np.float32) * np.float32(
        speed_step
    )
    angles = np.arange(heading_total, dtype=np.float32) * np.float32(heading_step)
    waves = [np.cos(angles), np.sin(angles)]
    bounds = []
    for wave in waves:
        product = wave[:, None] * speed_row[None, :]
        bounds.append((float(product.min()), float(product.max())))
    waves = jnp.asarray(np.stack(waves)[..., None] * np.ones(cross_count, np.float32))

    vmem = pl.BlockSpec(memory_space=pltpu.VMEM)
    tile = (speed_count, cross_count)

    def shape(*dims):
        return jax.ShapeDtypeStruct(dims + tile, jnp.float32)

    field = shape(planes, headings)
    short = rim * headings
    middle = max(short + 1, rim * planes)

    longest = middle + 1
    rows = pltpu.VMEM((planes,) + tile, jnp.float32)
    cells = math.prod(level_set.shape)

    def call(kernel, ins, outs, scratch=(), work=0):
        return pl.pallas_call(
            kernel,
            out_shape=outs,
            in_specs=[vmem] * len(ins),
            out_specs=[vmem] * len(outs),
            scratch_shapes=list(scratch),
            compiler_params=pltpu.CompilerParams(vmem_limit_bytes=16 * 1024 * 1024),
            cost_estimate=pl.CostEstimate(
                flops=work * cells, bytes_accessed=work * cells, transcendentals=0
            ),
        )(*ins)

    wind = jnp.transpose(wind_field, (1, 0, 2))
    many = 16
    groups, lanes = -(-planes * headings // many), many * speed_count
    room = [
        pltpu.VMEM((groups, cross_count + 8, lanes), jnp.float32),
        pltpu.VMEM((groups, cross_count, lanes), jnp.float32),
        pltpu.VMEM((groups, cross_count, lanes), jnp.float32),
        pltpu.VMEM(level_set.shape, jnp.float32),
    ]
    values = level_set
    size = lax.axis_size(axis)
    pairs = [(i, i + 1) for i in range(reach, size - 1, 2)]
    if wrap and reach and size % 2 == 0:
        pairs.append((size - 1, 0))
    pairs += [(j, i) for i, j in pairs]
    pairs += [(i, i) for i in range(size) if i not in dict(pairs)]
    return lax.ppermute(value, axis, pairs)


def local(level_set, wind_field, target_mask, target_depth):
    planes, headings, speed_count, cross_count = level_set.shape
    heading_total = headings * lax.axis_size("head")
    heading_step = 2.0 * math.pi / heading_total
    speed_step = (speed_high - speed_low) / (speed_count - 1)
    speed_row = np.float32(speed_low) + np.arange(speed_count, dtype=np.float32) * np.float32(
        speed_step
    )
    angles = np.arange(heading_total, dtype=np.float32) * np.float32(heading_step)
    waves = [np.cos(angles), np.sin(angles)]
    bounds = []
    for wave in waves:
        product = wave[:, None] * speed_row[None, :]
        bounds.append((float(product.min()), float(product.max())))
    waves = jnp.asarray(np.stack(waves)[..., None] * np.ones(cross_count, np.float32))

    vmem = pl.BlockSpec(memory_space=pltpu.VMEM)
    tile = (speed_count, cross_count)

    def shape(*dims):
        return jax.ShapeDtypeStruct(dims + tile, jnp.float32)

    field = shape(planes, headings)
    short = rim * headings
    middle = max(short + 1, rim * planes)

    longest = middle + 1
    rows = pltpu.VMEM((planes,) + tile, jnp.float32)
    cells = math.prod(level_set.shape)

    def call(kernel, ins, outs, scratch=(), work=0):
        return pl.pallas_call(
            kernel,
            out_shape=outs,
            in_specs=[vmem] * len(ins),
            out_specs=[vmem] * len(outs),
            scratch_shapes=list(scratch),
            compiler_params=pltpu.CompilerParams(vmem_limit_bytes=16 * 1024 * 1024),
            cost_estimate=pl.CostEstimate(
                flops=work * cells, bytes_accessed=work * cells, transcendentals=0
            ),
        )(*ins)

    wind = jnp.transpose(wind_field, (1, 0, 2))
    many = 16
    groups, lanes = -(-planes * headings // many), many * speed_count
    room = [
        pltpu.VMEM((groups, cross_count + 8, lanes), jnp.float32),
        pltpu.VMEM((groups, cross_count, lanes), jnp.float32),
        pltpu.VMEM((groups, cross_count, lanes), jnp.float32),
        pltpu.VMEM(level_set.shape, jnp.float32),
    ]
    values, pk = level_set, None
    size = lax.axis_size("gx")

    def spread(most, reach):
        if size & (size - 1):
            pairs = [(i, (i + reach) % size) for i in range(size)]
        else:
            pairs = [(i, i ^ reach) for i in range(size)]
        return lax.ppermute(most, "gx", pairs)

    far_shapes = [shape(short), shape(longest + 1), shape(longest + 1)]
    x_last, t_out, t_last = call(far_kernel, [values], far_shapes)
    (x_out,) = call(near_kernel, [values, wind], [shape(longest)])
    far_shapes = [shape(short), shape(middle), shape(middle)]
    for section in (1, 2, 3):
        opening = section == 1
        x_near = trade(x_out, "gx", 0)
        t_near = trade(t_out, "head", 0)
        t_far = trade(t_last, "head", 1, True)
        x_far = trade(x_last, "gx", 1)
        free = functools.partial(free_kernel, opening, speed_step)
        turning = functools.partial(heading_kernel, heading_step)
        if opening:
            (most,) = call(meeting_kernel, [wind, x_near], [shape()])
            other = spread(most, 2)
            ins = [values, wind, waves]
            spun, part, extra = call(free, ins, [field] * 3, room, work=300)
            reach = 4
            while reach < size:
                most = jnp.maximum(most, other)
                most, part = lax.optimization_barrier((most, part))
                other = spread(most, reach)
                reach *= 2
        else:
            values, x_near = lax.optimization_barrier((values, x_near))
            spun, part = call(free, [values, wind, waves, pk], [field] * 2, room)
        (part,) = call(turning, [values, spun, part, t_near, t_far], [field], work=1000)
        if opening:
            ins = [values, part, x_near, x_far, wind, waves]
            first = functools.partial(first_kernel, speed_step)
            part, gap = call(first, ins, [field] * 2, [rows])
            closing = functools.partial(closing_kernel, bounds, heading_step, speed_step)
            ins = [values, part, gap, extra, target_mask, target_depth, most, other]
            outs = [field, shape(longest), *far_shapes, shape()]
            values, x_out, x_last, t_out, t_last, pk = call(closing, ins, outs, [rows])
        else:
            more = section == 2
            ins = [level_set, values, part, x_near, wind, waves, target_mask, target_depth, pk]
            outs = [field] + ([shape(longest)] if more else [])
            last = functools.partial(section_kernel, section, (0, planes - rim), speed_step)
            early, *x_next = call(last, ins, outs, [rows, rows])
            ins = ins[:3] + [x_far] + ins[4:] + [early]
            outs = [field] + (far_shapes if more else [])
            last = functools.partial(section_kernel, section, (planes - rim, planes), speed_step)
            values, *far_next = call(last, ins, outs, [rows, rows])
            if more:
                (x_out,), (x_last, t_out, t_last) = x_next, far_next
    return values


def solution(mesh):
    return jax.shard_map(
        local,
        mesh=mesh,
        in_specs=(P("gx", "head", None, None), P(None, "gx", None), P("gx", None), P("gx", None)),
        out_specs=P("gx", "head", None, None),
        check_vma=False,
    )
```

```python
import functools
import math

import jax
import jax.numpy as jnp
import numpy as np
from jax import lax
from jax.experimental import pallas as pl
from jax.experimental.pallas import tpu as pltpu
from jax.sharding import PartitionSpec as P

epsilon = 1e-06
courant = 0.5
spacing = 0.05
turn_limit = 1.0
thrust_limit = 0.5
speed_low = 0.5
speed_high = 1.5
rim = 3
gain = 1.0 / (12.0 * spacing)


def inverse(value):
    return pltpu.reciprocal(value, approx=True)


def weights_of(e1, e2, turn, eps):
    level = turn * turn * (4.0 / 3.0) + eps
    ia = inverse(level + e2 * (e2 + turn))
    ib = inverse(level + e2 * e1)
    ic = inverse(level + e1 * (e1 - turn))
    return ia * ia, ib * ib * 6.0, ic * ic


def sides(fl, f0, fr, a2, a1, b1, b0, c0, c1):
    a3 = a1 * 3.0
    c3 = c0 * 3.0
    minus = ((fl + fl) * a2 + f0 * c3) * inverse(a2 + b1 + c3)
    plus = ((fr + fr) * c1 + f0 * a3) * inverse(c1 + b0 + a3)
    return minus, plus


def row_terms(cells, step):
    count = len(cells) - 2 * rim
    eps = epsilon * step * step
    slope = [cells[i + 1] - cells[i] for i in range(len(cells) - 1)]
    bend = {m: slope[m + 3] - slope[m + 2] for m in range(-2, count + 2)}
    turn = {m: bend[m + 1] - bend[m] for m in range(-2, count + 1)}
    jerk = {m: turn[m] - turn[m - 1] for m in range(-1, count + 1)}
    a, b, c = {}, {}, {}
    for m in turn:
        a[m], b[m], c[m] = weights_of(bend[m], bend[m + 1], turn[m], eps)
    out = []
    for i in range(count):
        base = (cells[i + 4] - cells[i + 2]) * 6.0 - (turn[i - 1] + turn[i])
        minus, plus = sides(
            jerk[i - 1], jerk[i], jerk[i + 1], a[i - 2], a[i - 1], b[i - 1], b[i], c[i], c[i + 1]
        )
        out.append((base + (plus - minus), (plus + minus) - jerk[i]))
    return out


def batches(total, most):
    return max(k for k in range(1, most + 1) if total % k == 0)


def splat(row, tile):
    return jnp.broadcast_to(row, tile)


def speeds_of(tile, speed_step):
    place = lax.broadcasted_iota(jnp.int32, tile, 0).astype(jnp.float32)
    return speed_low + place * speed_step


def odd_place(axis):
    return lax.rem(lax.axis_index(axis), 2) == 1


def put_extremes(wind_ref, most_ref):
    rows = [wind_ref[i] for i in range(wind_ref.shape[0])]
    most_ref[...] = jnp.zeros_like(most_ref)
    most_ref[0:2, :] = functools.reduce(jnp.maximum, rows)
    most_ref[2:4, :] = -functools.reduce(jnp.minimum, rows)


def extremes_kernel(wind_ref, most_ref):
    put_extremes(wind_ref, most_ref.at[0])


def opening_kernel(level_ref, x_near, x_far, t_near, t_far):
    cut_near(level_ref, x_near)
    cut_far(level_ref, x_far)
    cut_headings(level_ref, t_near, t_far)


def meeting_kernel(own_ref, other_ref, most_ref):
    most_ref[...] = jnp.maximum(own_ref[0], other_ref[0])


def flows_into(flow_ref, speed_step, wind_ref, waves_ref):
    planes, headings = flow_ref.shape[:2]
    tile = flow_ref.shape[2:]
    first = lax.axis_index("head") * headings
    pace = speeds_of(tile, speed_step) * gain
    tables = [
        splat(waves_ref[1, pl.ds(first + j, 1), :], tile) * pace for j in range(headings)
    ]
    for i in range(planes):
        wind = splat(wind_ref[i, 1:2, :] * gain, tile)
        for j in range(headings):
            flow_ref[i, j] = tables[j] + wind


def free_kernel(split, speed_step, s_ref, *rest):
    planes, headings, speeds, width = s_ref.shape
    cells = planes * headings

    def rows_of(ref):
        return ref.reshape(cells * speeds, width)

    if split:
        wind_ref, waves_ref, speed_ref, out_ref, extra_ref, flow_ref = rest[:-3]
        flows_into(flow_ref, speed_step, wind_ref, waves_ref)
        extra_rows = rows_of(extra_ref)
    else:
        flow_ref, pk_ref, speed_ref, out_ref = rest[:-3]
        peak = splat(pk_ref[1:2, :] * gain, (16 * speeds, width))
    turned_ref, mean_ref, gap_ref = rest[-3:]
    gain_v = thrust_limit / (12.0 * speed_step)
    s_rows, speed_rows = rows_of(s_ref), rows_of(speed_ref)
    out_rows, flow_rows = rows_of(out_ref), rows_of(flow_ref)
    few, many = 8, turned_ref.shape[2] // speeds
    groups = turned_ref.shape[0]
    lanes = many * speeds
    high = 8
    lines = width // high

    def along_speed(n):
        start = jnp.minimum(n * few, cells - few) * speeds
        spots = [pl.ds(start + v, few, stride=speeds) for v in range(speeds)]
        rows = [s_rows[spot, :] for spot in spots]
        ends = [rows[0]] * rim + rows + [rows[-1]] * rim
        for spot, (mean, gap) in zip(spots, row_terms(ends, speed_step)):
            speed_rows[spot, :] = gain_v * (gap - jnp.abs(mean))

    def span(n):
        return pl.ds(pl.multiple_of(jnp.minimum(n * many, cells - many) * speeds, speeds), lanes)

    def turn_in(n):
        turned = s_rows[span(n), :].T
        turned_ref[n, rim : rim + width, :] = turned
        for k in range(rim):
            turned_ref[n, k : k + 1, :] = turned[:1]
            turned_ref[n, rim + width + k : rim + width + k + 1, :] = turned[-1:]

    def along_y(n):
        ends = [turned_ref[n, pl.ds(k, high, stride=lines), :] for k in range(lines + 2 * rim)]
        for k, (mean, gap) in enumerate(row_terms(ends, spacing)):
            mean_ref[n, pl.ds(k, high, stride=lines), :] = mean
            gap_ref[n, pl.ds(k, high, stride=lines), :] = gap

    def turn_out(n):
        mean = mean_ref[n].T
        gap = gap_ref[n].T
        drift = mean * flow_rows[span(n), :]
        if split:
            out_rows[span(n), :] = drift
            extra_rows[span(n), :] = gap
        else:
            out_rows[span(n), :] = drift + gap * peak

    def step(n, carry):
        turn_out(jnp.maximum(n - 1, 0))
        along_y(n)
        turn_in(jnp.minimum(n + 1, groups - 1))
        along_speed(2 * n)
        along_speed(2 * n + 1)
        return carry

    turn_in(0)
    lax.fori_loop(0, groups, step, 0)
    turn_out(groups - 1)


def heading_kernel(heading_step, s_ref, speed_ref, part_ref, near_ref, far_ref, out_ref):
    planes, headings = s_ref.shape[:2]
    gain_t = turn_limit / (12.0 * heading_step)
    odd = odd_place("head")
    wide = batches(planes, 3)

    def step(n, carry):
        for w in range(wide):
            i = n * wide + w
            ghosts = [(near_ref[i * rim + k], far_ref[i * rim + k]) for k in range(rim)]
            lows = [jnp.where(odd, near, far) for near, far in ghosts]
            highs = [jnp.where(odd, far, near) for near, far in ghosts]
            cells = lows + [s_ref[i, j] for j in range(headings)] + highs
            for j, (mean, gap) in enumerate(row_terms(cells, heading_step)):
                own = speed_ref[i, j] + part_ref[i, j]
                out_ref[i, j] = own + gain_t * (gap - jnp.abs(mean))
        return carry

    lax.fori_loop(0, planes // wide, step, 0)


def peaks_into(pk_ref, most, bounds, heading_step, speed_step):
    most = jnp.max(most, axis=1, keepdims=True)
    peaks = [
        jnp.maximum(most[q : q + 1] + bounds[q][1], most[q + 2 : q + 3] - bounds[q][0])
        for q in range(2)
    ]
    time_step = courant / (
        peaks[0] / spacing
        + peaks[1] / spacing
        + turn_limit / heading_step
        + thrust_limit / speed_step
    )
    width = pk_ref.shape[1]
    for row, value in enumerate(peaks + [time_step]):
        pk_ref[row : row + 1, :] = splat(value, (1, width))


def plane_at(i, planes):
    return jnp.where(odd_place("gx"), i, planes - 1 - i)


def alone(reach):
    place, size = lax.axis_index("gx"), lax.axis_size("gx")
    if reach == 0:
        return (place == size - 1) if size % 2 else place < 0
    return (place == 0) | (place == size - 1) if size % 2 == 0 else place == 0


def cut_near(field_ref, x_near):
    planes, headings = field_ref.shape[:2]
    for k in range(rim):
        i = jnp.where(alone(0), 0, k)
        x_near[k * headings : (k + 1) * headings] = field_ref[plane_at(i, planes)]


def cut_far(field_ref, x_far):
    planes, headings = field_ref.shape[:2]
    for k in range(rim):
        i = planes - 1 - jnp.where(alone(1), 0, k)
        x_far[k * headings : (k + 1) * headings] = field_ref[plane_at(i, planes)]


def cut_headings(field_ref, t_near, t_far):
    planes, headings = field_ref.shape[:2]
    t_low = jnp.where(odd_place("head"), 0, headings - rim)
    for k in range(rim):
        for i in range(planes):
            t_near[i * rim + k] = field_ref[i, t_low + k]
            t_far[i * rim + k] = field_ref[i, headings - rim - t_low + k]


def splat_targets(mask_ref, depth_ref, target_ref):
    for i in range(target_ref.shape[0]):
        depth = depth_ref[i : i + 1, :]
        target = jnp.where(mask_ref[i : i + 1, :] == 1, -depth, depth)
        target_ref[i] = splat(target, target_ref.shape[1:])


def across_planes(
    span, speed_step, s_ref, near_ref, far_ref, wind_ref, waves_ref, flow_ref, use
):
    planes, headings = s_ref.shape[:2]
    tile = s_ref.shape[2:]
    side = jnp.where(odd_place("gx"), gain, -gain).astype(jnp.float32)
    spots = [plane_at(i, planes) for i in range(planes)]
    for i in range(planes):
        flow_ref[i] = splat(wind_ref[i, 0:1, :] * side, tile)
    pace = speeds_of(tile, speed_step) * side
    first = lax.axis_index("head") * headings
    low, high = span
    wide = batches(headings, max(1, 54 // (high - low)))

    def line(i, j):
        if i < 0:
            return near_ref[(-1 - i) * headings + j]
        if i >= planes:
            return far_ref[(i - planes) * headings + j]
        return s_ref[spots[i], j]

    def step(n, carry):
        for w in range(wide):
            j = n * wide + w
            cells = [line(i, j) for i in range(low - rim, high + rim)]
            table = splat(waves_ref[0, pl.ds(first + j, 1), :], tile) * pace
            for k, (mean, gap) in enumerate(row_terms(cells, spacing)):
                spot = spots[low + k]
                use(spot, j, mean * (table + flow_ref[spot]), gap, cells[k + rim])
        return carry

    lax.fori_loop(0, headings // wide, step, 0)


def first_kernel(
    speed_step, s_ref, part_ref, near_ref, far_ref, wind_ref, waves_ref, out_ref, gap_ref, flow_ref
):
    def use(i, j, drift, gap, cell):
        out_ref[i, j] = part_ref[i, j] + drift
        gap_ref[i, j] = gap

    across_planes(
        (0, s_ref.shape[0]), speed_step, s_ref, near_ref, far_ref, wind_ref, waves_ref, flow_ref, use
    )


def closing_kernel(
    bounds, heading_step, speed_step, s_ref, part_ref, gap_x_ref, gap_y_ref, mask_ref, depth_ref,
    most_ref, other_ref, out_ref, x_near, x_far, t_near, t_far, pk_ref, target_ref
):
    planes, headings = s_ref.shape[:2]
    tile = s_ref.shape[2:]
    most = jnp.maximum(most_ref[...], other_ref[...])
    peaks_into(pk_ref, most, bounds, heading_step, speed_step)
    splat_targets(mask_ref, depth_ref, target_ref)
    peak_x = splat(pk_ref[0:1, :] * gain, tile)
    peak_y = splat(pk_ref[1:2, :] * gain, tile)
    time_step = splat(pk_ref[2:3, :], tile)

    def plane(i, carry):
        for j in range(headings):
            rate = part_ref[i, j] + (gap_x_ref[i, j] * peak_x + gap_y_ref[i, j] * peak_y)
            out_ref[i, j] = jnp.minimum(s_ref[i, j] + time_step * rate, target_ref[i])
        return carry

    lax.fori_loop(0, planes, plane, 0)
    cut_near(out_ref, x_near)
    cut_far(out_ref, x_far)
    cut_headings(out_ref, t_near, t_far)


def section_kernel(
    section, span, speed_step, base_ref, s_ref, part_ref, ghosts_ref, wind_ref, waves_ref,
    mask_ref, depth_ref, pk_ref, *refs
):
    planes = s_ref.shape[0]
    refs, (flow_ref, target_ref) = list(refs[:-2]), refs[-2:]
    early_ref = refs.pop(0) if span[0] > 0 else None
    out_ref = refs.pop(0)
    tile = s_ref.shape[2:]
    splat_targets(mask_ref, depth_ref, target_ref)
    peak_x = splat(pk_ref[0:1, :] * gain, tile)
    time_step = splat(pk_ref[2:3, :], tile)
    base_share = 0.75 if section == 2 else 1.0 / 3.0
    own_share = 0.25 if section == 2 else 2.0 / 3.0

    def use(i, j, drift, gap, cell):
        rate = part_ref[i, j] + (drift + gap * peak_x)
        moved = base_share * base_ref[i, j] + own_share * (cell + time_step * rate)
        out_ref[i, j] = jnp.minimum(moved, target_ref[i])

    near_ref, far_ref = (None, ghosts_ref) if span[0] > 0 else (ghosts_ref, None)
    across_planes(
        span, speed_step, s_ref, near_ref, far_ref, wind_ref, waves_ref, flow_ref, use
    )
    for i in range(span[0]):
        spot = plane_at(i, planes)
        out_ref[spot] = early_ref[spot]
    if section == 2 and span[0] == 0:
        cut_near(out_ref, *refs)
    elif section == 2:
        cut_far(out_ref, refs[0])
        cut_headings(out_ref, *refs[1:])


def trade(value, axis, reach, wrap=False):
    size = lax.axis_size(axis)
    pairs = [(i, i + 1) for i in range(reach, size - 1, 2)]
    if wrap and reach and size % 2 == 0:
        pairs.append((size - 1, 0))
    pairs += [(j, i) for i, j in pairs]
    pairs += [(i, i) for i in range(size) if i not in dict(pairs)]
    return lax.ppermute(value, axis, pairs)


def local(level_set, wind_field, target_mask, target_depth):
    planes, headings, speed_count, cross_count = level_set.shape
    heading_total = headings * lax.axis_size("head")
    heading_step = 2.0 * math.pi / heading_total
    speed_step = (speed_high - speed_low) / (speed_count - 1)
    speed_row = np.float32(speed_low) + np.arange(speed_count, dtype=np.float32) * np.float32(
        speed_step
    )
    angles = np.arange(heading_total, dtype=np.float32) * np.float32(heading_step)
    waves = [np.cos(angles), np.sin(angles)]
    bounds = []
    for wave in waves:
        product = wave[:, None] * speed_row[None, :]
        bounds.append((float(product.min()), float(product.max())))
    waves = jnp.asarray(np.stack(waves)[..., None] * np.ones(cross_count, np.float32))

    vmem = pl.BlockSpec(memory_space=pltpu.VMEM)
    tile = (speed_count, cross_count)

    def shape(*dims):
        return jax.ShapeDtypeStruct(dims + tile, jnp.float32)

    field = shape(planes, headings)
    short = rim * headings
    middle = max(short + 1, rim * planes)

    longest = middle + 1
    rows = pltpu.VMEM((planes,) + tile, jnp.float32)
    cells = math.prod(level_set.shape)

    def call(kernel, ins, outs, scratch=(), work=0):
        return pl.pallas_call(
            kernel,
            out_shape=outs,
            in_specs=[vmem] * len(ins),
            out_specs=[vmem] * len(outs),
            scratch_shapes=list(scratch),
            compiler_params=pltpu.CompilerParams(vmem_limit_bytes=16 * 1024 * 1024),
            cost_estimate=pl.CostEstimate(
                flops=work * cells, bytes_accessed=work * cells, transcendentals=0
            ),
        )(*ins)

    wind = jnp.transpose(wind_field, (1, 0, 2))
    many = 16
    groups, lanes = -(-planes * headings // many), many * speed_count
    room = [
        pltpu.VMEM((groups, cross_count + 8, lanes), jnp.float32),
        pltpu.VMEM((groups, cross_count, lanes), jnp.float32),
        pltpu.VMEM((groups, cross_count, lanes), jnp.float32),
    ]
    values = level_set
    size = lax.axis_size(axis)
    pairs = [(i, i + 1) for i in range(reach, size - 1, 2)]
    if wrap and reach and size % 2 == 0:
        pairs.append((size - 1, 0))
    pairs += [(j, i) for i, j in pairs]
    pairs += [(i, i) for i in range(size) if i not in dict(pairs)]
    return lax.ppermute(value, axis, pairs)


def local(level_set, wind_field, target_mask, target_depth):
    planes, headings, speed_count, cross_count = level_set.shape
    heading_total = headings * lax.axis_size("head")
    heading_step = 2.0 * math.pi / heading_total
    speed_step = (speed_high - speed_low) / (speed_count - 1)
    speed_row = np.float32(speed_low) + np.arange(speed_count, dtype=np.float32) * np.float32(
        speed_step
    )
    angles = np.arange(heading_total, dtype=np.float32) * np.float32(heading_step)
    waves = [np.cos(angles), np.sin(angles)]
    bounds = []
    for wave in waves:
        product = wave[:, None] * speed_row[None, :]
        bounds.append((float(product.min()), float(product.max())))
    waves = jnp.asarray(np.stack(waves)[..., None] * np.ones(cross_count, np.float32))

    vmem = pl.BlockSpec(memory_space=pltpu.VMEM)
    tile = (speed_count, cross_count)

    def shape(*dims):
        return jax.ShapeDtypeStruct(dims + tile, jnp.float32)

    field = shape(planes, headings)
    short = rim * headings
    middle = max(short + 1, rim * planes)

    longest = middle + 1
    rows = pltpu.VMEM((planes,) + tile, jnp.float32)
    cells = math.prod(level_set.shape)

    def call(kernel, ins, outs, scratch=(), work=0):
        return pl.pallas_call(
            kernel,
            out_shape=outs,
            in_specs=[vmem] * len(ins),
            out_specs=[vmem] * len(outs),
            scratch_shapes=list(scratch),
            compiler_params=pltpu.CompilerParams(vmem_limit_bytes=16 * 1024 * 1024),
            cost_estimate=pl.CostEstimate(
                flops=work * cells, bytes_accessed=work * cells, transcendentals=0
            ),
        )(*ins)

    wind = jnp.transpose(wind_field, (1, 0, 2))
    many = 16
    groups, lanes = -(-planes * headings // many), many * speed_count
    room = [
        pltpu.VMEM((groups, cross_count + 8, lanes), jnp.float32),
        pltpu.VMEM((groups, cross_count, lanes), jnp.float32),
        pltpu.VMEM((groups, cross_count, lanes), jnp.float32),
    ]
    values, pk = level_set, None
    size = lax.axis_size("gx")

    def spread(most, reach):
        if size & (size - 1):
            pairs = [(i, (i + reach) % size) for i in range(size)]
        else:
            pairs = [(i, i ^ reach) for i in range(size)]
        return lax.ppermute(most, "gx", pairs)

    (most,) = call(extremes_kernel, [wind], [shape(longest + 2)])
    other = spread(most, 1)
    x_shapes = [shape(longest), shape(longest + 1)]
    x_out, x_last, t_out, t_last = call(opening_kernel, [values], x_shapes + [shape(middle)] * 2)
    far_shapes = [shape(short), shape(middle), shape(middle)]
    for section in (1, 2, 3):
        opening = section == 1
        x_near = trade(x_out, "gx", 0)
        t_near = trade(t_out, "head", 0)
        t_far = trade(t_last, "head", 1, True)
        x_far = trade(x_last, "gx", 1)
        free = functools.partial(free_kernel, opening, speed_step)
        turning = functools.partial(heading_kernel, heading_step)
        if opening:
            (most,) = call(meeting_kernel, [most, other], [shape()])
            other = spread(most, 2)
            ins = [values, wind, waves]
            spun, part, extra, flow = call(free, ins, [field] * 4, room, work=300)
            reach = 4
            while reach < size:
                most = jnp.maximum(most, other)
                most, part = lax.optimization_barrier((most, part))
                other = spread(most, reach)
                reach *= 2
            part, x_far = lax.optimization_barrier((part, x_far))
        else:
            if section == 3:
                values, x_near = lax.optimization_barrier((values, x_near))
            spun, part = call(free, [values, flow, pk], [field] * 2, room)
            if section == 2:
                part, x_near = lax.optimization_barrier((part, x_near))
        (part,) = call(turning, [values, spun, part, t_near, t_far], [field], work=1000)
        if opening:
            ins = [values, part, x_near, x_far, wind, waves]
            first = functools.partial(first_kernel, speed_step)
            part, gap = call(first, ins, [field] * 2, [rows])
            closing = functools.partial(closing_kernel, bounds, heading_step, speed_step)
            ins = [values, part, gap, extra, target_mask, target_depth, most, other]
            outs = [field, shape(longest), *far_shapes, shape()]
            values, x_out, x_last, t_out, t_last, pk = call(closing, ins, outs, [rows])
        else:
            more = section == 2
            ins = [level_set, values, part, x_near, wind, waves, target_mask, target_depth, pk]
            outs = [field] + ([shape(longest)] if more else [])
            last = functools.partial(section_kernel, section, (0, planes - rim), speed_step)
            early, *x_next = call(last, ins, outs, [rows, rows])
            ins = ins[:3] + [x_far] + ins[4:] + [early]
            outs = [field] + (far_shapes if more else [])
            last = functools.partial(section_kernel, section, (planes - rim, planes), speed_step)
            values, *far_next = call(last, ins, outs, [rows, rows])
            if more:
                (x_out,), (x_last, t_out, t_last) = x_next, far_next
    return values


def solution(mesh):
    return jax.shard_map(
        local,
        mesh=mesh,
        in_specs=(P("gx", "head", None, None), P(None, "gx", None), P("gx", None), P("gx", None)),
        out_specs=P("gx", "head", None, None),
        check_vma=False,
    )
```

```python
import functools
import math

import jax
import jax.numpy as jnp
import numpy as np
from jax import lax
from jax.experimental import pallas as pl
from jax.experimental.pallas import tpu as pltpu
from jax.sharding import PartitionSpec as P

epsilon = 1e-06
courant = 0.5
spacing = 0.05
turn_limit = 1.0
thrust_limit = 0.5
speed_low = 0.5
speed_high = 1.5
rim = 3
gain = 1.0 / (12.0 * spacing)


def inverse(value):
    return pltpu.reciprocal(value, approx=True)


def weights_of(e1, e2, turn, eps):
    level = turn * turn * (4.0 / 3.0) + eps
    ia = inverse(level + e2 * (e2 + turn))
    ib = inverse(level + e2 * e1)
    ic = inverse(level + e1 * (e1 - turn))
    return ia * ia, ib * ib * 6.0, ic * ic


def sides(fl, f0, fr, a2, a1, b1, b0, c0, c1):
    a3 = a1 * 3.0
    c3 = c0 * 3.0
    minus = ((fl + fl) * a2 + f0 * c3) * inverse(a2 + b1 + c3)
    plus = ((fr + fr) * c1 + f0 * a3) * inverse(c1 + b0 + a3)
    return minus, plus


def row_terms(cells, step, closed=False):
    eps = epsilon * step * step
    count = len(cells) if closed else len(cells) - 2 * rim
    shift = 0 if closed else rim
    slope = {m: cells[m + 1 + shift] - cells[m + shift] for m in range(-shift, count + shift - 1)}
    a, b, c = {}, {}, {}
    if closed:
        bend = {m: slope[m] - slope[m - 1] for m in range(1, count - 1)}
        bend[0], bend[count - 1] = slope[0], -slope[count - 2]
        turn = {m: bend[m + 1] - bend[m] for m in range(count - 1)}
        turn[-1], turn[count - 1] = bend[0], -bend[count - 1]
        jerk = {m: turn[m] - turn[m - 1] for m in range(count)}
        jerk[-1], jerk[count] = bend[0], bend[count - 1]
        rise = {m: slope[m] + slope[m - 1] for m in range(1, count - 1)}
        rise[0], rise[count - 1] = slope[0], slope[count - 2]
        a[-2] = c[count] = 1.0 / (eps * eps)
        for m, (e1, e2) in ((-1, (None, bend[0])), (count - 1, (bend[count - 1], None))):
            square = turn[m] * turn[m]
            level = square * (4.0 / 3.0) + eps
            ib, outer = inverse(level), inverse(level + (square + square))
            b[m] = ib * ib * 6.0
            (c if e2 is None else a)[m] = outer * outer
        inner = range(count - 1)
    else:
        bend = {m: slope[m] - slope[m - 1] for m in range(-2, count + 2)}
        turn = {m: bend[m + 1] - bend[m] for m in range(-2, count + 1)}
        jerk = {m: turn[m] - turn[m - 1] for m in range(-1, count + 1)}
        rise = {m: cells[m + 1 + rim] - cells[m - 1 + rim] for m in range(count)}
        inner = range(-2, count + 1)
    for m in inner:
        a[m], b[m], c[m] = weights_of(bend[m], bend[m + 1], turn[m], eps)
    out = []
    for i in range(count):
        base = rise[i] * 6.0 - (turn[i - 1] + turn[i])
        minus, plus = sides(
            jerk[i - 1], jerk[i], jerk[i + 1], a[i - 2], a[i - 1], b[i - 1], b[i], c[i], c[i + 1]
        )
        out.append((base + (plus - minus), (plus + minus) - jerk[i]))
    return out


def batches(total, most):
    return max(k for k in range(1, most + 1) if total % k == 0)


def splat(row, tile):
    return jnp.broadcast_to(row, tile)


def speeds_of(tile, speed_step):
    place = lax.broadcasted_iota(jnp.int32, tile, 0).astype(jnp.float32)
    return speed_low + place * speed_step


def odd_place(axis):
    return lax.rem(lax.axis_index(axis), 2) == 1


def put_extremes(wind_ref, most_ref):
    rows = [wind_ref[i] for i in range(wind_ref.shape[0])]
    most_ref[...] = jnp.zeros_like(most_ref)
    most_ref[0:2, :] = functools.reduce(jnp.maximum, rows)
    most_ref[2:4, :] = -functools.reduce(jnp.minimum, rows)


def extremes_kernel(wind_ref, most_ref):
    put_extremes(wind_ref, most_ref.at[0])


def opening_kernel(level_ref, x_near, x_far, t_near, t_far):
    cut_near(level_ref, x_near)
    cut_far(level_ref, x_far)
    cut_headings(level_ref, t_near, t_far)


def meeting_kernel(own_ref, other_ref, most_ref):
    most_ref[...] = jnp.maximum(own_ref[0], other_ref[0])


def flows_into(flow_ref, speed_step, wind_ref, waves_ref):
    planes, headings = flow_ref.shape[:2]
    tile = flow_ref.shape[2:]
    first = lax.axis_index("head") * headings
    pace = speeds_of(tile, speed_step) * gain
    tables = [
        splat(waves_ref[1, pl.ds(first + j, 1), :], tile) * pace for j in range(headings)
    ]
    for i in range(planes):
        wind = splat(wind_ref[i, 1:2, :] * gain, tile)
        for j in range(headings):
            flow_ref[i, j] = tables[j] + wind


def free_kernel(split, speed_step, s_ref, *rest):
    planes, headings, speeds, width = s_ref.shape
    cells = planes * headings

    def rows_of(ref):
        return ref.reshape(cells * speeds, width)

    if split:
        wind_ref, waves_ref, speed_ref, out_ref, extra_ref, flow_ref = rest[:-3]
        flows_into(flow_ref, speed_step, wind_ref, waves_ref)
        extra_rows = rows_of(extra_ref)
    else:
        flow_ref, pk_ref, speed_ref, out_ref = rest[:-3]
        peak = splat(pk_ref[1:2, :] * gain, (16 * speeds, width))
    turned_ref, mean_ref, gap_ref = rest[-3:]
    gain_v = thrust_limit / (12.0 * speed_step)
    s_rows, speed_rows = rows_of(s_ref), rows_of(speed_ref)
    out_rows, flow_rows = rows_of(out_ref), rows_of(flow_ref)
    few, many = 8, turned_ref.shape[2] // speeds
    groups = turned_ref.shape[0]
    lanes = many * speeds
    high = 8
    lines = width // high

    def along_speed(n):
        start = jnp.minimum(n * few, cells - few) * speeds
        spots = [pl.ds(start + v, few, stride=speeds) for v in range(speeds)]
        rows = [s_rows[spot, :] for spot in spots]
        for spot, (mean, gap) in zip(spots, row_terms(rows, speed_step, True)):
            speed_rows[spot, :] = gain_v * (gap - jnp.abs(mean))

    def span(n):
        return pl.ds(pl.multiple_of(jnp.minimum(n * many, cells - many) * speeds, speeds), lanes)

    def turn_in(n):
        turned = s_rows[span(n), :].T
        turned_ref[n, rim : rim + width, :] = turned
        for k in range(rim):
            turned_ref[n, k : k + 1, :] = turned[:1]
            turned_ref[n, rim + width + k : rim + width + k + 1, :] = turned[-1:]

    def along_y(n):
        ends = [turned_ref[n, pl.ds(k, high, stride=lines), :] for k in range(lines + 2 * rim)]
        for k, (mean, gap) in enumerate(row_terms(ends, spacing)):
            mean_ref[n, pl.ds(k, high, stride=lines), :] = mean
            gap_ref[n, pl.ds(k, high, stride=lines), :] = gap

    def turn_out(n):
        mean = mean_ref[n].T
        gap = gap_ref[n].T
        drift = mean * flow_rows[span(n), :]
        if split:
            out_rows[span(n), :] = drift
            extra_rows[span(n), :] = gap
        else:
            out_rows[span(n), :] = drift + gap * peak

    def step(n, carry):
        turn_out(jnp.maximum(n - 1, 0))
        along_y(n)
        turn_in(jnp.minimum(n + 1, groups - 1))
        along_speed(2 * n)
        along_speed(2 * n + 1)
        return carry

    turn_in(0)
    lax.fori_loop(0, groups, step, 0)
    turn_out(groups - 1)


def heading_kernel(heading_step, s_ref, speed_ref, part_ref, near_ref, far_ref, out_ref):
    planes, headings = s_ref.shape[:2]
    gain_t = turn_limit / (12.0 * heading_step)
    odd = odd_place("head")
    wide = batches(planes, 3)

    def step(n, carry):
        for w in range(wide):
            i = n * wide + w
            ghosts = [(near_ref[i * rim + k], far_ref[i * rim + k]) for k in range(rim)]
            lows = [jnp.where(odd, near, far) for near, far in ghosts]
            highs = [jnp.where(odd, far, near) for near, far in ghosts]
            cells = lows + [s_ref[i, j] for j in range(headings)] + highs
            for j, (mean, gap) in enumerate(row_terms(cells, heading_step)):
                own = speed_ref[i, j] + part_ref[i, j]
                out_ref[i, j] = own + gain_t * (gap - jnp.abs(mean))
        return carry

    lax.fori_loop(0, planes // wide, step, 0)


def peaks_into(pk_ref, most, bounds, heading_step, speed_step):
    most = jnp.max(most, axis=1, keepdims=True)
    peaks = [
        jnp.maximum(most[q : q + 1] + bounds[q][1], most[q + 2 : q + 3] - bounds[q][0])
        for q in range(2)
    ]
    time_step = courant / (
        peaks[0] / spacing
        + peaks[1] / spacing
        + turn_limit / heading_step
        + thrust_limit / speed_step
    )
    width = pk_ref.shape[1]
    for row, value in enumerate(peaks + [time_step]):
        pk_ref[row : row + 1, :] = splat(value, (1, width))


def plane_at(i, planes):
    return jnp.where(odd_place("gx"), i, planes - 1 - i)


def alone(reach):
    place, size = lax.axis_index("gx"), lax.axis_size("gx")
    if reach == 0:
        return (place == size - 1) if size % 2 else place < 0
    return (place == 0) | (place == size - 1) if size % 2 == 0 else place == 0


def cut_near(field_ref, x_near):
    planes, headings = field_ref.shape[:2]
    for k in range(rim):
        i = jnp.where(alone(0), 0, k)
        x_near[k * headings : (k + 1) * headings] = field_ref[plane_at(i, planes)]


def cut_far(field_ref, x_far):
    planes, headings = field_ref.shape[:2]
    for k in range(rim):
        i = planes - 1 - jnp.where(alone(1), 0, k)
        x_far[k * headings : (k + 1) * headings] = field_ref[plane_at(i, planes)]


def cut_headings(field_ref, t_near, t_far):
    planes, headings = field_ref.shape[:2]
    t_low = jnp.where(odd_place("head"), 0, headings - rim)
    for k in range(rim):
        for i in range(planes):
            t_near[i * rim + k] = field_ref[i, t_low + k]
            t_far[i * rim + k] = field_ref[i, headings - rim - t_low + k]


def splat_targets(mask_ref, depth_ref, target_ref):
    for i in range(target_ref.shape[0]):
        depth = depth_ref[i : i + 1, :]
        target = jnp.where(mask_ref[i : i + 1, :] == 1, -depth, depth)
        target_ref[i] = splat(target, target_ref.shape[1:])


def across_planes(
    span, speed_step, s_ref, near_ref, far_ref, wind_ref, waves_ref, flow_ref, use
):
    planes, headings = s_ref.shape[:2]
    tile = s_ref.shape[2:]
    side = jnp.where(odd_place("gx"), gain, -gain).astype(jnp.float32)
    spots = [plane_at(i, planes) for i in range(planes)]
    for i in range(planes):
        flow_ref[i] = splat(wind_ref[i, 0:1, :] * side, tile)
    pace = speeds_of(tile, speed_step) * side
    first = lax.axis_index("head") * headings
    low, high = span
    wide = batches(headings, max(1, 54 // (high - low)))

    def line(i, j):
        if i < 0:
            return near_ref[(-1 - i) * headings + j]
        if i >= planes:
            return far_ref[(i - planes) * headings + j]
        return s_ref[spots[i], j]

    def step(n, carry):
        for w in range(wide):
            j = n * wide + w
            cells = [line(i, j) for i in range(low - rim, high + rim)]
            table = splat(waves_ref[0, pl.ds(first + j, 1), :], tile) * pace
            for k, (mean, gap) in enumerate(row_terms(cells, spacing)):
                spot = spots[low + k]
                use(spot, j, mean * (table + flow_ref[spot]), gap, cells[k + rim])
        return carry

    lax.fori_loop(0, headings // wide, step, 0)


def first_kernel(
    speed_step, s_ref, part_ref, near_ref, far_ref, wind_ref, waves_ref, out_ref, gap_ref, flow_ref
):
    def use(i, j, drift, gap, cell):
        out_ref[i, j] = part_ref[i, j] + drift
        gap_ref[i, j] = gap

    across_planes(
        (0, s_ref.shape[0]), speed_step, s_ref, near_ref, far_ref, wind_ref, waves_ref, flow_ref, use
    )


def closing_kernel(
    bounds, heading_step, speed_step, s_ref, part_ref, gap_x_ref, gap_y_ref, mask_ref, depth_ref,
    most_ref, other_ref, out_ref, x_near, x_far, t_near, t_far, pk_ref, target_ref
):
    planes, headings = s_ref.shape[:2]
    tile = s_ref.shape[2:]
    most = jnp.maximum(most_ref[...], other_ref[...])
    peaks_into(pk_ref, most, bounds, heading_step, speed_step)
    splat_targets(mask_ref, depth_ref, target_ref)
    peak_x = splat(pk_ref[0:1, :] * gain, tile)
    peak_y = splat(pk_ref[1:2, :] * gain, tile)
    time_step = splat(pk_ref[2:3, :], tile)

    def plane(i, carry):
        for j in range(headings):
            rate = part_ref[i, j] + (gap_x_ref[i, j] * peak_x + gap_y_ref[i, j] * peak_y)
            out_ref[i, j] = jnp.minimum(s_ref[i, j] + time_step * rate, target_ref[i])
        return carry

    lax.fori_loop(0, planes, plane, 0)
    cut_near(out_ref, x_near)
    cut_far(out_ref, x_far)
    cut_headings(out_ref, t_near, t_far)


def section_kernel(
    section, span, speed_step, base_ref, s_ref, part_ref, ghosts_ref, wind_ref, waves_ref,
    mask_ref, depth_ref, pk_ref, *refs
):
    planes = s_ref.shape[0]
    refs, (flow_ref, target_ref) = list(refs[:-2]), refs[-2:]
    early_ref = refs.pop(0) if span[0] > 0 else None
    out_ref = refs.pop(0)
    tile = s_ref.shape[2:]
    splat_targets(mask_ref, depth_ref, target_ref)
    peak_x = splat(pk_ref[0:1, :] * gain, tile)
    time_step = splat(pk_ref[2:3, :], tile)
    base_share = 0.75 if section == 2 else 1.0 / 3.0
    own_share = 0.25 if section == 2 else 2.0 / 3.0

    def use(i, j, drift, gap, cell):
        rate = part_ref[i, j] + (drift + gap * peak_x)
        moved = base_share * base_ref[i, j] + own_share * (cell + time_step * rate)
        out_ref[i, j] = jnp.minimum(moved, target_ref[i])

    near_ref, far_ref = (None, ghosts_ref) if span[0] > 0 else (ghosts_ref, None)
    across_planes(
        span, speed_step, s_ref, near_ref, far_ref, wind_ref, waves_ref, flow_ref, use
    )
    for i in range(span[0]):
        spot = plane_at(i, planes)
        out_ref[spot] = early_ref[spot]
    if section == 2 and span[0] == 0:
        cut_near(out_ref, *refs)
    elif section == 2:
        cut_far(out_ref, refs[0])
        cut_headings(out_ref, *refs[1:])


def trade(value, axis, reach, wrap=False):
    size = lax.axis_size(axis)
    pairs = [(i, i + 1) for i in range(reach, size - 1, 2)]
    if wrap and reach and size % 2 == 0:
        pairs.append((size - 1, 0))
    pairs += [(j, i) for i, j in pairs]
    pairs += [(i, i) for i in range(size) if i not in dict(pairs)]
    return lax.ppermute(value, axis, pairs)


def local(level_set, wind_field, target_mask, target_depth):
    planes, headings, speed_count, cross_count = level_set.shape
    heading_total = headings * lax.axis_size("head")
    heading_step = 2.0 * math.pi / heading_total
    speed_step = (speed_high - speed_low) / (speed_count - 1)
    speed_row = np.float32(speed_low) + np.arange(speed_count, dtype=np.float32) * np.float32(
        speed_step
    )
    angles = np.arange(heading_total, dtype=np.float32) * np.float32(heading_step)
    waves = [np.cos(angles), np.sin(angles)]
    bounds = []
    for wave in waves:
        product = wave[:, None] * speed_row[None, :]
        bounds.append((float(product.min()), float(product.max())))
    waves = jnp.asarray(np.stack(waves)[..., None] * np.ones(cross_count, np.float32))

    vmem = pl.BlockSpec(memory_space=pltpu.VMEM)
    tile = (speed_count, cross_count)

    def shape(*dims):
        return jax.ShapeDtypeStruct(dims + tile, jnp.float32)

    field = shape(planes, headings)
    short = rim * headings
    middle = max(short + 1, rim * planes)

    longest = middle + 1
    rows = pltpu.VMEM((planes,) + tile, jnp.float32)
    cells = math.prod(level_set.shape)

    def call(kernel, ins, outs, scratch=(), work=0):
        return pl.pallas_call(
            kernel,
            out_shape=outs,
            in_specs=[vmem] * len(ins),
            out_specs=[vmem] * len(outs),
            scratch_shapes=list(scratch),
            compiler_params=pltpu.CompilerParams(vmem_limit_bytes=16 * 1024 * 1024),
            cost_estimate=pl.CostEstimate(
                flops=work * cells, bytes_accessed=work * cells, transcendentals=0
            ),
        )(*ins)

    wind = jnp.transpose(wind_field, (1, 0, 2))
    many = 16
    groups, lanes = -(-planes * headings // many), many * speed_count
    room = [
        pltpu.VMEM((groups, cross_count + 8, lanes), jnp.float32),
        pltpu.VMEM((groups, cross_count, lanes), jnp.float32),
        pltpu.VMEM((groups, cross_count, lanes), jnp.float32),
    ]
    values = level_set
    size = lax.axis_size(axis)
    pairs = [(i, i + 1) for i in range(reach, size - 1, 2)]
    if wrap and reach and size % 2 == 0:
        pairs.append((size - 1, 0))
    pairs += [(j, i) for i, j in pairs]
    pairs += [(i, i) for i in range(size) if i not in dict(pairs)]
    return lax.ppermute(value, axis, pairs)


def local(level_set, wind_field, target_mask, target_depth):
    planes, headings, speed_count, cross_count = level_set.shape
    heading_total = headings * lax.axis_size("head")
    heading_step = 2.0 * math.pi / heading_total
    speed_step = (speed_high - speed_low) / (speed_count - 1)
    speed_row = np.float32(speed_low) + np.arange(speed_count, dtype=np.float32) * np.float32(
        speed_step
    )
    angles = np.arange(heading_total, dtype=np.float32) * np.float32(heading_step)
    waves = [np.cos(angles), np.sin(angles)]
    bounds = []
    for wave in waves:
        product = wave[:, None] * speed_row[None, :]
        bounds.append((float(product.min()), float(product.max())))
    waves = jnp.asarray(np.stack(waves)[..., None] * np.ones(cross_count, np.float32))

    vmem = pl.BlockSpec(memory_space=pltpu.VMEM)
    tile = (speed_count, cross_count)

    def shape(*dims):
        return jax.ShapeDtypeStruct(dims + tile, jnp.float32)

    field = shape(planes, headings)
    short = rim * headings
    middle = max(short + 1, rim * planes)

    longest = middle + 1
    rows = pltpu.VMEM((planes,) + tile, jnp.float32)
    cells = math.prod(level_set.shape)

    def call(kernel, ins, outs, scratch=(), work=0):
        return pl.pallas_call(
            kernel,
            out_shape=outs,
            in_specs=[vmem] * len(ins),
            out_specs=[vmem] * len(outs),
            scratch_shapes=list(scratch),
            compiler_params=pltpu.CompilerParams(vmem_limit_bytes=16 * 1024 * 1024),
            cost_estimate=pl.CostEstimate(
                flops=work * cells, bytes_accessed=work * cells, transcendentals=0
            ),
        )(*ins)

    wind = jnp.transpose(wind_field, (1, 0, 2))
    many = 16
    groups, lanes = -(-planes * headings // many), many * speed_count
    room = [
        pltpu.VMEM((groups, cross_count + 8, lanes), jnp.float32),
        pltpu.VMEM((groups, cross_count, lanes), jnp.float32),
        pltpu.VMEM((groups, cross_count, lanes), jnp.float32),
    ]
    values, pk = level_set, None
    size = lax.axis_size("gx")

    def spread(most, reach):
        if size & (size - 1):
            pairs = [(i, (i + reach) % size) for i in range(size)]
        else:
            pairs = [(i, i ^ reach) for i in range(size)]
        return lax.ppermute(most, "gx", pairs)

    (most,) = call(extremes_kernel, [wind], [shape(longest + 2)])
    other = spread(most, 1)
    x_shapes = [shape(longest), shape(longest + 1)]
    x_out, x_last, t_out, t_last = call(opening_kernel, [values], x_shapes + [shape(middle)] * 2)
    far_shapes = [shape(short), shape(rim * planes), shape(middle)]
    for section in (1, 2, 3):
        opening = section == 1
        if not opening:
            x_near = trade(x_out, "gx", 0)
        t_near = trade(t_out, "head", 0)
        t_far = trade(t_last, "head", 1, True)
        x_far = trade(x_last, "gx", 1)
        free = functools.partial(free_kernel, opening, speed_step)
        turning = functools.partial(heading_kernel, heading_step)
        if opening:
            (most,) = call(meeting_kernel, [most, other], [shape()])
            other = spread(most, 2)
            values, most = lax.optimization_barrier((values, most))
            ins = [values, wind, waves]
            spun, part, extra, flow = call(free, ins, [field] * 4, room, work=300)
            x_out, part = lax.optimization_barrier((x_out, part))
            x_near = trade(x_out, "gx", 0)
            part, x_far = lax.optimization_barrier((part, x_far))
        else:
            if section == 3:
                values, x_near = lax.optimization_barrier((values, x_near))
            spun, part = call(free, [values, flow, pk], [field] * 2, room)
            if section == 2:
                part, x_near = lax.optimization_barrier((part, x_near))
        (part,) = call(turning, [values, spun, part, t_near, t_far], [field], work=1000)
        if opening:
            reach = 4
            while reach < size:
                most = jnp.maximum(most, other)
                most, part = lax.optimization_barrier((most, part))
                other = spread(most, reach)
                reach *= 2
            ins = [values, part, x_near, x_far, wind, waves]
            first = functools.partial(first_kernel, speed_step)
            part, gap = call(first, ins, [field] * 2, [rows])
            closing = functools.partial(closing_kernel, bounds, heading_step, speed_step)
            ins = [values, part, gap, extra, target_mask, target_depth, most, other]
            outs = [field, shape(longest), *far_shapes, shape()]
            values, x_out, x_last, t_out, t_last, pk = call(closing, ins, outs, [rows])
        else:
            more = section == 2
            ins = [level_set, values, part, x_near, wind, waves, target_mask, target_depth, pk]
            outs = [field] + ([shape(longest)] if more else [])
            last = functools.partial(section_kernel, section, (0, planes - rim), speed_step)
            early, *x_next = call(last, ins, outs, [rows, rows])
            ins = ins[:3] + [x_far] + ins[4:] + [early]
            outs = [field] + (far_shapes if more else [])
            last = functools.partial(section_kernel, section, (planes - rim, planes), speed_step)
            values, *far_next = call(last, ins, outs, [rows, rows])
            if more:
                (x_out,), (x_last, t_out, t_last) = x_next, far_next
    return values


def solution(mesh):
    return jax.shard_map(
        local,
        mesh=mesh,
        in_specs=(P("gx", "head", None, None), P(None, "gx", None), P("gx", None), P("gx", None)),
        out_specs=P("gx", "head", None, None),
        check_vma=False,
    )
```

```python
import functools
import math

import jax
import jax.numpy as jnp
import numpy as np
from jax import lax
from jax.experimental import pallas as pl
from jax.experimental.pallas import tpu as pltpu
from jax.sharding import PartitionSpec as P

epsilon = 1e-06
courant = 0.5
spacing = 0.05
turn_limit = 1.0
thrust_limit = 0.5
speed_low = 0.5
speed_high = 1.5
rim = 3
gain = 1.0 / (12.0 * spacing)


def inverse(value):
    return pltpu.reciprocal(value, approx=True)


def weights_of(e1, e2, turn, eps):
    level = turn * turn * (4.0 / 3.0) + eps
    ia = inverse(level + e2 * (e2 + turn))
    ib = inverse(level + e2 * e1)
    ic = inverse(level + e1 * (e1 - turn))
    return ia * ia, ib * ib * 6.0, ic * ic


def sides(fl, f0, fr, a2, a1, b1, b0, c0, c1):
    a3 = a1 * 3.0
    c3 = c0 * 3.0
    minus = ((fl + fl) * a2 + f0 * c3) * inverse(a2 + b1 + c3)
    plus = ((fr + fr) * c1 + f0 * a3) * inverse(c1 + b0 + a3)
    return minus, plus


def row_terms(cells, step, closed=False):
    eps = epsilon * step * step
    count = len(cells) if closed else len(cells) - 2 * rim
    shift = 0 if closed else rim
    slope = {m: cells[m + 1 + shift] - cells[m + shift] for m in range(-shift, count + shift - 1)}
    a, b, c = {}, {}, {}
    if closed:
        bend = {m: slope[m] - slope[m - 1] for m in range(1, count - 1)}
        bend[0], bend[count - 1] = slope[0], -slope[count - 2]
        turn = {m: bend[m + 1] - bend[m] for m in range(count - 1)}
        turn[-1], turn[count - 1] = bend[0], -bend[count - 1]
        jerk = {m: turn[m] - turn[m - 1] for m in range(count)}
        jerk[-1], jerk[count] = bend[0], bend[count - 1]
        rise = {m: slope[m] + slope[m - 1] for m in range(1, count - 1)}
        rise[0], rise[count - 1] = slope[0], slope[count - 2]
        a[-2] = c[count] = 1.0 / (eps * eps)
        for m, (e1, e2) in ((-1, (None, bend[0])), (count - 1, (bend[count - 1], None))):
            square = turn[m] * turn[m]
            level = square * (4.0 / 3.0) + eps
            ib, outer = inverse(level), inverse(level + (square + square))
            b[m] = ib * ib * 6.0
            (c if e2 is None else a)[m] = outer * outer
        inner = range(count - 1)
    else:
        bend = {m: slope[m] - slope[m - 1] for m in range(-2, count + 2)}
        turn = {m: bend[m + 1] - bend[m] for m in range(-2, count + 1)}
        jerk = {m: turn[m] - turn[m - 1] for m in range(-1, count + 1)}
        rise = {m: cells[m + 1 + rim] - cells[m - 1 + rim] for m in range(count)}
        inner = range(-2, count + 1)
    for m in inner:
        a[m], b[m], c[m] = weights_of(bend[m], bend[m + 1], turn[m], eps)
    out = []
    for i in range(count):
        base = rise[i] * 6.0 - (turn[i - 1] + turn[i])
        minus, plus = sides(
            jerk[i - 1], jerk[i], jerk[i + 1], a[i - 2], a[i - 1], b[i - 1], b[i], c[i], c[i + 1]
        )
        out.append((base + (plus - minus), (plus + minus) - jerk[i]))
    return out


def batches(total, most):
    return max(k for k in range(1, most + 1) if total % k == 0)


def splat(row, tile):
    return jnp.broadcast_to(row, tile)


def speeds_of(tile, speed_step):
    place = lax.broadcasted_iota(jnp.int32, tile, 0).astype(jnp.float32)
    return speed_low + place * speed_step


def odd_place(axis):
    return lax.rem(lax.axis_index(axis), 2) == 1


def put_extremes(wind_ref, most_ref):
    rows = [wind_ref[i] for i in range(wind_ref.shape[0])]
    most_ref[...] = jnp.zeros_like(most_ref)
    most_ref[0:2, :] = functools.reduce(jnp.maximum, rows)
    most_ref[2:4, :] = -functools.reduce(jnp.minimum, rows)


def extremes_kernel(wind_ref, most_ref):
    put_extremes(wind_ref, most_ref.at[0])


def opening_kernel(level_ref, x_near, x_far, t_near, t_far):
    cut_near(level_ref, x_near)
    cut_far(level_ref, x_far)
    cut_headings(level_ref, t_near, t_far)


def meeting_kernel(own_ref, other_ref, most_ref):
    most_ref[...] = jnp.maximum(own_ref[0], other_ref[0])


def flows_into(flow_ref, speed_step, wind_ref, waves_ref):
    planes, headings = flow_ref.shape[:2]
    tile = flow_ref.shape[2:]
    first = lax.axis_index("head") * headings
    pace = speeds_of(tile, speed_step) * gain
    tables = [
        splat(waves_ref[1, pl.ds(first + j, 1), :], tile) * pace for j in range(headings)
    ]
    for i in range(planes):
        wind = splat(wind_ref[i, 1:2, :] * gain, tile)
        for j in range(headings):
            flow_ref[i, j] = tables[j] + wind


def free_kernel(split, speed_step, s_ref, *rest):
    planes, headings, speeds, width = s_ref.shape
    cells = planes * headings

    def rows_of(ref):
        return ref.reshape(cells * speeds, width)

    if split:
        wind_ref, waves_ref, speed_ref, out_ref, extra_ref, flow_ref = rest[:-3]
        flows_into(flow_ref, speed_step, wind_ref, waves_ref)
        extra_rows = rows_of(extra_ref)
    else:
        flow_ref, pk_ref, speed_ref, out_ref = rest[:-3]
        peak = splat(pk_ref[1:2, :] * gain, (16 * speeds, width))
    turned_ref, mean_ref, gap_ref = rest[-3:]
    gain_v = thrust_limit / (12.0 * speed_step)
    s_rows, speed_rows = rows_of(s_ref), rows_of(speed_ref)
    out_rows, flow_rows = rows_of(out_ref), rows_of(flow_ref)
    few, many = 8, turned_ref.shape[2] // speeds
    groups = turned_ref.shape[0]
    lanes = many * speeds
    high = 8
    lines = width // high

    def along_speed(n):
        start = jnp.minimum(n * few, cells - few) * speeds
        spots = [pl.ds(start + v, few, stride=speeds) for v in range(speeds)]
        rows = [s_rows[spot, :] for spot in spots]
        for spot, (mean, gap) in zip(spots, row_terms(rows, speed_step, True)):
            speed_rows[spot, :] = gain_v * (gap - jnp.abs(mean))

    def span(n):
        return pl.ds(pl.multiple_of(jnp.minimum(n * many, cells - many) * speeds, speeds), lanes)

    def turn_in(n):
        turned = s_rows[span(n), :].T
        turned_ref[n, rim : rim + width, :] = turned
        for k in range(rim):
            turned_ref[n, k : k + 1, :] = turned[:1]
            turned_ref[n, rim + width + k : rim + width + k + 1, :] = turned[-1:]

    def along_y(n):
        ends = [turned_ref[n, pl.ds(k, high, stride=lines), :] for k in range(lines + 2 * rim)]
        for k, (mean, gap) in enumerate(row_terms(ends, spacing)):
            mean_ref[n, pl.ds(k, high, stride=lines), :] = mean
            gap_ref[n, pl.ds(k, high, stride=lines), :] = gap

    def turn_out(n):
        mean = mean_ref[n].T
        gap = gap_ref[n].T
        drift = mean * flow_rows[span(n), :]
        if split:
            out_rows[span(n), :] = drift
            extra_rows[span(n), :] = gap
        else:
            out_rows[span(n), :] = drift + gap * peak

    def step(n, carry):
        turn_out(jnp.maximum(n - 1, 0))
        along_y(n)
        turn_in(jnp.minimum(n + 1, groups - 1))
        along_speed(2 * n)
        along_speed(2 * n + 1)
        return carry

    turn_in(0)
    lax.fori_loop(0, groups, step, 0)
    turn_out(groups - 1)


def heading_kernel(heading_step, s_ref, speed_ref, part_ref, near_ref, far_ref, out_ref):
    planes, headings = s_ref.shape[:2]
    gain_t = turn_limit / (12.0 * heading_step)
    odd = odd_place("head")
    wide = batches(planes, 3)

    def step(n, carry):
        for w in range(wide):
            i = n * wide + w
            ghosts = [(near_ref[i * rim + k], far_ref[i * rim + k]) for k in range(rim)]
            lows = [jnp.where(odd, near, far) for near, far in ghosts]
            highs = [jnp.where(odd, far, near) for near, far in ghosts]
            cells = lows + [s_ref[i, j] for j in range(headings)] + highs
            for j, (mean, gap) in enumerate(row_terms(cells, heading_step)):
                own = speed_ref[i, j] + part_ref[i, j]
                out_ref[i, j] = own + gain_t * (gap - jnp.abs(mean))
        return carry

    lax.fori_loop(0, planes // wide, step, 0)


def peaks_into(pk_ref, most, bounds, heading_step, speed_step):
    most = jnp.max(most, axis=1, keepdims=True)
    peaks = [
        jnp.maximum(most[q : q + 1] + bounds[q][1], most[q + 2 : q + 3] - bounds[q][0])
        for q in range(2)
    ]
    time_step = courant / (
        peaks[0] / spacing
        + peaks[1] / spacing
        + turn_limit / heading_step
        + thrust_limit / speed_step
    )
    width = pk_ref.shape[1]
    for row, value in enumerate(peaks + [time_step]):
        pk_ref[row : row + 1, :] = splat(value, (1, width))


def plane_at(i, planes):
    return jnp.where(odd_place("gx"), i, planes - 1 - i)


def alone(reach):
    place, size = lax.axis_index("gx"), lax.axis_size("gx")
    if reach == 0:
        return (place == size - 1) if size % 2 else place < 0
    return (place == 0) | (place == size - 1) if size % 2 == 0 else place == 0


def cut_near(field_ref, x_near):
    planes, headings = field_ref.shape[:2]
    for k in range(rim):
        i = jnp.where(alone(0), 0, k)
        x_near[k * headings : (k + 1) * headings] = field_ref[plane_at(i, planes)]


def cut_far(field_ref, x_far):
    planes, headings = field_ref.shape[:2]
    for k in range(rim):
        i = planes - 1 - jnp.where(alone(1), 0, k)
        x_far[k * headings : (k + 1) * headings] = field_ref[plane_at(i, planes)]


def cut_headings(field_ref, t_near, t_far):
    planes, headings = field_ref.shape[:2]
    t_low = jnp.where(odd_place("head"), 0, headings - rim)
    for k in range(rim):
        for i in range(planes):
            t_near[i * rim + k] = field_ref[i, t_low + k]
            t_far[i * rim + k] = field_ref[i, headings - rim - t_low + k]


def splat_targets(mask_ref, depth_ref, target_ref):
    for i in range(target_ref.shape[0]):
        depth = depth_ref[i : i + 1, :]
        target = jnp.where(mask_ref[i : i + 1, :] == 1, -depth, depth)
        target_ref[i] = splat(target, target_ref.shape[1:])


def across_planes(
    span, speed_step, s_ref, near_ref, far_ref, wind_ref, waves_ref, flow_ref, use
):
    planes, headings = s_ref.shape[:2]
    tile = s_ref.shape[2:]
    side = jnp.where(odd_place("gx"), gain, -gain).astype(jnp.float32)
    spots = [plane_at(i, planes) for i in range(planes)]
    for i in range(planes):
        flow_ref[i] = splat(wind_ref[i, 0:1, :] * side, tile)
    pace = speeds_of(tile, speed_step) * side
    first = lax.axis_index("head") * headings
    low, high = span
    wide = batches(headings, max(1, 54 // (high - low)))

    def line(i, j):
        if i < 0:
            return near_ref[(-1 - i) * headings + j]
        if i >= planes:
            return far_ref[(i - planes) * headings + j]
        return s_ref[spots[i], j]

    def step(n, carry):
        for w in range(wide):
            j = n * wide + w
            cells = [line(i, j) for i in range(low - rim, high + rim)]
            table = splat(waves_ref[0, pl.ds(first + j, 1), :], tile) * pace
            for k, (mean, gap) in enumerate(row_terms(cells, spacing)):
                spot = spots[low + k]
                use(spot, j, mean * (table + flow_ref[spot]), gap, cells[k + rim])
        return carry

    lax.fori_loop(0, headings // wide, step, 0)


def first_kernel(
    speed_step, s_ref, part_ref, near_ref, far_ref, wind_ref, waves_ref, out_ref, gap_ref, flow_ref
):
    def use(i, j, drift, gap, cell):
        out_ref[i, j] = part_ref[i, j] + drift
        gap_ref[i, j] = gap

    across_planes(
        (0, s_ref.shape[0]), speed_step, s_ref, near_ref, far_ref, wind_ref, waves_ref, flow_ref, use
    )


def closing_kernel(
    bounds, heading_step, speed_step, s_ref, part_ref, gap_x_ref, gap_y_ref, mask_ref, depth_ref,
    most_ref, other_ref, out_ref, x_near, x_far, t_near, t_far, pk_ref, target_ref
):
    planes, headings = s_ref.shape[:2]
    tile = s_ref.shape[2:]
    most = jnp.maximum(most_ref[...], other_ref[...])
    peaks_into(pk_ref, most, bounds, heading_step, speed_step)
    splat_targets(mask_ref, depth_ref, target_ref)
    peak_x = splat(pk_ref[0:1, :] * gain, tile)
    peak_y = splat(pk_ref[1:2, :] * gain, tile)
    time_step = splat(pk_ref[2:3, :], tile)

    def plane(i, carry):
        for j in range(headings):
            rate = part_ref[i, j] + (gap_x_ref[i, j] * peak_x + gap_y_ref[i, j] * peak_y)
            out_ref[i, j] = jnp.minimum(s_ref[i, j] + time_step * rate, target_ref[i])
        return carry

    lax.fori_loop(0, planes, plane, 0)
    cut_near(out_ref, x_near)
    cut_far(out_ref, x_far)
    cut_headings(out_ref, t_near, t_far)


def section_kernel(
    section, span, speed_step, base_ref, s_ref, part_ref, ghosts_ref, wind_ref, waves_ref,
    mask_ref, depth_ref, pk_ref, *refs
):
    planes = s_ref.shape[0]
    refs, (flow_ref, target_ref) = list(refs[:-2]), refs[-2:]
    early_ref = refs.pop(0) if span[0] > 0 else None
    out_ref = refs.pop(0)
    tile = s_ref.shape[2:]
    splat_targets(mask_ref, depth_ref, target_ref)
    peak_x = splat(pk_ref[0:1, :] * gain, tile)
    time_step = splat(pk_ref[2:3, :], tile)
    base_share = 0.75 if section == 2 else 1.0 / 3.0
    own_share = 0.25 if section == 2 else 2.0 / 3.0

    def use(i, j, drift, gap, cell):
        rate = part_ref[i, j] + (drift + gap * peak_x)
        moved = base_share * base_ref[i, j] + own_share * (cell + time_step * rate)
        out_ref[i, j] = jnp.minimum(moved, target_ref[i])

    near_ref, far_ref = (None, ghosts_ref) if span[0] > 0 else (ghosts_ref, None)
    across_planes(
        span, speed_step, s_ref, near_ref, far_ref, wind_ref, waves_ref, flow_ref, use
    )
    for i in range(span[0]):
        spot = plane_at(i, planes)
        out_ref[spot] = early_ref[spot]
    if section == 2 and span[0] == 0:
        cut_near(out_ref, *refs)
    elif section == 2:
        cut_far(out_ref, refs[0])
        cut_headings(out_ref, *refs[1:])


def trade(value, axis, reach, wrap=False):
    size = lax.axis_size(axis)
    pairs = [(i, i + 1) for i in range(reach, size - 1, 2)]
    if wrap and reach and size % 2 == 0:
        pairs.append((size - 1, 0))
    pairs += [(j, i) for i, j in pairs]
    pairs += [(i, i) for i in range(size) if i not in dict(pairs)]
    return lax.ppermute(value, axis, pairs)


def local(level_set, wind_field, target_mask, target_depth):
    planes, headings, speed_count, cross_count = level_set.shape
    heading_total = headings * lax.axis_size("head")
    heading_step = 2.0 * math.pi / heading_total
    speed_step = (speed_high - speed_low) / (speed_count - 1)
    speed_row = np.float32(speed_low) + np.arange(speed_count, dtype=np.float32) * np.float32(
        speed_step
    )
    angles = np.arange(heading_total, dtype=np.float32) * np.float32(heading_step)
    waves = [np.cos(angles), np.sin(angles)]
    bounds = []
    for wave in waves:
        product = wave[:, None] * speed_row[None, :]
        bounds.append((float(product.min()), float(product.max())))
    waves = jnp.asarray(np.stack(waves)[..., None] * np.ones(cross_count, np.float32))

    vmem = pl.BlockSpec(memory_space=pltpu.VMEM)
    tile = (speed_count, cross_count)

    def shape(*dims):
        return jax.ShapeDtypeStruct(dims + tile, jnp.float32)

    field = shape(planes, headings)
    short = rim * headings
    middle = max(short + 1, rim * planes)

    longest = middle + 1
    rows = pltpu.VMEM((planes,) + tile, jnp.float32)
    cells = math.prod(level_set.shape)

    def call(kernel, ins, outs, scratch=(), work=0):
        return pl.pallas_call(
            kernel,
            out_shape=outs,
            in_specs=[vmem] * len(ins),
            out_specs=[vmem] * len(outs),
            scratch_shapes=list(scratch),
            compiler_params=pltpu.CompilerParams(vmem_limit_bytes=16 * 1024 * 1024),
            cost_estimate=pl.CostEstimate(
                flops=work * cells, bytes_accessed=work * cells, transcendentals=0
            ),
        )(*ins)

    wind = jnp.transpose(wind_field, (1, 0, 2))
    many = 16
    groups, lanes = -(-planes * headings // many), many * speed_count
    room = [
        pltpu.VMEM((groups, cross_count + 8, lanes), jnp.float32),
        pltpu.VMEM((groups, cross_count, lanes), jnp.float32),
        pltpu.VMEM((groups, cross_count, lanes), jnp.float32),
    ]
    values = level_set
    size = lax.axis_size(axis)
    pairs = [(i, i + 1) for i in range(reach, size - 1, 2)]
    if wrap and reach and size % 2 == 0:
        pairs.append((size - 1, 0))
    pairs += [(j, i) for i, j in pairs]
    pairs += [(i, i) for i in range(size) if i not in dict(pairs)]
    return lax.ppermute(value, axis, pairs)


def local(level_set, wind_field, target_mask, target_depth):
    planes, headings, speed_count, cross_count = level_set.shape
    heading_total = headings * lax.axis_size("head")
    heading_step = 2.0 * math.pi / heading_total
    speed_step = (speed_high - speed_low) / (speed_count - 1)
    speed_row = np.float32(speed_low) + np.arange(speed_count, dtype=np.float32) * np.float32(
        speed_step
    )
    angles = np.arange(heading_total, dtype=np.float32) * np.float32(heading_step)
    waves = [np.cos(angles), np.sin(angles)]
    bounds = []
    for wave in waves:
        product = wave[:, None] * speed_row[None, :]
        bounds.append((float(product.min()), float(product.max())))
    waves = jnp.asarray(np.stack(waves)[..., None] * np.ones(cross_count, np.float32))

    vmem = pl.BlockSpec(memory_space=pltpu.VMEM)
    tile = (speed_count, cross_count)

    def shape(*dims):
        return jax.ShapeDtypeStruct(dims + tile, jnp.float32)

    field = shape(planes, headings)
    short = rim * headings
    middle = max(short + 1, rim * planes)

    longest = middle + 1
    rows = pltpu.VMEM((planes,) + tile, jnp.float32)
    cells = math.prod(level_set.shape)

    def call(kernel, ins, outs, scratch=(), work=0):
        return pl.pallas_call(
            kernel,
            out_shape=outs,
            in_specs=[vmem] * len(ins),
            out_specs=[vmem] * len(outs),
            scratch_shapes=list(scratch),
            compiler_params=pltpu.CompilerParams(vmem_limit_bytes=16 * 1024 * 1024),
            cost_estimate=pl.CostEstimate(
                flops=work * cells, bytes_accessed=work * cells, transcendentals=0
            ),
        )(*ins)

    wind = jnp.transpose(wind_field, (1, 0, 2))
    many = 16
    groups, lanes = -(-planes * headings // many), many * speed_count
    room = [
        pltpu.VMEM((groups, cross_count + 8, lanes), jnp.float32),
        pltpu.VMEM((groups, cross_count, lanes), jnp.float32),
        pltpu.VMEM((groups, cross_count, lanes), jnp.float32),
    ]
    values, pk = level_set, None
    size = lax.axis_size("gx")

    def spread(most, reach):
        if size & (size - 1):
            pairs = [(i, (i + reach) % size) for i in range(size)]
        else:
            pairs = [(i, i ^ reach) for i in range(size)]
        return lax.ppermute(most, "gx", pairs)

    (most,) = call(extremes_kernel, [wind], [shape(longest + 2)])
    other = spread(most, 1)
    x_shapes = [shape(longest + 1), shape(longest)]
    x_out, x_last, t_out, t_last = call(opening_kernel, [values], x_shapes + [shape(middle)] * 2)
    far_shapes = [shape(short), shape(rim * planes), shape(middle)]
    for section in (1, 2, 3):
        opening = section == 1
        x_near = trade(x_out, "gx", 0)
        t_near = trade(t_out, "head", 0)
        t_far = trade(t_last, "head", 1, True)
        x_far = trade(x_last, "gx", 1)
        free = functools.partial(free_kernel, opening, speed_step)
        turning = functools.partial(heading_kernel, heading_step)
        if opening:
            (most,) = call(meeting_kernel, [most, other], [shape()])
            other = spread(most, 2)
            ins = [values, wind, waves]
            spun, part, extra, flow = call(free, ins, [field] * 4, room, work=300)
            reach = 4
            while reach < size:
                most = jnp.maximum(most, other)
                most, part = lax.optimization_barrier((most, part))
                other = spread(most, reach)
                reach *= 2
            part, x_near, x_far = lax.optimization_barrier((part, x_near, x_far))
        else:
            if section == 3:
                values, x_near = lax.optimization_barrier((values, x_near))
            spun, part = call(free, [values, flow, pk], [field] * 2, room)
            if section == 2:
                part, x_near = lax.optimization_barrier((part, x_near))
        (part,) = call(turning, [values, spun, part, t_near, t_far], [field], work=1000)
        if opening:
            ins = [values, part, x_near, x_far, wind, waves]
            first = functools.partial(first_kernel, speed_step)
            part, gap = call(first, ins, [field] * 2, [rows])
            closing = functools.partial(closing_kernel, bounds, heading_step, speed_step)
            ins = [values, part, gap, extra, target_mask, target_depth, most, other]
            outs = [field, shape(longest), *far_shapes, shape()]
            values, x_out, x_last, t_out, t_last, pk = call(closing, ins, outs, [rows])
        else:
            more = section == 2
            ins = [level_set, values, part, x_near, wind, waves, target_mask, target_depth, pk]
            outs = [field] + ([shape(longest)] if more else [])
            last = functools.partial(section_kernel, section, (0, planes - rim), speed_step)
            early, *x_next = call(last, ins, outs, [rows, rows])
            ins = ins[:3] + [x_far] + ins[4:] + [early]
            outs = [field] + (far_shapes if more else [])
            last = functools.partial(section_kernel, section, (planes - rim, planes), speed_step)
            values, *far_next = call(last, ins, outs, [rows, rows])
            if more:
                (x_out,), (x_last, t_out, t_last) = x_next, far_next
    return values


def solution(mesh):
    return jax.shard_map(
        local,
        mesh=mesh,
        in_specs=(P("gx", "head", None, None), P(None, "gx", None), P("gx", None), P("gx", None)),
        out_specs=P("gx", "head", None, None),
        check_vma=False,
    )
```

```python
import functools
import math

import jax
import jax.numpy as jnp
import numpy as np
from jax import lax
from jax.experimental import pallas as pl
from jax.experimental.pallas import tpu as pltpu
from jax.sharding import PartitionSpec as P

epsilon = 1e-06
courant = 0.5
spacing = 0.05
turn_limit = 1.0
thrust_limit = 0.5
speed_low = 0.5
speed_high = 1.5
rim = 3
gain = 1.0 / (12.0 * spacing)


def inverse(value):
    return pltpu.reciprocal(value, approx=True)


def weights_of(e1, e2, turn, eps):
    level = turn * turn * (4.0 / 3.0) + eps
    ia = inverse(level + e2 * (e2 + turn))
    ib = inverse(level + e2 * e1)
    ic = inverse(level + e1 * (e1 - turn))
    return ia * ia, ib * ib * 6.0, ic * ic


def sides(fl, f0, fr, a2, a1, b1, b0, c0, c1):
    a3 = a1 * 3.0
    c3 = c0 * 3.0
    minus = ((fl + fl) * a2 + f0 * c3) * inverse(a2 + b1 + c3)
    plus = ((fr + fr) * c1 + f0 * a3) * inverse(c1 + b0 + a3)
    return minus, plus


def row_terms(cells, step, closed=False):
    eps = epsilon * step * step
    count = len(cells) if closed else len(cells) - 2 * rim
    shift = 0 if closed else rim
    slope = {m: cells[m + 1 + shift] - cells[m + shift] for m in range(-shift, count + shift - 1)}
    a, b, c = {}, {}, {}
    if closed:
        bend = {m: slope[m] - slope[m - 1] for m in range(1, count - 1)}
        bend[0], bend[count - 1] = slope[0], -slope[count - 2]
        turn = {m: bend[m + 1] - bend[m] for m in range(count - 1)}
        turn[-1], turn[count - 1] = bend[0], -bend[count - 1]
        jerk = {m: turn[m] - turn[m - 1] for m in range(count)}
        jerk[-1], jerk[count] = bend[0], bend[count - 1]
        rise = {m: slope[m] + slope[m - 1] for m in range(1, count - 1)}
        rise[0], rise[count - 1] = slope[0], slope[count - 2]
        a[-2] = c[count] = 1.0 / (eps * eps)
        for m, (e1, e2) in ((-1, (None, bend[0])), (count - 1, (bend[count - 1], None))):
            square = turn[m] * turn[m]
            level = square * (4.0 / 3.0) + eps
            ib, outer = inverse(level), inverse(level + (square + square))
            b[m] = ib * ib * 6.0
            (c if e2 is None else a)[m] = outer * outer
        inner = range(count - 1)
    else:
        bend = {m: slope[m] - slope[m - 1] for m in range(-2, count + 2)}
        turn = {m: bend[m + 1] - bend[m] for m in range(-2, count + 1)}
        jerk = {m: turn[m] - turn[m - 1] for m in range(-1, count + 1)}
        rise = {m: cells[m + 1 + rim] - cells[m - 1 + rim] for m in range(count)}
        inner = range(-2, count + 1)
    for m in inner:
        a[m], b[m], c[m] = weights_of(bend[m], bend[m + 1], turn[m], eps)
    out = []
    for i in range(count):
        base = rise[i] * 6.0 - (turn[i - 1] + turn[i])
        minus, plus = sides(
            jerk[i - 1], jerk[i], jerk[i + 1], a[i - 2], a[i - 1], b[i - 1], b[i], c[i], c[i + 1]
        )
        out.append((base + (plus - minus), (plus + minus) - jerk[i]))
    return out


def batches(total, most):
    return max(k for k in range(1, most + 1) if total % k == 0)


def splat(row, tile):
    return jnp.broadcast_to(row, tile)


def speeds_of(tile, speed_step):
    place = lax.broadcasted_iota(jnp.int32, tile, 0).astype(jnp.float32)
    return speed_low + place * speed_step


def odd_place(axis):
    return lax.rem(lax.axis_index(axis), 2) == 1


def put_extremes(wind_ref, most_ref):
    rows = [wind_ref[i] for i in range(wind_ref.shape[0])]
    most_ref[...] = jnp.zeros_like(most_ref)
    most_ref[0:2, :] = functools.reduce(jnp.maximum, rows)
    most_ref[2:4, :] = -functools.reduce(jnp.minimum, rows)


def extremes_kernel(wind_ref, most_ref):
    put_extremes(wind_ref, most_ref.at[0:8])


def opening_kernel(level_ref, x_near, x_far, t_near, t_far):
    cut_near(level_ref, x_near)
    cut_far(level_ref, x_far)
    cut_headings(level_ref, t_near, t_far)


def flows_into(flow_ref, speed_step, wind_ref, waves_ref):
    planes, headings = flow_ref.shape[:2]
    tile = flow_ref.shape[2:]
    first = lax.axis_index("head") * headings
    pace = speeds_of(tile, speed_step) * gain
    tables = [
        splat(waves_ref[1, pl.ds(first + j, 1), :], tile) * pace for j in range(headings)
    ]
    for i in range(planes):
        wind = splat(wind_ref[i, 1:2, :] * gain, tile)
        for j in range(headings):
            flow_ref[i, j] = tables[j] + wind


def free_kernel(split, speed_step, s_ref, *rest):
    planes, headings, speeds, width = s_ref.shape
    cells = planes * headings

    def rows_of(ref):
        return ref.reshape(cells * speeds, width)

    if split:
        wind_ref, waves_ref, speed_ref, out_ref, extra_ref, flow_ref = rest[:-3]
        flows_into(flow_ref, speed_step, wind_ref, waves_ref)
        extra_rows = rows_of(extra_ref)
    else:
        flow_ref, pk_ref, speed_ref, out_ref = rest[:-3]
        peak = splat(pk_ref[1:2, :] * gain, (16 * speeds, width))
    turned_ref, mean_ref, gap_ref = rest[-3:]
    gain_v = thrust_limit / (12.0 * speed_step)
    s_rows, speed_rows = rows_of(s_ref), rows_of(speed_ref)
    out_rows, flow_rows = rows_of(out_ref), rows_of(flow_ref)
    few, many = 8, turned_ref.shape[2] // speeds
    groups = turned_ref.shape[0]
    lanes = many * speeds
    high = 8
    lines = width // high

    def along_speed(n):
        start = jnp.minimum(n * few, cells - few) * speeds
        spots = [pl.ds(start + v, few, stride=speeds) for v in range(speeds)]
        rows = [s_rows[spot, :] for spot in spots]
        for spot, (mean, gap) in zip(spots, row_terms(rows, speed_step, True)):
            speed_rows[spot, :] = gain_v * (gap - jnp.abs(mean))

    def span(n):
        return pl.ds(pl.multiple_of(jnp.minimum(n * many, cells - many) * speeds, speeds), lanes)

    def turn_in(n):
        turned = s_rows[span(n), :].T
        turned_ref[n, rim : rim + width, :] = turned
        for k in range(rim):
            turned_ref[n, k : k + 1, :] = turned[:1]
            turned_ref[n, rim + width + k : rim + width + k + 1, :] = turned[-1:]

    def along_y(n):
        ends = [turned_ref[n, pl.ds(k, high, stride=lines), :] for k in range(lines + 2 * rim)]
        for k, (mean, gap) in enumerate(row_terms(ends, spacing)):
            mean_ref[n, pl.ds(k, high, stride=lines), :] = mean
            gap_ref[n, pl.ds(k, high, stride=lines), :] = gap

    def turn_out(n):
        mean = mean_ref[n].T
        gap = gap_ref[n].T
        drift = mean * flow_rows[span(n), :]
        if split:
            out_rows[span(n), :] = drift
            extra_rows[span(n), :] = gap
        else:
            out_rows[span(n), :] = drift + gap * peak

    def step(n, carry):
        turn_out(jnp.maximum(n - 1, 0))
        along_y(n)
        turn_in(jnp.minimum(n + 1, groups - 1))
        along_speed(2 * n)
        along_speed(2 * n + 1)
        return carry

    turn_in(0)
    lax.fori_loop(0, groups, step, 0)
    turn_out(groups - 1)


def heading_kernel(heading_step, s_ref, speed_ref, part_ref, near_ref, far_ref, out_ref):
    planes, headings = s_ref.shape[:2]
    gain_t = turn_limit / (12.0 * heading_step)
    odd = odd_place("head")
    wide = batches(planes, 3)

    def step(n, carry):
        for w in range(wide):
            i = n * wide + w
            ghosts = [(near_ref[i * rim + k], far_ref[i * rim + k]) for k in range(rim)]
            lows = [jnp.where(odd, near, far) for near, far in ghosts]
            highs = [jnp.where(odd, far, near) for near, far in ghosts]
            cells = lows + [s_ref[i, j] for j in range(headings)] + highs
            for j, (mean, gap) in enumerate(row_terms(cells, heading_step)):
                own = speed_ref[i, j] + part_ref[i, j]
                out_ref[i, j] = own + gain_t * (gap - jnp.abs(mean))
        return carry

    lax.fori_loop(0, planes // wide, step, 0)


def peaks_into(pk_ref, most, bounds, heading_step, speed_step):
    most = jnp.max(most, axis=1, keepdims=True)
    peaks = [
        jnp.maximum(most[q : q + 1] + bounds[q][1], most[q + 2 : q + 3] - bounds[q][0])
        for q in range(2)
    ]
    time_step = courant / (
        peaks[0] / spacing
        + peaks[1] / spacing
        + turn_limit / heading_step
        + thrust_limit / speed_step
    )
    width = pk_ref.shape[1]
    for row, value in enumerate(peaks + [time_step]):
        pk_ref[row : row + 1, :] = splat(value, (1, width))


def plane_at(i, planes):
    return jnp.where(odd_place("gx"), i, planes - 1 - i)


def alone(reach):
    place, size = lax.axis_index("gx"), lax.axis_size("gx")
    if reach == 0:
        return (place == size - 1) if size % 2 else place < 0
    return (place == 0) | (place == size - 1) if size % 2 == 0 else place == 0


def cut_near(field_ref, x_near):
    planes, headings = field_ref.shape[:2]
    for k in range(rim):
        i = jnp.where(alone(0), 0, k)
        x_near[k * headings : (k + 1) * headings] = field_ref[plane_at(i, planes)]


def cut_far(field_ref, x_far):
    planes, headings = field_ref.shape[:2]
    for k in range(rim):
        i = planes - 1 - jnp.where(alone(1), 0, k)
        x_far[k * headings : (k + 1) * headings] = field_ref[plane_at(i, planes)]


def cut_headings(field_ref, t_near, t_far):
    planes, headings = field_ref.shape[:2]
    t_low = jnp.where(odd_place("head"), 0, headings - rim)
    for k in range(rim):
        for i in range(planes):
            t_near[i * rim + k] = field_ref[i, t_low + k]
            t_far[i * rim + k] = field_ref[i, headings - rim - t_low + k]


def splat_targets(mask_ref, depth_ref, target_ref):
    for i in range(target_ref.shape[0]):
        depth = depth_ref[i : i + 1, :]
        target = jnp.where(mask_ref[i : i + 1, :] == 1, -depth, depth)
        target_ref[i] = splat(target, target_ref.shape[1:])


def across_planes(
    span, speed_step, s_ref, near_ref, far_ref, wind_ref, waves_ref, flow_ref, use
):
    planes, headings = s_ref.shape[:2]
    tile = s_ref.shape[2:]
    side = jnp.where(odd_place("gx"), gain, -gain).astype(jnp.float32)
    spots = [plane_at(i, planes) for i in range(planes)]
    for i in range(planes):
        flow_ref[i] = splat(wind_ref[i, 0:1, :] * side, tile)
    pace = speeds_of(tile, speed_step) * side
    first = lax.axis_index("head") * headings
    low, high = span
    wide = batches(headings, max(1, 54 // (high - low)))

    def line(i, j):
        if i < 0:
            return near_ref[(-1 - i) * headings + j]
        if i >= planes:
            return far_ref[(i - planes) * headings + j]
        return s_ref[spots[i], j]

    def step(n, carry):
        for w in range(wide):
            j = n * wide + w
            cells = [line(i, j) for i in range(low - rim, high + rim)]
            table = splat(waves_ref[0, pl.ds(first + j, 1), :], tile) * pace
            for k, (mean, gap) in enumerate(row_terms(cells, spacing)):
                spot = spots[low + k]
                use(spot, j, mean * (table + flow_ref[spot]), gap, cells[k + rim])
        return carry

    lax.fori_loop(0, headings // wide, step, 0)


def first_kernel(
    speed_step, s_ref, part_ref, near_ref, far_ref, wind_ref, waves_ref, out_ref, gap_ref, flow_ref
):
    def use(i, j, drift, gap, cell):
        out_ref[i, j] = part_ref[i, j] + drift
        gap_ref[i, j] = gap

    across_planes(
        (0, s_ref.shape[0]), speed_step, s_ref, near_ref, far_ref, wind_ref, waves_ref, flow_ref, use
    )


def closing_kernel(
    bounds, heading_step, speed_step, s_ref, part_ref, gap_x_ref, gap_y_ref, mask_ref, depth_ref,
    most_ref, out_ref, x_near, x_far, t_near, t_far, pk_ref, target_ref
):
    planes, headings = s_ref.shape[:2]
    tile = s_ref.shape[2:]
    most = functools.reduce(jnp.maximum, [most_ref[g, 0:8, :] for g in range(most_ref.shape[0])])
    peaks_into(pk_ref, most, bounds, heading_step, speed_step)
    splat_targets(mask_ref, depth_ref, target_ref)
    peak_x = splat(pk_ref[0:1, :] * gain, tile)
    peak_y = splat(pk_ref[1:2, :] * gain, tile)
    time_step = splat(pk_ref[2:3, :], tile)

    def plane(i, carry):
        for j in range(headings):
            rate = part_ref[i, j] + (gap_x_ref[i, j] * peak_x + gap_y_ref[i, j] * peak_y)
            out_ref[i, j] = jnp.minimum(s_ref[i, j] + time_step * rate, target_ref[i])
        return carry

    lax.fori_loop(0, planes, plane, 0)
    cut_near(out_ref, x_near)
    cut_far(out_ref, x_far)
    cut_headings(out_ref, t_near, t_far)


def section_kernel(
    section, span, speed_step, base_ref, s_ref, part_ref, ghosts_ref, wind_ref, waves_ref,
    mask_ref, depth_ref, pk_ref, *refs
):
    planes = s_ref.shape[0]
    refs, (flow_ref, target_ref) = list(refs[:-2]), refs[-2:]
    early_ref = refs.pop(0) if span[0] > 0 else None
    out_ref = refs.pop(0)
    tile = s_ref.shape[2:]
    splat_targets(mask_ref, depth_ref, target_ref)
    peak_x = splat(pk_ref[0:1, :] * gain, tile)
    time_step = splat(pk_ref[2:3, :], tile)
    base_share = 0.75 if section == 2 else 1.0 / 3.0
    own_share = 0.25 if section == 2 else 2.0 / 3.0

    def use(i, j, drift, gap, cell):
        rate = part_ref[i, j] + (drift + gap * peak_x)
        moved = base_share * base_ref[i, j] + own_share * (cell + time_step * rate)
        out_ref[i, j] = jnp.minimum(moved, target_ref[i])

    near_ref, far_ref = (None, ghosts_ref) if span[0] > 0 else (ghosts_ref, None)
    across_planes(
        span, speed_step, s_ref, near_ref, far_ref, wind_ref, waves_ref, flow_ref, use
    )
    for i in range(span[0]):
        spot = plane_at(i, planes)
        out_ref[spot] = early_ref[spot]
    if section == 2 and span[0] == 0:
        cut_near(out_ref, *refs)
    elif section == 2:
        cut_far(out_ref, refs[0])
        cut_headings(out_ref, *refs[1:])


def trade(value, axis, reach, wrap=False):
    size = lax.axis_size(axis)
    pairs = [(i, i + 1) for i in range(reach, size - 1, 2)]
    if wrap and reach and size % 2 == 0:
        pairs.append((size - 1, 0))
    pairs += [(j, i) for i, j in pairs]
    pairs += [(i, i) for i in range(size) if i not in dict(pairs)]
    return lax.ppermute(value, axis, pairs)


def local(level_set, wind_field, target_mask, target_depth):
    planes, headings, speed_count, cross_count = level_set.shape
    heading_total = headings * lax.axis_size("head")
    heading_step = 2.0 * math.pi / heading_total
    speed_step = (speed_high - speed_low) / (speed_count - 1)
    speed_row = np.float32(speed_low) + np.arange(speed_count, dtype=np.float32) * np.float32(
        speed_step
    )
    angles = np.arange(heading_total, dtype=np.float32) * np.float32(heading_step)
    waves = [np.cos(angles), np.sin(angles)]
    bounds = []
    for wave in waves:
        product = wave[:, None] * speed_row[None, :]
        bounds.append((float(product.min()), float(product.max())))
    waves = jnp.asarray(np.stack(waves)[..., None] * np.ones(cross_count, np.float32))

    vmem = pl.BlockSpec(memory_space=pltpu.VMEM)
    tile = (speed_count, cross_count)

    def shape(*dims):
        return jax.ShapeDtypeStruct(dims + tile, jnp.float32)

    field = shape(planes, headings)
    short = rim * headings
    middle = max(short + 1, rim * planes)

    longest = middle + 1
    rows = pltpu.VMEM((planes,) + tile, jnp.float32)
    cells = math.prod(level_set.shape)

    def call(kernel, ins, outs, scratch=(), work=0):
        return pl.pallas_call(
            kernel,
            out_shape=outs,
            in_specs=[vmem] * len(ins),
            out_specs=[vmem] * len(outs),
            scratch_shapes=list(scratch),
            compiler_params=pltpu.CompilerParams(vmem_limit_bytes=16 * 1024 * 1024),
            cost_estimate=pl.CostEstimate(
                flops=work * cells, bytes_accessed=work * cells, transcendentals=0
            ),
        )(*ins)

    wind = jnp.transpose(wind_field, (1, 0, 2))
    many = 16
    groups, lanes = -(-planes * headings // many), many * speed_count
    room = [
        pltpu.VMEM((groups, cross_count + 8, lanes), jnp.float32),
        pltpu.VMEM((groups, cross_count, lanes), jnp.float32),
        pltpu.VMEM((groups, cross_count, lanes), jnp.float32),
    ]
    values = level_set
    size = lax.axis_size(axis)
    pairs = [(i, i + 1) for i in range(reach, size - 1, 2)]
    if wrap and reach and size % 2 == 0:
        pairs.append((size - 1, 0))
    pairs += [(j, i) for i, j in pairs]
    pairs += [(i, i) for i in range(size) if i not in dict(pairs)]
    return lax.ppermute(value, axis, pairs)


def local(level_set, wind_field, target_mask, target_depth):
    planes, headings, speed_count, cross_count = level_set.shape
    heading_total = headings * lax.axis_size("head")
    heading_step = 2.0 * math.pi / heading_total
    speed_step = (speed_high - speed_low) / (speed_count - 1)
    speed_row = np.float32(speed_low) + np.arange(speed_count, dtype=np.float32) * np.float32(
        speed_step
    )
    angles = np.arange(heading_total, dtype=np.float32) * np.float32(heading_step)
    waves = [np.cos(angles), np.sin(angles)]
    bounds = []
    for wave in waves:
        product = wave[:, None] * speed_row[None, :]
        bounds.append((float(product.min()), float(product.max())))
    waves = jnp.asarray(np.stack(waves)[..., None] * np.ones(cross_count, np.float32))

    vmem = pl.BlockSpec(memory_space=pltpu.VMEM)
    tile = (speed_count, cross_count)

    def shape(*dims):
        return jax.ShapeDtypeStruct(dims + tile, jnp.float32)

    field = shape(planes, headings)
    short = rim * headings
    middle = max(short + 1, rim * planes)

    longest = middle + 1
    rows = pltpu.VMEM((planes,) + tile, jnp.float32)
    cells = math.prod(level_set.shape)

    def call(kernel, ins, outs, scratch=(), work=0):
        return pl.pallas_call(
            kernel,
            out_shape=outs,
            in_specs=[vmem] * len(ins),
            out_specs=[vmem] * len(outs),
            scratch_shapes=list(scratch),
            compiler_params=pltpu.CompilerParams(vmem_limit_bytes=16 * 1024 * 1024),
            cost_estimate=pl.CostEstimate(
                flops=work * cells, bytes_accessed=work * cells, transcendentals=0
            ),
        )(*ins)

    wind = jnp.transpose(wind_field, (1, 0, 2))
    many = 16
    groups, lanes = -(-planes * headings // many), many * speed_count
    room = [
        pltpu.VMEM((groups, cross_count + 8, lanes), jnp.float32),
        pltpu.VMEM((groups, cross_count, lanes), jnp.float32),
        pltpu.VMEM((groups, cross_count, lanes), jnp.float32),
    ]
    values, pk = level_set, None
    most_shape = jax.ShapeDtypeStruct((64, cross_count), jnp.float32)
    (most,) = call(extremes_kernel, [wind], [most_shape])
    most = lax.all_gather(most, "gx")
    x_shapes = [shape(longest + 1), shape(longest)]
    x_out, x_last, t_out, t_last = call(opening_kernel, [values], x_shapes + [shape(middle)] * 2)
    far_shapes = [shape(short), shape(rim * planes), shape(middle)]
    for section in (1, 2, 3):
        opening = section == 1
        x_near = trade(x_out, "gx", 0)
        t_near = trade(t_out, "head", 0)
        t_far = trade(t_last, "head", 1, True)
        x_far = trade(x_last, "gx", 1)
        free = functools.partial(free_kernel, opening, speed_step)
        turning = functools.partial(heading_kernel, heading_step)
        if opening:
            ins = [values, wind, waves]
            spun, part, extra, flow = call(free, ins, [field] * 4, room, work=300)
            part, x_near, x_far = lax.optimization_barrier((part, x_near, x_far))
        else:
            if section == 3:
                values, x_near = lax.optimization_barrier((values, x_near))
            spun, part = call(free, [values, flow, pk], [field] * 2, room)
            if section == 2:
                part, x_near = lax.optimization_barrier((part, x_near))
        (part,) = call(turning, [values, spun, part, t_near, t_far], [field], work=1000)
        if opening:
            ins = [values, part, x_near, x_far, wind, waves]
            first = functools.partial(first_kernel, speed_step)
            part, gap = call(first, ins, [field] * 2, [rows])
            closing = functools.partial(closing_kernel, bounds, heading_step, speed_step)
            ins = [values, part, gap, extra, target_mask, target_depth, most]
            outs = [field, shape(longest), *far_shapes, shape()]
            values, x_out, x_last, t_out, t_last, pk = call(closing, ins, outs, [rows])
        else:
            more = section == 2
            ins = [level_set, values, part, x_near, wind, waves, target_mask, target_depth, pk]
            outs = [field] + ([shape(longest)] if more else [])
            last = functools.partial(section_kernel, section, (0, planes - rim), speed_step)
            early, *x_next = call(last, ins, outs, [rows, rows])
            ins = ins[:3] + [x_far] + ins[4:] + [early]
            outs = [field] + (far_shapes if more else [])
            last = functools.partial(section_kernel, section, (planes - rim, planes), speed_step)
            values, *far_next = call(last, ins, outs, [rows, rows])
            if more:
                (x_out,), (x_last, t_out, t_last) = x_next, far_next
    return values


def solution(mesh):
    return jax.shard_map(
        local,
        mesh=mesh,
        in_specs=(P("gx", "head", None, None), P(None, "gx", None), P("gx", None), P("gx", None)),
        out_specs=P("gx", "head", None, None),
        check_vma=False,
    )
```

```python
import functools
import math

import jax
import jax.numpy as jnp
import numpy as np
from jax import lax
from jax.experimental import pallas as pl
from jax.experimental.pallas import tpu as pltpu
from jax.sharding import PartitionSpec as P

epsilon = 1e-06
courant = 0.5
spacing = 0.05
turn_limit = 1.0
thrust_limit = 0.5
speed_low = 0.5
speed_high = 1.5
rim = 3
gain = 1.0 / (12.0 * spacing)


def inverse(value):
    return pltpu.reciprocal(value, approx=True)


def weights_of(e1, e2, turn, eps):
    level = turn * turn * (4.0 / 3.0) + eps
    ia = inverse(level + e2 * (e2 + turn))
    ib = inverse(level + e2 * e1)
    ic = inverse(level + e1 * (e1 - turn))
    return ia * ia, ib * ib * 6.0, ic * ic


def sides(fl, f0, fr, a2, a1, b1, b0, c0, c1):
    a3 = a1 * 3.0
    c3 = c0 * 3.0
    minus = ((fl + fl) * a2 + f0 * c3) * inverse(a2 + b1 + c3)
    plus = ((fr + fr) * c1 + f0 * a3) * inverse(c1 + b0 + a3)
    return minus, plus


def row_terms(cells, step, closed=False):
    eps = epsilon * step * step
    count = len(cells) if closed else len(cells) - 2 * rim
    shift = 0 if closed else rim
    slope = {m: cells[m + 1 + shift] - cells[m + shift] for m in range(-shift, count + shift - 1)}
    a, b, c = {}, {}, {}
    if closed:
        bend = {m: slope[m] - slope[m - 1] for m in range(1, count - 1)}
        bend[0], bend[count - 1] = slope[0], -slope[count - 2]
        turn = {m: bend[m + 1] - bend[m] for m in range(count - 1)}
        turn[-1], turn[count - 1] = bend[0], -bend[count - 1]
        jerk = {m: turn[m] - turn[m - 1] for m in range(count)}
        jerk[-1], jerk[count] = bend[0], bend[count - 1]
        rise = {m: slope[m] + slope[m - 1] for m in range(1, count - 1)}
        rise[0], rise[count - 1] = slope[0], slope[count - 2]
        a[-2] = c[count] = 1.0 / (eps * eps)
        for m, (e1, e2) in ((-1, (None, bend[0])), (count - 1, (bend[count - 1], None))):
            square = turn[m] * turn[m]
            level = square * (4.0 / 3.0) + eps
            ib, outer = inverse(level), inverse(level + (square + square))
            b[m] = ib * ib * 6.0
            (c if e2 is None else a)[m] = outer * outer
        inner = range(count - 1)
    else:
        bend = {m: slope[m] - slope[m - 1] for m in range(-2, count + 2)}
        turn = {m: bend[m + 1] - bend[m] for m in range(-2, count + 1)}
        jerk = {m: turn[m] - turn[m - 1] for m in range(-1, count + 1)}
        rise = {m: cells[m + 1 + rim] - cells[m - 1 + rim] for m in range(count)}
        inner = range(-2, count + 1)
    for m in inner:
        a[m], b[m], c[m] = weights_of(bend[m], bend[m + 1], turn[m], eps)
    out = []
    for i in range(count):
        base = rise[i] * 6.0 - (turn[i - 1] + turn[i])
        minus, plus = sides(
            jerk[i - 1], jerk[i], jerk[i + 1], a[i - 2], a[i - 1], b[i - 1], b[i], c[i], c[i + 1]
        )
        out.append((base + (plus - minus), (plus + minus) - jerk[i]))
    return out


def batches(total, most):
    return max(k for k in range(1, most + 1) if total % k == 0)


def splat(row, tile):
    return jnp.broadcast_to(row, tile)


def speeds_of(tile, speed_step):
    place = lax.broadcasted_iota(jnp.int32, tile, 0).astype(jnp.float32)
    return speed_low + place * speed_step


def odd_place(axis):
    return lax.rem(lax.axis_index(axis), 2) == 1


def put_extremes(wind_ref, most_ref):
    rows = [wind_ref[i] for i in range(wind_ref.shape[0])]
    most_ref[...] = jnp.zeros_like(most_ref)
    most_ref[0:2, :] = functools.reduce(jnp.maximum, rows)
    most_ref[2:4, :] = -functools.reduce(jnp.minimum, rows)


def opening_kernel(level_in, wind_in, level_ref, x_near, x_far, t_near, t_far, wind_ref, sems):
    planes = level_ref.shape[0]
    step = batches(planes, 3)
    pairs = [(wind_in, wind_ref)] + [
        (level_in.at[pl.ds(i, step)], level_ref.at[pl.ds(i, step)])
        for i in range(0, planes, step)
    ]
    copies = [
        pltpu.make_async_copy(src, dst, sems.at[k]) for k, (src, dst) in enumerate(pairs)
    ]
    for copy in copies:
        copy.start()
    copies[0].wait()
    put_extremes(wind_ref, x_near.at[x_near.shape[0] - 1])
    for copy in copies[1:]:
        copy.wait()
    cut_near(level_ref, x_near)
    cut_far(level_ref, x_far)
    cut_headings(level_ref, t_near, t_far)


def meeting_kernel(x_out, x_near, most_ref):
    spot = x_near.shape[0] - 1
    most_ref[...] = jnp.maximum(x_out[spot], x_near[spot])


def flows_into(flow_ref, speed_step, wind_ref, waves_ref):
    planes, headings = flow_ref.shape[:2]
    tile = flow_ref.shape[2:]
    first = lax.axis_index("head") * headings
    pace = speeds_of(tile, speed_step) * gain
    tables = [
        splat(waves_ref[1, pl.ds(first + j, 1), :], tile) * pace for j in range(headings)
    ]
    for i in range(planes):
        wind = splat(wind_ref[i, 1:2, :] * gain, tile)
        for j in range(headings):
            flow_ref[i, j] = tables[j] + wind


def free_kernel(split, speed_step, s_ref, *rest):
    planes, headings, speeds, width = s_ref.shape
    cells = planes * headings

    def rows_of(ref):
        return ref.reshape(cells * speeds, width)

    if split:
        wind_ref, waves_ref, speed_ref, out_ref, extra_ref, flow_ref = rest[:-3]
        flows_into(flow_ref, speed_step, wind_ref, waves_ref)
        extra_rows = rows_of(extra_ref)
    else:
        flow_ref, pk_ref, speed_ref, out_ref = rest[:-3]
        peak = splat(pk_ref[1:2, :] * gain, (16 * speeds, width))
    turned_ref, mean_ref, gap_ref = rest[-3:]
    gain_v = thrust_limit / (12.0 * speed_step)
    s_rows, speed_rows = rows_of(s_ref), rows_of(speed_ref)
    out_rows, flow_rows = rows_of(out_ref), rows_of(flow_ref)
    few, many = 8, turned_ref.shape[2] // speeds
    groups = turned_ref.shape[0]
    lanes = many * speeds
    high = 8
    lines = width // high

    def along_speed(n):
        start = jnp.minimum(n * few, cells - few) * speeds
        spots = [pl.ds(start + v, few, stride=speeds) for v in range(speeds)]
        rows = [s_rows[spot, :] for spot in spots]
        for spot, (mean, gap) in zip(spots, row_terms(rows, speed_step, True)):
            speed_rows[spot, :] = gain_v * (gap - jnp.abs(mean))

    def span(n):
        return pl.ds(pl.multiple_of(jnp.minimum(n * many, cells - many) * speeds, speeds), lanes)

    def turn_in(n):
        turned = s_rows[span(n), :].T
        turned_ref[n, rim : rim + width, :] = turned
        for k in range(rim):
            turned_ref[n, k : k + 1, :] = turned[:1]
            turned_ref[n, rim + width + k : rim + width + k + 1, :] = turned[-1:]

    def along_y(n):
        ends = [turned_ref[n, pl.ds(k, high, stride=lines), :] for k in range(lines + 2 * rim)]
        for k, (mean, gap) in enumerate(row_terms(ends, spacing)):
            mean_ref[n, pl.ds(k, high, stride=lines), :] = mean
            gap_ref[n, pl.ds(k, high, stride=lines), :] = gap

    def turn_out(n):
        mean = mean_ref[n].T
        gap = gap_ref[n].T
        drift = mean * flow_rows[span(n), :]
        if split:
            out_rows[span(n), :] = drift
            extra_rows[span(n), :] = gap
        else:
            out_rows[span(n), :] = drift + gap * peak

    def step(n, carry):
        turn_out(jnp.maximum(n - 1, 0))
        along_y(n)
        turn_in(jnp.minimum(n + 1, groups - 1))
        along_speed(2 * n)
        along_speed(2 * n + 1)
        return carry

    turn_in(0)
    lax.fori_loop(0, groups, step, 0)
    turn_out(groups - 1)


def heading_kernel(heading_step, s_ref, speed_ref, part_ref, near_ref, far_ref, out_ref):
    planes, headings = s_ref.shape[:2]
    gain_t = turn_limit / (12.0 * heading_step)
    odd = odd_place("head")
    wide = batches(planes, 3)

    def step(n, carry):
        for w in range(wide):
            i = n * wide + w
            ghosts = [(near_ref[i * rim + k], far_ref[i * rim + k]) for k in range(rim)]
            lows = [jnp.where(odd, near, far) for near, far in ghosts]
            highs = [jnp.where(odd, far, near) for near, far in ghosts]
            cells = lows + [s_ref[i, j] for j in range(headings)] + highs
            for j, (mean, gap) in enumerate(row_terms(cells, heading_step)):
                own = speed_ref[i, j] + part_ref[i, j]
                out_ref[i, j] = own + gain_t * (gap - jnp.abs(mean))
        return carry

    lax.fori_loop(0, planes // wide, step, 0)


def peaks_into(pk_ref, most, bounds, heading_step, speed_step):
    most = jnp.max(most, axis=1, keepdims=True)
    peaks = [
        jnp.maximum(most[q : q + 1] + bounds[q][1], most[q + 2 : q + 3] - bounds[q][0])
        for q in range(2)
    ]
    time_step = courant / (
        peaks[0] / spacing
        + peaks[1] / spacing
        + turn_limit / heading_step
        + thrust_limit / speed_step
    )
    width = pk_ref.shape[1]
    for row, value in enumerate(peaks + [time_step]):
        pk_ref[row : row + 1, :] = splat(value, (1, width))


def plane_at(i, planes):
    return jnp.where(odd_place("gx"), i, planes - 1 - i)


def alone(reach):
    place, size = lax.axis_index("gx"), lax.axis_size("gx")
    if reach == 0:
        return (place == size - 1) if size % 2 else place < 0
    return (place == 0) | (place == size - 1) if size % 2 == 0 else place == 0


def cut_near(field_ref, x_near):
    planes, headings = field_ref.shape[:2]
    for k in range(rim):
        i = jnp.where(alone(0), 0, k)
        x_near[k * headings : (k + 1) * headings] = field_ref[plane_at(i, planes)]


def cut_far(field_ref, x_far):
    planes, headings = field_ref.shape[:2]
    for k in range(rim):
        i = planes - 1 - jnp.where(alone(1), 0, k)
        x_far[k * headings : (k + 1) * headings] = field_ref[plane_at(i, planes)]


def cut_headings(field_ref, t_near, t_far):
    planes, headings = field_ref.shape[:2]
    t_low = jnp.where(odd_place("head"), 0, headings - rim)
    for k in range(rim):
        for i in range(planes):
            t_near[i * rim + k] = field_ref[i, t_low + k]
            t_far[i * rim + k] = field_ref[i, headings - rim - t_low + k]


def splat_targets(mask_ref, depth_ref, target_ref):
    for i in range(target_ref.shape[0]):
        depth = depth_ref[i : i + 1, :]
        target = jnp.where(mask_ref[i : i + 1, :] == 1, -depth, depth)
        target_ref[i] = splat(target, target_ref.shape[1:])


def across_planes(
    span, speed_step, s_ref, near_ref, far_ref, wind_ref, waves_ref, flow_ref, use
):
    planes, headings = s_ref.shape[:2]
    tile = s_ref.shape[2:]
    side = jnp.where(odd_place("gx"), gain, -gain).astype(jnp.float32)
    spots = [plane_at(i, planes) for i in range(planes)]
    for i in range(planes):
        flow_ref[i] = splat(wind_ref[i, 0:1, :] * side, tile)
    pace = speeds_of(tile, speed_step) * side
    first = lax.axis_index("head") * headings
    low, high = span
    wide = batches(headings, max(1, 54 // (high - low)))

    def line(i, j):
        if i < 0:
            return near_ref[(-1 - i) * headings + j]
        if i >= planes:
            return far_ref[(i - planes) * headings + j]
        return s_ref[spots[i], j]

    def step(n, carry):
        for w in range(wide):
            j = n * wide + w
            cells = [line(i, j) for i in range(low - rim, high + rim)]
            table = splat(waves_ref[0, pl.ds(first + j, 1), :], tile) * pace
            for k, (mean, gap) in enumerate(row_terms(cells, spacing)):
                spot = spots[low + k]
                use(spot, j, mean * (table + flow_ref[spot]), gap, cells[k + rim])
        return carry

    lax.fori_loop(0, headings // wide, step, 0)


def first_kernel(
    speed_step, s_ref, part_ref, near_ref, far_ref, wind_ref, waves_ref, out_ref, gap_ref, flow_ref
):
    def use(i, j, drift, gap, cell):
        out_ref[i, j] = part_ref[i, j] + drift
        gap_ref[i, j] = gap

    across_planes(
        (0, s_ref.shape[0]), speed_step, s_ref, near_ref, far_ref, wind_ref, waves_ref, flow_ref, use
    )


def closing_kernel(
    bounds, heading_step, speed_step, s_ref, part_ref, gap_x_ref, gap_y_ref, mask_ref, depth_ref,
    most_ref, other_ref, out_ref, x_near, x_far, t_near, t_far, pk_ref, target_ref
):
    planes, headings = s_ref.shape[:2]
    tile = s_ref.shape[2:]
    most = jnp.maximum(most_ref[...], other_ref[...])
    peaks_into(pk_ref, most, bounds, heading_step, speed_step)
    splat_targets(mask_ref, depth_ref, target_ref)
    peak_x = splat(pk_ref[0:1, :] * gain, tile)
    peak_y = splat(pk_ref[1:2, :] * gain, tile)
    time_step = splat(pk_ref[2:3, :], tile)

    def plane(i, carry):
        for j in range(headings):
            rate = part_ref[i, j] + (gap_x_ref[i, j] * peak_x + gap_y_ref[i, j] * peak_y)
            out_ref[i, j] = jnp.minimum(s_ref[i, j] + time_step * rate, target_ref[i])
        return carry

    lax.fori_loop(0, planes, plane, 0)
    cut_near(out_ref, x_near)
    cut_far(out_ref, x_far)
    cut_headings(out_ref, t_near, t_far)


def section_kernel(
    section, span, speed_step, base_ref, s_ref, part_ref, ghosts_ref, wind_ref, waves_ref,
    mask_ref, depth_ref, pk_ref, *refs
):
    planes = s_ref.shape[0]
    refs, (flow_ref, target_ref) = list(refs[:-2]), refs[-2:]
    early_ref = refs.pop(0) if span[0] > 0 else None
    out_ref = refs.pop(0)
    tile = s_ref.shape[2:]
    splat_targets(mask_ref, depth_ref, target_ref)
    peak_x = splat(pk_ref[0:1, :] * gain, tile)
    time_step = splat(pk_ref[2:3, :], tile)
    base_share = 0.75 if section == 2 else 1.0 / 3.0
    own_share = 0.25 if section == 2 else 2.0 / 3.0

    def use(i, j, drift, gap, cell):
        rate = part_ref[i, j] + (drift + gap * peak_x)
        moved = base_share * base_ref[i, j] + own_share * (cell + time_step * rate)
        out_ref[i, j] = jnp.minimum(moved, target_ref[i])

    near_ref, far_ref = (None, ghosts_ref) if span[0] > 0 else (ghosts_ref, None)
    across_planes(
        span, speed_step, s_ref, near_ref, far_ref, wind_ref, waves_ref, flow_ref, use
    )
    for i in range(span[0]):
        spot = plane_at(i, planes)
        out_ref[spot] = early_ref[spot]
    if section == 2 and span[0] == 0:
        cut_near(out_ref, *refs)
    elif section == 2:
        cut_far(out_ref, refs[0])
        cut_headings(out_ref, *refs[1:])


def trade(value, axis, reach, wrap=False):
    size = lax.axis_size(axis)
    pairs = [(i, i + 1) for i in range(reach, size - 1, 2)]
    if wrap and reach and size % 2 == 0:
        pairs.append((size - 1, 0))
    pairs += [(j, i) for i, j in pairs]
    pairs += [(i, i) for i in range(size) if i not in dict(pairs)]
    return lax.ppermute(value, axis, pairs)


def local(level_set, wind_field, target_mask, target_depth):
    planes, headings, speed_count, cross_count = level_set.shape
    heading_total = headings * lax.axis_size("head")
    heading_step = 2.0 * math.pi / heading_total
    speed_step = (speed_high - speed_low) / (speed_count - 1)
    speed_row = np.float32(speed_low) + np.arange(speed_count, dtype=np.float32) * np.float32(
        speed_step
    )
    angles = np.arange(heading_total, dtype=np.float32) * np.float32(heading_step)
    waves = [np.cos(angles), np.sin(angles)]
    bounds = []
    for wave in waves:
        product = wave[:, None] * speed_row[None, :]
        bounds.append((float(product.min()), float(product.max())))
    waves = jnp.asarray(np.stack(waves)[..., None] * np.ones(cross_count, np.float32))

    vmem = pl.BlockSpec(memory_space=pltpu.VMEM)
    tile = (speed_count, cross_count)

    def shape(*dims):
        return jax.ShapeDtypeStruct(dims + tile, jnp.float32)

    field = shape(planes, headings)
    short = rim * headings
    middle = max(short + 1, rim * planes)

    longest = middle + 1
    rows = pltpu.VMEM((planes,) + tile, jnp.float32)
    cells = math.prod(level_set.shape)

    def call(kernel, ins, outs, scratch=(), work=0):
        return pl.pallas_call(
            kernel,
            out_shape=outs,
            in_specs=[vmem] * len(ins),
            out_specs=[vmem] * len(outs),
            scratch_shapes=list(scratch),
            compiler_params=pltpu.CompilerParams(vmem_limit_bytes=16 * 1024 * 1024),
            cost_estimate=pl.CostEstimate(
                flops=work * cells, bytes_accessed=work * cells, transcendentals=0
            ),
        )(*ins)

    wind = jnp.transpose(wind_field, (1, 0, 2))
    many = 16
    groups, lanes = -(-planes * headings // many), many * speed_count
    room = [
        pltpu.VMEM((groups, cross_count + 8, lanes), jnp.float32),
        pltpu.VMEM((groups, cross_count, lanes), jnp.float32),
        pltpu.VMEM((groups, cross_count, lanes), jnp.float32),
    ]
    size = lax.axis_size(axis)
    pairs = [(i, i + 1) for i in range(reach, size - 1, 2)]
    if wrap and reach and size % 2 == 0:
        pairs.append((size - 1, 0))
    pairs += [(j, i) for i, j in pairs]
    pairs += [(i, i) for i in range(size) if i not in dict(pairs)]
    return lax.ppermute(value, axis, pairs)


def local(level_set, wind_field, target_mask, target_depth):
    planes, headings, speed_count, cross_count = level_set.shape
    heading_total = headings * lax.axis_size("head")
    heading_step = 2.0 * math.pi / heading_total
    speed_step = (speed_high - speed_low) / (speed_count - 1)
    speed_row = np.float32(speed_low) + np.arange(speed_count, dtype=np.float32) * np.float32(
        speed_step
    )
    angles = np.arange(heading_total, dtype=np.float32) * np.float32(heading_step)
    waves = [np.cos(angles), np.sin(angles)]
    bounds = []
    for wave in waves:
        product = wave[:, None] * speed_row[None, :]
        bounds.append((float(product.min()), float(product.max())))
    waves = jnp.asarray(np.stack(waves)[..., None] * np.ones(cross_count, np.float32))

    vmem = pl.BlockSpec(memory_space=pltpu.VMEM)
    tile = (speed_count, cross_count)

    def shape(*dims):
        return jax.ShapeDtypeStruct(dims + tile, jnp.float32)

    field = shape(planes, headings)
    short = rim * headings
    middle = max(short + 1, rim * planes)

    longest = middle + 1
    rows = pltpu.VMEM((planes,) + tile, jnp.float32)
    cells = math.prod(level_set.shape)

    def call(kernel, ins, outs, scratch=(), work=0):
        return pl.pallas_call(
            kernel,
            out_shape=outs,
            in_specs=[vmem] * len(ins),
            out_specs=[vmem] * len(outs),
            scratch_shapes=list(scratch),
            compiler_params=pltpu.CompilerParams(vmem_limit_bytes=16 * 1024 * 1024),
            cost_estimate=pl.CostEstimate(
                flops=work * cells, bytes_accessed=work * cells, transcendentals=0
            ),
        )(*ins)

    wind = jnp.transpose(wind_field, (1, 0, 2))
    many = 16
    groups, lanes = -(-planes * headings // many), many * speed_count
    room = [
        pltpu.VMEM((groups, cross_count + 8, lanes), jnp.float32),
        pltpu.VMEM((groups, cross_count, lanes), jnp.float32),
        pltpu.VMEM((groups, cross_count, lanes), jnp.float32),
    ]
    values, pk = level_set, None
    size = lax.axis_size("gx")

    def spread(most, reach):
        if size & (size - 1):
            pairs = [(i, (i + reach) % size) for i in range(size)]
        else:
            pairs = [(i, i ^ reach) for i in range(size)]
        return lax.ppermute(most, "gx", pairs)

    level, x_out, x_last, t_out, t_last = pl.pallas_call(
        opening_kernel,
        out_shape=[field, shape(longest + 1), shape(longest), shape(middle), shape(middle)],
        in_specs=[pl.BlockSpec(memory_space=pltpu.HBM)] * 2,
        out_specs=[vmem] * 5,
        scratch_shapes=[pltpu.VMEM(wind.shape, jnp.float32), pltpu.SemaphoreType.DMA((planes + 1,))],
        compiler_params=pltpu.CompilerParams(vmem_limit_bytes=16 * 1024 * 1024),
        cost_estimate=pl.CostEstimate(flops=0, bytes_accessed=0, transcendentals=0),
    )(level_set, wind)
    values = level
    far_shapes = [shape(short), shape(rim * planes), shape(middle)]
    for section in (1, 2, 3):
        opening = section == 1
        x_near = trade(x_out, "gx", 0)
        t_near = trade(t_out, "head", 0)
        t_far = trade(t_last, "head", 1, True)
        x_far = trade(x_last, "gx", 1)
        free = functools.partial(free_kernel, opening, speed_step)
        turning = functools.partial(heading_kernel, heading_step)
        if opening:
            (most,) = call(meeting_kernel, [x_out, x_near], [shape()])
            other = spread(most, 2)
            ins = [values, wind, waves]
            spun, part, extra, flow = call(free, ins, [field] * 4, room, work=300)
            reach = 4
            while reach < size:
                most = jnp.maximum(most, other)
                most, part = lax.optimization_barrier((most, part))
                other = spread(most, reach)
                reach *= 2
            part, x_far = lax.optimization_barrier((part, x_far))
        else:
            if section == 3:
                values, x_near = lax.optimization_barrier((values, x_near))
            spun, part = call(free, [values, flow, pk], [field] * 2, room)
            if section == 2:
                part, x_near = lax.optimization_barrier((part, x_near))
        (part,) = call(turning, [values, spun, part, t_near, t_far], [field], work=1000)
        if opening:
            ins = [values, part, x_near, x_far, wind, waves]
            first = functools.partial(first_kernel, speed_step)
            part, gap = call(first, ins, [field] * 2, [rows])
            closing = functools.partial(closing_kernel, bounds, heading_step, speed_step)
            ins = [values, part, gap, extra, target_mask, target_depth, most, other]
            outs = [field, shape(longest), *far_shapes, shape()]
            values, x_out, x_last, t_out, t_last, pk = call(closing, ins, outs, [rows])
        else:
            more = section == 2
            ins = [level, values, part, x_near, wind, waves, target_mask, target_depth, pk]
            outs = [field] + ([shape(longest)] if more else [])
            last = functools.partial(section_kernel, section, (0, planes - rim), speed_step)
            early, *x_next = call(last, ins, outs, [rows, rows])
            ins = ins[:3] + [x_far] + ins[4:] + [early]
            outs = [field] + (far_shapes if more else [])
            last = functools.partial(section_kernel, section, (planes - rim, planes), speed_step)
            values, *far_next = call(last, ins, outs, [rows, rows])
            if more:
                (x_out,), (x_last, t_out, t_last) = x_next, far_next
    return values


def solution(mesh):
    return jax.shard_map(
        local,
        mesh=mesh,
        in_specs=(P("gx", "head", None, None), P(None, "gx", None), P("gx", None), P("gx", None)),
        out_specs=P("gx", "head", None, None),
        check_vma=False,
    )
```

```python
import functools
import math

import jax
import jax.numpy as jnp
import numpy as np
from jax import lax
from jax.experimental import pallas as pl
from jax.experimental.pallas import tpu as pltpu
from jax.sharding import PartitionSpec as P

epsilon = 1e-06
courant = 0.5
spacing = 0.05
turn_limit = 1.0
thrust_limit = 0.5
speed_low = 0.5
speed_high = 1.5
rim = 3
gain = 1.0 / (12.0 * spacing)


def inverse(value):
    return pltpu.reciprocal(value, approx=True)


def weights_of(e1, e2, turn, eps):
    level = turn * turn * (4.0 / 3.0) + eps
    ia = inverse(level + e2 * (e2 + turn))
    ib = inverse(level + e2 * e1)
    ic = inverse(level + e1 * (e1 - turn))
    return ia * ia, ib * ib * 6.0, ic * ic


def sides(fl, f0, fr, a2, a1, b1, b0, c0, c1):
    a3 = a1 * 3.0
    c3 = c0 * 3.0
    minus = ((fl + fl) * a2 + f0 * c3) * inverse(a2 + b1 + c3)
    plus = ((fr + fr) * c1 + f0 * a3) * inverse(c1 + b0 + a3)
    return minus, plus


def row_terms(cells, step, closed=False):
    eps = epsilon * step * step
    count = len(cells) if closed else len(cells) - 2 * rim
    shift = 0 if closed else rim
    slope = {m: cells[m + 1 + shift] - cells[m + shift] for m in range(-shift, count + shift - 1)}
    a, b, c = {}, {}, {}
    if closed:
        bend = {m: slope[m] - slope[m - 1] for m in range(1, count - 1)}
        bend[0], bend[count - 1] = slope[0], -slope[count - 2]
        turn = {m: bend[m + 1] - bend[m] for m in range(count - 1)}
        turn[-1], turn[count - 1] = bend[0], -bend[count - 1]
        jerk = {m: turn[m] - turn[m - 1] for m in range(count)}
        jerk[-1], jerk[count] = bend[0], bend[count - 1]
        rise = {m: slope[m] + slope[m - 1] for m in range(1, count - 1)}
        rise[0], rise[count - 1] = slope[0], slope[count - 2]
        a[-2] = c[count] = 1.0 / (eps * eps)
        for m, (e1, e2) in ((-1, (None, bend[0])), (count - 1, (bend[count - 1], None))):
            square = turn[m] * turn[m]
            level = square * (4.0 / 3.0) + eps
            ib, outer = inverse(level), inverse(level + (square + square))
            b[m] = ib * ib * 6.0
            (c if e2 is None else a)[m] = outer * outer
        inner = range(count - 1)
    else:
        bend = {m: slope[m] - slope[m - 1] for m in range(-2, count + 2)}
        turn = {m: bend[m + 1] - bend[m] for m in range(-2, count + 1)}
        jerk = {m: turn[m] - turn[m - 1] for m in range(-1, count + 1)}
        rise = {m: cells[m + 1 + rim] - cells[m - 1 + rim] for m in range(count)}
        inner = range(-2, count + 1)
    for m in inner:
        a[m], b[m], c[m] = weights_of(bend[m], bend[m + 1], turn[m], eps)
    out = []
    for i in range(count):
        base = rise[i] * 6.0 - (turn[i - 1] + turn[i])
        minus, plus = sides(
            jerk[i - 1], jerk[i], jerk[i + 1], a[i - 2], a[i - 1], b[i - 1], b[i], c[i], c[i + 1]
        )
        out.append((base + (plus - minus), (plus + minus) - jerk[i]))
    return out


def batches(total, most):
    return max(k for k in range(1, most + 1) if total % k == 0)


def splat(row, tile):
    return jnp.broadcast_to(row, tile)


def speeds_of(tile, speed_step):
    place = lax.broadcasted_iota(jnp.int32, tile, 0).astype(jnp.float32)
    return speed_low + place * speed_step


def odd_place(axis):
    return lax.rem(lax.axis_index(axis), 2) == 1


def put_extremes(wind_ref, most_ref):
    rows = [wind_ref[i] for i in range(wind_ref.shape[0])]
    most_ref[...] = jnp.zeros_like(most_ref)
    most_ref[0:2, :] = functools.reduce(jnp.maximum, rows)
    most_ref[2:4, :] = -functools.reduce(jnp.minimum, rows)


def extremes_kernel(wind_ref, most_ref):
    put_extremes(wind_ref, most_ref.at[0])


def opening_kernel(level_ref, x_near, x_far, t_near, t_far):
    cut_near(level_ref, x_near)
    cut_far(level_ref, x_far)
    cut_headings(level_ref, t_near, t_far)


def meeting_kernel(own_ref, other_ref, most_ref):
    most_ref[...] = jnp.maximum(own_ref[0], other_ref[0])


def flows_into(flow_ref, speed_step, wind_ref, waves_ref):
    planes, headings = flow_ref.shape[:2]
    tile = flow_ref.shape[2:]
    first = lax.axis_index("head") * headings
    pace = speeds_of(tile, speed_step) * gain
    tables = [
        splat(waves_ref[1, pl.ds(first + j, 1), :], tile) * pace for j in range(headings)
    ]
    for i in range(planes):
        wind = splat(wind_ref[i, 1:2, :] * gain, tile)
        for j in range(headings):
            flow_ref[i, j] = tables[j] + wind


def free_kernel(split, speed_step, s_ref, *rest):
    planes, headings, speeds, width = s_ref.shape
    cells = planes * headings

    def rows_of(ref):
        return ref.reshape(cells * speeds, width)

    if split:
        wind_ref, waves_ref, speed_ref, out_ref, extra_ref, flow_t_ref = rest[:6]
        turned_ref, drift_ref, gap_ref, flow_ref = rest[6:]
        flows_into(flow_ref, speed_step, wind_ref, waves_ref)
        extra_rows, flow_rows = rows_of(extra_ref), rows_of(flow_ref)
    else:
        flow_t_ref, pk_ref, speed_ref, out_ref, turned_ref, drift_ref = rest
        peak = splat(pk_ref[1:2, :] * gain, (speeds, width))
    gain_v = thrust_limit / (12.0 * speed_step)
    s_rows, speed_rows, out_rows = rows_of(s_ref), rows_of(speed_ref), rows_of(out_ref)
    few, many = 8, turned_ref.shape[2] // speeds
    groups = turned_ref.shape[0]
    lanes = many * speeds
    high = 8
    lines = width // high

    def along_speed(n):
        start = jnp.minimum(n * few, cells - few) * speeds
        spots = [pl.ds(start + v, few, stride=speeds) for v in range(speeds)]
        rows = [s_rows[spot, :] for spot in spots]
        for spot, (mean, gap) in zip(spots, row_terms(rows, speed_step, True)):
            speed_rows[spot, :] = gain_v * (gap - jnp.abs(mean))

    def span(n):
        return pl.ds(pl.multiple_of(jnp.minimum(n * many, cells - many) * speeds, speeds), lanes)

    def turn_in(n):
        turned = s_rows[span(n), :].T
        turned_ref[n, rim : rim + width, :] = turned
        for k in range(rim):
            turned_ref[n, k : k + 1, :] = turned[:1]
            turned_ref[n, rim + width + k : rim + width + k + 1, :] = turned[-1:]
        if split:
            flow_t_ref[n] = flow_rows[span(n), :].T

    def along_y(n):
        ends = [turned_ref[n, pl.ds(k, high, stride=lines), :] for k in range(lines + 2 * rim)]
        for k, (mean, gap) in enumerate(row_terms(ends, spacing)):
            spot = pl.ds(k, high, stride=lines)
            drift = mean * flow_t_ref[n, spot, :]
            if split:
                drift_ref[n, spot, :] = drift
                gap_ref[n, spot, :] = gap
            else:
                drift_ref[n, spot, :] = drift + gap * peak

    def turn_out(n):
        out_rows[span(n), :] = drift_ref[n].T
        if split:
            extra_rows[span(n), :] = gap_ref[n].T

    def step(n, carry):
        turn_out(jnp.maximum(n - 1, 0))
        along_y(n)
        turn_in(jnp.minimum(n + 1, groups - 1))
        along_speed(2 * n)
        along_speed(2 * n + 1)
        return carry

    turn_in(0)
    lax.fori_loop(0, groups, step, 0)
    turn_out(groups - 1)


def heading_kernel(heading_step, s_ref, speed_ref, part_ref, near_ref, far_ref, out_ref):
    planes, headings = s_ref.shape[:2]
    gain_t = turn_limit / (12.0 * heading_step)
    odd = odd_place("head")
    wide = batches(planes, 9)

    def step(n, carry):
        for w in range(wide):
            i = n * wide + w
            ghosts = [(near_ref[i * rim + k], far_ref[i * rim + k]) for k in range(rim)]
            lows = [jnp.where(odd, near, far) for near, far in ghosts]
            highs = [jnp.where(odd, far, near) for near, far in ghosts]
            cells = lows + [s_ref[i, j] for j in range(headings)] + highs
            for j, (mean, gap) in enumerate(row_terms(cells, heading_step)):
                own = speed_ref[i, j] + part_ref[i, j]
                out_ref[i, j] = own + gain_t * (gap - jnp.abs(mean))
        return carry

    lax.fori_loop(0, planes // wide, step, 0)


def peaks_into(pk_ref, most, bounds, heading_step, speed_step):
    most = jnp.max(most, axis=1, keepdims=True)
    peaks = [
        jnp.maximum(most[q : q + 1] + bounds[q][1], most[q + 2 : q + 3] - bounds[q][0])
        for q in range(2)
    ]
    time_step = courant / (
        peaks[0] / spacing
        + peaks[1] / spacing
        + turn_limit / heading_step
        + thrust_limit / speed_step
    )
    width = pk_ref.shape[1]
    for row, value in enumerate(peaks + [time_step]):
        pk_ref[row : row + 1, :] = splat(value, (1, width))


def plane_at(i, planes):
    return jnp.where(odd_place("gx"), i, planes - 1 - i)


def alone(reach):
    place, size = lax.axis_index("gx"), lax.axis_size("gx")
    if reach == 0:
        return (place == size - 1) if size % 2 else place < 0
    return (place == 0) | (place == size - 1) if size % 2 == 0 else place == 0


def cut_near(field_ref, x_near):
    planes, headings = field_ref.shape[:2]
    for k in range(rim):
        i = jnp.where(alone(0), 0, k)
        x_near[k * headings : (k + 1) * headings] = field_ref[plane_at(i, planes)]


def cut_far(field_ref, x_far):
    planes, headings = field_ref.shape[:2]
    for k in range(rim):
        i = planes - 1 - jnp.where(alone(1), 0, k)
        x_far[k * headings : (k + 1) * headings] = field_ref[plane_at(i, planes)]


def cut_headings(field_ref, t_near, t_far):
    planes, headings = field_ref.shape[:2]
    t_low = jnp.where(odd_place("head"), 0, headings - rim)
    for k in range(rim):
        for i in range(planes):
            t_near[i * rim + k] = field_ref[i, t_low + k]
            t_far[i * rim + k] = field_ref[i, headings - rim - t_low + k]


def splat_targets(mask_ref, depth_ref, target_ref):
    for i in range(target_ref.shape[0]):
        depth = depth_ref[i : i + 1, :]
        target = jnp.where(mask_ref[i : i + 1, :] == 1, -depth, depth)
        target_ref[i] = splat(target, target_ref.shape[1:])


def across_planes(
    span, speed_step, s_ref, near_ref, far_ref, wind_ref, waves_ref, flow_ref, use
):
    planes, headings = s_ref.shape[:2]
    tile = s_ref.shape[2:]
    side = jnp.where(odd_place("gx"), gain, -gain).astype(jnp.float32)
    spots = [plane_at(i, planes) for i in range(planes)]
    for i in range(planes):
        flow_ref[i] = splat(wind_ref[i, 0:1, :] * side, tile)
    pace = speeds_of(tile, speed_step) * side
    first = lax.axis_index("head") * headings
    low, high = span
    wide = batches(headings, max(1, 54 // (high - low)))

    def line(i, j):
        if i < 0:
            return near_ref[(-1 - i) * headings + j]
        if i >= planes:
            return far_ref[(i - planes) * headings + j]
        return s_ref[spots[i], j]

    def step(n, carry):
        for w in range(wide):
            j = n * wide + w
            cells = [line(i, j) for i in range(low - rim, high + rim)]
            table = splat(waves_ref[0, pl.ds(first + j, 1), :], tile) * pace
            for k, (mean, gap) in enumerate(row_terms(cells, spacing)):
                spot = spots[low + k]
                use(spot, j, mean * (table + flow_ref[spot]), gap, cells[k + rim])
        return carry

    lax.fori_loop(0, headings // wide, step, 0)


def first_kernel(
    speed_step, s_ref, part_ref, near_ref, far_ref, wind_ref, waves_ref, out_ref, gap_ref, flow_ref
):
    def use(i, j, drift, gap, cell):
        out_ref[i, j] = part_ref[i, j] + drift
        gap_ref[i, j] = gap

    across_planes(
        (0, s_ref.shape[0]), speed_step, s_ref, near_ref, far_ref, wind_ref, waves_ref, flow_ref, use
    )


def closing_kernel(
    bounds, heading_step, speed_step, s_ref, part_ref, gap_x_ref, gap_y_ref, mask_ref, depth_ref,
    most_ref, other_ref, out_ref, x_near, x_far, t_near, t_far, pk_ref, target_ref
):
    planes, headings = s_ref.shape[:2]
    tile = s_ref.shape[2:]
    most = jnp.maximum(most_ref[...], other_ref[...])
    peaks_into(pk_ref, most, bounds, heading_step, speed_step)
    splat_targets(mask_ref, depth_ref, target_ref)
    peak_x = splat(pk_ref[0:1, :] * gain, tile)
    peak_y = splat(pk_ref[1:2, :] * gain, tile)
    time_step = splat(pk_ref[2:3, :], tile)

    def plane(i, carry):
        for j in range(headings):
            rate = part_ref[i, j] + (gap_x_ref[i, j] * peak_x + gap_y_ref[i, j] * peak_y)
            out_ref[i, j] = jnp.minimum(s_ref[i, j] + time_step * rate, target_ref[i])
        return carry

    lax.fori_loop(0, planes, plane, 0)
    cut_near(out_ref, x_near)
    cut_far(out_ref, x_far)
    cut_headings(out_ref, t_near, t_far)


def section_kernel(
    section, span, speed_step, base_ref, s_ref, part_ref, ghosts_ref, wind_ref, waves_ref,
    mask_ref, depth_ref, pk_ref, *refs
):
    planes = s_ref.shape[0]
    refs, (flow_ref, target_ref) = list(refs[:-2]), refs[-2:]
    early_ref = refs.pop(0) if span[0] > 0 else None
    out_ref = refs.pop(0)
    tile = s_ref.shape[2:]
    splat_targets(mask_ref, depth_ref, target_ref)
    peak_x = splat(pk_ref[0:1, :] * gain, tile)
    time_step = splat(pk_ref[2:3, :], tile)
    base_share = 0.75 if section == 2 else 1.0 / 3.0
    own_share = 0.25 if section == 2 else 2.0 / 3.0

    def use(i, j, drift, gap, cell):
        rate = part_ref[i, j] + (drift + gap * peak_x)
        moved = base_share * base_ref[i, j] + own_share * (cell + time_step * rate)
        out_ref[i, j] = jnp.minimum(moved, target_ref[i])

    near_ref, far_ref = (None, ghosts_ref) if span[0] > 0 else (ghosts_ref, None)
    across_planes(
        span, speed_step, s_ref, near_ref, far_ref, wind_ref, waves_ref, flow_ref, use
    )
    for i in range(span[0]):
        spot = plane_at(i, planes)
        out_ref[spot] = early_ref[spot]
    if section == 2 and span[0] == 0:
        cut_near(out_ref, *refs)
    elif section == 2:
        cut_far(out_ref, refs[0])
        cut_headings(out_ref, *refs[1:])


def trade(value, axis, reach, wrap=False):
    size = lax.axis_size(axis)
    pairs = [(i, i + 1) for i in range(reach, size - 1, 2)]
    if wrap and reach and size % 2 == 0:
        pairs.append((size - 1, 0))
    pairs += [(j, i) for i, j in pairs]
    pairs += [(i, i) for i in range(size) if i not in dict(pairs)]
    return lax.ppermute(value, axis, pairs)


def local(level_set, wind_field, target_mask, target_depth):
    planes, headings, speed_count, cross_count = level_set.shape
    heading_total = headings * lax.axis_size("head")
    heading_step = 2.0 * math.pi / heading_total
    speed_step = (speed_high - speed_low) / (speed_count - 1)
    speed_row = np.float32(speed_low) + np.arange(speed_count, dtype=np.float32) * np.float32(
        speed_step
    )
    angles = np.arange(heading_total, dtype=np.float32) * np.float32(heading_step)
    waves = [np.cos(angles), np.sin(angles)]
    bounds = []
    for wave in waves:
        product = wave[:, None] * speed_row[None, :]
        bounds.append((float(product.min()), float(product.max())))
    waves = jnp.asarray(np.stack(waves)[..., None] * np.ones(cross_count, np.float32))

    vmem = pl.BlockSpec(memory_space=pltpu.VMEM)
    tile = (speed_count, cross_count)

    def shape(*dims):
        return jax.ShapeDtypeStruct(dims + tile, jnp.float32)

    field = shape(planes, headings)
    short = rim * headings
    middle = max(short + 1, rim * planes)

    longest = middle + 1
    rows = pltpu.VMEM((planes,) + tile, jnp.float32)
    cells = math.prod(level_set.shape)

    def call(kernel, ins, outs, scratch=(), work=0):
        return pl.pallas_call(
            kernel,
            out_shape=outs,
            in_specs=[vmem] * len(ins),
            out_specs=[vmem] * len(outs),
            scratch_shapes=list(scratch),
            compiler_params=pltpu.CompilerParams(vmem_limit_bytes=16 * 1024 * 1024),
            cost_estimate=pl.CostEstimate(
                flops=work * cells, bytes_accessed=work * cells, transcendentals=0
            ),
        )(*ins)

    wind = jnp.transpose(wind_field, (1, 0, 2))
    many = 16
    groups, lanes = -(-planes * headings // many), many * speed_count
    turned = (groups, cross_count, lanes)
    room = [
        pltpu.VMEM((groups, cross_count + 8, lanes), jnp.float32),
        pltpu.VMEM(turned, jnp.float32),
    ]
    wide_room = room + [pltpu.VMEM(turned, jnp.float32), pltpu.VMEM(level_set.shape, jnp.float32)]
    values = level_set
    size = lax.axis_size("gx")

    def spread(most, reach):
        if size & (size - 1):
            pairs = [(i, (i + reach) % size) for i in range(size)]
        else:
            pairs = [(i, i ^ reach) for i in range(size)]
        return lax.ppermute(most, "gx", pairs)

    (most,) = call(extremes_kernel, [wind], [shape(longest + 2)])
    other = spread(most, 1)
    x_shapes = [shape(longest), shape(longest + 1)]
    x_out, x_last, t_out, t_last = call(opening_kernel, [values], x_shapes + [shape(middle)] * 2)
    far_shapes = [shape(short), shape(rim * planes), shape(middle)]
    for section in (1, 2, 3):
        opening = section == 1
        x_near = trade(x_out, "gx", 0)
        t_near = trade(t_out, "head", 0)
        t_far = trade(t_last, "head", 1, True)
        x_far = trade(x_last, "gx", 1)
        free = functools.partial(free_kernel, opening, speed_step)
        turning = functools.partial(heading_kernel, heading_step)
        if opening:
            (most,) = call(meeting_kernel, [most, other], [shape()])
            other = spread(most, 2)
            ins = [values, wind, waves]
            spun, part, extra, flow = call(
                free, ins, [field] * 3 + [jax.ShapeDtypeStruct(turned, jnp.float32)], wide_room, work=300
            )
            reach = 4
            while reach < size:
                most = jnp.maximum(most, other)
                most, part = lax.optimization_barrier((most, part))
                other = spread(most, reach)
                reach *= 2
            part, x_far = lax.optimization_barrier((part, x_far))
        else:
            if section == 3:
                values, x_near = lax.optimization_barrier((values, x_near))
            spun, part = call(free, [values, flow, pk], [field] * 2, room)
            if section == 2:
                part, x_near = lax.optimization_barrier((part, x_near))
        (part,) = call(turning, [values, spun, part, t_near, t_far], [field], work=1000)
        if opening:
            ins = [values, part, x_near, x_far, wind, waves]
            first = functools.partial(first_kernel, speed_step)
            part, gap = call(first, ins, [field] * 2, [rows])
            closing = functools.partial(closing_kernel, bounds, heading_step, speed_step)
            ins = [values, part, gap, extra, target_mask, target_depth, most, other]
            outs = [field, shape(longest), *far_shapes, shape()]
            values, x_out, x_last, t_out, t_last, pk = call(closing, ins, outs, [rows])
        else:
            more = section == 2
            ins = [level_set, values, part, x_near, wind, waves, target_mask, target_depth, pk]
            outs = [field] + ([shape(longest)] if more else [])
            last = functools.partial(section_kernel, section, (0, planes - rim), speed_step)
            early, *x_next = call(last, ins, outs, [rows, rows])
            ins = ins[:3] + [x_far] + ins[4:] + [early]
            outs = [field] + (far_shapes if more else [])
            last = functools.partial(section_kernel, section, (planes - rim, planes), speed_step)
            values, *far_next = call(last, ins, outs, [rows, rows])
            if more:
                (x_out,), (x_last, t_out, t_last) = x_next, far_next
    return values


def solution(mesh):
    return jax.shard_map(
        local,
        mesh=mesh,
        in_specs=(P("gx", "head", None, None), P(None, "gx", None), P("gx", None), P("gx", None)),
        out_specs=P("gx", "head", None, None),
        check_vma=False,
    )
```

```python
import functools
import math

import jax
import jax.numpy as jnp
import numpy as np
from jax import lax
from jax.experimental import pallas as pl
from jax.experimental.pallas import tpu as pltpu
from jax.sharding import PartitionSpec as P

epsilon = 1e-06
courant = 0.5
spacing = 0.05
turn_limit = 1.0
thrust_limit = 0.5
speed_low = 0.5
speed_high = 1.5
rim = 3
gain = 1.0 / (12.0 * spacing)


def inverse(value):
    return pltpu.reciprocal(value, approx=True)


def weights_of(e1, e2, turn, eps):
    level = turn * turn * (4.0 / 3.0) + eps
    ia = inverse(level + e2 * (e2 + turn))
    ib = inverse(level + e2 * e1)
    ic = inverse(level + e1 * (e1 - turn))
    return ia * ia, ib * ib * 6.0, ic * ic


def sides(fl, f0, fr, a2, a1, b1, b0, c0, c1):
    a3 = a1 * 3.0
    c3 = c0 * 3.0
    minus = ((fl + fl) * a2 + f0 * c3) * inverse(a2 + b1 + c3)
    plus = ((fr + fr) * c1 + f0 * a3) * inverse(c1 + b0 + a3)
    return minus, plus


def row_terms(cells, step, closed=False):
    eps = epsilon * step * step
    count = len(cells) if closed else len(cells) - 2 * rim
    shift = 0 if closed else rim
    slope = {m: cells[m + 1 + shift] - cells[m + shift] for m in range(-shift, count + shift - 1)}
    a, b, c = {}, {}, {}
    if closed:
        bend = {m: slope[m] - slope[m - 1] for m in range(1, count - 1)}
        bend[0], bend[count - 1] = slope[0], -slope[count - 2]
        turn = {m: bend[m + 1] - bend[m] for m in range(count - 1)}
        turn[-1], turn[count - 1] = bend[0], -bend[count - 1]
        jerk = {m: turn[m] - turn[m - 1] for m in range(count)}
        jerk[-1], jerk[count] = bend[0], bend[count - 1]
        rise = {m: slope[m] + slope[m - 1] for m in range(1, count - 1)}
        rise[0], rise[count - 1] = slope[0], slope[count - 2]
        a[-2] = c[count] = 1.0 / (eps * eps)
        for m, (e1, e2) in ((-1, (None, bend[0])), (count - 1, (bend[count - 1], None))):
            square = turn[m] * turn[m]
            level = square * (4.0 / 3.0) + eps
            ib, outer = inverse(level), inverse(level + (square + square))
            b[m] = ib * ib * 6.0
            (c if e2 is None else a)[m] = outer * outer
        inner = range(count - 1)
    else:
        bend = {m: slope[m] - slope[m - 1] for m in range(-2, count + 2)}
        turn = {m: bend[m + 1] - bend[m] for m in range(-2, count + 1)}
        jerk = {m: turn[m] - turn[m - 1] for m in range(-1, count + 1)}
        rise = {m: cells[m + 1 + rim] - cells[m - 1 + rim] for m in range(count)}
        inner = range(-2, count + 1)
    for m in inner:
        a[m], b[m], c[m] = weights_of(bend[m], bend[m + 1], turn[m], eps)
    out = []
    for i in range(count):
        base = rise[i] * 6.0 - (turn[i - 1] + turn[i])
        minus, plus = sides(
            jerk[i - 1], jerk[i], jerk[i + 1], a[i - 2], a[i - 1], b[i - 1], b[i], c[i], c[i + 1]
        )
        out.append((base + (plus - minus), (plus + minus) - jerk[i]))
    return out


def batches(total, most):
    return max(k for k in range(1, most + 1) if total % k == 0)


def splat(row, tile):
    return jnp.broadcast_to(row, tile)


def speeds_of(tile, speed_step):
    place = lax.broadcasted_iota(jnp.int32, tile, 0).astype(jnp.float32)
    return speed_low + place * speed_step


def odd_place(axis):
    return lax.rem(lax.axis_index(axis), 2) == 1


def put_extremes(wind_ref, most_ref):
    rows = [wind_ref[i] for i in range(wind_ref.shape[0])]
    most_ref[...] = jnp.zeros_like(most_ref)
    most_ref[0:2, :] = functools.reduce(jnp.maximum, rows)
    most_ref[2:4, :] = -functools.reduce(jnp.minimum, rows)


def extremes_kernel(wind_ref, most_ref):
    put_extremes(wind_ref, most_ref.at[0])


def opening_kernel(level_ref, x_near, x_far, t_near, t_far):
    cut_near(level_ref, x_near)
    cut_far(level_ref, x_far)
    cut_headings(level_ref, t_near, t_far)


def meeting_kernel(own_ref, other_ref, most_ref):
    most_ref[...] = jnp.maximum(own_ref[0], other_ref[0])


def flows_into(flow_ref, speed_step, wind_ref, waves_ref):
    planes, headings = flow_ref.shape[:2]
    tile = flow_ref.shape[2:]
    first = lax.axis_index("head") * headings
    pace = speeds_of(tile, speed_step) * gain
    tables = [
        splat(waves_ref[1, pl.ds(first + j, 1), :], tile) * pace for j in range(headings)
    ]
    for i in range(planes):
        wind = splat(wind_ref[i, 1:2, :] * gain, tile)
        for j in range(headings):
            flow_ref[i, j] = tables[j] + wind


def free_kernel(split, speed_step, s_ref, *rest):
    planes, headings, speeds, width = s_ref.shape
    cells = planes * headings

    def rows_of(ref):
        return ref.reshape(cells * speeds, width)

    if split:
        wind_ref, waves_ref, speed_ref, out_ref, extra_ref, flow_t_ref = rest[:6]
        turned_ref, drift_ref, gap_ref, flow_ref = rest[6:]
        flows_into(flow_ref, speed_step, wind_ref, waves_ref)
        extra_rows, flow_rows = rows_of(extra_ref), rows_of(flow_ref)
    else:
        flow_t_ref, pk_ref, speed_ref, out_ref, turned_ref, drift_ref = rest
        peak = splat(pk_ref[1:2, :] * gain, (speeds, width))
    gain_v = thrust_limit / (12.0 * speed_step)
    s_rows, speed_rows, out_rows = rows_of(s_ref), rows_of(speed_ref), rows_of(out_ref)
    few, many = 8, turned_ref.shape[2] // speeds
    groups = turned_ref.shape[0]
    lanes = many * speeds
    high = 8
    lines = width // high

    def along_speed(n):
        start = min(n * few, cells - few) * speeds
        spots = [pl.ds(start + v, few, stride=speeds) for v in range(speeds)]
        rows = [s_rows[spot, :] for spot in spots]
        for spot, (mean, gap) in zip(spots, row_terms(rows, speed_step, True)):
            speed_rows[spot, :] = gain_v * (gap - jnp.abs(mean))

    def span(n):
        return pl.ds(min(n * many, cells - many) * speeds, lanes)

    def turn_in(n):
        turned = s_rows[span(n), :].T
        turned_ref[n, rim : rim + width, :] = turned
        for k in range(rim):
            turned_ref[n, k : k + 1, :] = turned[:1]
            turned_ref[n, rim + width + k : rim + width + k + 1, :] = turned[-1:]
        if split:
            flow_t_ref[n] = flow_rows[span(n), :].T

    def along_y(n):
        ends = [turned_ref[n, pl.ds(k, high, stride=lines), :] for k in range(lines + 2 * rim)]
        for k, (mean, gap) in enumerate(row_terms(ends, spacing)):
            spot = pl.ds(k, high, stride=lines)
            drift = mean * flow_t_ref[n, spot, :]
            if split:
                drift_ref[n, spot, :] = drift
                gap_ref[n, spot, :] = gap
            else:
                drift_ref[n, spot, :] = drift + gap * peak

    def turn_out(n):
        out_rows[span(n), :] = drift_ref[n].T
        if split:
            extra_rows[span(n), :] = gap_ref[n].T

    turn_in(0)
    for n in range(groups):
        if n > 0:
            turn_out(n - 1)
        along_y(n)
        if n + 1 < groups:
            turn_in(n + 1)
        for k in (2 * n, 2 * n + 1):
            if k * few < cells:
                along_speed(k)
    turn_out(groups - 1)


def heading_kernel(heading_step, s_ref, speed_ref, part_ref, near_ref, far_ref, out_ref):
    planes, headings = s_ref.shape[:2]
    gain_t = turn_limit / (12.0 * heading_step)
    odd = odd_place("head")
    wide = batches(planes, 9)

    def step(n, carry):
        for w in range(wide):
            i = n * wide + w
            ghosts = [(near_ref[i * rim + k], far_ref[i * rim + k]) for k in range(rim)]
            lows = [jnp.where(odd, near, far) for near, far in ghosts]
            highs = [jnp.where(odd, far, near) for near, far in ghosts]
            cells = lows + [s_ref[i, j] for j in range(headings)] + highs
            for j, (mean, gap) in enumerate(row_terms(cells, heading_step)):
                own = speed_ref[i, j] + part_ref[i, j]
                out_ref[i, j] = own + gain_t * (gap - jnp.abs(mean))
        return carry

    lax.fori_loop(0, planes // wide, step, 0)


def peaks_into(pk_ref, most, bounds, heading_step, speed_step):
    most = jnp.max(most, axis=1, keepdims=True)
    peaks = [
        jnp.maximum(most[q : q + 1] + bounds[q][1], most[q + 2 : q + 3] - bounds[q][0])
        for q in range(2)
    ]
    time_step = courant / (
        peaks[0] / spacing
        + peaks[1] / spacing
        + turn_limit / heading_step
        + thrust_limit / speed_step
    )
    width = pk_ref.shape[1]
    for row, value in enumerate(peaks + [time_step]):
        pk_ref[row : row + 1, :] = splat(value, (1, width))


def plane_at(i, planes):
    return jnp.where(odd_place("gx"), i, planes - 1 - i)


def alone(reach):
    place, size = lax.axis_index("gx"), lax.axis_size("gx")
    if reach == 0:
        return (place == size - 1) if size % 2 else place < 0
    return (place == 0) | (place == size - 1) if size % 2 == 0 else place == 0


def cut_near(field_ref, x_near):
    planes, headings = field_ref.shape[:2]
    for k in range(rim):
        i = jnp.where(alone(0), 0, k)
        x_near[k * headings : (k + 1) * headings] = field_ref[plane_at(i, planes)]


def cut_far(field_ref, x_far):
    planes, headings = field_ref.shape[:2]
    for k in range(rim):
        i = planes - 1 - jnp.where(alone(1), 0, k)
        x_far[k * headings : (k + 1) * headings] = field_ref[plane_at(i, planes)]


def cut_headings(field_ref, t_near, t_far):
    planes, headings = field_ref.shape[:2]
    t_low = jnp.where(odd_place("head"), 0, headings - rim)
    for k in range(rim):
        for i in range(planes):
            t_near[i * rim + k] = field_ref[i, t_low + k]
            t_far[i * rim + k] = field_ref[i, headings - rim - t_low + k]


def splat_targets(mask_ref, depth_ref, target_ref):
    for i in range(target_ref.shape[0]):
        depth = depth_ref[i : i + 1, :]
        target = jnp.where(mask_ref[i : i + 1, :] == 1, -depth, depth)
        target_ref[i] = splat(target, target_ref.shape[1:])


def across_planes(
    span, speed_step, s_ref, near_ref, far_ref, wind_ref, waves_ref, flow_ref, use
):
    planes, headings = s_ref.shape[:2]
    tile = s_ref.shape[2:]
    side = jnp.where(odd_place("gx"), gain, -gain).astype(jnp.float32)
    spots = [plane_at(i, planes) for i in range(planes)]
    for i in range(planes):
        flow_ref[i] = splat(wind_ref[i, 0:1, :] * side, tile)
    pace = speeds_of(tile, speed_step) * side
    first = lax.axis_index("head") * headings
    low, high = span
    wide = batches(headings, max(1, 72 // (high - low)))

    def line(i, j):
        if i < 0:
            return near_ref[(-1 - i) * headings + j]
        if i >= planes:
            return far_ref[(i - planes) * headings + j]
        return s_ref[spots[i], j]

    def step(n, carry):
        for w in range(wide):
            j = n * wide + w
            cells = [line(i, j) for i in range(low - rim, high + rim)]
            table = splat(waves_ref[0, pl.ds(first + j, 1), :], tile) * pace
            for k, (mean, gap) in enumerate(row_terms(cells, spacing)):
                spot = spots[low + k]
                use(spot, j, mean * (table + flow_ref[spot]), gap, cells[k + rim])
        return carry

    lax.fori_loop(0, headings // wide, step, 0)


def first_kernel(
    speed_step, s_ref, part_ref, near_ref, far_ref, wind_ref, waves_ref, out_ref, gap_ref, flow_ref
):
    def use(i, j, drift, gap, cell):
        out_ref[i, j] = part_ref[i, j] + drift
        gap_ref[i, j] = gap

    across_planes(
        (0, s_ref.shape[0]), speed_step, s_ref, near_ref, far_ref, wind_ref, waves_ref, flow_ref, use
    )


def closing_kernel(
    bounds, heading_step, speed_step, s_ref, part_ref, gap_x_ref, gap_y_ref, mask_ref, depth_ref,
    most_ref, other_ref, out_ref, x_near, x_far, t_near, t_far, pk_ref, target_ref
):
    planes, headings = s_ref.shape[:2]
    tile = s_ref.shape[2:]
    most = jnp.maximum(most_ref[...], other_ref[...])
    peaks_into(pk_ref, most, bounds, heading_step, speed_step)
    splat_targets(mask_ref, depth_ref, target_ref)
    peak_x = splat(pk_ref[0:1, :] * gain, tile)
    peak_y = splat(pk_ref[1:2, :] * gain, tile)
    time_step = splat(pk_ref[2:3, :], tile)

    def plane(i, carry):
        for j in range(headings):
            rate = part_ref[i, j] + (gap_x_ref[i, j] * peak_x + gap_y_ref[i, j] * peak_y)
            out_ref[i, j] = jnp.minimum(s_ref[i, j] + time_step * rate, target_ref[i])
        return carry

    lax.fori_loop(0, planes, plane, 0)
    cut_near(out_ref, x_near)
    cut_far(out_ref, x_far)
    cut_headings(out_ref, t_near, t_far)


def section_kernel(
    section, span, speed_step, base_ref, s_ref, part_ref, ghosts_ref, wind_ref, waves_ref,
    mask_ref, depth_ref, pk_ref, *refs
):
    planes = s_ref.shape[0]
    refs, (flow_ref, target_ref) = list(refs[:-2]), refs[-2:]
    early_ref = refs.pop(0) if span[0] > 0 else None
    out_ref = refs.pop(0)
    tile = s_ref.shape[2:]
    splat_targets(mask_ref, depth_ref, target_ref)
    peak_x = splat(pk_ref[0:1, :] * gain, tile)
    time_step = splat(pk_ref[2:3, :], tile)
    base_share = 0.75 if section == 2 else 1.0 / 3.0
    own_share = 0.25 if section == 2 else 2.0 / 3.0

    def use(i, j, drift, gap, cell):
        rate = part_ref[i, j] + (drift + gap * peak_x)
        moved = base_share * base_ref[i, j] + own_share * (cell + time_step * rate)
        out_ref[i, j] = jnp.minimum(moved, target_ref[i])

    near_ref, far_ref = (None, ghosts_ref) if span[0] > 0 else (ghosts_ref, None)
    across_planes(
        span, speed_step, s_ref, near_ref, far_ref, wind_ref, waves_ref, flow_ref, use
    )
    for i in range(span[0]):
        spot = plane_at(i, planes)
        out_ref[spot] = early_ref[spot]
    if section == 2 and span[0] == 0:
        cut_near(out_ref, *refs)
    elif section == 2:
        cut_far(out_ref, refs[0])
        cut_headings(out_ref, *refs[1:])


def trade(value, axis, reach, wrap=False):
    size = lax.axis_size(axis)
    pairs = [(i, i + 1) for i in range(reach, size - 1, 2)]
    if wrap and reach and size % 2 == 0:
        pairs.append((size - 1, 0))
    pairs += [(j, i) for i, j in pairs]
    pairs += [(i, i) for i in range(size) if i not in dict(pairs)]
    return lax.ppermute(value, axis, pairs)


def local(level_set, wind_field, target_mask, target_depth):
    planes, headings, speed_count, cross_count = level_set.shape
    heading_total = headings * lax.axis_size("head")
    heading_step = 2.0 * math.pi / heading_total
    speed_step = (speed_high - speed_low) / (speed_count - 1)
    speed_row = np.float32(speed_low) + np.arange(speed_count, dtype=np.float32) * np.float32(
        speed_step
    )
    angles = np.arange(heading_total, dtype=np.float32) * np.float32(heading_step)
    waves = [np.cos(angles), np.sin(angles)]
    bounds = []
    for wave in waves:
        product = wave[:, None] * speed_row[None, :]
        bounds.append((float(product.min()), float(product.max())))
    waves = jnp.asarray(np.stack(waves)[..., None] * np.ones(cross_count, np.float32))

    vmem = pl.BlockSpec(memory_space=pltpu.VMEM)
    tile = (speed_count, cross_count)

    def shape(*dims):
        return jax.ShapeDtypeStruct(dims + tile, jnp.float32)

    field = shape(planes, headings)
    short = rim * headings
    middle = max(short + 1, rim * planes)

    longest = middle + 1
    rows = pltpu.VMEM((planes,) + tile, jnp.float32)
    cells = math.prod(level_set.shape)

    def call(kernel, ins, outs, scratch=(), work=0):
        return pl.pallas_call(
            kernel,
            out_shape=outs,
            in_specs=[vmem] * len(ins),
            out_specs=[vmem] * len(outs),
            scratch_shapes=list(scratch),
            compiler_params=pltpu.CompilerParams(vmem_limit_bytes=16 * 1024 * 1024),
            cost_estimate=pl.CostEstimate(
                flops=work * cells, bytes_accessed=work * cells, transcendentals=0
            ),
        )(*ins)

    wind = jnp.transpose(wind_field, (1, 0, 2))
    many = 16
    groups, lanes = -(-planes * headings // many), many * speed_count
    turned = (groups, cross_count, lanes)
    room = [
        pltpu.VMEM((groups, cross_count + 8, lanes), jnp.float32),
        pltpu.VMEM(turned, jnp.float32),
    ]
    wide_room = room + [pltpu.VMEM(turned, jnp.float32), pltpu.VMEM(level_set.shape, jnp.float32)]
    values = level_set
    size = lax.axis_size("gx")

    def spread(most, reach):
        if size & (size - 1):
            pairs = [(i, (i + reach) % size) for i in range(size)]
        else:
            pairs = [(i, i ^ reach) for i in range(size)]
        return lax.ppermute(most, "gx", pairs)

    (most,) = call(extremes_kernel, [wind], [shape(longest + 2)])
    other = spread(most, 1)
    x_shapes = [shape(longest + 1), shape(longest)]
    x_out, x_last, t_out, t_last = call(opening_kernel, [values], x_shapes + [shape(middle)] * 2)
    far_shapes = [shape(short), shape(rim * planes), shape(middle)]
    for section in (1, 2, 3):
        opening = section == 1
        x_near = trade(x_out, "gx", 0)
        t_near = trade(t_out, "head", 0)
        t_far = trade(t_last, "head", 1, True)
        x_far = trade(x_last, "gx", 1)
        free = functools.partial(free_kernel, opening, speed_step)
        turning = functools.partial(heading_kernel, heading_step)
        if opening:
            (most,) = call(meeting_kernel, [most, other], [shape()])
            other = spread(most, 2)
            ins = [values, wind, waves]
            spun, part, extra, flow = call(
                free, ins, [field] * 3 + [jax.ShapeDtypeStruct(turned, jnp.float32)], wide_room, work=300
            )
            reach = 4
            while reach < size:
                most = jnp.maximum(most, other)
                most, part = lax.optimization_barrier((most, part))
                other = spread(most, reach)
                reach *= 2
        else:
            if section == 3:
                values, x_near = lax.optimization_barrier((values, x_near))
            spun, part = call(free, [values, flow, pk], [field] * 2, room)
            if section == 2:
                part, x_near = lax.optimization_barrier((part, x_near))
        weight = 0 if opening else 1000
        (part,) = call(turning, [values, spun, part, t_near, t_far], [field], work=weight)
        if opening:
            ins = [values, part, x_near, x_far, wind, waves]
            first = functools.partial(first_kernel, speed_step)
            part, gap = call(first, ins, [field] * 2, [rows])
            closing = functools.partial(closing_kernel, bounds, heading_step, speed_step)
            ins = [values, part, gap, extra, target_mask, target_depth, most, other]
            outs = [field, shape(longest), *far_shapes, shape()]
            values, x_out, x_last, t_out, t_last, pk = call(closing, ins, outs, [rows])
        else:
            more = section == 2
            ins = [level_set, values, part, x_near, wind, waves, target_mask, target_depth, pk]
            outs = [field] + ([shape(longest)] if more else [])
            last = functools.partial(section_kernel, section, (0, planes - rim), speed_step)
            early, *x_next = call(last, ins, outs, [rows, rows])
            ins = ins[:3] + [x_far] + ins[4:] + [early]
            outs = [field] + (far_shapes if more else [])
            last = functools.partial(section_kernel, section, (planes - rim, planes), speed_step)
            values, *far_next = call(last, ins, outs, [rows, rows])
            if more:
                (x_out,), (x_last, t_out, t_last) = x_next, far_next
    return values


def solution(mesh):
    return jax.shard_map(
        local,
        mesh=mesh,
        in_specs=(P("gx", "head", None, None), P(None, "gx", None), P("gx", None), P("gx", None)),
        out_specs=P("gx", "head", None, None),
        check_vma=False,
    )
```

```python
import functools
import math

import jax
import jax.numpy as jnp
import numpy as np
from jax import lax
from jax.experimental import pallas as pl
from jax.experimental.pallas import tpu as pltpu
from jax.sharding import PartitionSpec as P

epsilon = 1e-06
courant = 0.5
spacing = 0.05
turn_limit = 1.0
thrust_limit = 0.5
speed_low = 0.5
speed_high = 1.5
rim = 3
gain = 1.0 / (12.0 * spacing)


def inverse(value):
    return pltpu.reciprocal(value, approx=True)


def weights_of(e1, e2, turn, eps):
    level = turn * turn * (4.0 / 3.0) + eps
    ia = inverse(level + e2 * (e2 + turn))
    ib = inverse(level + e2 * e1)
    ic = inverse(level + e1 * (e1 - turn))
    return ia * ia, ib * ib * 6.0, ic * ic


def sides(fl, f0, fr, a2, a1, b1, b0, c0, c1):
    a3 = a1 * 3.0
    c3 = c0 * 3.0
    minus = ((fl + fl) * a2 + f0 * c3) * inverse(a2 + b1 + c3)
    plus = ((fr + fr) * c1 + f0 * a3) * inverse(c1 + b0 + a3)
    return minus, plus


def row_terms(cells, step, closed=False):
    eps = epsilon * step * step
    count = len(cells) if closed else len(cells) - 2 * rim
    shift = 0 if closed else rim
    slope = {m: cells[m + 1 + shift] - cells[m + shift] for m in range(-shift, count + shift - 1)}
    a, b, c = {}, {}, {}
    if closed:
        bend = {m: slope[m] - slope[m - 1] for m in range(1, count - 1)}
        bend[0], bend[count - 1] = slope[0], -slope[count - 2]
        turn = {m: bend[m + 1] - bend[m] for m in range(count - 1)}
        turn[-1], turn[count - 1] = bend[0], -bend[count - 1]
        jerk = {m: turn[m] - turn[m - 1] for m in range(count)}
        jerk[-1], jerk[count] = bend[0], bend[count - 1]
        rise = {m: slope[m] + slope[m - 1] for m in range(1, count - 1)}
        rise[0], rise[count - 1] = slope[0], slope[count - 2]
        a[-2] = c[count] = 1.0 / (eps * eps)
        for m, (e1, e2) in ((-1, (None, bend[0])), (count - 1, (bend[count - 1], None))):
            square = turn[m] * turn[m]
            level = square * (4.0 / 3.0) + eps
            ib, outer = inverse(level), inverse(level + (square + square))
            b[m] = ib * ib * 6.0
            (c if e2 is None else a)[m] = outer * outer
        inner = range(count - 1)
    else:
        bend = {m: slope[m] - slope[m - 1] for m in range(-2, count + 2)}
        turn = {m: bend[m + 1] - bend[m] for m in range(-2, count + 1)}
        jerk = {m: turn[m] - turn[m - 1] for m in range(-1, count + 1)}
        rise = {m: cells[m + 1 + rim] - cells[m - 1 + rim] for m in range(count)}
        inner = range(-2, count + 1)
    for m in inner:
        a[m], b[m], c[m] = weights_of(bend[m], bend[m + 1], turn[m], eps)
    out = []
    for i in range(count):
        base = rise[i] * 6.0 - (turn[i - 1] + turn[i])
        minus, plus = sides(
            jerk[i - 1], jerk[i], jerk[i + 1], a[i - 2], a[i - 1], b[i - 1], b[i], c[i], c[i + 1]
        )
        out.append((base + (plus - minus), (plus + minus) - jerk[i]))
    return out


def batches(total, most):
    return max(k for k in range(1, most + 1) if total % k == 0)


def splat(row, tile):
    return jnp.broadcast_to(row, tile)


def speeds_of(tile, speed_step):
    place = lax.broadcasted_iota(jnp.int32, tile, 0).astype(jnp.float32)
    return speed_low + place * speed_step


def odd_place(axis):
    return lax.rem(lax.axis_index(axis), 2) == 1


def put_extremes(wind_ref, most_ref):
    rows = [wind_ref[i] for i in range(wind_ref.shape[0])]
    most_ref[...] = jnp.zeros_like(most_ref)
    most_ref[0:2, :] = functools.reduce(jnp.maximum, rows)
    most_ref[2:4, :] = -functools.reduce(jnp.minimum, rows)


def extremes_kernel(wind_ref, most_ref):
    put_extremes(wind_ref, most_ref.at[0])
    for g in range(1, most_ref.shape[0]):
        most_ref[g] = most_ref[0]


def opening_kernel(level_ref, x_near, x_far, t_near, t_far):
    cut_near(level_ref, x_near)
    cut_far(level_ref, x_far)
    cut_headings(level_ref, t_near, t_far)


def flows_into(flow_ref, speed_step, wind_ref, waves_ref):
    planes, headings = flow_ref.shape[:2]
    tile = flow_ref.shape[2:]
    first = lax.axis_index("head") * headings
    pace = speeds_of(tile, speed_step) * gain
    tables = [
        splat(waves_ref[1, pl.ds(first + j, 1), :], tile) * pace for j in range(headings)
    ]
    for i in range(planes):
        wind = splat(wind_ref[i, 1:2, :] * gain, tile)
        for j in range(headings):
            flow_ref[i, j] = tables[j] + wind


def free_kernel(split, speed_step, s_ref, *rest):
    planes, headings, speeds, width = s_ref.shape
    cells = planes * headings

    def rows_of(ref):
        return ref.reshape(cells * speeds, width)

    if split:
        wind_ref, waves_ref, speed_ref, out_ref, extra_ref, flow_t_ref = rest[:6]
        turned_ref, drift_ref, gap_ref, flow_ref = rest[6:]
        flows_into(flow_ref, speed_step, wind_ref, waves_ref)
        extra_rows, flow_rows = rows_of(extra_ref), rows_of(flow_ref)
    else:
        flow_t_ref, pk_ref, speed_ref, out_ref, turned_ref, drift_ref = rest
        peak = splat(pk_ref[1:2, :] * gain, (speeds, width))
    gain_v = thrust_limit / (12.0 * speed_step)
    s_rows, speed_rows, out_rows = rows_of(s_ref), rows_of(speed_ref), rows_of(out_ref)
    few, many = 8, turned_ref.shape[2] // speeds
    groups = turned_ref.shape[0]
    lanes = many * speeds
    high = 8
    lines = width // high

    def along_speed(n):
        start = min(n * few, cells - few) * speeds
        spots = [pl.ds(start + v, few, stride=speeds) for v in range(speeds)]
        rows = [s_rows[spot, :] for spot in spots]
        for spot, (mean, gap) in zip(spots, row_terms(rows, speed_step, True)):
            speed_rows[spot, :] = gain_v * (gap - jnp.abs(mean))

    def span(n):
        return pl.ds(min(n * many, cells - many) * speeds, lanes)

    def turn_in(n):
        turned = s_rows[span(n), :].T
        turned_ref[n, rim : rim + width, :] = turned
        for k in range(rim):
            turned_ref[n, k : k + 1, :] = turned[:1]
            turned_ref[n, rim + width + k : rim + width + k + 1, :] = turned[-1:]
        if split:
            flow_t_ref[n] = flow_rows[span(n), :].T

    def along_y(n):
        ends = [turned_ref[n, pl.ds(k, high, stride=lines), :] for k in range(lines + 2 * rim)]
        for k, (mean, gap) in enumerate(row_terms(ends, spacing)):
            spot = pl.ds(k, high, stride=lines)
            drift = mean * flow_t_ref[n, spot, :]
            if split:
                drift_ref[n, spot, :] = drift
                gap_ref[n, spot, :] = gap
            else:
                drift_ref[n, spot, :] = drift + gap * peak

    def turn_out(n):
        out_rows[span(n), :] = drift_ref[n].T
        if split:
            extra_rows[span(n), :] = gap_ref[n].T

    turn_in(0)
    for n in range(groups):
        if n > 0:
            turn_out(n - 1)
        along_y(n)
        if n + 1 < groups:
            turn_in(n + 1)
        for k in (2 * n, 2 * n + 1):
            if k * few < cells:
                along_speed(k)
    turn_out(groups - 1)


def heading_kernel(heading_step, s_ref, speed_ref, part_ref, near_ref, far_ref, out_ref):
    planes, headings = s_ref.shape[:2]
    gain_t = turn_limit / (12.0 * heading_step)
    odd = odd_place("head")
    wide = batches(planes, 9)

    def step(n, carry):
        for w in range(wide):
            i = n * wide + w
            ghosts = [(near_ref[i * rim + k], far_ref[i * rim + k]) for k in range(rim)]
            lows = [jnp.where(odd, near, far) for near, far in ghosts]
            highs = [jnp.where(odd, far, near) for near, far in ghosts]
            cells = lows + [s_ref[i, j] for j in range(headings)] + highs
            for j, (mean, gap) in enumerate(row_terms(cells, heading_step)):
                own = speed_ref[i, j] + part_ref[i, j]
                out_ref[i, j] = own + gain_t * (gap - jnp.abs(mean))
        return carry

    lax.fori_loop(0, planes // wide, step, 0)


def peaks_into(pk_ref, most, bounds, heading_step, speed_step):
    most = jnp.max(most, axis=1, keepdims=True)
    peaks = [
        jnp.maximum(most[q : q + 1] + bounds[q][1], most[q + 2 : q + 3] - bounds[q][0])
        for q in range(2)
    ]
    time_step = courant / (
        peaks[0] / spacing
        + peaks[1] / spacing
        + turn_limit / heading_step
        + thrust_limit / speed_step
    )
    width = pk_ref.shape[1]
    for row, value in enumerate(peaks + [time_step]):
        pk_ref[row : row + 1, :] = splat(value, (1, width))


def plane_at(i, planes):
    return jnp.where(odd_place("gx"), i, planes - 1 - i)


def alone(reach):
    place, size = lax.axis_index("gx"), lax.axis_size("gx")
    if reach == 0:
        return (place == size - 1) if size % 2 else place < 0
    return (place == 0) | (place == size - 1) if size % 2 == 0 else place == 0


def cut_near(field_ref, x_near):
    planes, headings = field_ref.shape[:2]
    for k in range(rim):
        i = jnp.where(alone(0), 0, k)
        x_near[k * headings : (k + 1) * headings] = field_ref[plane_at(i, planes)]


def cut_far(field_ref, x_far):
    planes, headings = field_ref.shape[:2]
    for k in range(rim):
        i = planes - 1 - jnp.where(alone(1), 0, k)
        x_far[k * headings : (k + 1) * headings] = field_ref[plane_at(i, planes)]


def cut_headings(field_ref, t_near, t_far):
    planes, headings = field_ref.shape[:2]
    t_low = jnp.where(odd_place("head"), 0, headings - rim)
    for k in range(rim):
        for i in range(planes):
            t_near[i * rim + k] = field_ref[i, t_low + k]
            t_far[i * rim + k] = field_ref[i, headings - rim - t_low + k]


def splat_targets(mask_ref, depth_ref, target_ref):
    for i in range(target_ref.shape[0]):
        depth = depth_ref[i : i + 1, :]
        target = jnp.where(mask_ref[i : i + 1, :] == 1, -depth, depth)
        target_ref[i] = splat(target, target_ref.shape[1:])


def across_planes(
    span, speed_step, s_ref, near_ref, far_ref, wind_ref, waves_ref, flow_ref, use
):
    planes, headings = s_ref.shape[:2]
    tile = s_ref.shape[2:]
    side = jnp.where(odd_place("gx"), gain, -gain).astype(jnp.float32)
    spots = [plane_at(i, planes) for i in range(planes)]
    for i in range(planes):
        flow_ref[i] = splat(wind_ref[i, 0:1, :] * side, tile)
    pace = speeds_of(tile, speed_step) * side
    first = lax.axis_index("head") * headings
    low, high = span
    wide = batches(headings, max(1, 72 // (high - low)))

    def line(i, j):
        if i < 0:
            return near_ref[(-1 - i) * headings + j]
        if i >= planes:
            return far_ref[(i - planes) * headings + j]
        return s_ref[spots[i], j]

    def step(n, carry):
        for w in range(wide):
            j = n * wide + w
            cells = [line(i, j) for i in range(low - rim, high + rim)]
            table = splat(waves_ref[0, pl.ds(first + j, 1), :], tile) * pace
            for k, (mean, gap) in enumerate(row_terms(cells, spacing)):
                spot = spots[low + k]
                use(spot, j, mean * (table + flow_ref[spot]), gap, cells[k + rim])
        return carry

    lax.fori_loop(0, headings // wide, step, 0)


def first_kernel(
    speed_step, s_ref, part_ref, near_ref, far_ref, wind_ref, waves_ref, out_ref, gap_ref, flow_ref
):
    def use(i, j, drift, gap, cell):
        out_ref[i, j] = part_ref[i, j] + drift
        gap_ref[i, j] = gap

    across_planes(
        (0, s_ref.shape[0]), speed_step, s_ref, near_ref, far_ref, wind_ref, waves_ref, flow_ref, use
    )


def closing_kernel(
    bounds, heading_step, speed_step, s_ref, part_ref, gap_x_ref, gap_y_ref, mask_ref, depth_ref,
    most_ref, out_ref, x_near, x_far, t_near, t_far, pk_ref, target_ref
):
    planes, headings = s_ref.shape[:2]
    tile = s_ref.shape[2:]
    most = functools.reduce(jnp.maximum, [most_ref[g] for g in range(most_ref.shape[0])])
    peaks_into(pk_ref, most, bounds, heading_step, speed_step)
    splat_targets(mask_ref, depth_ref, target_ref)
    peak_x = splat(pk_ref[0:1, :] * gain, tile)
    peak_y = splat(pk_ref[1:2, :] * gain, tile)
    time_step = splat(pk_ref[2:3, :], tile)

    def plane(i, carry):
        for j in range(headings):
            rate = part_ref[i, j] + (gap_x_ref[i, j] * peak_x + gap_y_ref[i, j] * peak_y)
            out_ref[i, j] = jnp.minimum(s_ref[i, j] + time_step * rate, target_ref[i])
        return carry

    lax.fori_loop(0, planes, plane, 0)
    cut_near(out_ref, x_near)
    cut_far(out_ref, x_far)
    cut_headings(out_ref, t_near, t_far)


def section_kernel(
    section, span, speed_step, base_ref, s_ref, part_ref, ghosts_ref, wind_ref, waves_ref,
    mask_ref, depth_ref, pk_ref, *refs
):
    planes = s_ref.shape[0]
    refs, (flow_ref, target_ref) = list(refs[:-2]), refs[-2:]
    early_ref = refs.pop(0) if span[0] > 0 else None
    out_ref = refs.pop(0)
    tile = s_ref.shape[2:]
    splat_targets(mask_ref, depth_ref, target_ref)
    peak_x = splat(pk_ref[0:1, :] * gain, tile)
    time_step = splat(pk_ref[2:3, :], tile)
    base_share = 0.75 if section == 2 else 1.0 / 3.0
    own_share = 0.25 if section == 2 else 2.0 / 3.0

    def use(i, j, drift, gap, cell):
        rate = part_ref[i, j] + (drift + gap * peak_x)
        moved = base_share * base_ref[i, j] + own_share * (cell + time_step * rate)
        out_ref[i, j] = jnp.minimum(moved, target_ref[i])

    near_ref, far_ref = (None, ghosts_ref) if span[0] > 0 else (ghosts_ref, None)
    across_planes(
        span, speed_step, s_ref, near_ref, far_ref, wind_ref, waves_ref, flow_ref, use
    )
    for i in range(span[0]):
        spot = plane_at(i, planes)
        out_ref[spot] = early_ref[spot]
    if section == 2 and span[0] == 0:
        cut_near(out_ref, *refs)
    elif section == 2:
        cut_far(out_ref, refs[0])
        cut_headings(out_ref, *refs[1:])


def trade(value, axis, reach, wrap=False):
    size = lax.axis_size(axis)
    pairs = [(i, i + 1) for i in range(reach, size - 1, 2)]
    if wrap and reach and size % 2 == 0:
        pairs.append((size - 1, 0))
    pairs += [(j, i) for i, j in pairs]
    pairs += [(i, i) for i in range(size) if i not in dict(pairs)]
    return lax.ppermute(value, axis, pairs)


def local(level_set, wind_field, target_mask, target_depth):
    planes, headings, speed_count, cross_count = level_set.shape
    heading_total = headings * lax.axis_size("head")
    heading_step = 2.0 * math.pi / heading_total
    speed_step = (speed_high - speed_low) / (speed_count - 1)
    speed_row = np.float32(speed_low) + np.arange(speed_count, dtype=np.float32) * np.float32(
        speed_step
    )
    angles = np.arange(heading_total, dtype=np.float32) * np.float32(heading_step)
    waves = [np.cos(angles), np.sin(angles)]
    bounds = []
    for wave in waves:
        product = wave[:, None] * speed_row[None, :]
        bounds.append((float(product.min()), float(product.max())))
    waves = jnp.asarray(np.stack(waves)[..., None] * np.ones(cross_count, np.float32))

    vmem = pl.BlockSpec(memory_space=pltpu.VMEM)
    tile = (speed_count, cross_count)

    def shape(*dims):
        return jax.ShapeDtypeStruct(dims + tile, jnp.float32)

    field = shape(planes, headings)
    short = rim * headings
    middle = max(short + 1, rim * planes)

    longest = middle + 1
    rows = pltpu.VMEM((planes,) + tile, jnp.float32)
    cells = math.prod(level_set.shape)

    def call(kernel, ins, outs, scratch=(), work=0):
        return pl.pallas_call(
            kernel,
            out_shape=outs,
            in_specs=[vmem] * len(ins),
            out_specs=[vmem] * len(outs),
            scratch_shapes=list(scratch),
            compiler_params=pltpu.CompilerParams(vmem_limit_bytes=16 * 1024 * 1024),
            cost_estimate=pl.CostEstimate(
                flops=work * cells, bytes_accessed=work * cells, transcendentals=0
            ),
        )(*ins)

    wind = jnp.transpose(wind_field, (1, 0, 2))
    many = 16
    groups, lanes = -(-planes * headings // many), many * speed_count
    turned = (groups, cross_count, lanes)
    room = [
        pltpu.VMEM((groups, cross_count + 8, lanes), jnp.float32),
        pltpu.VMEM(turned, jnp.float32),
    ]
    wide_room = room + [pltpu.VMEM(turned, jnp.float32), pltpu.VMEM(level_set.shape, jnp.float32)]
    values = level_set
    (most,) = call(extremes_kernel, [wind], [shape(lax.axis_size("gx"))])
    most = lax.all_to_all(most, "gx", 0, 0)
    x_shapes = [shape(longest + 1), shape(longest)]
    x_out, x_last, t_out, t_last = call(opening_kernel, [values], x_shapes + [shape(middle)] * 2)
    far_shapes = [shape(short), shape(rim * planes), shape(middle)]
    for section in (1, 2, 3):
        opening = section == 1
        x_near = trade(x_out, "gx", 0)
        t_near = trade(t_out, "head", 0)
        t_far = trade(t_last, "head", 1, True)
        x_far = trade(x_last, "gx", 1)
        free = functools.partial(free_kernel, opening, speed_step)
        turning = functools.partial(heading_kernel, heading_step)
        if opening:
            ins = [values, wind, waves]
            spun, part, extra, flow = call(
                free, ins, [field] * 3 + [jax.ShapeDtypeStruct(turned, jnp.float32)], wide_room, work=300
            )
        else:
            if section == 3:
                values, x_near = lax.optimization_barrier((values, x_near))
            spun, part = call(free, [values, flow, pk], [field] * 2, room)
            if section == 2:
                part, x_near = lax.optimization_barrier((part, x_near))
        weight = 0 if opening else 1000
        (part,) = call(turning, [values, spun, part, t_near, t_far], [field], work=weight)
        if opening:
            ins = [values, part, x_near, x_far, wind, waves]
            first = functools.partial(first_kernel, speed_step)
            part, gap = call(first, ins, [field] * 2, [rows])
            closing = functools.partial(closing_kernel, bounds, heading_step, speed_step)
            ins = [values, part, gap, extra, target_mask, target_depth, most]
            outs = [field, shape(longest), *far_shapes, shape()]
            values, x_out, x_last, t_out, t_last, pk = call(closing, ins, outs, [rows])
        else:
            more = section == 2
            ins = [level_set, values, part, x_near, wind, waves, target_mask, target_depth, pk]
            outs = [field] + ([shape(longest)] if more else [])
            last = functools.partial(section_kernel, section, (0, planes - rim), speed_step)
            early, *x_next = call(last, ins, outs, [rows, rows])
            ins = ins[:3] + [x_far] + ins[4:] + [early]
            outs = [field] + (far_shapes if more else [])
            last = functools.partial(section_kernel, section, (planes - rim, planes), speed_step)
            values, *far_next = call(last, ins, outs, [rows, rows])
            if more:
                (x_out,), (x_last, t_out, t_last) = x_next, far_next
    return values


def solution(mesh):
    return jax.shard_map(
        local,
        mesh=mesh,
        in_specs=(P("gx", "head", None, None), P(None, "gx", None), P("gx", None), P("gx", None)),
        out_specs=P("gx", "head", None, None),
        check_vma=False,
    )
```

```python
import functools
import math

import jax
import jax.numpy as jnp
import numpy as np
from jax import lax
from jax.experimental import pallas as pl
from jax.experimental.pallas import tpu as pltpu
from jax.sharding import PartitionSpec as P

epsilon = 1e-06
courant = 0.5
spacing = 0.05
turn_limit = 1.0
thrust_limit = 0.5
speed_low = 0.5
speed_high = 1.5
rim = 3
gain = 1.0 / (12.0 * spacing)


def inverse(value):
    return pltpu.reciprocal(value, approx=True)


def weights_of(e1, e2, turn, eps):
    level = turn * turn * (4.0 / 3.0) + eps
    ia = inverse(level + e2 * (e2 + turn))
    ib = inverse(level + e2 * e1)
    ic = inverse(level + e1 * (e1 - turn))
    return ia * ia, ib * ib * 6.0, ic * ic


def sides(fl, f0, fr, a2, a1, b1, b0, c0, c1):
    a3 = a1 * 3.0
    c3 = c0 * 3.0
    minus = ((fl + fl) * a2 + f0 * c3) * inverse(a2 + b1 + c3)
    plus = ((fr + fr) * c1 + f0 * a3) * inverse(c1 + b0 + a3)
    return minus, plus


def row_terms(cells, step, closed=False):
    eps = epsilon * step * step
    count = len(cells) if closed else len(cells) - 2 * rim
    shift = 0 if closed else rim
    slope = {m: cells[m + 1 + shift] - cells[m + shift] for m in range(-shift, count + shift - 1)}
    a, b, c = {}, {}, {}
    if closed:
        bend = {m: slope[m] - slope[m - 1] for m in range(1, count - 1)}
        bend[0], bend[count - 1] = slope[0], -slope[count - 2]
        turn = {m: bend[m + 1] - bend[m] for m in range(count - 1)}
        turn[-1], turn[count - 1] = bend[0], -bend[count - 1]
        jerk = {m: turn[m] - turn[m - 1] for m in range(count)}
        jerk[-1], jerk[count] = bend[0], bend[count - 1]
        rise = {m: slope[m] + slope[m - 1] for m in range(1, count - 1)}
        rise[0], rise[count - 1] = slope[0], slope[count - 2]
        a[-2] = c[count] = 1.0 / (eps * eps)
        for m, (e1, e2) in ((-1, (None, bend[0])), (count - 1, (bend[count - 1], None))):
            square = turn[m] * turn[m]
            level = square * (4.0 / 3.0) + eps
            ib, outer = inverse(level), inverse(level + (square + square))
            b[m] = ib * ib * 6.0
            (c if e2 is None else a)[m] = outer * outer
        inner = range(count - 1)
    else:
        bend = {m: slope[m] - slope[m - 1] for m in range(-2, count + 2)}
        turn = {m: bend[m + 1] - bend[m] for m in range(-2, count + 1)}
        jerk = {m: turn[m] - turn[m - 1] for m in range(-1, count + 1)}
        rise = {m: cells[m + 1 + rim] - cells[m - 1 + rim] for m in range(count)}
        inner = range(-2, count + 1)
    for m in inner:
        a[m], b[m], c[m] = weights_of(bend[m], bend[m + 1], turn[m], eps)
    out = []
    for i in range(count):
        base = rise[i] * 6.0 - (turn[i - 1] + turn[i])
        minus, plus = sides(
            jerk[i - 1], jerk[i], jerk[i + 1], a[i - 2], a[i - 1], b[i - 1], b[i], c[i], c[i + 1]
        )
        out.append((base + (plus - minus), (plus + minus) - jerk[i]))
    return out


def batches(total, most):
    return max(k for k in range(1, most + 1) if total % k == 0)


def splat(row, tile):
    return jnp.broadcast_to(row, tile)


def speeds_of(tile, speed_step):
    place = lax.broadcasted_iota(jnp.int32, tile, 0).astype(jnp.float32)
    return speed_low + place * speed_step


def odd_place(axis):
    return lax.rem(lax.axis_index(axis), 2) == 1


def put_extremes(wind_ref, most_ref):
    rows = [wind_ref[i] for i in range(wind_ref.shape[0])]
    most_ref[...] = jnp.zeros_like(most_ref)
    most_ref[0:2, :] = functools.reduce(jnp.maximum, rows)
    most_ref[2:4, :] = -functools.reduce(jnp.minimum, rows)


def extremes_kernel(wind_ref, most_ref):
    put_extremes(wind_ref, most_ref.at[0])


def opening_kernel(level_ref, x_near, x_far, t_near, t_far):
    cut_near(level_ref, x_near)
    cut_far(level_ref, x_far)
    cut_headings(level_ref, t_near, t_far)


def meeting_kernel(own_ref, other_ref, most_ref):
    for g in range(most_ref.shape[0]):
        most_ref[g] = jnp.maximum(own_ref[0], other_ref[0])


def flows_into(flow_ref, speed_step, wind_ref, waves_ref):
    planes, headings = flow_ref.shape[:2]
    tile = flow_ref.shape[2:]
    first = lax.axis_index("head") * headings
    pace = speeds_of(tile, speed_step) * gain
    tables = [
        splat(waves_ref[1, pl.ds(first + j, 1), :], tile) * pace for j in range(headings)
    ]
    for i in range(planes):
        wind = splat(wind_ref[i, 1:2, :] * gain, tile)
        for j in range(headings):
            flow_ref[i, j] = tables[j] + wind


def free_kernel(split, speed_step, s_ref, *rest):
    planes, headings, speeds, width = s_ref.shape
    cells = planes * headings

    def rows_of(ref):
        return ref.reshape(cells * speeds, width)

    if split:
        wind_ref, waves_ref, speed_ref, out_ref, extra_ref, flow_t_ref = rest[:6]
        turned_ref, drift_ref, gap_ref, flow_ref = rest[6:]
        flows_into(flow_ref, speed_step, wind_ref, waves_ref)
        extra_rows, flow_rows = rows_of(extra_ref), rows_of(flow_ref)
    else:
        flow_t_ref, pk_ref, speed_ref, out_ref, turned_ref, drift_ref = rest
        peak = splat(pk_ref[1:2, :] * gain, (speeds, width))
    gain_v = thrust_limit / (12.0 * speed_step)
    s_rows, speed_rows, out_rows = rows_of(s_ref), rows_of(speed_ref), rows_of(out_ref)
    few, many = 8, turned_ref.shape[2] // speeds
    groups = turned_ref.shape[0]
    lanes = many * speeds
    high = 8
    lines = width // high

    def along_speed(n):
        start = min(n * few, cells - few) * speeds
        spots = [pl.ds(start + v, few, stride=speeds) for v in range(speeds)]
        rows = [s_rows[spot, :] for spot in spots]
        for spot, (mean, gap) in zip(spots, row_terms(rows, speed_step, True)):
            speed_rows[spot, :] = gain_v * (gap - jnp.abs(mean))

    def span(n):
        return pl.ds(min(n * many, cells - many) * speeds, lanes)

    def turn_in(n):
        turned = s_rows[span(n), :].T
        turned_ref[n, rim : rim + width, :] = turned
        for k in range(rim):
            turned_ref[n, k : k + 1, :] = turned[:1]
            turned_ref[n, rim + width + k : rim + width + k + 1, :] = turned[-1:]
        if split:
            flow_t_ref[n] = flow_rows[span(n), :].T

    def along_y(n):
        ends = [turned_ref[n, pl.ds(k, high, stride=lines), :] for k in range(lines + 2 * rim)]
        for k, (mean, gap) in enumerate(row_terms(ends, spacing)):
            spot = pl.ds(k, high, stride=lines)
            drift = mean * flow_t_ref[n, spot, :]
            if split:
                drift_ref[n, spot, :] = drift
                gap_ref[n, spot, :] = gap
            else:
                drift_ref[n, spot, :] = drift + gap * peak

    def turn_out(n):
        out_rows[span(n), :] = drift_ref[n].T
        if split:
            extra_rows[span(n), :] = gap_ref[n].T

    turn_in(0)
    for n in range(groups):
        if n > 0:
            turn_out(n - 1)
        along_y(n)
        if n + 1 < groups:
            turn_in(n + 1)
        for k in (2 * n, 2 * n + 1):
            if k * few < cells:
                along_speed(k)
    turn_out(groups - 1)


def heading_kernel(heading_step, s_ref, speed_ref, part_ref, near_ref, far_ref, out_ref):
    planes, headings = s_ref.shape[:2]
    gain_t = turn_limit / (12.0 * heading_step)
    odd = odd_place("head")
    wide = batches(planes, 9)

    def step(n, carry):
        for w in range(wide):
            i = n * wide + w
            ghosts = [(near_ref[i * rim + k], far_ref[i * rim + k]) for k in range(rim)]
            lows = [jnp.where(odd, near, far) for near, far in ghosts]
            highs = [jnp.where(odd, far, near) for near, far in ghosts]
            cells = lows + [s_ref[i, j] for j in range(headings)] + highs
            for j, (mean, gap) in enumerate(row_terms(cells, heading_step)):
                own = speed_ref[i, j] + part_ref[i, j]
                out_ref[i, j] = own + gain_t * (gap - jnp.abs(mean))
        return carry

    lax.fori_loop(0, planes // wide, step, 0)


def peaks_into(pk_ref, most, bounds, heading_step, speed_step):
    most = jnp.max(most, axis=1, keepdims=True)
    peaks = [
        jnp.maximum(most[q : q + 1] + bounds[q][1], most[q + 2 : q + 3] - bounds[q][0])
        for q in range(2)
    ]
    time_step = courant / (
        peaks[0] / spacing
        + peaks[1] / spacing
        + turn_limit / heading_step
        + thrust_limit / speed_step
    )
    width = pk_ref.shape[1]
    for row, value in enumerate(peaks + [time_step]):
        pk_ref[row : row + 1, :] = splat(value, (1, width))


def plane_at(i, planes):
    return jnp.where(odd_place("gx"), i, planes - 1 - i)


def alone(reach):
    place, size = lax.axis_index("gx"), lax.axis_size("gx")
    if reach == 0:
        return (place == size - 1) if size % 2 else place < 0
    return (place == 0) | (place == size - 1) if size % 2 == 0 else place == 0


def cut_near(field_ref, x_near):
    planes, headings = field_ref.shape[:2]
    for k in range(rim):
        i = jnp.where(alone(0), 0, k)
        x_near[k * headings : (k + 1) * headings] = field_ref[plane_at(i, planes)]


def cut_far(field_ref, x_far):
    planes, headings = field_ref.shape[:2]
    for k in range(rim):
        i = planes - 1 - jnp.where(alone(1), 0, k)
        x_far[k * headings : (k + 1) * headings] = field_ref[plane_at(i, planes)]


def cut_headings(field_ref, t_near, t_far):
    planes, headings = field_ref.shape[:2]
    t_low = jnp.where(odd_place("head"), 0, headings - rim)
    for k in range(rim):
        for i in range(planes):
            t_near[i * rim + k] = field_ref[i, t_low + k]
            t_far[i * rim + k] = field_ref[i, headings - rim - t_low + k]


def splat_targets(mask_ref, depth_ref, target_ref):
    for i in range(target_ref.shape[0]):
        depth = depth_ref[i : i + 1, :]
        target = jnp.where(mask_ref[i : i + 1, :] == 1, -depth, depth)
        target_ref[i] = splat(target, target_ref.shape[1:])


def across_planes(
    span, speed_step, s_ref, near_ref, far_ref, wind_ref, waves_ref, flow_ref, use
):
    planes, headings = s_ref.shape[:2]
    tile = s_ref.shape[2:]
    side = jnp.where(odd_place("gx"), gain, -gain).astype(jnp.float32)
    spots = [plane_at(i, planes) for i in range(planes)]
    for i in range(planes):
        flow_ref[i] = splat(wind_ref[i, 0:1, :] * side, tile)
    pace = speeds_of(tile, speed_step) * side
    first = lax.axis_index("head") * headings
    low, high = span
    wide = batches(headings, max(1, 72 // (high - low)))

    def line(i, j):
        if i < 0:
            return near_ref[(-1 - i) * headings + j]
        if i >= planes:
            return far_ref[(i - planes) * headings + j]
        return s_ref[spots[i], j]

    def step(n, carry):
        for w in range(wide):
            j = n * wide + w
            cells = [line(i, j) for i in range(low - rim, high + rim)]
            table = splat(waves_ref[0, pl.ds(first + j, 1), :], tile) * pace
            for k, (mean, gap) in enumerate(row_terms(cells, spacing)):
                spot = spots[low + k]
                use(spot, j, mean * (table + flow_ref[spot]), gap, cells[k + rim])
        return carry

    lax.fori_loop(0, headings // wide, step, 0)


def first_kernel(
    speed_step, s_ref, part_ref, near_ref, far_ref, wind_ref, waves_ref, out_ref, gap_ref, flow_ref
):
    def use(i, j, drift, gap, cell):
        out_ref[i, j] = part_ref[i, j] + drift
        gap_ref[i, j] = gap

    across_planes(
        (0, s_ref.shape[0]), speed_step, s_ref, near_ref, far_ref, wind_ref, waves_ref, flow_ref, use
    )


def closing_kernel(
    bounds, heading_step, speed_step, s_ref, part_ref, gap_x_ref, gap_y_ref, mask_ref, depth_ref,
    most_ref, out_ref, x_near, x_far, t_near, t_far, pk_ref, target_ref
):
    planes, headings = s_ref.shape[:2]
    tile = s_ref.shape[2:]
    most = functools.reduce(jnp.maximum, [most_ref[g] for g in range(most_ref.shape[0])])
    peaks_into(pk_ref, most, bounds, heading_step, speed_step)
    splat_targets(mask_ref, depth_ref, target_ref)
    peak_x = splat(pk_ref[0:1, :] * gain, tile)
    peak_y = splat(pk_ref[1:2, :] * gain, tile)
    time_step = splat(pk_ref[2:3, :], tile)

    def plane(i, carry):
        for j in range(headings):
            rate = part_ref[i, j] + (gap_x_ref[i, j] * peak_x + gap_y_ref[i, j] * peak_y)
            out_ref[i, j] = jnp.minimum(s_ref[i, j] + time_step * rate, target_ref[i])
        return carry

    lax.fori_loop(0, planes, plane, 0)
    cut_near(out_ref, x_near)
    cut_far(out_ref, x_far)
    cut_headings(out_ref, t_near, t_far)


def section_kernel(
    section, span, speed_step, base_ref, s_ref, part_ref, ghosts_ref, wind_ref, waves_ref,
    mask_ref, depth_ref, pk_ref, *refs
):
    planes = s_ref.shape[0]
    refs, (flow_ref, target_ref) = list(refs[:-2]), refs[-2:]
    early_ref = refs.pop(0) if span[0] > 0 else None
    out_ref = refs.pop(0)
    tile = s_ref.shape[2:]
    splat_targets(mask_ref, depth_ref, target_ref)
    peak_x = splat(pk_ref[0:1, :] * gain, tile)
    time_step = splat(pk_ref[2:3, :], tile)
    base_share = 0.75 if section == 2 else 1.0 / 3.0
    own_share = 0.25 if section == 2 else 2.0 / 3.0

    def use(i, j, drift, gap, cell):
        rate = part_ref[i, j] + (drift + gap * peak_x)
        moved = base_share * base_ref[i, j] + own_share * (cell + time_step * rate)
        out_ref[i, j] = jnp.minimum(moved, target_ref[i])

    near_ref, far_ref = (None, ghosts_ref) if span[0] > 0 else (ghosts_ref, None)
    across_planes(
        span, speed_step, s_ref, near_ref, far_ref, wind_ref, waves_ref, flow_ref, use
    )
    for i in range(span[0]):
        spot = plane_at(i, planes)
        out_ref[spot] = early_ref[spot]
    if section == 2 and span[0] == 0:
        cut_near(out_ref, *refs)
    elif section == 2:
        cut_far(out_ref, refs[0])
        cut_headings(out_ref, *refs[1:])


def trade(value, axis, reach, wrap=False):
    size = lax.axis_size(axis)
    pairs = [(i, i + 1) for i in range(reach, size - 1, 2)]
    if wrap and reach and size % 2 == 0:
        pairs.append((size - 1, 0))
    pairs += [(j, i) for i, j in pairs]
    pairs += [(i, i) for i in range(size) if i not in dict(pairs)]
    return lax.ppermute(value, axis, pairs)


def local(level_set, wind_field, target_mask, target_depth):
    planes, headings, speed_count, cross_count = level_set.shape
    heading_total = headings * lax.axis_size("head")
    heading_step = 2.0 * math.pi / heading_total
    speed_step = (speed_high - speed_low) / (speed_count - 1)
    speed_row = np.float32(speed_low) + np.arange(speed_count, dtype=np.float32) * np.float32(
        speed_step
    )
    angles = np.arange(heading_total, dtype=np.float32) * np.float32(heading_step)
    waves = [np.cos(angles), np.sin(angles)]
    bounds = []
    for wave in waves:
        product = wave[:, None] * speed_row[None, :]
        bounds.append((float(product.min()), float(product.max())))
    waves = jnp.asarray(np.stack(waves)[..., None] * np.ones(cross_count, np.float32))

    vmem = pl.BlockSpec(memory_space=pltpu.VMEM)
    tile = (speed_count, cross_count)

    def shape(*dims):
        return jax.ShapeDtypeStruct(dims + tile, jnp.float32)

    field = shape(planes, headings)
    short = rim * headings
    middle = max(short + 1, rim * planes)

    longest = middle + 1
    rows = pltpu.VMEM((planes,) + tile, jnp.float32)
    cells = math.prod(level_set.shape)

    def call(kernel, ins, outs, scratch=(), work=0):
        return pl.pallas_call(
            kernel,
            out_shape=outs,
            in_specs=[vmem] * len(ins),
            out_specs=[vmem] * len(outs),
            scratch_shapes=list(scratch),
            compiler_params=pltpu.CompilerParams(vmem_limit_bytes=16 * 1024 * 1024),
            cost_estimate=pl.CostEstimate(
                flops=work * cells, bytes_accessed=work * cells, transcendentals=0
            ),
        )(*ins)

    wind = jnp.transpose(wind_field, (1, 0, 2))
    many = 16
    groups, lanes = -(-planes * headings // many), many * speed_count
    turned = (groups, cross_count, lanes)
    room = [
        pltpu.VMEM((groups, cross_count + 8, lanes), jnp.float32),
        pltpu.VMEM(turned, jnp.float32),
    ]
    wide_room = room + [pltpu.VMEM(turned, jnp.float32), pltpu.VMEM(level_set.shape, jnp.float32)]
    values = level_set
    size = lax.axis_size("gx")

    pairs = [(i, i + 1) for i in range(0, size - 1, 2)]
    pairs += [(j, i) for i, j in pairs]
    pairs += [(i, i) for i in range(size) if i not in dict(pairs)]

    (most,) = call(extremes_kernel, [wind], [shape(longest + 2)])
    other = lax.ppermute(most, "gx", pairs)
    x_shapes = [shape(longest + 1), shape(longest)]
    x_out, x_last, t_out, t_last = call(opening_kernel, [values], x_shapes + [shape(middle)] * 2)
    far_shapes = [shape(short), shape(rim * planes), shape(middle)]
    for section in (1, 2, 3):
        opening = section == 1
        x_near = trade(x_out, "gx", 0)
        t_near = trade(t_out, "head", 0)
        t_far = trade(t_last, "head", 1, True)
        x_far = trade(x_last, "gx", 1)
        free = functools.partial(free_kernel, opening, speed_step)
        turning = functools.partial(heading_kernel, heading_step)
        if opening:
            step = 1 if size % 2 else 2
            groups = [list(range(k, size, step)) for k in range(step)]
            (most,) = call(meeting_kernel, [most, other], [shape(size // step)])
            values, most = lax.optimization_barrier((values, most))
            most = lax.all_to_all(most, "gx", 0, 0, axis_index_groups=groups)
            ins = [values, wind, waves]
            spun, part, extra, flow = call(
                free, ins, [field] * 3 + [jax.ShapeDtypeStruct(turned, jnp.float32)], wide_room, work=300
            )
        else:
            if section == 3:
                values, x_near = lax.optimization_barrier((values, x_near))
            spun, part = call(free, [values, flow, pk], [field] * 2, room)
            if section == 2:
                part, x_near = lax.optimization_barrier((part, x_near))
        weight = 0 if opening else 1000
        (part,) = call(turning, [values, spun, part, t_near, t_far], [field], work=weight)
        if opening:
            ins = [values, part, x_near, x_far, wind, waves]
            first = functools.partial(first_kernel, speed_step)
            part, gap = call(first, ins, [field] * 2, [rows])
            closing = functools.partial(closing_kernel, bounds, heading_step, speed_step)
            ins = [values, part, gap, extra, target_mask, target_depth, most]
            outs = [field, shape(longest), *far_shapes, shape()]
            values, x_out, x_last, t_out, t_last, pk = call(closing, ins, outs, [rows])
        else:
            more = section == 2
            ins = [level_set, values, part, x_near, wind, waves, target_mask, target_depth, pk]
            outs = [field] + ([shape(longest)] if more else [])
            last = functools.partial(section_kernel, section, (0, planes - rim), speed_step)
            early, *x_next = call(last, ins, outs, [rows, rows])
            ins = ins[:3] + [x_far] + ins[4:] + [early]
            outs = [field] + (far_shapes if more else [])
            last = functools.partial(section_kernel, section, (planes - rim, planes), speed_step)
            values, *far_next = call(last, ins, outs, [rows, rows])
            if more:
                (x_out,), (x_last, t_out, t_last) = x_next, far_next
    return values


def solution(mesh):
    return jax.shard_map(
        local,
        mesh=mesh,
        in_specs=(P("gx", "head", None, None), P(None, "gx", None), P("gx", None), P("gx", None)),
        out_specs=P("gx", "head", None, None),
        check_vma=False,
    )
```

```python
import functools
import math

import jax
import jax.numpy as jnp
import numpy as np
from jax import lax
from jax.experimental import pallas as pl
from jax.experimental.pallas import tpu as pltpu
from jax.sharding import PartitionSpec as P

epsilon = 1e-06
courant = 0.5
spacing = 0.05
turn_limit = 1.0
thrust_limit = 0.5
speed_low = 0.5
speed_high = 1.5
rim = 3
gain = 1.0 / (12.0 * spacing)


def inverse(value):
    return pltpu.reciprocal(value, approx=True)


def weights_of(e1, e2, turn, eps):
    level = turn * turn * (4.0 / 3.0) + eps
    ia = inverse(level + e2 * (e2 + turn))
    ib = inverse(level + e2 * e1)
    ic = inverse(level + e1 * (e1 - turn))
    return ia * ia, ib * ib * 6.0, ic * ic


def sides(fl, f0, fr, a2, a1, b1, b0, c0, c1):
    a3 = a1 * 3.0
    c3 = c0 * 3.0
    minus = ((fl + fl) * a2 + f0 * c3) * inverse(a2 + b1 + c3)
    plus = ((fr + fr) * c1 + f0 * a3) * inverse(c1 + b0 + a3)
    return minus, plus


def row_terms(cells, step, closed=False):
    eps = epsilon * step * step
    count = len(cells) if closed else len(cells) - 2 * rim
    shift = 0 if closed else rim
    slope = {m: cells[m + 1 + shift] - cells[m + shift] for m in range(-shift, count + shift - 1)}
    a, b, c = {}, {}, {}
    if closed:
        bend = {m: slope[m] - slope[m - 1] for m in range(1, count - 1)}
        bend[0], bend[count - 1] = slope[0], -slope[count - 2]
        turn = {m: bend[m + 1] - bend[m] for m in range(count - 1)}
        turn[-1], turn[count - 1] = bend[0], -bend[count - 1]
        jerk = {m: turn[m] - turn[m - 1] for m in range(count)}
        jerk[-1], jerk[count] = bend[0], bend[count - 1]
        rise = {m: slope[m] + slope[m - 1] for m in range(1, count - 1)}
        rise[0], rise[count - 1] = slope[0], slope[count - 2]
        a[-2] = c[count] = 1.0 / (eps * eps)
        for m, (e1, e2) in ((-1, (None, bend[0])), (count - 1, (bend[count - 1], None))):
            square = turn[m] * turn[m]
            level = square * (4.0 / 3.0) + eps
            ib, outer = inverse(level), inverse(level + (square + square))
            b[m] = ib * ib * 6.0
            (c if e2 is None else a)[m] = outer * outer
        inner = range(count - 1)
    else:
        bend = {m: slope[m] - slope[m - 1] for m in range(-2, count + 2)}
        turn = {m: bend[m + 1] - bend[m] for m in range(-2, count + 1)}
        jerk = {m: turn[m] - turn[m - 1] for m in range(-1, count + 1)}
        rise = {m: cells[m + 1 + rim] - cells[m - 1 + rim] for m in range(count)}
        inner = range(-2, count + 1)
    for m in inner:
        a[m], b[m], c[m] = weights_of(bend[m], bend[m + 1], turn[m], eps)
    out = []
    for i in range(count):
        base = rise[i] * 6.0 - (turn[i - 1] + turn[i])
        minus, plus = sides(
            jerk[i - 1], jerk[i], jerk[i + 1], a[i - 2], a[i - 1], b[i - 1], b[i], c[i], c[i + 1]
        )
        out.append((base + (plus - minus), (plus + minus) - jerk[i]))
    return out


def batches(total, most):
    return max(k for k in range(1, most + 1) if total % k == 0)


def splat(row, tile):
    return jnp.broadcast_to(row, tile)


def speeds_of(tile, speed_step):
    place = lax.broadcasted_iota(jnp.int32, tile, 0).astype(jnp.float32)
    return speed_low + place * speed_step


def odd_place(axis):
    return lax.rem(lax.axis_index(axis), 2) == 1


def put_extremes(wind_ref, most_ref):
    rows = [wind_ref[i] for i in range(wind_ref.shape[0])]
    most_ref[...] = jnp.zeros_like(most_ref)
    most_ref[0:2, :] = functools.reduce(jnp.maximum, rows)
    most_ref[2:4, :] = -functools.reduce(jnp.minimum, rows)


def extremes_kernel(wind_ref, most_ref):
    put_extremes(wind_ref, most_ref.at[0])


def opening_kernel(level_ref, x_near, x_far, t_near, t_far):
    cut_near(level_ref, x_near)
    cut_far(level_ref, x_far)
    cut_headings(level_ref, t_near, t_far)


def meeting_kernel(own_ref, other_ref, most_ref):
    most_ref[...] = jnp.maximum(own_ref[0], other_ref[0])


def flows_into(flow_ref, speed_step, wind_ref, waves_ref):
    planes, headings = flow_ref.shape[:2]
    tile = flow_ref.shape[2:]
    first = lax.axis_index("head") * headings
    pace = speeds_of(tile, speed_step) * gain
    tables = [
        splat(waves_ref[1, pl.ds(first + j, 1), :], tile) * pace for j in range(headings)
    ]
    for i in range(planes):
        wind = splat(wind_ref[i, 1:2, :] * gain, tile)
        for j in range(headings):
            flow_ref[i, j] = tables[j] + wind


def free_kernel(split, speed_step, s_ref, *rest):
    planes, headings, speeds, width = s_ref.shape
    cells = planes * headings

    def rows_of(ref):
        return ref.reshape(cells * speeds, width)

    if split:
        wind_ref, waves_ref, speed_ref, out_ref, extra_ref, flow_t_ref = rest[:6]
        turned_ref, drift_ref, gap_ref, flow_ref = rest[6:]
        flows_into(flow_ref, speed_step, wind_ref, waves_ref)
        extra_rows, flow_rows = rows_of(extra_ref), rows_of(flow_ref)
    else:
        flow_t_ref, pk_ref, speed_ref, out_ref, turned_ref, drift_ref = rest
        peak = splat(pk_ref[1:2, :] * gain, (speeds, width))
    gain_v = thrust_limit / (12.0 * speed_step)
    s_rows, speed_rows, out_rows = rows_of(s_ref), rows_of(speed_ref), rows_of(out_ref)
    few, many = 8, turned_ref.shape[2] // speeds
    groups = turned_ref.shape[0]
    lanes = many * speeds
    high = 8
    lines = width // high

    def along_speed(n):
        start = min(n * few, cells - few) * speeds
        spots = [pl.ds(start + v, few, stride=speeds) for v in range(speeds)]
        rows = [s_rows[spot, :] for spot in spots]
        for spot, (mean, gap) in zip(spots, row_terms(rows, speed_step, True)):
            speed_rows[spot, :] = gain_v * (gap - jnp.abs(mean))

    def span(n):
        return pl.ds(min(n * many, cells - many) * speeds, lanes)

    def turn_in(n):
        turned = s_rows[span(n), :].T
        turned_ref[n, rim : rim + width, :] = turned
        for k in range(rim):
            turned_ref[n, k : k + 1, :] = turned[:1]
            turned_ref[n, rim + width + k : rim + width + k + 1, :] = turned[-1:]
        if split:
            flow_t_ref[n] = flow_rows[span(n), :].T

    def along_y(n):
        ends = [turned_ref[n, pl.ds(k, high, stride=lines), :] for k in range(lines + 2 * rim)]
        for k, (mean, gap) in enumerate(row_terms(ends, spacing)):
            spot = pl.ds(k, high, stride=lines)
            drift = mean * flow_t_ref[n, spot, :]
            if split:
                drift_ref[n, spot, :] = drift
                gap_ref[n, spot, :] = gap
            else:
                drift_ref[n, spot, :] = drift + gap * peak

    def turn_out(n):
        out_rows[span(n), :] = drift_ref[n].T
        if split:
            extra_rows[span(n), :] = gap_ref[n].T

    turn_in(0)
    for n in range(groups):
        if n > 0:
            turn_out(n - 1)
        along_y(n)
        if n + 1 < groups:
            turn_in(n + 1)
        for k in (2 * n, 2 * n + 1):
            if k * few < cells:
                along_speed(k)
    turn_out(groups - 1)


def heading_kernel(heading_step, s_ref, speed_ref, part_ref, near_ref, far_ref, out_ref):
    planes, headings = s_ref.shape[:2]
    gain_t = turn_limit / (12.0 * heading_step)
    odd = odd_place("head")
    wide = batches(planes, 9)

    def step(n, carry):
        for w in range(wide):
            i = n * wide + w
            ghosts = [(near_ref[i * rim + k], far_ref[i * rim + k]) for k in range(rim)]
            lows = [jnp.where(odd, near, far) for near, far in ghosts]
            highs = [jnp.where(odd, far, near) for near, far in ghosts]
            cells = lows + [s_ref[i, j] for j in range(headings)] + highs
            for j, (mean, gap) in enumerate(row_terms(cells, heading_step)):
                own = speed_ref[i, j] + part_ref[i, j]
                out_ref[i, j] = own + gain_t * (gap - jnp.abs(mean))
        return carry

    lax.fori_loop(0, planes // wide, step, 0)


def peaks_into(pk_ref, most, bounds, heading_step, speed_step):
    most = jnp.max(most, axis=1, keepdims=True)
    peaks = [
        jnp.maximum(most[q : q + 1] + bounds[q][1], most[q + 2 : q + 3] - bounds[q][0])
        for q in range(2)
    ]
    time_step = courant / (
        peaks[0] / spacing
        + peaks[1] / spacing
        + turn_limit / heading_step
        + thrust_limit / speed_step
    )
    width = pk_ref.shape[1]
    for row, value in enumerate(peaks + [time_step]):
        pk_ref[row : row + 1, :] = splat(value, (1, width))


def plane_at(i, planes):
    return jnp.where(odd_place("gx"), i, planes - 1 - i)


def alone(reach):
    place, size = lax.axis_index("gx"), lax.axis_size("gx")
    if reach == 0:
        return (place == size - 1) if size % 2 else place < 0
    return (place == 0) | (place == size - 1) if size % 2 == 0 else place == 0


def cut_near(field_ref, x_near):
    planes, headings = field_ref.shape[:2]
    for k in range(rim):
        i = jnp.where(alone(0), 0, k)
        x_near[k * headings : (k + 1) * headings] = field_ref[plane_at(i, planes)]


def cut_far(field_ref, x_far):
    planes, headings = field_ref.shape[:2]
    for k in range(rim):
        i = planes - 1 - jnp.where(alone(1), 0, k)
        x_far[k * headings : (k + 1) * headings] = field_ref[plane_at(i, planes)]


def cut_headings(field_ref, t_near, t_far):
    planes, headings = field_ref.shape[:2]
    t_low = jnp.where(odd_place("head"), 0, headings - rim)
    for k in range(rim):
        for i in range(planes):
            t_near[i * rim + k] = field_ref[i, t_low + k]
            t_far[i * rim + k] = field_ref[i, headings - rim - t_low + k]


def splat_targets(mask_ref, depth_ref, target_ref):
    for i in range(target_ref.shape[0]):
        depth = depth_ref[i : i + 1, :]
        target = jnp.where(mask_ref[i : i + 1, :] == 1, -depth, depth)
        target_ref[i] = splat(target, target_ref.shape[1:])


def across_planes(
    span, speed_step, s_ref, near_ref, far_ref, wind_ref, waves_ref, flow_ref, use
):
    planes, headings = s_ref.shape[:2]
    tile = s_ref.shape[2:]
    side = jnp.where(odd_place("gx"), gain, -gain).astype(jnp.float32)
    spots = [plane_at(i, planes) for i in range(planes)]
    for i in range(planes):
        flow_ref[i] = splat(wind_ref[i, 0:1, :] * side, tile)
    pace = speeds_of(tile, speed_step) * side
    first = lax.axis_index("head") * headings
    low, high = span
    wide = batches(headings, max(1, 72 // (high - low)))

    def line(i, j):
        if i < 0:
            return near_ref[(-1 - i) * headings + j]
        if i >= planes:
            return far_ref[(i - planes) * headings + j]
        return s_ref[spots[i], j]

    def step(n, carry):
        for w in range(wide):
            j = n * wide + w
            cells = [line(i, j) for i in range(low - rim, high + rim)]
            table = splat(waves_ref[0, pl.ds(first + j, 1), :], tile) * pace
            for k, (mean, gap) in enumerate(row_terms(cells, spacing)):
                spot = spots[low + k]
                use(spot, j, mean * (table + flow_ref[spot]), gap, cells[k + rim])
        return carry

    lax.fori_loop(0, headings // wide, step, 0)


def first_kernel(
    speed_step, s_ref, part_ref, near_ref, far_ref, wind_ref, waves_ref, out_ref, gap_ref, flow_ref
):
    def use(i, j, drift, gap, cell):
        out_ref[i, j] = part_ref[i, j] + drift
        gap_ref[i, j] = gap

    across_planes(
        (0, s_ref.shape[0]), speed_step, s_ref, near_ref, far_ref, wind_ref, waves_ref, flow_ref, use
    )


def closing_kernel(
    bounds, heading_step, speed_step, s_ref, part_ref, gap_x_ref, gap_y_ref, mask_ref, depth_ref,
    most_ref, other_ref, out_ref, x_near, x_far, t_near, t_far, pk_ref, target_ref
):
    planes, headings = s_ref.shape[:2]
    tile = s_ref.shape[2:]
    most = jnp.maximum(most_ref[...], other_ref[...])
    peaks_into(pk_ref, most, bounds, heading_step, speed_step)
    splat_targets(mask_ref, depth_ref, target_ref)
    peak_x = splat(pk_ref[0:1, :] * gain, tile)
    peak_y = splat(pk_ref[1:2, :] * gain, tile)
    time_step = splat(pk_ref[2:3, :], tile)

    def plane(i, carry):
        for j in range(headings):
            rate = part_ref[i, j] + (gap_x_ref[i, j] * peak_x + gap_y_ref[i, j] * peak_y)
            out_ref[i, j] = jnp.minimum(s_ref[i, j] + time_step * rate, target_ref[i])
        return carry

    lax.fori_loop(0, planes, plane, 0)
    cut_near(out_ref, x_near)
    cut_far(out_ref, x_far)
    cut_headings(out_ref, t_near, t_far)


def section_kernel(
    section, span, speed_step, base_ref, s_ref, part_ref, ghosts_ref, wind_ref, waves_ref,
    mask_ref, depth_ref, pk_ref, *refs
):
    planes = s_ref.shape[0]
    refs, (flow_ref, target_ref) = list(refs[:-2]), refs[-2:]
    early_ref = refs.pop(0) if span[0] > 0 else None
    out_ref = refs.pop(0)
    tile = s_ref.shape[2:]
    splat_targets(mask_ref, depth_ref, target_ref)
    peak_x = splat(pk_ref[0:1, :] * gain, tile)
    time_step = splat(pk_ref[2:3, :], tile)
    base_share = 0.75 if section == 2 else 1.0 / 3.0
    own_share = 0.25 if section == 2 else 2.0 / 3.0

    def use(i, j, drift, gap, cell):
        rate = part_ref[i, j] + (drift + gap * peak_x)
        moved = base_share * base_ref[i, j] + own_share * (cell + time_step * rate)
        out_ref[i, j] = jnp.minimum(moved, target_ref[i])

    near_ref, far_ref = (None, ghosts_ref) if span[0] > 0 else (ghosts_ref, None)
    across_planes(
        span, speed_step, s_ref, near_ref, far_ref, wind_ref, waves_ref, flow_ref, use
    )
    for i in range(span[0]):
        spot = plane_at(i, planes)
        out_ref[spot] = early_ref[spot]
    if section == 2 and span[0] == 0:
        cut_near(out_ref, *refs)
    elif section == 2:
        cut_far(out_ref, refs[0])
        cut_headings(out_ref, *refs[1:])


def trade(value, axis, reach, wrap=False):
    size = lax.axis_size(axis)
    pairs = [(i, i + 1) for i in range(reach, size - 1, 2)]
    if wrap and reach and size % 2 == 0:
        pairs.append((size - 1, 0))
    pairs += [(j, i) for i, j in pairs]
    pairs += [(i, i) for i in range(size) if i not in dict(pairs)]
    return lax.ppermute(value, axis, pairs)


def local(level_set, wind_field, target_mask, target_depth):
    planes, headings, speed_count, cross_count = level_set.shape
    heading_total = headings * lax.axis_size("head")
    heading_step = 2.0 * math.pi / heading_total
    speed_step = (speed_high - speed_low) / (speed_count - 1)
    speed_row = np.float32(speed_low) + np.arange(speed_count, dtype=np.float32) * np.float32(
        speed_step
    )
    angles = np.arange(heading_total, dtype=np.float32) * np.float32(heading_step)
    waves = [np.cos(angles), np.sin(angles)]
    bounds = []
    for wave in waves:
        product = wave[:, None] * speed_row[None, :]
        bounds.append((float(product.min()), float(product.max())))
    waves = jnp.asarray(np.stack(waves)[..., None] * np.ones(cross_count, np.float32))

    vmem = pl.BlockSpec(memory_space=pltpu.VMEM)
    tile = (speed_count, cross_count)

    def shape(*dims):
        return jax.ShapeDtypeStruct(dims + tile, jnp.float32)

    field = shape(planes, headings)
    short = rim * headings
    middle = max(short + 1, rim * planes)

    longest = middle + 1
    rows = pltpu.VMEM((planes,) + tile, jnp.float32)
    cells = math.prod(level_set.shape)

    def call(kernel, ins, outs, scratch=(), work=0):
        return pl.pallas_call(
            kernel,
            out_shape=outs,
            in_specs=[vmem] * len(ins),
            out_specs=[vmem] * len(outs),
            scratch_shapes=list(scratch),
            compiler_params=pltpu.CompilerParams(vmem_limit_bytes=16 * 1024 * 1024),
            cost_estimate=pl.CostEstimate(
                flops=work * cells, bytes_accessed=work * cells, transcendentals=0
            ),
        )(*ins)

    wind = jnp.transpose(wind_field, (1, 0, 2))
    many = 16
    groups, lanes = -(-planes * headings // many), many * speed_count
    turned = (groups, cross_count, lanes)
    room = [
        pltpu.VMEM((groups, cross_count + 8, lanes), jnp.float32),
        pltpu.VMEM(turned, jnp.float32),
    ]
    wide_room = room + [pltpu.VMEM(turned, jnp.float32), pltpu.VMEM(level_set.shape, jnp.float32)]
    values = level_set
    size = lax.axis_size("gx")

    def spread(most, reach):
        if size & (size - 1):
            pairs = [(i, (i + reach) % size) for i in range(size)]
        else:
            pairs = [(i, i ^ reach) for i in range(size)]
        return lax.ppermute(most, "gx", pairs)

    (most,) = call(extremes_kernel, [wind], [shape(longest + 2)])
    other = spread(most, 1)
    x_shapes = [shape(longest), shape(longest + 1)]
    x_out, x_last, t_out, t_last = call(opening_kernel, [values], x_shapes + [shape(middle)] * 2)
    far_shapes = [shape(short), shape(rim * planes), shape(middle)]
    for section in (1, 2, 3):
        opening = section == 1
        x_near = trade(x_out, "gx", 0)
        t_near = trade(t_out, "head", 0)
        t_far = trade(t_last, "head", 1, True)
        x_far = trade(x_last, "gx", 1)
        free = functools.partial(free_kernel, opening, speed_step)
        turning = functools.partial(heading_kernel, heading_step)
        if opening:
            (most,) = call(meeting_kernel, [most, other], [shape()])
            other = spread(most, 2)
            ins = [values, wind, waves]
            spun, part, extra, flow = call(
                free, ins, [field] * 3 + [jax.ShapeDtypeStruct(turned, jnp.float32)], wide_room, work=300
            )
            reach = 4
            while reach < size:
                most = jnp.maximum(most, other)
                most, part = lax.optimization_barrier((most, part))
                other = spread(most, reach)
                reach *= 2
            part, x_far = lax.optimization_barrier((part, x_far))
        else:
            if section == 3:
                values, x_near = lax.optimization_barrier((values, x_near))
            spun, part = call(free, [values, flow, pk], [field] * 2, room)
            if section == 2:
                part, x_near = lax.optimization_barrier((part, x_near))
        (part,) = call(turning, [values, spun, part, t_near, t_far], [field], work=1000)
        if opening:
            ins = [values, part, x_near, x_far, wind, waves]
            first = functools.partial(first_kernel, speed_step)
            part, gap = call(first, ins, [field] * 2, [rows])
            closing = functools.partial(closing_kernel, bounds, heading_step, speed_step)
            ins = [values, part, gap, extra, target_mask, target_depth, most, other]
            outs = [field, shape(longest), *far_shapes, shape()]
            values, x_out, x_last, t_out, t_last, pk = call(closing, ins, outs, [rows])
        else:
            more = section == 2
            ins = [level_set, values, part, x_near, wind, waves, target_mask, target_depth, pk]
            outs = [field] + ([shape(longest)] if more else [])
            last = functools.partial(section_kernel, section, (0, planes - rim), speed_step)
            early, *x_next = call(last, ins, outs, [rows, rows])
            ins = ins[:3] + [x_far] + ins[4:] + [early]
            outs = [field] + (far_shapes if more else [])
            last = functools.partial(section_kernel, section, (planes - rim, planes), speed_step)
            values, *far_next = call(last, ins, outs, [rows, rows])
            if more:
                (x_out,), (x_last, t_out, t_last) = x_next, far_next
    return values


def solution(mesh):
    return jax.shard_map(
        local,
        mesh=mesh,
        in_specs=(P("gx", "head", None, None), P(None, "gx", None), P("gx", None), P("gx", None)),
        out_specs=P("gx", "head", None, None),
        check_vma=False,
    )
```

```python
import functools
import math

import jax
import jax.numpy as jnp
import numpy as np
from jax import lax
from jax.experimental import pallas as pl
from jax.experimental.pallas import tpu as pltpu
from jax.sharding import PartitionSpec as P

epsilon = 1e-06
courant = 0.5
spacing = 0.05
turn_limit = 1.0
thrust_limit = 0.5
speed_low = 0.5
speed_high = 1.5
rim = 3
gain = 1.0 / (12.0 * spacing)


def inverse(value):
    return pltpu.reciprocal(value, approx=True)


def weights_of(e1, e2, turn, eps):
    level = turn * turn * (4.0 / 3.0) + eps
    ia = inverse(level + e2 * (e2 + turn))
    ib = inverse(level + e2 * e1)
    ic = inverse(level + e1 * (e1 - turn))
    return ia * ia, ib * ib * 6.0, ic * ic


def sides(fl, f0, fr, a2, a1, b1, b0, c0, c1):
    a3 = a1 * 3.0
    c3 = c0 * 3.0
    minus = ((fl + fl) * a2 + f0 * c3) * inverse(a2 + b1 + c3)
    plus = ((fr + fr) * c1 + f0 * a3) * inverse(c1 + b0 + a3)
    return minus, plus


def row_terms(cells, step, closed=False):
    eps = epsilon * step * step
    count = len(cells) if closed else len(cells) - 2 * rim
    shift = 0 if closed else rim
    slope = {m: cells[m + 1 + shift] - cells[m + shift] for m in range(-shift, count + shift - 1)}
    a, b, c = {}, {}, {}
    if closed:
        bend = {m: slope[m] - slope[m - 1] for m in range(1, count - 1)}
        bend[0], bend[count - 1] = slope[0], -slope[count - 2]
        turn = {m: bend[m + 1] - bend[m] for m in range(count - 1)}
        turn[-1], turn[count - 1] = bend[0], -bend[count - 1]
        jerk = {m: turn[m] - turn[m - 1] for m in range(count)}
        jerk[-1], jerk[count] = bend[0], bend[count - 1]
        rise = {m: slope[m] + slope[m - 1] for m in range(1, count - 1)}
        rise[0], rise[count - 1] = slope[0], slope[count - 2]
        a[-2] = c[count] = 1.0 / (eps * eps)
        for m, (e1, e2) in ((-1, (None, bend[0])), (count - 1, (bend[count - 1], None))):
            square = turn[m] * turn[m]
            level = square * (4.0 / 3.0) + eps
            ib, outer = inverse(level), inverse(level + (square + square))
            b[m] = ib * ib * 6.0
            (c if e2 is None else a)[m] = outer * outer
        inner = range(count - 1)
    else:
        bend = {m: slope[m] - slope[m - 1] for m in range(-2, count + 2)}
        turn = {m: bend[m + 1] - bend[m] for m in range(-2, count + 1)}
        jerk = {m: turn[m] - turn[m - 1] for m in range(-1, count + 1)}
        rise = {m: cells[m + 1 + rim] - cells[m - 1 + rim] for m in range(count)}
        inner = range(-2, count + 1)
    for m in inner:
        a[m], b[m], c[m] = weights_of(bend[m], bend[m + 1], turn[m], eps)
    out = []
    for i in range(count):
        base = rise[i] * 6.0 - (turn[i - 1] + turn[i])
        minus, plus = sides(
            jerk[i - 1], jerk[i], jerk[i + 1], a[i - 2], a[i - 1], b[i - 1], b[i], c[i], c[i + 1]
        )
        out.append((base + (plus - minus), (plus + minus) - jerk[i]))
    return out


def batches(total, most):
    return max(k for k in range(1, most + 1) if total % k == 0)


def splat(row, tile):
    return jnp.broadcast_to(row, tile)


def speeds_of(tile, speed_step):
    place = lax.broadcasted_iota(jnp.int32, tile, 0).astype(jnp.float32)
    return speed_low + place * speed_step


def odd_place(axis):
    return lax.rem(lax.axis_index(axis), 2) == 1


def put_extremes(wind_ref, most_ref):
    rows = [wind_ref[i] for i in range(wind_ref.shape[0])]
    most_ref[...] = jnp.zeros_like(most_ref)
    most_ref[0:2, :] = functools.reduce(jnp.maximum, rows)
    most_ref[2:4, :] = -functools.reduce(jnp.minimum, rows)


def extremes_kernel(wind_ref, most_ref):
    put_extremes(wind_ref, most_ref.at[0])


def opening_kernel(level_ref, x_near, x_far, t_near, t_far):
    cut_near(level_ref, x_near)
    cut_far(level_ref, x_far)
    cut_headings(level_ref, t_near, t_far)


def meeting_kernel(own_ref, other_ref, most_ref):
    most_ref[...] = jnp.maximum(own_ref[0], other_ref[0])


def flows_into(flow_ref, speed_step, wind_ref, waves_ref):
    planes, headings = flow_ref.shape[:2]
    tile = flow_ref.shape[2:]
    first = lax.axis_index("head") * headings
    pace = speeds_of(tile, speed_step) * gain
    tables = [
        splat(waves_ref[1, pl.ds(first + j, 1), :], tile) * pace for j in range(headings)
    ]
    for i in range(planes):
        wind = splat(wind_ref[i, 1:2, :] * gain, tile)
        for j in range(headings):
            flow_ref[i, j] = tables[j] + wind


def free_kernel(split, speed_step, s_ref, *rest):
    planes, headings, speeds, width = s_ref.shape
    cells = planes * headings

    def rows_of(ref):
        return ref.reshape(cells * speeds, width)

    if split:
        wind_ref, waves_ref, speed_ref, out_ref, extra_ref, flow_t_ref = rest[:6]
        turned_ref, drift_ref, gap_ref, flow_ref = rest[6:]
        flows_into(flow_ref, speed_step, wind_ref, waves_ref)
        extra_rows, flow_rows = rows_of(extra_ref), rows_of(flow_ref)
    else:
        flow_t_ref, pk_ref, speed_ref, out_ref, turned_ref, drift_ref = rest
        peak = splat(pk_ref[1:2, :] * gain, (speeds, width))
    gain_v = thrust_limit / (12.0 * speed_step)
    s_rows, speed_rows, out_rows = rows_of(s_ref), rows_of(speed_ref), rows_of(out_ref)
    few, many = 8, turned_ref.shape[2] // speeds
    groups = turned_ref.shape[0]
    lanes = many * speeds
    high = 8
    lines = width // high

    def along_speed(n):
        start = min(n * few, cells - few) * speeds
        spots = [pl.ds(start + v, few, stride=speeds) for v in range(speeds)]
        rows = [s_rows[spot, :] for spot in spots]
        for spot, (mean, gap) in zip(spots, row_terms(rows, speed_step, True)):
            speed_rows[spot, :] = gain_v * (gap - jnp.abs(mean))

    def span(n):
        return pl.ds(min(n * many, cells - many) * speeds, lanes)

    def turn_in(n):
        turned = s_rows[span(n), :].T
        turned_ref[n, rim : rim + width, :] = turned
        for k in range(rim):
            turned_ref[n, k : k + 1, :] = turned[:1]
            turned_ref[n, rim + width + k : rim + width + k + 1, :] = turned[-1:]
        if split:
            flow_t_ref[n] = flow_rows[span(n), :].T

    def along_y(n):
        ends = [turned_ref[n, pl.ds(k, high, stride=lines), :] for k in range(lines + 2 * rim)]
        for k, (mean, gap) in enumerate(row_terms(ends, spacing)):
            spot = pl.ds(k, high, stride=lines)
            drift = mean * flow_t_ref[n, spot, :]
            if split:
                drift_ref[n, spot, :] = drift
                gap_ref[n, spot, :] = gap
            else:
                drift_ref[n, spot, :] = drift + gap * peak

    def turn_out(n):
        out_rows[span(n), :] = drift_ref[n].T
        if split:
            extra_rows[span(n), :] = gap_ref[n].T

    turn_in(0)
    for n in range(groups):
        if n > 0:
            turn_out(n - 1)
        along_y(n)
        if n + 1 < groups:
            turn_in(n + 1)
        for k in (2 * n, 2 * n + 1):
            if k * few < cells:
                along_speed(k)
    turn_out(groups - 1)


def heading_kernel(heading_step, s_ref, speed_ref, part_ref, near_ref, far_ref, out_ref):
    planes, headings = s_ref.shape[:2]
    gain_t = turn_limit / (12.0 * heading_step)
    odd = odd_place("head")
    wide = batches(planes, 9)

    def step(n, carry):
        for w in range(wide):
            i = n * wide + w
            ghosts = [(near_ref[i * rim + k], far_ref[i * rim + k]) for k in range(rim)]
            lows = [jnp.where(odd, near, far) for near, far in ghosts]
            highs = [jnp.where(odd, far, near) for near, far in ghosts]
            cells = lows + [s_ref[i, j] for j in range(headings)] + highs
            for j, (mean, gap) in enumerate(row_terms(cells, heading_step)):
                own = speed_ref[i, j] + part_ref[i, j]
                out_ref[i, j] = own + gain_t * (gap - jnp.abs(mean))
        return carry

    lax.fori_loop(0, planes // wide, step, 0)


def peaks_into(pk_ref, most, bounds, heading_step, speed_step):
    most = jnp.max(most, axis=1, keepdims=True)
    peaks = [
        jnp.maximum(most[q : q + 1] + bounds[q][1], most[q + 2 : q + 3] - bounds[q][0])
        for q in range(2)
    ]
    time_step = courant / (
        peaks[0] / spacing
        + peaks[1] / spacing
        + turn_limit / heading_step
        + thrust_limit / speed_step
    )
    width = pk_ref.shape[1]
    for row, value in enumerate(peaks + [time_step]):
        pk_ref[row : row + 1, :] = splat(value, (1, width))


def plane_at(i, planes):
    return jnp.where(odd_place("gx"), i, planes - 1 - i)


def alone(reach):
    place, size = lax.axis_index("gx"), lax.axis_size("gx")
    if reach == 0:
        return (place == size - 1) if size % 2 else place < 0
    return (place == 0) | (place == size - 1) if size % 2 == 0 else place == 0


def cut_near(field_ref, x_near):
    planes, headings = field_ref.shape[:2]
    for k in range(rim):
        i = jnp.where(alone(0), 0, k)
        x_near[k * headings : (k + 1) * headings] = field_ref[plane_at(i, planes)]


def cut_far(field_ref, x_far):
    planes, headings = field_ref.shape[:2]
    for k in range(rim):
        i = planes - 1 - jnp.where(alone(1), 0, k)
        x_far[k * headings : (k + 1) * headings] = field_ref[plane_at(i, planes)]


def cut_headings(field_ref, t_near, t_far):
    planes, headings = field_ref.shape[:2]
    t_low = jnp.where(odd_place("head"), 0, headings - rim)
    for k in range(rim):
        for i in range(planes):
            t_near[i * rim + k] = field_ref[i, t_low + k]
            t_far[i * rim + k] = field_ref[i, headings - rim - t_low + k]


def splat_targets(mask_ref, depth_ref, target_ref):
    for i in range(target_ref.shape[0]):
        depth = depth_ref[i : i + 1, :]
        target = jnp.where(mask_ref[i : i + 1, :] == 1, -depth, depth)
        target_ref[i] = splat(target, target_ref.shape[1:])


def across_planes(
    span, speed_step, s_ref, near_ref, far_ref, wind_ref, waves_ref, flow_ref, use
):
    planes, headings = s_ref.shape[:2]
    tile = s_ref.shape[2:]
    side = jnp.where(odd_place("gx"), gain, -gain).astype(jnp.float32)
    spots = [plane_at(i, planes) for i in range(planes)]
    for i in range(planes):
        flow_ref[i] = splat(wind_ref[i, 0:1, :] * side, tile)
    pace = speeds_of(tile, speed_step) * side
    first = lax.axis_index("head") * headings
    low, high = span
    wide = batches(headings, max(1, 72 // (high - low)))

    def line(i, j):
        if i < 0:
            return near_ref[(-1 - i) * headings + j]
        if i >= planes:
            return far_ref[(i - planes) * headings + j]
        return s_ref[spots[i], j]

    def step(n, carry):
        for w in range(wide):
            j = n * wide + w
            cells = [line(i, j) for i in range(low - rim, high + rim)]
            table = splat(waves_ref[0, pl.ds(first + j, 1), :], tile) * pace
            for k, (mean, gap) in enumerate(row_terms(cells, spacing)):
                spot = spots[low + k]
                use(spot, j, mean * (table + flow_ref[spot]), gap, cells[k + rim])
        return carry

    lax.fori_loop(0, headings // wide, step, 0)


def first_kernel(
    speed_step, s_ref, part_ref, near_ref, far_ref, wind_ref, waves_ref, out_ref, gap_ref, flow_ref
):
    def use(i, j, drift, gap, cell):
        out_ref[i, j] = part_ref[i, j] + drift
        gap_ref[i, j] = gap

    across_planes(
        (0, s_ref.shape[0]), speed_step, s_ref, near_ref, far_ref, wind_ref, waves_ref, flow_ref, use
    )


def closing_kernel(
    bounds, heading_step, speed_step, s_ref, part_ref, gap_x_ref, gap_y_ref, mask_ref, depth_ref,
    most_ref, other_ref, out_ref, x_near, x_far, t_near, t_far, pk_ref, target_ref
):
    planes, headings = s_ref.shape[:2]
    tile = s_ref.shape[2:]
    most = jnp.maximum(most_ref[...], other_ref[...])
    peaks_into(pk_ref, most, bounds, heading_step, speed_step)
    splat_targets(mask_ref, depth_ref, target_ref)
    peak_x = splat(pk_ref[0:1, :] * gain, tile)
    peak_y = splat(pk_ref[1:2, :] * gain, tile)
    time_step = splat(pk_ref[2:3, :], tile)

    def plane(i, carry):
        for j in range(headings):
            rate = part_ref[i, j] + (gap_x_ref[i, j] * peak_x + gap_y_ref[i, j] * peak_y)
            out_ref[i, j] = jnp.minimum(s_ref[i, j] + time_step * rate, target_ref[i])
        return carry

    lax.fori_loop(0, planes, plane, 0)
    cut_near(out_ref, x_near)
    cut_far(out_ref, x_far)
    cut_headings(out_ref, t_near, t_far)


def section_kernel(
    section, span, speed_step, base_ref, s_ref, part_ref, ghosts_ref, wind_ref, waves_ref,
    mask_ref, depth_ref, pk_ref, *refs
):
    planes = s_ref.shape[0]
    refs, (flow_ref, target_ref) = list(refs[:-2]), refs[-2:]
    early_ref = refs.pop(0) if span[0] > 0 else None
    out_ref = refs.pop(0)
    tile = s_ref.shape[2:]
    splat_targets(mask_ref, depth_ref, target_ref)
    peak_x = splat(pk_ref[0:1, :] * gain, tile)
    time_step = splat(pk_ref[2:3, :], tile)
    base_share = 0.75 if section == 2 else 1.0 / 3.0
    own_share = 0.25 if section == 2 else 2.0 / 3.0

    def use(i, j, drift, gap, cell):
        rate = part_ref[i, j] + (drift + gap * peak_x)
        moved = base_share * base_ref[i, j] + own_share * (cell + time_step * rate)
        out_ref[i, j] = jnp.minimum(moved, target_ref[i])

    near_ref, far_ref = (None, ghosts_ref) if span[0] > 0 else (ghosts_ref, None)
    across_planes(
        span, speed_step, s_ref, near_ref, far_ref, wind_ref, waves_ref, flow_ref, use
    )
    for i in range(span[0]):
        spot = plane_at(i, planes)
        out_ref[spot] = early_ref[spot]
    if section == 2 and span[0] == 0:
        cut_near(out_ref, *refs)
    elif section == 2:
        cut_far(out_ref, refs[0])
        cut_headings(out_ref, *refs[1:])


def trade(value, axis, reach, wrap=False):
    size = lax.axis_size(axis)
    pairs = [(i, i + 1) for i in range(reach, size - 1, 2)]
    if wrap and reach and size % 2 == 0:
        pairs.append((size - 1, 0))
    pairs += [(j, i) for i, j in pairs]
    pairs += [(i, i) for i in range(size) if i not in dict(pairs)]
    return lax.ppermute(value, axis, pairs)


def local(level_set, wind_field, target_mask, target_depth):
    planes, headings, speed_count, cross_count = level_set.shape
    heading_total = headings * lax.axis_size("head")
    heading_step = 2.0 * math.pi / heading_total
    speed_step = (speed_high - speed_low) / (speed_count - 1)
    speed_row = np.float32(speed_low) + np.arange(speed_count, dtype=np.float32) * np.float32(
        speed_step
    )
    angles = np.arange(heading_total, dtype=np.float32) * np.float32(heading_step)
    waves = [np.cos(angles), np.sin(angles)]
    bounds = []
    for wave in waves:
        product = wave[:, None] * speed_row[None, :]
        bounds.append((float(product.min()), float(product.max())))
    waves = jnp.asarray(np.stack(waves)[..., None] * np.ones(cross_count, np.float32))

    vmem = pl.BlockSpec(memory_space=pltpu.VMEM)
    tile = (speed_count, cross_count)

    def shape(*dims):
        return jax.ShapeDtypeStruct(dims + tile, jnp.float32)

    field = shape(planes, headings)
    short = rim * headings
    middle = max(short + 1, rim * planes)

    longest = middle + 1
    rows = pltpu.VMEM((planes,) + tile, jnp.float32)
    cells = math.prod(level_set.shape)

    def call(kernel, ins, outs, scratch=(), work=0):
        return pl.pallas_call(
            kernel,
            out_shape=outs,
            in_specs=[vmem] * len(ins),
            out_specs=[vmem] * len(outs),
            scratch_shapes=list(scratch),
            compiler_params=pltpu.CompilerParams(vmem_limit_bytes=16 * 1024 * 1024),
            cost_estimate=pl.CostEstimate(
                flops=work * cells, bytes_accessed=work * cells, transcendentals=0
            ),
        )(*ins)

    wind = jnp.transpose(wind_field, (1, 0, 2))
    many = 16
    groups, lanes = -(-planes * headings // many), many * speed_count
    turned = (groups, cross_count, lanes)
    room = [
        pltpu.VMEM((groups, cross_count + 8, lanes), jnp.float32),
        pltpu.VMEM(turned, jnp.float32),
    ]
    wide_room = room + [pltpu.VMEM(turned, jnp.float32), pltpu.VMEM(level_set.shape, jnp.float32)]
    values = level_set
    size = lax.axis_size("gx")

    def spread(most, reach):
        if size & (size - 1):
            pairs = [(i, (i + reach) % size) for i in range(size)]
        else:
            pairs = [(i, i ^ reach) for i in range(size)]
        return lax.ppermute(most, "gx", pairs)

    (most,) = call(extremes_kernel, [wind], [shape(longest + 2)])
    other = spread(most, 1)
    x_shapes = [shape(longest), shape(longest + 1)]
    x_out, x_last, t_out, t_last = call(opening_kernel, [values], x_shapes + [shape(middle)] * 2)
    far_shapes = [shape(short), shape(rim * planes), shape(middle)]
    for section in (1, 2, 3):
        opening = section == 1
        x_near = trade(x_out, "gx", 0)
        t_near = trade(t_out, "head", 0)
        t_far = trade(t_last, "head", 1, True)
        x_far = trade(x_last, "gx", 1)
        free = functools.partial(free_kernel, opening, speed_step)
        turning = functools.partial(heading_kernel, heading_step)
        if opening:
            (most,) = call(meeting_kernel, [most, other], [shape()])
            other = spread(most, 2)
            ins = [values, wind, waves]
            spun, part, extra, flow = call(
                free, ins, [field] * 3 + [jax.ShapeDtypeStruct(turned, jnp.float32)], wide_room, work=300
            )
            reach = 4
            while reach < size:
                most = jnp.maximum(most, other)
                most, part = lax.optimization_barrier((most, part))
                other = spread(most, reach)
                reach *= 2
        else:
            if section == 3:
                values, x_near = lax.optimization_barrier((values, x_near))
            spun, part = call(free, [values, flow, pk], [field] * 2, room)
            if section == 2:
                part, x_near = lax.optimization_barrier((part, x_near))
        weight = 0 if opening else 1000
        (part,) = call(turning, [values, spun, part, t_near, t_far], [field], work=weight)
        if opening:
            ins = [values, part, x_near, x_far, wind, waves]
            first = functools.partial(first_kernel, speed_step)
            part, gap = call(first, ins, [field] * 2, [rows])
            closing = functools.partial(closing_kernel, bounds, heading_step, speed_step)
            ins = [values, part, gap, extra, target_mask, target_depth, most, other]
            outs = [field, shape(longest), *far_shapes, shape()]
            values, x_out, x_last, t_out, t_last, pk = call(closing, ins, outs, [rows])
        else:
            more = section == 2
            ins = [level_set, values, part, x_near, wind, waves, target_mask, target_depth, pk]
            outs = [field] + ([shape(longest)] if more else [])
            last = functools.partial(section_kernel, section, (0, planes - rim), speed_step)
            early, *x_next = call(last, ins, outs, [rows, rows])
            ins = ins[:3] + [x_far] + ins[4:] + [early]
            outs = [field] + (far_shapes if more else [])
            last = functools.partial(section_kernel, section, (planes - rim, planes), speed_step)
            values, *far_next = call(last, ins, outs, [rows, rows])
            if more:
                (x_out,), (x_last, t_out, t_last) = x_next, far_next
    return values


def solution(mesh):
    return jax.shard_map(
        local,
        mesh=mesh,
        in_specs=(P("gx", "head", None, None), P(None, "gx", None), P("gx", None), P("gx", None)),
        out_specs=P("gx", "head", None, None),
        check_vma=False,
    )
```

```python
import functools
import math

import jax
import jax.numpy as jnp
import numpy as np
from jax import lax
from jax.experimental import pallas as pl
from jax.experimental.pallas import tpu as pltpu
from jax.sharding import PartitionSpec as P

epsilon = 1e-06
courant = 0.5
spacing = 0.05
turn_limit = 1.0
thrust_limit = 0.5
speed_low = 0.5
speed_high = 1.5
rim = 3
gain = 1.0 / (12.0 * spacing)


def inverse(value):
    return pltpu.reciprocal(value, approx=True)


def weights_of(e1, e2, turn, eps):
    level = turn * turn * (4.0 / 3.0) + eps
    ia = inverse(level + e2 * (e2 + turn))
    ib = inverse(level + e2 * e1)
    ic = inverse(level + e1 * (e1 - turn))
    return ia * ia, ib * ib * 6.0, ic * ic


def sides(fl, f0, fr, a2, a1, b1, b0, c0, c1):
    a3 = a1 * 3.0
    c3 = c0 * 3.0
    minus = ((fl + fl) * a2 + f0 * c3) * inverse(a2 + b1 + c3)
    plus = ((fr + fr) * c1 + f0 * a3) * inverse(c1 + b0 + a3)
    return minus, plus


def row_terms(cells, step, closed=False):
    eps = epsilon * step * step
    count = len(cells) if closed else len(cells) - 2 * rim
    shift = 0 if closed else rim
    slope = {m: cells[m + 1 + shift] - cells[m + shift] for m in range(-shift, count + shift - 1)}
    a, b, c = {}, {}, {}
    if closed:
        bend = {m: slope[m] - slope[m - 1] for m in range(1, count - 1)}
        bend[0], bend[count - 1] = slope[0], -slope[count - 2]
        turn = {m: bend[m + 1] - bend[m] for m in range(count - 1)}
        turn[-1], turn[count - 1] = bend[0], -bend[count - 1]
        jerk = {m: turn[m] - turn[m - 1] for m in range(count)}
        jerk[-1], jerk[count] = bend[0], bend[count - 1]
        rise = {m: slope[m] + slope[m - 1] for m in range(1, count - 1)}
        rise[0], rise[count - 1] = slope[0], slope[count - 2]
        a[-2] = c[count] = 1.0 / (eps * eps)
        for m, (e1, e2) in ((-1, (None, bend[0])), (count - 1, (bend[count - 1], None))):
            square = turn[m] * turn[m]
            level = square * (4.0 / 3.0) + eps
            ib, outer = inverse(level), inverse(level + (square + square))
            b[m] = ib * ib * 6.0
            (c if e2 is None else a)[m] = outer * outer
        inner = range(count - 1)
    else:
        bend = {m: slope[m] - slope[m - 1] for m in range(-2, count + 2)}
        turn = {m: bend[m + 1] - bend[m] for m in range(-2, count + 1)}
        jerk = {m: turn[m] - turn[m - 1] for m in range(-1, count + 1)}
        rise = {m: cells[m + 1 + rim] - cells[m - 1 + rim] for m in range(count)}
        inner = range(-2, count + 1)
    for m in inner:
        a[m], b[m], c[m] = weights_of(bend[m], bend[m + 1], turn[m], eps)
    out = []
    for i in range(count):
        base = rise[i] * 6.0 - (turn[i - 1] + turn[i])
        minus, plus = sides(
            jerk[i - 1], jerk[i], jerk[i + 1], a[i - 2], a[i - 1], b[i - 1], b[i], c[i], c[i + 1]
        )
        out.append((base + (plus - minus), (plus + minus) - jerk[i]))
    return out


def batches(total, most):
    return max(k for k in range(1, most + 1) if total % k == 0)


def splat(row, tile):
    return jnp.broadcast_to(row, tile)


def speeds_of(tile, speed_step):
    place = lax.broadcasted_iota(jnp.int32, tile, 0).astype(jnp.float32)
    return speed_low + place * speed_step


def odd_place(axis):
    return lax.rem(lax.axis_index(axis), 2) == 1


def put_extremes(wind_ref, most_ref):
    rows = [wind_ref[i] for i in range(wind_ref.shape[0])]
    most_ref[...] = jnp.zeros_like(most_ref)
    most_ref[0:2, :] = functools.reduce(jnp.maximum, rows)
    most_ref[2:4, :] = -functools.reduce(jnp.minimum, rows)


def extremes_kernel(wind_ref, most_ref):
    put_extremes(wind_ref, most_ref.at[0])


def opening_kernel(level_ref, x_near, x_far, t_near, t_far):
    cut_near(level_ref, x_near)
    cut_far(level_ref, x_far)
    cut_headings(level_ref, t_near, t_far)


def meeting_kernel(own_ref, other_ref, most_ref):
    most_ref[...] = jnp.maximum(own_ref[0], other_ref[0])


def flows_into(flow_ref, speed_step, wind_ref, waves_ref):
    planes, headings = flow_ref.shape[:2]
    tile = flow_ref.shape[2:]
    first = lax.axis_index("head") * headings
    pace = speeds_of(tile, speed_step) * gain
    tables = [
        splat(waves_ref[1, pl.ds(first + j, 1), :], tile) * pace for j in range(headings)
    ]
    for i in range(planes):
        wind = splat(wind_ref[i, 1:2, :] * gain, tile)
        for j in range(headings):
            flow_ref[i, j] = tables[j] + wind


def free_kernel(split, speed_step, s_ref, *rest):
    planes, headings, speeds, width = s_ref.shape
    cells = planes * headings

    def rows_of(ref):
        return ref.reshape(cells * speeds, width)

    if split:
        wind_ref, waves_ref, speed_ref, out_ref, extra_ref, flow_t_ref = rest[:6]
        turned_ref, drift_ref, gap_ref, flow_ref = rest[6:]
        flows_into(flow_ref, speed_step, wind_ref, waves_ref)
        extra_rows, flow_rows = rows_of(extra_ref), rows_of(flow_ref)
    else:
        flow_t_ref, pk_ref, speed_ref, out_ref, turned_ref, drift_ref = rest
        peak = splat(pk_ref[1:2, :] * gain, (speeds, width))
    gain_v = thrust_limit / (12.0 * speed_step)
    s_rows, speed_rows, out_rows = rows_of(s_ref), rows_of(speed_ref), rows_of(out_ref)
    few, many = 8, turned_ref.shape[2] // speeds
    groups = turned_ref.shape[0]
    lanes = many * speeds
    high = 8
    lines = width // high

    def along_speed(n):
        start = min(n * few, cells - few) * speeds
        spots = [pl.ds(start + v, few, stride=speeds) for v in range(speeds)]
        rows = [s_rows[spot, :] for spot in spots]
        for spot, (mean, gap) in zip(spots, row_terms(rows, speed_step, True)):
            speed_rows[spot, :] = gain_v * (gap - jnp.abs(mean))

    def span(n):
        return pl.ds(min(n * many, cells - many) * speeds, lanes)

    def turn_in(n):
        turned = s_rows[span(n), :].T
        turned_ref[n, rim : rim + width, :] = turned
        for k in range(rim):
            turned_ref[n, k : k + 1, :] = turned[:1]
            turned_ref[n, rim + width + k : rim + width + k + 1, :] = turned[-1:]
        if split:
            flow_t_ref[n] = flow_rows[span(n), :].T

    def along_y(n):
        ends = [turned_ref[n, pl.ds(k, high, stride=lines), :] for k in range(lines + 2 * rim)]
        for k, (mean, gap) in enumerate(row_terms(ends, spacing)):
            spot = pl.ds(k, high, stride=lines)
            drift = mean * flow_t_ref[n, spot, :]
            if split:
                drift_ref[n, spot, :] = drift
                gap_ref[n, spot, :] = gap
            else:
                drift_ref[n, spot, :] = drift + gap * peak

    def turn_out(n):
        out_rows[span(n), :] = drift_ref[n].T
        if split:
            extra_rows[span(n), :] = gap_ref[n].T

    turn_in(0)
    for n in range(groups):
        if n > 0:
            turn_out(n - 1)
        along_y(n)
        if n + 1 < groups:
            turn_in(n + 1)
        for k in (2 * n, 2 * n + 1):
            if k * few < cells:
                along_speed(k)
    turn_out(groups - 1)


def heading_kernel(heading_step, s_ref, speed_ref, part_ref, near_ref, far_ref, out_ref):
    planes, headings = s_ref.shape[:2]
    gain_t = turn_limit / (12.0 * heading_step)
    odd = odd_place("head")
    wide = batches(planes, 9)

    def step(n, carry):
        for w in range(wide):
            i = n * wide + w
            ghosts = [(near_ref[i * rim + k], far_ref[i * rim + k]) for k in range(rim)]
            lows = [jnp.where(odd, near, far) for near, far in ghosts]
            highs = [jnp.where(odd, far, near) for near, far in ghosts]
            cells = lows + [s_ref[i, j] for j in range(headings)] + highs
            for j, (mean, gap) in enumerate(row_terms(cells, heading_step)):
                own = speed_ref[i, j] + part_ref[i, j]
                out_ref[i, j] = own + gain_t * (gap - jnp.abs(mean))
        return carry

    lax.fori_loop(0, planes // wide, step, 0)


def peaks_into(pk_ref, most, bounds, heading_step, speed_step):
    most = jnp.max(most, axis=1, keepdims=True)
    peaks = [
        jnp.maximum(most[q : q + 1] + bounds[q][1], most[q + 2 : q + 3] - bounds[q][0])
        for q in range(2)
    ]
    time_step = courant / (
        peaks[0] / spacing
        + peaks[1] / spacing
        + turn_limit / heading_step
        + thrust_limit / speed_step
    )
    width = pk_ref.shape[1]
    for row, value in enumerate(peaks + [time_step]):
        pk_ref[row : row + 1, :] = splat(value, (1, width))


def plane_at(i, planes):
    return jnp.where(odd_place("gx"), i, planes - 1 - i)


def alone(reach):
    place, size = lax.axis_index("gx"), lax.axis_size("gx")
    if reach == 0:
        return (place == size - 1) if size % 2 else place < 0
    return (place == 0) | (place == size - 1) if size % 2 == 0 else place == 0


def cut_near(field_ref, x_near):
    planes, headings = field_ref.shape[:2]
    for k in range(rim):
        i = jnp.where(alone(0), 0, k)
        x_near[k * headings : (k + 1) * headings] = field_ref[plane_at(i, planes)]


def cut_far(field_ref, x_far):
    planes, headings = field_ref.shape[:2]
    for k in range(rim):
        i = planes - 1 - jnp.where(alone(1), 0, k)
        x_far[k * headings : (k + 1) * headings] = field_ref[plane_at(i, planes)]


def cut_headings(field_ref, t_near, t_far):
    planes, headings = field_ref.shape[:2]
    t_low = jnp.where(odd_place("head"), 0, headings - rim)
    for k in range(rim):
        for i in range(planes):
            t_near[i * rim + k] = field_ref[i, t_low + k]
            t_far[i * rim + k] = field_ref[i, headings - rim - t_low + k]


def splat_targets(mask_ref, depth_ref, target_ref):
    for i in range(target_ref.shape[0]):
        depth = depth_ref[i : i + 1, :]
        target = jnp.where(mask_ref[i : i + 1, :] == 1, -depth, depth)
        target_ref[i] = splat(target, target_ref.shape[1:])


def across_planes(
    span, speed_step, s_ref, near_ref, far_ref, wind_ref, waves_ref, flow_ref, use
):
    planes, headings = s_ref.shape[:2]
    tile = s_ref.shape[2:]
    side = jnp.where(odd_place("gx"), gain, -gain).astype(jnp.float32)
    spots = [plane_at(i, planes) for i in range(planes)]
    for i in range(planes):
        flow_ref[i] = splat(wind_ref[i, 0:1, :] * side, tile)
    pace = speeds_of(tile, speed_step) * side
    first = lax.axis_index("head") * headings
    low, high = span
    wide = batches(headings, max(1, 108 // (high - low)))

    def line(i, j):
        if i < 0:
            return near_ref[(-1 - i) * headings + j]
        if i >= planes:
            return far_ref[(i - planes) * headings + j]
        return s_ref[spots[i], j]

    def step(n, carry):
        for w in range(wide):
            j = n * wide + w
            cells = [line(i, j) for i in range(low - rim, high + rim)]
            table = splat(waves_ref[0, pl.ds(first + j, 1), :], tile) * pace
            for k, (mean, gap) in enumerate(row_terms(cells, spacing)):
                spot = spots[low + k]
                use(spot, j, mean * (table + flow_ref[spot]), gap, cells[k + rim])
        return carry

    lax.fori_loop(0, headings // wide, step, 0)


def first_kernel(
    speed_step, s_ref, part_ref, near_ref, far_ref, wind_ref, waves_ref, out_ref, gap_ref, flow_ref
):
    def use(i, j, drift, gap, cell):
        out_ref[i, j] = part_ref[i, j] + drift
        gap_ref[i, j] = gap

    across_planes(
        (0, s_ref.shape[0]), speed_step, s_ref, near_ref, far_ref, wind_ref, waves_ref, flow_ref, use
    )


def closing_kernel(
    bounds, heading_step, speed_step, s_ref, part_ref, gap_x_ref, gap_y_ref, mask_ref, depth_ref,
    most_ref, other_ref, out_ref, x_near, x_far, t_near, t_far, pk_ref, target_ref
):
    planes, headings = s_ref.shape[:2]
    tile = s_ref.shape[2:]
    most = jnp.maximum(most_ref[...], other_ref[...])
    peaks_into(pk_ref, most, bounds, heading_step, speed_step)
    splat_targets(mask_ref, depth_ref, target_ref)
    peak_x = splat(pk_ref[0:1, :] * gain, tile)
    peak_y = splat(pk_ref[1:2, :] * gain, tile)
    time_step = splat(pk_ref[2:3, :], tile)

    wide = batches(planes, 3)

    def step(n, carry):
        for w in range(wide):
            i = n * wide + w
            for j in range(headings):
                rate = part_ref[i, j] + (gap_x_ref[i, j] * peak_x + gap_y_ref[i, j] * peak_y)
                out_ref[i, j] = jnp.minimum(s_ref[i, j] + time_step * rate, target_ref[i])
        return carry

    lax.fori_loop(0, planes // wide, step, 0)
    cut_near(out_ref, x_near)
    cut_far(out_ref, x_far)
    cut_headings(out_ref, t_near, t_far)


def section_kernel(
    section, span, speed_step, base_ref, s_ref, part_ref, ghosts_ref, wind_ref, waves_ref,
    mask_ref, depth_ref, pk_ref, *refs
):
    planes = s_ref.shape[0]
    refs, (flow_ref, target_ref) = list(refs[:-2]), refs[-2:]
    early_ref = refs.pop(0) if span[0] > 0 else None
    out_ref = refs.pop(0)
    tile = s_ref.shape[2:]
    splat_targets(mask_ref, depth_ref, target_ref)
    peak_x = splat(pk_ref[0:1, :] * gain, tile)
    time_step = splat(pk_ref[2:3, :], tile)
    base_share = 0.75 if section == 2 else 1.0 / 3.0
    own_share = 0.25 if section == 2 else 2.0 / 3.0

    def use(i, j, drift, gap, cell):
        rate = part_ref[i, j] + (drift + gap * peak_x)
        moved = base_share * base_ref[i, j] + own_share * (cell + time_step * rate)
        out_ref[i, j] = jnp.minimum(moved, target_ref[i])

    near_ref, far_ref = (None, ghosts_ref) if span[0] > 0 else (ghosts_ref, None)
    across_planes(
        span, speed_step, s_ref, near_ref, far_ref, wind_ref, waves_ref, flow_ref, use
    )
    for i in range(span[0]):
        spot = plane_at(i, planes)
        out_ref[spot] = early_ref[spot]
    if section == 2 and span[0] == 0:
        cut_near(out_ref, *refs)
    elif section == 2:
        cut_far(out_ref, refs[0])
        cut_headings(out_ref, *refs[1:])


def trade(value, axis, reach, wrap=False):
    size = lax.axis_size(axis)
    pairs = [(i, i + 1) for i in range(reach, size - 1, 2)]
    if wrap and reach and size % 2 == 0:
        pairs.append((size - 1, 0))
    pairs += [(j, i) for i, j in pairs]
    pairs += [(i, i) for i in range(size) if i not in dict(pairs)]
    return lax.ppermute(value, axis, pairs)


def local(level_set, wind_field, target_mask, target_depth):
    planes, headings, speed_count, cross_count = level_set.shape
    heading_total = headings * lax.axis_size("head")
    heading_step = 2.0 * math.pi / heading_total
    speed_step = (speed_high - speed_low) / (speed_count - 1)
    speed_row = np.float32(speed_low) + np.arange(speed_count, dtype=np.float32) * np.float32(
        speed_step
    )
    angles = np.arange(heading_total, dtype=np.float32) * np.float32(heading_step)
    waves = [np.cos(angles), np.sin(angles)]
    bounds = []
    for wave in waves:
        product = wave[:, None] * speed_row[None, :]
        bounds.append((float(product.min()), float(product.max())))
    waves = jnp.asarray(np.stack(waves)[..., None] * np.ones(cross_count, np.float32))

    vmem = pl.BlockSpec(memory_space=pltpu.VMEM)
    tile = (speed_count, cross_count)

    def shape(*dims):
        return jax.ShapeDtypeStruct(dims + tile, jnp.float32)

    field = shape(planes, headings)
    short = rim * headings
    middle = max(short + 1, rim * planes)

    longest = middle + 1
    rows = pltpu.VMEM((planes,) + tile, jnp.float32)
    cells = math.prod(level_set.shape)

    def call(kernel, ins, outs, scratch=(), work=0):
        return pl.pallas_call(
            kernel,
            out_shape=outs,
            in_specs=[vmem] * len(ins),
            out_specs=[vmem] * len(outs),
            scratch_shapes=list(scratch),
            compiler_params=pltpu.CompilerParams(vmem_limit_bytes=16 * 1024 * 1024),
            cost_estimate=pl.CostEstimate(
                flops=work * cells, bytes_accessed=work * cells, transcendentals=0
            ),
        )(*ins)

    wind = jnp.transpose(wind_field, (1, 0, 2))
    many = 16
    groups, lanes = -(-planes * headings // many), many * speed_count
    turned = (groups, cross_count, lanes)
    room = [
        pltpu.VMEM((groups, cross_count + 8, lanes), jnp.float32),
        pltpu.VMEM(turned, jnp.float32),
    ]
    wide_room = room + [pltpu.VMEM(turned, jnp.float32), pltpu.VMEM(level_set.shape, jnp.float32)]
    values = level_set
    size = lax.axis_size("gx")

    def spread(most, reach):
        if size & (size - 1):
            pairs = [(i, (i + reach) % size) for i in range(size)]
        else:
            pairs = [(i, i ^ reach) for i in range(size)]
        return lax.ppermute(most, "gx", pairs)

    (most,) = call(extremes_kernel, [wind], [shape(longest + 2)])
    other = spread(most, 1)
    x_shapes = [shape(longest), shape(longest + 1)]
    x_out, x_last, t_out, t_last = call(opening_kernel, [values], x_shapes + [shape(middle)] * 2)
    far_shapes = [shape(short), shape(rim * planes), shape(middle)]
    for section in (1, 2, 3):
        opening = section == 1
        x_near = trade(x_out, "gx", 0)
        t_near = trade(t_out, "head", 0)
        t_far = trade(t_last, "head", 1, True)
        x_far = trade(x_last, "gx", 1)
        free = functools.partial(free_kernel, opening, speed_step)
        turning = functools.partial(heading_kernel, heading_step)
        if opening:
            (most,) = call(meeting_kernel, [most, other], [shape()])
            other = spread(most, 2)
            ins = [values, wind, waves]
            spun, part, extra, flow = call(
                free, ins, [field] * 3 + [jax.ShapeDtypeStruct(turned, jnp.float32)], wide_room, work=300
            )
            reach = 4
            while reach < size:
                most = jnp.maximum(most, other)
                most, part = lax.optimization_barrier((most, part))
                other = spread(most, reach)
                reach *= 2
        else:
            if section == 3:
                values, x_near = lax.optimization_barrier((values, x_near))
            spun, part = call(free, [values, flow, pk], [field] * 2, room)
            if section == 2:
                part, x_near = lax.optimization_barrier((part, x_near))
        weight = 0 if opening else 1000
        (part,) = call(turning, [values, spun, part, t_near, t_far], [field], work=weight)
        if opening:
            ins = [values, part, x_near, x_far, wind, waves]
            first = functools.partial(first_kernel, speed_step)
            part, gap = call(first, ins, [field] * 2, [rows])
            closing = functools.partial(closing_kernel, bounds, heading_step, speed_step)
            ins = [values, part, gap, extra, target_mask, target_depth, most, other]
            outs = [field, shape(longest), *far_shapes, shape()]
            values, x_out, x_last, t_out, t_last, pk = call(closing, ins, outs, [rows])
        else:
            more = section == 2
            ins = [level_set, values, part, x_near, wind, waves, target_mask, target_depth, pk]
            outs = [field] + ([shape(longest)] if more else [])
            last = functools.partial(section_kernel, section, (0, planes - rim), speed_step)
            early, *x_next = call(last, ins, outs, [rows, rows])
            ins = ins[:3] + [x_far] + ins[4:] + [early]
            outs = [field] + (far_shapes if more else [])
            last = functools.partial(section_kernel, section, (planes - rim, planes), speed_step)
            values, *far_next = call(last, ins, outs, [rows, rows])
            if more:
                (x_out,), (x_last, t_out, t_last) = x_next, far_next
    return values


def solution(mesh):
    return jax.shard_map(
        local,
        mesh=mesh,
        in_specs=(P("gx", "head", None, None), P(None, "gx", None), P("gx", None), P("gx", None)),
        out_specs=P("gx", "head", None, None),
        check_vma=False,
    )
```

```python
import functools
import math

import jax
import jax.numpy as jnp
import numpy as np
from jax import lax
from jax.experimental import pallas as pl
from jax.experimental.pallas import tpu as pltpu
from jax.sharding import PartitionSpec as P

epsilon = 1e-06
courant = 0.5
spacing = 0.05
turn_limit = 1.0
thrust_limit = 0.5
speed_low = 0.5
speed_high = 1.5
rim = 3
gain = 1.0 / (12.0 * spacing)


def inverse(value):
    return pltpu.reciprocal(value, approx=True)


def weights_of(e1, e2, turn, eps):
    level = turn * turn * (4.0 / 3.0) + eps
    ia = inverse(level + e2 * (e2 + turn))
    ib = inverse(level + e2 * e1)
    ic = inverse(level + e1 * (e1 - turn))
    return ia * ia, ib * ib * 6.0, ic * ic


def sides(fl, f0, fr, a2, a1, b1, b0, c0, c1):
    a3 = a1 * 3.0
    c3 = c0 * 3.0
    minus = ((fl + fl) * a2 + f0 * c3) * inverse(a2 + b1 + c3)
    plus = ((fr + fr) * c1 + f0 * a3) * inverse(c1 + b0 + a3)
    return minus, plus


def row_terms(cells, step, closed=False):
    eps = epsilon * step * step
    count = len(cells) if closed else len(cells) - 2 * rim
    shift = 0 if closed else rim
    slope = {m: cells[m + 1 + shift] - cells[m + shift] for m in range(-shift, count + shift - 1)}
    a, b, c = {}, {}, {}
    if closed:
        bend = {m: slope[m] - slope[m - 1] for m in range(1, count - 1)}
        bend[0], bend[count - 1] = slope[0], -slope[count - 2]
        turn = {m: bend[m + 1] - bend[m] for m in range(count - 1)}
        turn[-1], turn[count - 1] = bend[0], -bend[count - 1]
        jerk = {m: turn[m] - turn[m - 1] for m in range(count)}
        jerk[-1], jerk[count] = bend[0], bend[count - 1]
        rise = {m: slope[m] + slope[m - 1] for m in range(1, count - 1)}
        rise[0], rise[count - 1] = slope[0], slope[count - 2]
        a[-2] = c[count] = 1.0 / (eps * eps)
        for m, (e1, e2) in ((-1, (None, bend[0])), (count - 1, (bend[count - 1], None))):
            square = turn[m] * turn[m]
            level = square * (4.0 / 3.0) + eps
            ib, outer = inverse(level), inverse(level + (square + square))
            b[m] = ib * ib * 6.0
            (c if e2 is None else a)[m] = outer * outer
        inner = range(count - 1)
    else:
        bend = {m: slope[m] - slope[m - 1] for m in range(-2, count + 2)}
        turn = {m: bend[m + 1] - bend[m] for m in range(-2, count + 1)}
        jerk = {m: turn[m] - turn[m - 1] for m in range(-1, count + 1)}
        rise = {m: cells[m + 1 + rim] - cells[m - 1 + rim] for m in range(count)}
        inner = range(-2, count + 1)
    for m in inner:
        a[m], b[m], c[m] = weights_of(bend[m], bend[m + 1], turn[m], eps)
    out = []
    for i in range(count):
        base = rise[i] * 6.0 - (turn[i - 1] + turn[i])
        minus, plus = sides(
            jerk[i - 1], jerk[i], jerk[i + 1], a[i - 2], a[i - 1], b[i - 1], b[i], c[i], c[i + 1]
        )
        out.append((base + (plus - minus), (plus + minus) - jerk[i]))
    return out


def batches(total, most):
    return max(k for k in range(1, most + 1) if total % k == 0)


def repeat(count, step):
    if count == 1:
        step(0, 0)
    else:
        lax.fori_loop(0, count, step, 0)


def splat(row, tile):
    return jnp.broadcast_to(row, tile)


def speeds_of(tile, speed_step):
    place = lax.broadcasted_iota(jnp.int32, tile, 0).astype(jnp.float32)
    return speed_low + place * speed_step


def odd_place(axis):
    return lax.rem(lax.axis_index(axis), 2) == 1


def put_extremes(wind_ref, most_ref):
    rows = [wind_ref[i] for i in range(wind_ref.shape[0])]
    most_ref[...] = jnp.zeros_like(most_ref)
    most_ref[0:2, :] = functools.reduce(jnp.maximum, rows)
    most_ref[2:4, :] = -functools.reduce(jnp.minimum, rows)


def extremes_kernel(wind_ref, most_ref):
    put_extremes(wind_ref, most_ref.at[0])


def opening_kernel(level_ref, x_near, x_far, t_near, t_far):
    cut_near(level_ref, x_near)
    cut_far(level_ref, x_far)
    cut_headings(level_ref, t_near, t_far)


def meeting_kernel(own_ref, other_ref, most_ref):
    most_ref[...] = jnp.maximum(own_ref[0], other_ref[0])


def flows_into(flow_ref, speed_step, wind_ref, waves_ref):
    planes, headings = flow_ref.shape[:2]
    tile = flow_ref.shape[2:]
    first = lax.axis_index("head") * headings
    pace = speeds_of(tile, speed_step) * gain
    tables = [
        splat(waves_ref[1, pl.ds(first + j, 1), :], tile) * pace for j in range(headings)
    ]
    for i in range(planes):
        wind = splat(wind_ref[i, 1:2, :] * gain, tile)
        for j in range(headings):
            flow_ref[i, j] = tables[j] + wind


def free_kernel(split, speed_step, s_ref, *rest):
    planes, headings, speeds, width = s_ref.shape
    cells = planes * headings

    def rows_of(ref):
        return ref.reshape(cells * speeds, width)

    if split:
        wind_ref, waves_ref, speed_ref, out_ref, extra_ref, flow_t_ref = rest[:6]
        turned_ref, drift_ref, gap_ref, flow_ref = rest[6:]
        flows_into(flow_ref, speed_step, wind_ref, waves_ref)
        extra_rows, flow_rows = rows_of(extra_ref), rows_of(flow_ref)
    else:
        flow_t_ref, pk_ref, speed_ref, out_ref, turned_ref, drift_ref = rest
        peak = splat(pk_ref[1:2, :] * gain, (speeds, width))
    gain_v = thrust_limit / (12.0 * speed_step)
    s_rows, speed_rows, out_rows = rows_of(s_ref), rows_of(speed_ref), rows_of(out_ref)
    few, many = 8, turned_ref.shape[2] // speeds
    groups = turned_ref.shape[0]
    lanes = many * speeds
    high = 8
    lines = width // high

    def along_speed(n):
        start = min(n * few, cells - few) * speeds
        spots = [pl.ds(start + v, few, stride=speeds) for v in range(speeds)]
        rows = [s_rows[spot, :] for spot in spots]
        for spot, (mean, gap) in zip(spots, row_terms(rows, speed_step, True)):
            speed_rows[spot, :] = gain_v * (gap - jnp.abs(mean))

    def span(n):
        return pl.ds(min(n * many, cells - many) * speeds, lanes)

    def turn_in(n):
        turned = s_rows[span(n), :].T
        turned_ref[n, rim : rim + width, :] = turned
        for k in range(rim):
            turned_ref[n, k : k + 1, :] = turned[:1]
            turned_ref[n, rim + width + k : rim + width + k + 1, :] = turned[-1:]
        if split:
            flow_t_ref[n] = flow_rows[span(n), :].T

    def along_y(n):
        ends = [turned_ref[n, pl.ds(k, high, stride=lines), :] for k in range(lines + 2 * rim)]
        for k, (mean, gap) in enumerate(row_terms(ends, spacing)):
            spot = pl.ds(k, high, stride=lines)
            drift = mean * flow_t_ref[n, spot, :]
            if split:
                drift_ref[n, spot, :] = drift
                gap_ref[n, spot, :] = gap
            else:
                drift_ref[n, spot, :] = drift + gap * peak

    def turn_out(n):
        out_rows[span(n), :] = drift_ref[n].T
        if split:
            extra_rows[span(n), :] = gap_ref[n].T

    turn_in(0)
    for n in range(groups):
        if n > 0:
            turn_out(n - 1)
        along_y(n)
        if n + 1 < groups:
            turn_in(n + 1)
        for k in (2 * n, 2 * n + 1):
            if k * few < cells:
                along_speed(k)
    turn_out(groups - 1)


def heading_kernel(heading_step, s_ref, speed_ref, part_ref, near_ref, far_ref, out_ref):
    planes, headings = s_ref.shape[:2]
    gain_t = turn_limit / (12.0 * heading_step)
    odd = odd_place("head")
    wide = batches(planes, 9)

    def step(n, carry):
        for w in range(wide):
            i = n * wide + w
            ghosts = [(near_ref[i * rim + k], far_ref[i * rim + k]) for k in range(rim)]
            lows = [jnp.where(odd, near, far) for near, far in ghosts]
            highs = [jnp.where(odd, far, near) for near, far in ghosts]
            cells = lows + [s_ref[i, j] for j in range(headings)] + highs
            for j, (mean, gap) in enumerate(row_terms(cells, heading_step)):
                own = speed_ref[i, j] + part_ref[i, j]
                out_ref[i, j] = own + gain_t * (gap - jnp.abs(mean))
        return carry

    repeat(planes // wide, step)


def peaks_into(pk_ref, most, bounds, heading_step, speed_step):
    most = jnp.max(most, axis=1, keepdims=True)
    peaks = [
        jnp.maximum(most[q : q + 1] + bounds[q][1], most[q + 2 : q + 3] - bounds[q][0])
        for q in range(2)
    ]
    time_step = courant / (
        peaks[0] / spacing
        + peaks[1] / spacing
        + turn_limit / heading_step
        + thrust_limit / speed_step
    )
    width = pk_ref.shape[1]
    for row, value in enumerate(peaks + [time_step]):
        pk_ref[row : row + 1, :] = splat(value, (1, width))


def plane_at(i, planes):
    return jnp.where(odd_place("gx"), i, planes - 1 - i)


def alone(reach):
    place, size = lax.axis_index("gx"), lax.axis_size("gx")
    if reach == 0:
        return (place == size - 1) if size % 2 else place < 0
    return (place == 0) | (place == size - 1) if size % 2 == 0 else place == 0


def cut_near(field_ref, x_near):
    planes, headings = field_ref.shape[:2]
    for k in range(rim):
        i = jnp.where(alone(0), 0, k)
        x_near[k * headings : (k + 1) * headings] = field_ref[plane_at(i, planes)]


def cut_far(field_ref, x_far):
    planes, headings = field_ref.shape[:2]
    for k in range(rim):
        i = planes - 1 - jnp.where(alone(1), 0, k)
        x_far[k * headings : (k + 1) * headings] = field_ref[plane_at(i, planes)]


def cut_headings(field_ref, t_near, t_far):
    planes, headings = field_ref.shape[:2]
    t_low = jnp.where(odd_place("head"), 0, headings - rim)
    for k in range(rim):
        for i in range(planes):
            t_near[i * rim + k] = field_ref[i, t_low + k]
            t_far[i * rim + k] = field_ref[i, headings - rim - t_low + k]


def splat_targets(mask_ref, depth_ref, target_ref):
    for i in range(target_ref.shape[0]):
        depth = depth_ref[i : i + 1, :]
        target = jnp.where(mask_ref[i : i + 1, :] == 1, -depth, depth)
        target_ref[i] = splat(target, target_ref.shape[1:])


def across_planes(
    span, speed_step, s_ref, near_ref, far_ref, wind_ref, waves_ref, flow_ref, use
):
    planes, headings = s_ref.shape[:2]
    tile = s_ref.shape[2:]
    side = jnp.where(odd_place("gx"), gain, -gain).astype(jnp.float32)
    spots = [plane_at(i, planes) for i in range(planes)]
    for i in range(planes):
        flow_ref[i] = splat(wind_ref[i, 0:1, :] * side, tile)
    pace = speeds_of(tile, speed_step) * side
    first = lax.axis_index("head") * headings
    low, high = span
    wide = batches(headings, max(1, 108 // (high - low)))

    def line(i, j):
        if i < 0:
            return near_ref[(-1 - i) * headings + j]
        if i >= planes:
            return far_ref[(i - planes) * headings + j]
        return s_ref[spots[i], j]

    def step(n, carry):
        for w in range(wide):
            j = n * wide + w
            cells = [line(i, j) for i in range(low - rim, high + rim)]
            table = splat(waves_ref[0, pl.ds(first + j, 1), :], tile) * pace
            for k, (mean, gap) in enumerate(row_terms(cells, spacing)):
                spot = spots[low + k]
                use(spot, j, mean * (table + flow_ref[spot]), gap, cells[k + rim])
        return carry

    repeat(headings // wide, step)


def first_kernel(
    speed_step, s_ref, part_ref, near_ref, far_ref, wind_ref, waves_ref, out_ref, gap_ref, flow_ref
):
    def use(i, j, drift, gap, cell):
        out_ref[i, j] = part_ref[i, j] + drift
        gap_ref[i, j] = gap

    across_planes(
        (0, s_ref.shape[0]), speed_step, s_ref, near_ref, far_ref, wind_ref, waves_ref, flow_ref, use
    )


def closing_kernel(
    bounds, heading_step, speed_step, s_ref, part_ref, gap_x_ref, gap_y_ref, mask_ref, depth_ref,
    most_ref, other_ref, out_ref, x_near, x_far, t_near, t_far, pk_ref, target_ref
):
    planes, headings = s_ref.shape[:2]
    tile = s_ref.shape[2:]
    most = jnp.maximum(most_ref[...], other_ref[...])
    peaks_into(pk_ref, most, bounds, heading_step, speed_step)
    splat_targets(mask_ref, depth_ref, target_ref)
    peak_x = splat(pk_ref[0:1, :] * gain, tile)
    peak_y = splat(pk_ref[1:2, :] * gain, tile)
    time_step = splat(pk_ref[2:3, :], tile)

    wide = batches(planes, 3)

    def step(n, carry):
        for w in range(wide):
            i = n * wide + w
            for j in range(headings):
                rate = part_ref[i, j] + (gap_x_ref[i, j] * peak_x + gap_y_ref[i, j] * peak_y)
                out_ref[i, j] = jnp.minimum(s_ref[i, j] + time_step * rate, target_ref[i])
        return carry

    repeat(planes // wide, step)
    cut_near(out_ref, x_near)
    cut_far(out_ref, x_far)
    cut_headings(out_ref, t_near, t_far)


def section_kernel(
    section, span, speed_step, base_ref, s_ref, part_ref, ghosts_ref, wind_ref, waves_ref,
    mask_ref, depth_ref, pk_ref, *refs
):
    planes = s_ref.shape[0]
    refs, (flow_ref, target_ref) = list(refs[:-2]), refs[-2:]
    early_ref = refs.pop(0) if span[0] > 0 else None
    out_ref = refs.pop(0)
    tile = s_ref.shape[2:]
    splat_targets(mask_ref, depth_ref, target_ref)
    peak_x = splat(pk_ref[0:1, :] * gain, tile)
    time_step = splat(pk_ref[2:3, :], tile)
    base_share = 0.75 if section == 2 else 1.0 / 3.0
    own_share = 0.25 if section == 2 else 2.0 / 3.0

    def use(i, j, drift, gap, cell):
        rate = part_ref[i, j] + (drift + gap * peak_x)
        moved = base_share * base_ref[i, j] + own_share * (cell + time_step * rate)
        out_ref[i, j] = jnp.minimum(moved, target_ref[i])

    for i in range(span[0]):
        spot = plane_at(i, planes)
        out_ref[spot] = early_ref[spot]
    near_ref, far_ref = (None, ghosts_ref) if span[0] > 0 else (ghosts_ref, None)
    across_planes(
        span, speed_step, s_ref, near_ref, far_ref, wind_ref, waves_ref, flow_ref, use
    )
    if section == 2 and span[0] == 0:
        cut_near(out_ref, *refs)
    elif section == 2:
        cut_far(out_ref, refs[0])
        cut_headings(out_ref, *refs[1:])


def trade(value, axis, reach, wrap=False):
    size = lax.axis_size(axis)
    pairs = [(i, i + 1) for i in range(reach, size - 1, 2)]
    if wrap and reach and size % 2 == 0:
        pairs.append((size - 1, 0))
    pairs += [(j, i) for i, j in pairs]
    pairs += [(i, i) for i in range(size) if i not in dict(pairs)]
    return lax.ppermute(value, axis, pairs)


def local(level_set, wind_field, target_mask, target_depth):
    planes, headings, speed_count, cross_count = level_set.shape
    heading_total = headings * lax.axis_size("head")
    heading_step = 2.0 * math.pi / heading_total
    speed_step = (speed_high - speed_low) / (speed_count - 1)
    speed_row = np.float32(speed_low) + np.arange(speed_count, dtype=np.float32) * np.float32(
        speed_step
    )
    angles = np.arange(heading_total, dtype=np.float32) * np.float32(heading_step)
    waves = [np.cos(angles), np.sin(angles)]
    bounds = []
    for wave in waves:
        product = wave[:, None] * speed_row[None, :]
        bounds.append((float(product.min()), float(product.max())))
    waves = jnp.asarray(np.stack(waves)[..., None] * np.ones(cross_count, np.float32))

    vmem = pl.BlockSpec(memory_space=pltpu.VMEM)
    tile = (speed_count, cross_count)

    def shape(*dims):
        return jax.ShapeDtypeStruct(dims + tile, jnp.float32)

    field = shape(planes, headings)
    short = rim * headings
    middle = max(short + 1, rim * planes)

    longest = middle + 1
    rows = pltpu.VMEM((planes,) + tile, jnp.float32)
    cells = math.prod(level_set.shape)

    def call(kernel, ins, outs, scratch=(), work=0):
        return pl.pallas_call(
            kernel,
            out_shape=outs,
            in_specs=[vmem] * len(ins),
            out_specs=[vmem] * len(outs),
            scratch_shapes=list(scratch),
            compiler_params=pltpu.CompilerParams(vmem_limit_bytes=16 * 1024 * 1024),
            cost_estimate=pl.CostEstimate(
                flops=work * cells, bytes_accessed=work * cells, transcendentals=0
            ),
        )(*ins)

    wind = jnp.transpose(wind_field, (1, 0, 2))
    many = 16
    groups, lanes = -(-planes * headings // many), many * speed_count
    turned = (groups, cross_count, lanes)
    room = [
        pltpu.VMEM((groups, cross_count + 8, lanes), jnp.float32),
        pltpu.VMEM(turned, jnp.float32),
    ]
    wide_room = room + [pltpu.VMEM(turned, jnp.float32), pltpu.VMEM(level_set.shape, jnp.float32)]
    values = level_set
    size = lax.axis_size("gx")

    def spread(most, reach):
        if size & (size - 1):
            pairs = [(i, (i + reach) % size) for i in range(size)]
        else:
            pairs = [(i, i ^ reach) for i in range(size)]
        return lax.ppermute(most, "gx", pairs)

    (most,) = call(extremes_kernel, [wind], [shape(longest + 2)])
    other = spread(most, 1)
    x_shapes = [shape(longest), shape(longest + 1)]
    x_out, x_last, t_out, t_last = call(opening_kernel, [values], x_shapes + [shape(middle)] * 2)
    far_shapes = [shape(short), shape(rim * planes), shape(middle)]
    for section in (1, 2, 3):
        opening = section == 1
        x_near = trade(x_out, "gx", 0)
        t_near = trade(t_out, "head", 0)
        t_far = trade(t_last, "head", 1, True)
        x_far = trade(x_last, "gx", 1)
        free = functools.partial(free_kernel, opening, speed_step)
        turning = functools.partial(heading_kernel, heading_step)
        if opening:
            (most,) = call(meeting_kernel, [most, other], [shape()])
            other = spread(most, 2)
            ins = [values, wind, waves]
            spun, part, extra, flow = call(
                free, ins, [field] * 3 + [jax.ShapeDtypeStruct(turned, jnp.float32)], wide_room, work=300
            )
            reach = 4
            while reach < size:
                most = jnp.maximum(most, other)
                most, part = lax.optimization_barrier((most, part))
                other = spread(most, reach)
                reach *= 2
        else:
            if section == 3:
                values, x_near = lax.optimization_barrier((values, x_near))
            spun, part = call(free, [values, flow, pk], [field] * 2, room)
            if section == 2:
                part, x_near = lax.optimization_barrier((part, x_near))
        weight = 0 if opening else 1000
        (part,) = call(turning, [values, spun, part, t_near, t_far], [field], work=weight)
        if opening:
            ins = [values, part, x_near, x_far, wind, waves]
            first = functools.partial(first_kernel, speed_step)
            part, gap = call(first, ins, [field] * 2, [rows])
            closing = functools.partial(closing_kernel, bounds, heading_step, speed_step)
            ins = [values, part, gap, extra, target_mask, target_depth, most, other]
            outs = [field, shape(longest), *far_shapes, shape()]
            values, x_out, x_last, t_out, t_last, pk = call(closing, ins, outs, [rows])
        else:
            more = section == 2
            ins = [level_set, values, part, x_near, wind, waves, target_mask, target_depth, pk]
            outs = [field] + ([shape(longest)] if more else [])
            last = functools.partial(section_kernel, section, (0, planes - rim), speed_step)
            early, *x_next = call(last, ins, outs, [rows, rows])
            ins = ins[:3] + [x_far] + ins[4:] + [early]
            outs = [field] + (far_shapes if more else [])
            last = functools.partial(section_kernel, section, (planes - rim, planes), speed_step)
            values, *far_next = call(last, ins, outs, [rows, rows])
            if more:
                (x_out,), (x_last, t_out, t_last) = x_next, far_next
    return values


def solution(mesh):
    return jax.shard_map(
        local,
        mesh=mesh,
        in_specs=(P("gx", "head", None, None), P(None, "gx", None), P("gx", None), P("gx", None)),
        out_specs=P("gx", "head", None, None),
        check_vma=False,
    )
```

```python
import functools
import math

import jax
import jax.numpy as jnp
import numpy as np
from jax import lax
from jax.experimental import pallas as pl
from jax.experimental.pallas import tpu as pltpu
from jax.sharding import PartitionSpec as P

epsilon = 1e-06
courant = 0.5
spacing = 0.05
turn_limit = 1.0
thrust_limit = 0.5
speed_low = 0.5
speed_high = 1.5
rim = 3
gain = 1.0 / (12.0 * spacing)


def inverse(value):
    return pltpu.reciprocal(value, approx=True)


def weights_of(e1, e2, turn, eps):
    level = turn * turn * (4.0 / 3.0) + eps
    ia = inverse(level + e2 * (e2 + turn))
    ib = inverse(level + e2 * e1)
    ic = inverse(level + e1 * (e1 - turn))
    return ia * ia, ib * ib * 6.0, ic * ic


def sides(fl, f0, fr, a2, a1, b1, b0, c0, c1):
    a3 = a1 * 3.0
    c3 = c0 * 3.0
    minus = ((fl + fl) * a2 + f0 * c3) * inverse(a2 + b1 + c3)
    plus = ((fr + fr) * c1 + f0 * a3) * inverse(c1 + b0 + a3)
    return minus, plus


def row_terms(cells, step, closed=False):
    eps = epsilon * step * step
    count = len(cells) if closed else len(cells) - 2 * rim
    shift = 0 if closed else rim
    slope = {m: cells[m + 1 + shift] - cells[m + shift] for m in range(-shift, count + shift - 1)}
    a, b, c = {}, {}, {}
    if closed:
        bend = {m: slope[m] - slope[m - 1] for m in range(1, count - 1)}
        bend[0], bend[count - 1] = slope[0], -slope[count - 2]
        turn = {m: bend[m + 1] - bend[m] for m in range(count - 1)}
        turn[-1], turn[count - 1] = bend[0], -bend[count - 1]
        jerk = {m: turn[m] - turn[m - 1] for m in range(count)}
        jerk[-1], jerk[count] = bend[0], bend[count - 1]
        rise = {m: slope[m] + slope[m - 1] for m in range(1, count - 1)}
        rise[0], rise[count - 1] = slope[0], slope[count - 2]
        a[-2] = c[count] = 1.0 / (eps * eps)
        for m, (e1, e2) in ((-1, (None, bend[0])), (count - 1, (bend[count - 1], None))):
            square = turn[m] * turn[m]
            level = square * (4.0 / 3.0) + eps
            ib, outer = inverse(level), inverse(level + (square + square))
            b[m] = ib * ib * 6.0
            (c if e2 is None else a)[m] = outer * outer
        inner = range(count - 1)
    else:
        bend = {m: slope[m] - slope[m - 1] for m in range(-2, count + 2)}
        turn = {m: bend[m + 1] - bend[m] for m in range(-2, count + 1)}
        jerk = {m: turn[m] - turn[m - 1] for m in range(-1, count + 1)}
        rise = {m: cells[m + 1 + rim] - cells[m - 1 + rim] for m in range(count)}
        inner = range(-2, count + 1)
    for m in inner:
        a[m], b[m], c[m] = weights_of(bend[m], bend[m + 1], turn[m], eps)
    out = []
    for i in range(count):
        base = rise[i] * 6.0 - (turn[i - 1] + turn[i])
        minus, plus = sides(
            jerk[i - 1], jerk[i], jerk[i + 1], a[i - 2], a[i - 1], b[i - 1], b[i], c[i], c[i + 1]
        )
        out.append((base + (plus - minus), (plus + minus) - jerk[i]))
    return out


def batches(total, most):
    return max(k for k in range(1, most + 1) if total % k == 0)


def splat(row, tile):
    return jnp.broadcast_to(row, tile)


def speeds_of(tile, speed_step):
    place = lax.broadcasted_iota(jnp.int32, tile, 0).astype(jnp.float32)
    return speed_low + place * speed_step


def odd_place(axis):
    return lax.rem(lax.axis_index(axis), 2) == 1


def put_extremes(wind_ref, most_ref):
    rows = [wind_ref[i] for i in range(wind_ref.shape[0])]
    most_ref[...] = jnp.zeros_like(most_ref)
    most_ref[0:2, :] = functools.reduce(jnp.maximum, rows)
    most_ref[2:4, :] = -functools.reduce(jnp.minimum, rows)


def extremes_kernel(wind_ref, most_ref):
    put_extremes(wind_ref, most_ref.at[0])


def opening_kernel(level_ref, x_near, x_far, t_near, t_far):
    cut_near(level_ref, x_near)
    cut_far(level_ref, x_far)
    cut_headings(level_ref, t_near, t_far)


def meeting_kernel(own_ref, other_ref, most_ref):
    most_ref[...] = jnp.maximum(own_ref[0], other_ref[0])


def flows_into(flow_ref, speed_step, wind_ref, waves_ref):
    planes, headings = flow_ref.shape[:2]
    tile = flow_ref.shape[2:]
    first = lax.axis_index("head") * headings
    pace = speeds_of(tile, speed_step) * gain
    tables = [
        splat(waves_ref[1, pl.ds(first + j, 1), :], tile) * pace for j in range(headings)
    ]
    for i in range(planes):
        wind = splat(wind_ref[i, 1:2, :] * gain, tile)
        for j in range(headings):
            flow_ref[i, j] = tables[j] + wind


def free_kernel(split, speed_step, s_ref, *rest):
    planes, headings, speeds, width = s_ref.shape
    cells = planes * headings

    def rows_of(ref):
        return ref.reshape(cells * speeds, width)

    if split:
        wind_ref, waves_ref, speed_ref, out_ref, extra_ref, flow_t_ref = rest[:6]
        turned_ref, drift_ref, gap_ref, flow_ref = rest[6:]
        flows_into(flow_ref, speed_step, wind_ref, waves_ref)
        extra_rows, flow_rows = rows_of(extra_ref), rows_of(flow_ref)
    else:
        flow_t_ref, pk_ref, speed_ref, out_ref, turned_ref, drift_ref = rest
        peak = splat(pk_ref[1:2, :] * gain, (speeds, width))
    gain_v = thrust_limit / (12.0 * speed_step)
    s_rows, speed_rows, out_rows = rows_of(s_ref), rows_of(speed_ref), rows_of(out_ref)
    few, many = 8, turned_ref.shape[2] // speeds
    groups = turned_ref.shape[0]
    lanes = many * speeds
    high = 8
    lines = width // high

    def along_speed(n):
        start = min(n * few, cells - few) * speeds
        spots = [pl.ds(start + v, few, stride=speeds) for v in range(speeds)]
        rows = [s_rows[spot, :] for spot in spots]
        for spot, (mean, gap) in zip(spots, row_terms(rows, speed_step, True)):
            speed_rows[spot, :] = gain_v * (gap - jnp.abs(mean))

    def span(n):
        return pl.ds(min(n * many, cells - many) * speeds, lanes)

    def turn_in(n):
        turned = s_rows[span(n), :].T
        turned_ref[n, rim : rim + width, :] = turned
        for k in range(rim):
            turned_ref[n, k : k + 1, :] = turned[:1]
            turned_ref[n, rim + width + k : rim + width + k + 1, :] = turned[-1:]
        if split:
            flow_t_ref[n] = flow_rows[span(n), :].T

    def along_y(n):
        ends = [turned_ref[n, pl.ds(k, high, stride=lines), :] for k in range(lines + 2 * rim)]
        for k, (mean, gap) in enumerate(row_terms(ends, spacing)):
            spot = pl.ds(k, high, stride=lines)
            drift = mean * flow_t_ref[n, spot, :]
            if split:
                drift_ref[n, spot, :] = drift
                gap_ref[n, spot, :] = gap
            else:
                drift_ref[n, spot, :] = drift + gap * peak

    def turn_out(n):
        out_rows[span(n), :] = drift_ref[n].T
        if split:
            extra_rows[span(n), :] = gap_ref[n].T

    turn_in(0)
    for n in range(groups):
        if n > 0:
            turn_out(n - 1)
        along_y(n)
        if n + 1 < groups:
            turn_in(n + 1)
        for k in (2 * n, 2 * n + 1):
            if k * few < cells:
                along_speed(k)
    turn_out(groups - 1)


def heading_kernel(heading_step, s_ref, speed_ref, part_ref, near_ref, far_ref, out_ref):
    planes, headings = s_ref.shape[:2]
    gain_t = turn_limit / (12.0 * heading_step)
    odd = odd_place("head")
    wide = batches(planes, 9)

    def step(n, carry):
        for w in range(wide):
            i = n * wide + w
            ghosts = [(near_ref[i * rim + k], far_ref[i * rim + k]) for k in range(rim)]
            lows = [jnp.where(odd, near, far) for near, far in ghosts]
            highs = [jnp.where(odd, far, near) for near, far in ghosts]
            cells = lows + [s_ref[i, j] for j in range(headings)] + highs
            for j, (mean, gap) in enumerate(row_terms(cells, heading_step)):
                own = speed_ref[i, j] + part_ref[i, j]
                out_ref[i, j] = own + gain_t * (gap - jnp.abs(mean))
        return carry

    lax.fori_loop(0, planes // wide, step, 0)


def peaks_into(pk_ref, most, bounds, heading_step, speed_step):
    most = jnp.max(most, axis=1, keepdims=True)
    peaks = [
        jnp.maximum(most[q : q + 1] + bounds[q][1], most[q + 2 : q + 3] - bounds[q][0])
        for q in range(2)
    ]
    time_step = courant / (
        peaks[0] / spacing
        + peaks[1] / spacing
        + turn_limit / heading_step
        + thrust_limit / speed_step
    )
    width = pk_ref.shape[1]
    for row, value in enumerate(peaks + [time_step]):
        pk_ref[row : row + 1, :] = splat(value, (1, width))


def plane_at(i, planes):
    return jnp.where(odd_place("gx"), i, planes - 1 - i)


def alone(reach):
    place, size = lax.axis_index("gx"), lax.axis_size("gx")
    if reach == 0:
        return (place == size - 1) if size % 2 else place < 0
    return (place == 0) | (place == size - 1) if size % 2 == 0 else place == 0


def cut_near(field_ref, x_near):
    planes, headings = field_ref.shape[:2]
    for k in range(rim):
        i = jnp.where(alone(0), 0, k)
        x_near[k * headings : (k + 1) * headings] = field_ref[plane_at(i, planes)]


def cut_far(field_ref, x_far):
    planes, headings = field_ref.shape[:2]
    for k in range(rim):
        i = planes - 1 - jnp.where(alone(1), 0, k)
        x_far[k * headings : (k + 1) * headings] = field_ref[plane_at(i, planes)]


def cut_headings(field_ref, t_near, t_far):
    planes, headings = field_ref.shape[:2]
    t_low = jnp.where(odd_place("head"), 0, headings - rim)
    for k in range(rim):
        for i in range(planes):
            t_near[i * rim + k] = field_ref[i, t_low + k]
            t_far[i * rim + k] = field_ref[i, headings - rim - t_low + k]


def splat_targets(mask_ref, depth_ref, target_ref):
    for i in range(target_ref.shape[0]):
        depth = depth_ref[i : i + 1, :]
        target = jnp.where(mask_ref[i : i + 1, :] == 1, -depth, depth)
        target_ref[i] = splat(target, target_ref.shape[1:])


def across_planes(
    span, speed_step, s_ref, near_ref, far_ref, wind_ref, waves_ref, flow_ref, use
):
    planes, headings = s_ref.shape[:2]
    tile = s_ref.shape[2:]
    side = jnp.where(odd_place("gx"), gain, -gain).astype(jnp.float32)
    spots = [plane_at(i, planes) for i in range(planes)]
    for i in range(planes):
        flow_ref[i] = splat(wind_ref[i, 0:1, :] * side, tile)
    pace = speeds_of(tile, speed_step) * side
    first = lax.axis_index("head") * headings
    low, high = span
    wide = batches(headings, max(1, 108 // (high - low)))

    def line(i, j):
        if i < 0:
            return near_ref[(-1 - i) * headings + j]
        if i >= planes:
            return far_ref[(i - planes) * headings + j]
        return s_ref[spots[i], j]

    def step(n, carry):
        for w in range(wide):
            j = n * wide + w
            cells = [line(i, j) for i in range(low - rim, high + rim)]
            table = splat(waves_ref[0, pl.ds(first + j, 1), :], tile) * pace
            for k, (mean, gap) in enumerate(row_terms(cells, spacing)):
                spot = spots[low + k]
                use(spot, j, mean * (table + flow_ref[spot]), gap, cells[k + rim])
        return carry

    lax.fori_loop(0, headings // wide, step, 0)


def first_kernel(
    speed_step, s_ref, part_ref, near_ref, far_ref, wind_ref, waves_ref, out_ref, gap_ref, flow_ref
):
    def use(i, j, drift, gap, cell):
        out_ref[i, j] = part_ref[i, j] + drift
        gap_ref[i, j] = gap

    across_planes(
        (0, s_ref.shape[0]), speed_step, s_ref, near_ref, far_ref, wind_ref, waves_ref, flow_ref, use
    )


def closing_kernel(
    bounds, heading_step, speed_step, s_ref, part_ref, gap_x_ref, gap_y_ref, mask_ref, depth_ref,
    most_ref, other_ref, out_ref, x_near, x_far, t_near, t_far, pk_ref, target_ref
):
    planes, headings = s_ref.shape[:2]
    tile = s_ref.shape[2:]
    most = jnp.maximum(most_ref[...], other_ref[...])
    peaks_into(pk_ref, most, bounds, heading_step, speed_step)
    splat_targets(mask_ref, depth_ref, target_ref)
    peak_x = splat(pk_ref[0:1, :] * gain, tile)
    peak_y = splat(pk_ref[1:2, :] * gain, tile)
    time_step = splat(pk_ref[2:3, :], tile)

    wide = batches(planes, 3)

    def step(n, carry):
        for w in range(wide):
            i = n * wide + w
            for j in range(headings):
                rate = part_ref[i, j] + (gap_x_ref[i, j] * peak_x + gap_y_ref[i, j] * peak_y)
                out_ref[i, j] = jnp.minimum(s_ref[i, j] + time_step * rate, target_ref[i])
        return carry

    lax.fori_loop(0, planes // wide, step, 0)
    cut_near(out_ref, x_near)
    cut_far(out_ref, x_far)
    cut_headings(out_ref, t_near, t_far)


def section_kernel(
    section, span, speed_step, base_ref, s_ref, part_ref, ghosts_ref, wind_ref, waves_ref,
    mask_ref, depth_ref, pk_ref, *refs
):
    planes = s_ref.shape[0]
    final = section == 3 and span[0] > 0
    refs = list(refs)
    if final:
        out_ref, sems = refs.pop(), refs.pop()
    refs, (flow_ref, target_ref) = refs[:-2], refs[-2:]
    early_ref = refs.pop(0) if span[0] > 0 else None
    if final:
        result_ref = refs.pop(0)
        early = pl.ds(jnp.where(odd_place("gx"), 0, planes - span[0]), span[0])
        late = pl.ds(jnp.where(odd_place("gx"), span[0], 0), planes - span[0])
        sends = [
            pltpu.make_async_copy(early_ref.at[early], result_ref.at[early], sems.at[0]),
            pltpu.make_async_copy(out_ref.at[late], result_ref.at[late], sems.at[1]),
        ]
        sends[0].start()
    else:
        out_ref = refs.pop(0)
    tile = s_ref.shape[2:]
    splat_targets(mask_ref, depth_ref, target_ref)
    peak_x = splat(pk_ref[0:1, :] * gain, tile)
    time_step = splat(pk_ref[2:3, :], tile)
    base_share = 0.75 if section == 2 else 1.0 / 3.0
    own_share = 0.25 if section == 2 else 2.0 / 3.0

    def use(i, j, drift, gap, cell):
        rate = part_ref[i, j] + (drift + gap * peak_x)
        moved = base_share * base_ref[i, j] + own_share * (cell + time_step * rate)
        out_ref[i, j] = jnp.minimum(moved, target_ref[i])

    near_ref, far_ref = (None, ghosts_ref) if span[0] > 0 else (ghosts_ref, None)
    across_planes(
        span, speed_step, s_ref, near_ref, far_ref, wind_ref, waves_ref, flow_ref, use
    )
    if final:
        sends[1].start()
        for send in sends:
            send.wait()
        return
    for i in range(span[0]):
        spot = plane_at(i, planes)
        out_ref[spot] = early_ref[spot]
    if section == 2 and span[0] == 0:
        cut_near(out_ref, *refs)
    elif section == 2:
        cut_far(out_ref, refs[0])
        cut_headings(out_ref, *refs[1:])


def trade(value, axis, reach, wrap=False):
    size = lax.axis_size(axis)
    pairs = [(i, i + 1) for i in range(reach, size - 1, 2)]
    if wrap and reach and size % 2 == 0:
        pairs.append((size - 1, 0))
    pairs += [(j, i) for i, j in pairs]
    pairs += [(i, i) for i in range(size) if i not in dict(pairs)]
    return lax.ppermute(value, axis, pairs)


def local(level_set, wind_field, target_mask, target_depth):
    planes, headings, speed_count, cross_count = level_set.shape
    heading_total = headings * lax.axis_size("head")
    heading_step = 2.0 * math.pi / heading_total
    speed_step = (speed_high - speed_low) / (speed_count - 1)
    speed_row = np.float32(speed_low) + np.arange(speed_count, dtype=np.float32) * np.float32(
        speed_step
    )
    angles = np.arange(heading_total, dtype=np.float32) * np.float32(heading_step)
    waves = [np.cos(angles), np.sin(angles)]
    bounds = []
    for wave in waves:
        product = wave[:, None] * speed_row[None, :]
        bounds.append((float(product.min()), float(product.max())))
    waves = jnp.asarray(np.stack(waves)[..., None] * np.ones(cross_count, np.float32))

    vmem = pl.BlockSpec(memory_space=pltpu.VMEM)
    tile = (speed_count, cross_count)

    def shape(*dims):
        return jax.ShapeDtypeStruct(dims + tile, jnp.float32)

    field = shape(planes, headings)
    short = rim * headings
    middle = max(short + 1, rim * planes)

    longest = middle + 1
    rows = pltpu.VMEM((planes,) + tile, jnp.float32)
    cells = math.prod(level_set.shape)

    def call(kernel, ins, outs, scratch=(), work=0, place=vmem):
        return pl.pallas_call(
            kernel,
            out_shape=outs,
            in_specs=[vmem] * len(ins),
            out_specs=[place] * len(outs),
            scratch_shapes=list(scratch),
            compiler_params=pltpu.CompilerParams(vmem_limit_bytes=16 * 1024 * 1024),
            cost_estimate=pl.CostEstimate(
                flops=work * cells, bytes_accessed=work * cells, transcendentals=0
            ),
        )(*ins)

    wind = jnp.transpose(wind_field, (1, 0, 2))
    many = 16
    groups, lanes = -(-planes * headings // many), many * speed_count
    turned = (groups, cross_count, lanes)
    room = [
        pltpu.VMEM((groups, cross_count + 8, lanes), jnp.float32),
        pltpu.VMEM(turned, jnp.float32),
    ]
    wide_room = room + [pltpu.VMEM(turned, jnp.float32), pltpu.VMEM(level_set.shape, jnp.float32)]
    values = level_set
    size = lax.axis_size("gx")

    def spread(most, reach):
        if size & (size - 1):
            pairs = [(i, (i + reach) % size) for i in range(size)]
        else:
            pairs = [(i, i ^ reach) for i in range(size)]
        return lax.ppermute(most, "gx", pairs)

    (most,) = call(extremes_kernel, [wind], [shape(longest + 2)])
    other = spread(most, 1)
    x_shapes = [shape(longest), shape(longest + 1)]
    x_out, x_last, t_out, t_last = call(opening_kernel, [values], x_shapes + [shape(middle)] * 2)
    far_shapes = [shape(short), shape(rim * planes), shape(middle)]
    for section in (1, 2, 3):
        opening = section == 1
        x_near = trade(x_out, "gx", 0)
        t_near = trade(t_out, "head", 0)
        t_far = trade(t_last, "head", 1, True)
        x_far = trade(x_last, "gx", 1)
        free = functools.partial(free_kernel, opening, speed_step)
        turning = functools.partial(heading_kernel, heading_step)
        if opening:
            (most,) = call(meeting_kernel, [most, other], [shape()])
            other = spread(most, 2)
            ins = [values, wind, waves]
            spun, part, extra, flow = call(
                free, ins, [field] * 3 + [jax.ShapeDtypeStruct(turned, jnp.float32)], wide_room, work=300
            )
            reach = 4
            while reach < size:
                most = jnp.maximum(most, other)
                most, part = lax.optimization_barrier((most, part))
                other = spread(most, reach)
                reach *= 2
        else:
            if section == 3:
                values, x_near = lax.optimization_barrier((values, x_near))
            spun, part = call(free, [values, flow, pk], [field] * 2, room)
            if section == 2:
                part, x_near = lax.optimization_barrier((part, x_near))
        weight = 0 if opening else 1000
        (part,) = call(turning, [values, spun, part, t_near, t_far], [field], work=weight)
        if opening:
            ins = [values, part, x_near, x_far, wind, waves]
            first = functools.partial(first_kernel, speed_step)
            part, gap = call(first, ins, [field] * 2, [rows])
            closing = functools.partial(closing_kernel, bounds, heading_step, speed_step)
            ins = [values, part, gap, extra, target_mask, target_depth, most, other]
            outs = [field, shape(longest), *far_shapes, shape()]
            values, x_out, x_last, t_out, t_last, pk = call(closing, ins, outs, [rows])
        else:
            more = section == 2
            ins = [level_set, values, part, x_near, wind, waves, target_mask, target_depth, pk]
            outs = [field] + ([shape(longest)] if more else [])
            last = functools.partial(section_kernel, section, (0, planes - rim), speed_step)
            early, *x_next = call(last, ins, outs, [rows, rows])
            ins = ins[:3] + [x_far] + ins[4:] + [early]
            outs = [field] + (far_shapes if more else [])
            last = functools.partial(section_kernel, section, (planes - rim, planes), speed_step)
            scratch, place = [rows, rows], vmem
            if not more:
                scratch += [pltpu.SemaphoreType.DMA((2,)), pltpu.VMEM(level_set.shape, jnp.float32)]
                place = pl.BlockSpec(memory_space=pltpu.HBM)
            values, *far_next = call(last, ins, outs, scratch, place=place)
            if more:
                (x_out,), (x_last, t_out, t_last) = x_next, far_next
    return values


def solution(mesh):
    return jax.shard_map(
        local,
        mesh=mesh,
        in_specs=(P("gx", "head", None, None), P(None, "gx", None), P("gx", None), P("gx", None)),
        out_specs=P("gx", "head", None, None),
        check_vma=False,
    )
```

```python
import functools
import math

import jax
import jax.numpy as jnp
import numpy as np
from jax import lax
from jax.experimental import pallas as pl
from jax.experimental.pallas import tpu as pltpu
from jax.sharding import PartitionSpec as P

epsilon = 1e-06
courant = 0.5
spacing = 0.05
turn_limit = 1.0
thrust_limit = 0.5
speed_low = 0.5
speed_high = 1.5
rim = 3
gain = 1.0 / (12.0 * spacing)


def inverse(value):
    return pltpu.reciprocal(value, approx=True)


def weights_of(e1, e2, turn, eps):
    level = turn * turn * (4.0 / 3.0) + eps
    ia = inverse(level + e2 * (e2 + turn))
    ib = inverse(level + e2 * e1)
    ic = inverse(level + e1 * (e1 - turn))
    return ia * ia, ib * ib * 6.0, ic * ic


def sides(fl, f0, fr, a2, a1, b1, b0, c0, c1):
    a3 = a1 * 3.0
    c3 = c0 * 3.0
    minus = ((fl + fl) * a2 + f0 * c3) * inverse(a2 + b1 + c3)
    plus = ((fr + fr) * c1 + f0 * a3) * inverse(c1 + b0 + a3)
    return minus, plus


def row_terms(cells, step, closed=False):
    eps = epsilon * step * step
    count = len(cells) if closed else len(cells) - 2 * rim
    shift = 0 if closed else rim
    slope = {m: cells[m + 1 + shift] - cells[m + shift] for m in range(-shift, count + shift - 1)}
    a, b, c = {}, {}, {}
    if closed:
        bend = {m: slope[m] - slope[m - 1] for m in range(1, count - 1)}
        bend[0], bend[count - 1] = slope[0], -slope[count - 2]
        turn = {m: bend[m + 1] - bend[m] for m in range(count - 1)}
        turn[-1], turn[count - 1] = bend[0], -bend[count - 1]
        jerk = {m: turn[m] - turn[m - 1] for m in range(count)}
        jerk[-1], jerk[count] = bend[0], bend[count - 1]
        rise = {m: slope[m] + slope[m - 1] for m in range(1, count - 1)}
        rise[0], rise[count - 1] = slope[0], slope[count - 2]
        a[-2] = c[count] = 1.0 / (eps * eps)
        for m, (e1, e2) in ((-1, (None, bend[0])), (count - 1, (bend[count - 1], None))):
            square = turn[m] * turn[m]
            level = square * (4.0 / 3.0) + eps
            ib, outer = inverse(level), inverse(level + (square + square))
            b[m] = ib * ib * 6.0
            (c if e2 is None else a)[m] = outer * outer
        inner = range(count - 1)
    else:
        bend = {m: slope[m] - slope[m - 1] for m in range(-2, count + 2)}
        turn = {m: bend[m + 1] - bend[m] for m in range(-2, count + 1)}
        jerk = {m: turn[m] - turn[m - 1] for m in range(-1, count + 1)}
        rise = {m: cells[m + 1 + rim] - cells[m - 1 + rim] for m in range(count)}
        inner = range(-2, count + 1)
    for m in inner:
        a[m], b[m], c[m] = weights_of(bend[m], bend[m + 1], turn[m], eps)
    out = []
    for i in range(count):
        base = rise[i] * 6.0 - (turn[i - 1] + turn[i])
        minus, plus = sides(
            jerk[i - 1], jerk[i], jerk[i + 1], a[i - 2], a[i - 1], b[i - 1], b[i], c[i], c[i + 1]
        )
        out.append((base + (plus - minus), (plus + minus) - jerk[i]))
    return out


def batches(total, most):
    return max(k for k in range(1, most + 1) if total % k == 0)


def splat(row, tile):
    return jnp.broadcast_to(row, tile)


def speeds_of(tile, speed_step):
    place = lax.broadcasted_iota(jnp.int32, tile, 0).astype(jnp.float32)
    return speed_low + place * speed_step


def odd_place(axis):
    return lax.rem(lax.axis_index(axis), 2) == 1


def put_extremes(wind_ref, most_ref):
    rows = [wind_ref[i] for i in range(wind_ref.shape[0])]
    most_ref[...] = jnp.zeros_like(most_ref)
    most_ref[0:2, :] = functools.reduce(jnp.maximum, rows)
    most_ref[2:4, :] = -functools.reduce(jnp.minimum, rows)


def extremes_kernel(wind_ref, most_ref):
    put_extremes(wind_ref, most_ref.at[0])


def opening_kernel(level_ref, x_near, x_far, t_near, t_far):
    cut_near(level_ref, x_near)
    cut_far(level_ref, x_far)
    cut_headings(level_ref, t_near, t_far)


def meeting_kernel(own_ref, other_ref, most_ref):
    most_ref[...] = jnp.maximum(own_ref[0], other_ref[0])


def flows_into(flow_ref, speed_step, wind_ref, waves_ref):
    planes, headings = flow_ref.shape[:2]
    tile = flow_ref.shape[2:]
    first = lax.axis_index("head") * headings
    pace = speeds_of(tile, speed_step) * gain
    tables = [
        splat(waves_ref[1, pl.ds(first + j, 1), :], tile) * pace for j in range(headings)
    ]
    for i in range(planes):
        wind = splat(wind_ref[i, 1:2, :] * gain, tile)
        for j in range(headings):
            flow_ref[i, j] = tables[j] + wind


def free_kernel(split, speed_step, s_ref, *rest):
    planes, headings, speeds, width = s_ref.shape
    cells = planes * headings

    def rows_of(ref):
        return ref.reshape(cells * speeds, width)

    if split:
        wind_ref, waves_ref, speed_ref, out_ref, extra_ref, flow_t_ref = rest[:6]
        turned_ref, drift_ref, gap_ref, flow_ref = rest[6:]
        flows_into(flow_ref, speed_step, wind_ref, waves_ref)
        extra_rows, flow_rows = rows_of(extra_ref), rows_of(flow_ref)
    else:
        flow_t_ref, pk_ref, speed_ref, out_ref, turned_ref, drift_ref = rest
        peak = splat(pk_ref[1:2, :] * gain, (speeds, width))
    gain_v = thrust_limit / (12.0 * speed_step)
    s_rows, speed_rows, out_rows = rows_of(s_ref), rows_of(speed_ref), rows_of(out_ref)
    few, many = 8, turned_ref.shape[2] // speeds
    groups = turned_ref.shape[0]
    lanes = many * speeds
    high = 8
    lines = width // high

    def along_speed(n):
        start = min(n * few, cells - few) * speeds
        spots = [pl.ds(start + v, few, stride=speeds) for v in range(speeds)]
        rows = [s_rows[spot, :] for spot in spots]
        for spot, (mean, gap) in zip(spots, row_terms(rows, speed_step, True)):
            speed_rows[spot, :] = gain_v * (gap - jnp.abs(mean))

    def span(n):
        return pl.ds(min(n * many, cells - many) * speeds, lanes)

    def turn_in(n):
        turned = s_rows[span(n), :].T
        turned_ref[n, rim : rim + width, :] = turned
        for k in range(rim):
            turned_ref[n, k : k + 1, :] = turned[:1]
            turned_ref[n, rim + width + k : rim + width + k + 1, :] = turned[-1:]
        if split:
            flow_t_ref[n] = flow_rows[span(n), :].T

    def along_y(n):
        ends = [turned_ref[n, pl.ds(k, high, stride=lines), :] for k in range(lines + 2 * rim)]
        for k, (mean, gap) in enumerate(row_terms(ends, spacing)):
            spot = pl.ds(k, high, stride=lines)
            drift = mean * flow_t_ref[n, spot, :]
            if split:
                drift_ref[n, spot, :] = drift
                gap_ref[n, spot, :] = gap
            else:
                drift_ref[n, spot, :] = drift + gap * peak

    def turn_out(n):
        out_rows[span(n), :] = drift_ref[n].T
        if split:
            extra_rows[span(n), :] = gap_ref[n].T

    turn_in(0)
    for n in range(groups):
        if n > 0:
            turn_out(n - 1)
        along_y(n)
        if n + 1 < groups:
            turn_in(n + 1)
        for k in (2 * n, 2 * n + 1):
            if k * few < cells:
                along_speed(k)
    turn_out(groups - 1)


def heading_kernel(heading_step, s_ref, speed_ref, part_ref, near_ref, far_ref, out_ref):
    planes, headings = s_ref.shape[:2]
    gain_t = turn_limit / (12.0 * heading_step)
    odd = odd_place("head")
    wide = batches(planes, 9)

    def step(n, carry):
        for w in range(wide):
            i = n * wide + w
            ghosts = [(near_ref[i * rim + k], far_ref[i * rim + k]) for k in range(rim)]
            lows = [jnp.where(odd, near, far) for near, far in ghosts]
            highs = [jnp.where(odd, far, near) for near, far in ghosts]
            cells = lows + [s_ref[i, j] for j in range(headings)] + highs
            for j, (mean, gap) in enumerate(row_terms(cells, heading_step)):
                own = speed_ref[i, j] + part_ref[i, j]
                out_ref[i, j] = own + gain_t * (gap - jnp.abs(mean))
        return carry

    lax.fori_loop(0, planes // wide, step, 0)


def peaks_into(pk_ref, most, bounds, heading_step, speed_step):
    most = jnp.max(most, axis=1, keepdims=True)
    peaks = [
        jnp.maximum(most[q : q + 1] + bounds[q][1], most[q + 2 : q + 3] - bounds[q][0])
        for q in range(2)
    ]
    time_step = courant / (
        peaks[0] / spacing
        + peaks[1] / spacing
        + turn_limit / heading_step
        + thrust_limit / speed_step
    )
    width = pk_ref.shape[1]
    for row, value in enumerate(peaks + [time_step]):
        pk_ref[row : row + 1, :] = splat(value, (1, width))


def plane_at(i, planes):
    return jnp.where(odd_place("gx"), i, planes - 1 - i)


def alone(reach):
    place, size = lax.axis_index("gx"), lax.axis_size("gx")
    if reach == 0:
        return (place == size - 1) if size % 2 else place < 0
    return (place == 0) | (place == size - 1) if size % 2 == 0 else place == 0


def cut_near(field_ref, x_near):
    planes, headings = field_ref.shape[:2]
    for k in range(rim):
        i = jnp.where(alone(0), 0, k)
        x_near[k * headings : (k + 1) * headings] = field_ref[plane_at(i, planes)]


def cut_far(field_ref, x_far):
    planes, headings = field_ref.shape[:2]
    for k in range(rim):
        i = planes - 1 - jnp.where(alone(1), 0, k)
        x_far[k * headings : (k + 1) * headings] = field_ref[plane_at(i, planes)]


def cut_headings(field_ref, t_near, t_far):
    planes, headings = field_ref.shape[:2]
    t_low = jnp.where(odd_place("head"), 0, headings - rim)
    for k in range(rim):
        for i in range(planes):
            t_near[i * rim + k] = field_ref[i, t_low + k]
            t_far[i * rim + k] = field_ref[i, headings - rim - t_low + k]


def splat_targets(mask_ref, depth_ref, target_ref):
    for i in range(target_ref.shape[0]):
        depth = depth_ref[i : i + 1, :]
        target = jnp.where(mask_ref[i : i + 1, :] == 1, -depth, depth)
        target_ref[i] = splat(target, target_ref.shape[1:])


def across_planes(
    span, speed_step, s_ref, near_ref, far_ref, wind_ref, waves_ref, flow_ref, use
):
    planes, headings = s_ref.shape[:2]
    tile = s_ref.shape[2:]
    side = jnp.where(odd_place("gx"), gain, -gain).astype(jnp.float32)
    spots = [plane_at(i, planes) for i in range(planes)]
    for i in range(planes):
        flow_ref[i] = splat(wind_ref[i, 0:1, :] * side, tile)
    pace = speeds_of(tile, speed_step) * side
    first = lax.axis_index("head") * headings
    low, high = span
    wide = batches(headings, max(1, 108 // (high - low)))

    def line(i, j):
        if i < 0:
            return near_ref[(-1 - i) * headings + j]
        if i >= planes:
            return far_ref[(i - planes) * headings + j]
        return s_ref[spots[i], j]

    def step(n, carry):
        for w in range(wide):
            j = n * wide + w
            cells = [line(i, j) for i in range(low - rim, high + rim)]
            table = splat(waves_ref[0, pl.ds(first + j, 1), :], tile) * pace
            for k, (mean, gap) in enumerate(row_terms(cells, spacing)):
                spot = spots[low + k]
                use(spot, j, mean * (table + flow_ref[spot]), gap, cells[k + rim])
        return carry

    lax.fori_loop(0, headings // wide, step, 0)


def first_kernel(
    speed_step, s_ref, part_ref, near_ref, far_ref, wind_ref, waves_ref, out_ref, gap_ref, flow_ref
):
    def use(i, j, drift, gap, cell):
        out_ref[i, j] = part_ref[i, j] + drift
        gap_ref[i, j] = gap

    across_planes(
        (0, s_ref.shape[0]), speed_step, s_ref, near_ref, far_ref, wind_ref, waves_ref, flow_ref, use
    )


def closing_kernel(
    bounds, heading_step, speed_step, s_ref, part_ref, gap_x_ref, gap_y_ref, mask_ref, depth_ref,
    most_ref, other_ref, out_ref, x_near, x_far, t_near, t_far, pk_ref, target_ref
):
    planes, headings = s_ref.shape[:2]
    tile = s_ref.shape[2:]
    most = jnp.maximum(most_ref[...], other_ref[...])
    peaks_into(pk_ref, most, bounds, heading_step, speed_step)
    splat_targets(mask_ref, depth_ref, target_ref)
    peak_x = splat(pk_ref[0:1, :] * gain, tile)
    peak_y = splat(pk_ref[1:2, :] * gain, tile)
    time_step = splat(pk_ref[2:3, :], tile)

    wide = batches(planes, 3)

    def step(n, carry):
        for w in range(wide):
            i = n * wide + w
            for j in range(headings):
                rate = part_ref[i, j] + (gap_x_ref[i, j] * peak_x + gap_y_ref[i, j] * peak_y)
                out_ref[i, j] = jnp.minimum(s_ref[i, j] + time_step * rate, target_ref[i])
        return carry

    lax.fori_loop(0, planes // wide, step, 0)
    cut_near(out_ref, x_near)
    cut_far(out_ref, x_far)
    cut_headings(out_ref, t_near, t_far)


def section_kernel(
    section, span, speed_step, base_ref, s_ref, part_ref, ghosts_ref, wind_ref, waves_ref,
    mask_ref, depth_ref, pk_ref, *refs
):
    planes = s_ref.shape[0]
    refs, (flow_ref, target_ref) = list(refs[:-2]), refs[-2:]
    early_ref = refs.pop(0) if span[0] > 0 else None
    out_ref = refs.pop(0)
    tile = s_ref.shape[2:]
    splat_targets(mask_ref, depth_ref, target_ref)
    peak_x = splat(pk_ref[0:1, :] * gain, tile)
    time_step = splat(pk_ref[2:3, :], tile)
    base_share = 0.75 if section == 2 else 1.0 / 3.0
    own_share = 0.25 if section == 2 else 2.0 / 3.0

    def use(i, j, drift, gap, cell):
        rate = part_ref[i, j] + (drift + gap * peak_x)
        moved = base_share * base_ref[i, j] + own_share * (cell + time_step * rate)
        out_ref[i, j] = jnp.minimum(moved, target_ref[i])

    near_ref, far_ref = (None, ghosts_ref) if span[0] > 0 else (ghosts_ref, None)
    across_planes(
        span, speed_step, s_ref, near_ref, far_ref, wind_ref, waves_ref, flow_ref, use
    )
    for i in range(span[0]):
        spot = plane_at(i, planes)
        out_ref[spot] = early_ref[spot]
    if section == 2 and span[0] == 0:
        cut_near(out_ref, *refs)
    elif section == 2:
        cut_far(out_ref, refs[0])
        cut_headings(out_ref, *refs[1:])


def trade(value, axis, reach, wrap=False):
    size = lax.axis_size(axis)
    pairs = [(i, i + 1) for i in range(reach, size - 1, 2)]
    if wrap and reach and size % 2 == 0:
        pairs.append((size - 1, 0))
    pairs += [(j, i) for i, j in pairs]
    pairs += [(i, i) for i in range(size) if i not in dict(pairs)]
    return lax.ppermute(value, axis, pairs)


def local(level_set, wind_field, target_mask, target_depth):
    planes, headings, speed_count, cross_count = level_set.shape
    heading_total = headings * lax.axis_size("head")
    heading_step = 2.0 * math.pi / heading_total
    speed_step = (speed_high - speed_low) / (speed_count - 1)
    speed_row = np.float32(speed_low) + np.arange(speed_count, dtype=np.float32) * np.float32(
        speed_step
    )
    angles = np.arange(heading_total, dtype=np.float32) * np.float32(heading_step)
    waves = [np.cos(angles), np.sin(angles)]
    bounds = []
    for wave in waves:
        product = wave[:, None] * speed_row[None, :]
        bounds.append((float(product.min()), float(product.max())))
    waves = jnp.asarray(np.stack(waves)[..., None] * np.ones(cross_count, np.float32))

    vmem = pl.BlockSpec(memory_space=pltpu.VMEM)
    tile = (speed_count, cross_count)

    def shape(*dims):
        return jax.ShapeDtypeStruct(dims + tile, jnp.float32)

    field = shape(planes, headings)
    short = rim * headings
    middle = max(short + 1, rim * planes)

    longest = middle + 1
    rows = pltpu.VMEM((planes,) + tile, jnp.float32)
    cells = math.prod(level_set.shape)

    def call(kernel, ins, outs, scratch=(), work=0):
        return pl.pallas_call(
            kernel,
            out_shape=outs,
            in_specs=[vmem] * len(ins),
            out_specs=[vmem] * len(outs),
            scratch_shapes=list(scratch),
            compiler_params=pltpu.CompilerParams(vmem_limit_bytes=16 * 1024 * 1024),
            cost_estimate=pl.CostEstimate(
                flops=work * cells, bytes_accessed=work * cells, transcendentals=0
            ),
        )(*ins)

    wind = jnp.transpose(wind_field, (1, 0, 2))
    many = 16
    groups, lanes = -(-planes * headings // many), many * speed_count
    turned = (groups, cross_count, lanes)
    room = [
        pltpu.VMEM((groups, cross_count + 8, lanes), jnp.float32),
        pltpu.VMEM(turned, jnp.float32),
    ]
    wide_room = room + [pltpu.VMEM(turned, jnp.float32), pltpu.VMEM(level_set.shape, jnp.float32)]
    values = level_set
    size = lax.axis_size("gx")

    def spread(most, reach):
        if size & (size - 1):
            pairs = [(i, (i + reach) % size) for i in range(size)]
        else:
            pairs = [(i, i ^ reach) for i in range(size)]
        return lax.ppermute(most, "gx", pairs)

    (most,) = call(extremes_kernel, [wind], [shape(longest + 2)])
    other = spread(most, 1)
    x_shapes = [shape(longest), shape(longest + 1)]
    x_out, x_last, t_out, t_last = call(opening_kernel, [values], x_shapes + [shape(middle)] * 2)
    far_shapes = [shape(short), shape(rim * planes), shape(middle)]
    for section in (1, 2, 3):
        opening = section == 1
        x_near = trade(x_out, "gx", 0)
        t_near = trade(t_out, "head", 0)
        t_far = trade(t_last, "head", 1, True)
        x_far = trade(x_last, "gx", 1)
        free = functools.partial(free_kernel, opening, speed_step)
        turning = functools.partial(heading_kernel, heading_step)
        if opening:
            (most,) = call(meeting_kernel, [most, other], [shape()])
            other = spread(most, 2)
            ins = [values, wind, waves]
            spun, part, extra, flow = call(
                free, ins, [field] * 3 + [jax.ShapeDtypeStruct(turned, jnp.float32)], wide_room, work=300
            )
            reach = 4
            while reach < size:
                most = jnp.maximum(most, other)
                most, part = lax.optimization_barrier((most, part))
                other = spread(most, reach)
                reach *= 2
        else:
            if section == 3:
                values, x_near = lax.optimization_barrier((values, x_near))
            spun, part = call(free, [values, flow, pk], [field] * 2, room)
            if section == 2:
                part, x_near = lax.optimization_barrier((part, x_near))
        weight = 0 if opening else 1000
        (part,) = call(turning, [values, spun, part, t_near, t_far], [field], work=weight)
        if opening:
            ins = [values, part, x_near, x_far, wind, waves]
            first = functools.partial(first_kernel, speed_step)
            part, gap = call(first, ins, [field] * 2, [rows])
            closing = functools.partial(closing_kernel, bounds, heading_step, speed_step)
            ins = [values, part, gap, extra, target_mask, target_depth, most, other]
            outs = [field, shape(longest), *far_shapes, shape()]
            values, x_out, x_last, t_out, t_last, pk = call(closing, ins, outs, [rows])
        else:
            more = section == 2
            ins = [level_set, values, part, x_near, wind, waves, target_mask, target_depth, pk]
            outs = [field] + ([shape(longest)] if more else [])
            last = functools.partial(section_kernel, section, (0, planes - rim), speed_step)
            early, *x_next = call(last, ins, outs, [rows, rows])
            ins = ins[:3] + [x_far] + ins[4:] + [early]
            outs = [field] + ([shape(short)] + [shape(rim * planes)] * 2 if more else [])
            last = functools.partial(section_kernel, section, (planes - rim, planes), speed_step)
            values, *far_next = call(last, ins, outs, [rows, rows])
            if more:
                (x_out,), (x_last, t_out, t_last) = x_next, far_next
    return values


def solution(mesh):
    return jax.shard_map(
        local,
        mesh=mesh,
        in_specs=(P("gx", "head", None, None), P(None, "gx", None), P("gx", None), P("gx", None)),
        out_specs=P("gx", "head", None, None),
        check_vma=False,
    )
```

```python
import functools
import math

import jax
import jax.numpy as jnp
import numpy as np
from jax import lax
from jax.experimental import pallas as pl
from jax.experimental.pallas import tpu as pltpu
from jax.sharding import PartitionSpec as P

epsilon = 1e-06
courant = 0.5
spacing = 0.05
turn_limit = 1.0
thrust_limit = 0.5
speed_low = 0.5
speed_high = 1.5
rim = 3
gain = 1.0 / (12.0 * spacing)


def inverse(value):
    return pltpu.reciprocal(value, approx=True)


def weights_of(e1, e2, turn, eps):
    level = turn * turn * (4.0 / 3.0) + eps
    ia = inverse(level + e2 * (e2 + turn))
    ib = inverse(level + e2 * e1)
    ic = inverse(level + e1 * (e1 - turn))
    return ia * ia, ib * ib * 6.0, ic * ic


def sides(fl, f0, fr, a2, a1, b1, b0, c0, c1):
    a3 = a1 * 3.0
    c3 = c0 * 3.0
    minus = ((fl + fl) * a2 + f0 * c3) * inverse(a2 + b1 + c3)
    plus = ((fr + fr) * c1 + f0 * a3) * inverse(c1 + b0 + a3)
    return minus, plus


def row_terms(cells, step, closed=False):
    eps = epsilon * step * step
    count = len(cells) if closed else len(cells) - 2 * rim
    shift = 0 if closed else rim
    slope = {m: cells[m + 1 + shift] - cells[m + shift] for m in range(-shift, count + shift - 1)}
    a, b, c = {}, {}, {}
    if closed:
        bend = {m: slope[m] - slope[m - 1] for m in range(1, count - 1)}
        bend[0], bend[count - 1] = slope[0], -slope[count - 2]
        turn = {m: bend[m + 1] - bend[m] for m in range(count - 1)}
        turn[-1], turn[count - 1] = bend[0], -bend[count - 1]
        jerk = {m: turn[m] - turn[m - 1] for m in range(count)}
        jerk[-1], jerk[count] = bend[0], bend[count - 1]
        rise = {m: slope[m] + slope[m - 1] for m in range(1, count - 1)}
        rise[0], rise[count - 1] = slope[0], slope[count - 2]
        a[-2] = c[count] = 1.0 / (eps * eps)
        for m, (e1, e2) in ((-1, (None, bend[0])), (count - 1, (bend[count - 1], None))):
            square = turn[m] * turn[m]
            level = square * (4.0 / 3.0) + eps
            ib, outer = inverse(level), inverse(level + (square + square))
            b[m] = ib * ib * 6.0
            (c if e2 is None else a)[m] = outer * outer
        inner = range(count - 1)
    else:
        bend = {m: slope[m] - slope[m - 1] for m in range(-2, count + 2)}
        turn = {m: bend[m + 1] - bend[m] for m in range(-2, count + 1)}
        jerk = {m: turn[m] - turn[m - 1] for m in range(-1, count + 1)}
        rise = {m: cells[m + 1 + rim] - cells[m - 1 + rim] for m in range(count)}
        inner = range(-2, count + 1)
    for m in inner:
        a[m], b[m], c[m] = weights_of(bend[m], bend[m + 1], turn[m], eps)
    out = []
    for i in range(count):
        base = rise[i] * 6.0 - (turn[i - 1] + turn[i])
        minus, plus = sides(
            jerk[i - 1], jerk[i], jerk[i + 1], a[i - 2], a[i - 1], b[i - 1], b[i], c[i], c[i + 1]
        )
        out.append((base + (plus - minus), (plus + minus) - jerk[i]))
    return out


def batches(total, most):
    return max(k for k in range(1, most + 1) if total % k == 0)


def splat(row, tile):
    return jnp.broadcast_to(row, tile)


def speeds_of(tile, speed_step):
    place = lax.broadcasted_iota(jnp.int32, tile, 0).astype(jnp.float32)
    return speed_low + place * speed_step


def odd_place(axis):
    return lax.rem(lax.axis_index(axis), 2) == 1


def put_extremes(wind_ref, most_ref):
    rows = [wind_ref[i] for i in range(wind_ref.shape[0])]
    most_ref[...] = jnp.zeros_like(most_ref)
    most_ref[0:2, :] = functools.reduce(jnp.maximum, rows)
    most_ref[2:4, :] = -functools.reduce(jnp.minimum, rows)


def extremes_kernel(wind_ref, most_ref):
    put_extremes(wind_ref, most_ref.at[0])


def opening_kernel(level_ref, x_near, x_far, t_near, t_far):
    cut_near(level_ref, x_near)
    cut_far(level_ref, x_far)
    cut_headings(level_ref, t_near, t_far)


def meeting_kernel(own_ref, other_ref, most_ref):
    most_ref[...] = jnp.maximum(own_ref[0], other_ref[0])


def flows_into(flow_ref, speed_step, wind_ref, waves_ref):
    planes, headings = flow_ref.shape[:2]
    tile = flow_ref.shape[2:]
    first = lax.axis_index("head") * headings
    pace = speeds_of(tile, speed_step) * gain
    tables = [
        splat(waves_ref[1, pl.ds(first + j, 1), :], tile) * pace for j in range(headings)
    ]
    for i in range(planes):
        wind = splat(wind_ref[i, 1:2, :] * gain, tile)
        for j in range(headings):
            flow_ref[i, j] = tables[j] + wind


def free_kernel(split, speed_step, s_ref, *rest):
    planes, headings, speeds, width = s_ref.shape
    cells = planes * headings

    def rows_of(ref):
        return ref.reshape(cells * speeds, width)

    if split:
        wind_ref, waves_ref, speed_ref, out_ref, extra_ref, flow_t_ref = rest[:6]
        turned_ref, drift_ref, gap_ref, flow_ref = rest[6:]
        flows_into(flow_ref, speed_step, wind_ref, waves_ref)
        extra_rows, flow_rows = rows_of(extra_ref), rows_of(flow_ref)
    else:
        flow_t_ref, pk_ref, speed_ref, out_ref, turned_ref, drift_ref = rest
        peak = splat(pk_ref[1:2, :] * gain, (speeds, width))
    gain_v = thrust_limit / (12.0 * speed_step)
    s_rows, speed_rows, out_rows = rows_of(s_ref), rows_of(speed_ref), rows_of(out_ref)
    few, many = 8, turned_ref.shape[2] // speeds
    groups = turned_ref.shape[0]
    lanes = many * speeds
    high = 8
    lines = width // high

    def along_speed(n):
        start = min(n * few, cells - few) * speeds
        spots = [pl.ds(start + v, few, stride=speeds) for v in range(speeds)]
        rows = [s_rows[spot, :] for spot in spots]
        for spot, (mean, gap) in zip(spots, row_terms(rows, speed_step, True)):
            speed_rows[spot, :] = gain_v * (gap - jnp.abs(mean))

    def span(n):
        return pl.ds(min(n * many, cells - many) * speeds, lanes)

    def turn_in(n):
        turned = s_rows[span(n), :].T
        turned_ref[n, rim : rim + width, :] = turned
        for k in range(rim):
            turned_ref[n, k : k + 1, :] = turned[:1]
            turned_ref[n, rim + width + k : rim + width + k + 1, :] = turned[-1:]
        if split:
            flow_t_ref[n] = flow_rows[span(n), :].T

    def along_y(n):
        ends = [turned_ref[n, pl.ds(k, high, stride=lines), :] for k in range(lines + 2 * rim)]
        for k, (mean, gap) in enumerate(row_terms(ends, spacing)):
            spot = pl.ds(k, high, stride=lines)
            drift = mean * flow_t_ref[n, spot, :]
            if split:
                drift_ref[n, spot, :] = drift
                gap_ref[n, spot, :] = gap
            else:
                drift_ref[n, spot, :] = drift + gap * peak

    def turn_out(n):
        out_rows[span(n), :] = drift_ref[n].T
        if split:
            extra_rows[span(n), :] = gap_ref[n].T

    turn_in(0)
    for n in range(groups):
        if n > 0:
            turn_out(n - 1)
        along_y(n)
        if n + 1 < groups:
            turn_in(n + 1)
        for k in (2 * n, 2 * n + 1):
            if k * few < cells:
                along_speed(k)
    turn_out(groups - 1)


def heading_kernel(heading_step, s_ref, speed_ref, part_ref, near_ref, far_ref, out_ref):
    planes, headings = s_ref.shape[:2]
    gain_t = turn_limit / (12.0 * heading_step)
    odd = odd_place("head")
    wide = batches(planes, 9)

    def step(n, carry):
        for w in range(wide):
            i = n * wide + w
            ghosts = [(near_ref[i * rim + k], far_ref[i * rim + k]) for k in range(rim)]
            lows = [jnp.where(odd, near, far) for near, far in ghosts]
            highs = [jnp.where(odd, far, near) for near, far in ghosts]
            cells = lows + [s_ref[i, j] for j in range(headings)] + highs
            for j, (mean, gap) in enumerate(row_terms(cells, heading_step)):
                own = speed_ref[i, j] + part_ref[i, j]
                out_ref[i, j] = own + gain_t * (gap - jnp.abs(mean))
        return carry

    lax.fori_loop(0, planes // wide, step, 0)


def peaks_into(pk_ref, most, bounds, heading_step, speed_step):
    most = jnp.max(most, axis=1, keepdims=True)
    peaks = [
        jnp.maximum(most[q : q + 1] + bounds[q][1], most[q + 2 : q + 3] - bounds[q][0])
        for q in range(2)
    ]
    time_step = courant / (
        peaks[0] / spacing
        + peaks[1] / spacing
        + turn_limit / heading_step
        + thrust_limit / speed_step
    )
    width = pk_ref.shape[1]
    for row, value in enumerate(peaks + [time_step]):
        pk_ref[row : row + 1, :] = splat(value, (1, width))


def plane_at(i, planes):
    return jnp.where(odd_place("gx"), i, planes - 1 - i)


def alone(reach):
    place, size = lax.axis_index("gx"), lax.axis_size("gx")
    if reach == 0:
        return (place == size - 1) if size % 2 else place < 0
    return (place == 0) | (place == size - 1) if size % 2 == 0 else place == 0


def cut_near(field_ref, x_near):
    planes, headings = field_ref.shape[:2]
    for k in range(rim):
        i = jnp.where(alone(0), 0, k)
        x_near[k * headings : (k + 1) * headings] = field_ref[plane_at(i, planes)]


def cut_far(field_ref, x_far):
    planes, headings = field_ref.shape[:2]
    for k in range(rim):
        i = planes - 1 - jnp.where(alone(1), 0, k)
        x_far[k * headings : (k + 1) * headings] = field_ref[plane_at(i, planes)]


def cut_headings(field_ref, t_near, t_far):
    planes, headings = field_ref.shape[:2]
    t_low = jnp.where(odd_place("head"), 0, headings - rim)
    for k in range(rim):
        for i in range(planes):
            t_near[i * rim + k] = field_ref[i, t_low + k]
            t_far[i * rim + k] = field_ref[i, headings - rim - t_low + k]


def splat_targets(mask_ref, depth_ref, target_ref):
    for i in range(target_ref.shape[0]):
        depth = depth_ref[i : i + 1, :]
        target = jnp.where(mask_ref[i : i + 1, :] == 1, -depth, depth)
        target_ref[i] = splat(target, target_ref.shape[1:])


def across_planes(
    span, speed_step, s_ref, near_ref, far_ref, wind_ref, waves_ref, flow_ref, use
):
    planes, headings = s_ref.shape[:2]
    tile = s_ref.shape[2:]
    side = jnp.where(odd_place("gx"), gain, -gain).astype(jnp.float32)
    spots = [plane_at(i, planes) for i in range(planes)]
    for i in range(planes):
        flow_ref[i] = splat(wind_ref[i, 0:1, :] * side, tile)
    pace = speeds_of(tile, speed_step) * side
    first = lax.axis_index("head") * headings
    low, high = span
    wide = batches(headings, max(1, 108 // (high - low)))

    def line(i, j):
        if i < 0:
            return near_ref[(-1 - i) * headings + j]
        if i >= planes:
            return far_ref[(i - planes) * headings + j]
        return s_ref[spots[i], j]

    def step(n, carry):
        for w in range(wide):
            j = n * wide + w
            cells = [line(i, j) for i in range(low - rim, high + rim)]
            table = splat(waves_ref[0, pl.ds(first + j, 1), :], tile) * pace
            for k, (mean, gap) in enumerate(row_terms(cells, spacing)):
                spot = spots[low + k]
                use(spot, j, mean * (table + flow_ref[spot]), gap, cells[k + rim])
        return carry

    lax.fori_loop(0, headings // wide, step, 0)


def first_kernel(
    speed_step, s_ref, part_ref, near_ref, far_ref, wind_ref, waves_ref, out_ref, gap_ref, flow_ref
):
    def use(i, j, drift, gap, cell):
        out_ref[i, j] = part_ref[i, j] + drift
        gap_ref[i, j] = gap

    across_planes(
        (0, s_ref.shape[0]), speed_step, s_ref, near_ref, far_ref, wind_ref, waves_ref, flow_ref, use
    )


def closing_kernel(
    bounds, heading_step, speed_step, s_ref, part_ref, gap_x_ref, gap_y_ref, mask_ref, depth_ref,
    most_ref, other_ref, out_ref, x_near, x_far, t_near, t_far, pk_ref, target_ref
):
    planes, headings = s_ref.shape[:2]
    tile = s_ref.shape[2:]
    most = jnp.maximum(most_ref[...], other_ref[...])
    peaks_into(pk_ref, most, bounds, heading_step, speed_step)
    splat_targets(mask_ref, depth_ref, target_ref)
    peak_x = splat(pk_ref[0:1, :] * gain, tile)
    peak_y = splat(pk_ref[1:2, :] * gain, tile)
    time_step = splat(pk_ref[2:3, :], tile)

    wide = batches(planes, 3)

    def step(n, carry):
        for w in range(wide):
            i = n * wide + w
            for j in range(headings):
                rate = part_ref[i, j] + (gap_x_ref[i, j] * peak_x + gap_y_ref[i, j] * peak_y)
                out_ref[i, j] = jnp.minimum(s_ref[i, j] + time_step * rate, target_ref[i])
        return carry

    lax.fori_loop(0, planes // wide, step, 0)
    cut_near(out_ref, x_near)
    cut_far(out_ref, x_far)
    cut_headings(out_ref, t_near, t_far)


def section_kernel(
    section, span, speed_step, base_ref, s_ref, part_ref, ghosts_ref, wind_ref, waves_ref,
    mask_ref, depth_ref, pk_ref, *refs
):
    planes = s_ref.shape[0]
    refs, (flow_ref, target_ref) = list(refs[:-2]), refs[-2:]
    early_ref = refs.pop(0) if span[0] > 0 else None
    out_ref = refs.pop(0)
    tile = s_ref.shape[2:]
    splat_targets(mask_ref, depth_ref, target_ref)
    peak_x = splat(pk_ref[0:1, :] * gain, tile)
    time_step = splat(pk_ref[2:3, :], tile)
    base_share = 0.75 if section == 2 else 1.0 / 3.0
    own_share = 0.25 if section == 2 else 2.0 / 3.0

    def use(i, j, drift, gap, cell):
        rate = part_ref[i, j] + (drift + gap * peak_x)
        moved = base_share * base_ref[i, j] + own_share * (cell + time_step * rate)
        out_ref[i, j] = jnp.minimum(moved, target_ref[i])

    near_ref, far_ref = (None, ghosts_ref) if span[0] > 0 else (ghosts_ref, None)
    across_planes(
        span, speed_step, s_ref, near_ref, far_ref, wind_ref, waves_ref, flow_ref, use
    )
    for i in range(span[0]):
        spot = plane_at(i, planes)
        out_ref[spot] = early_ref[spot]
    if section == 2 and span[0] == 0:
        cut_near(out_ref, *refs)
    elif section == 2:
        cut_far(out_ref, refs[0])
        cut_headings(out_ref, *refs[1:])


def trade(value, axis, reach, wrap=False):
    size = lax.axis_size(axis)
    pairs = [(i, i + 1) for i in range(reach, size - 1, 2)]
    if wrap and reach and size % 2 == 0:
        pairs.append((size - 1, 0))
    pairs += [(j, i) for i, j in pairs]
    pairs += [(i, i) for i in range(size) if i not in dict(pairs)]
    return lax.ppermute(value, axis, pairs)


def local(level_set, wind_field, target_mask, target_depth):
    planes, headings, speed_count, cross_count = level_set.shape
    heading_total = headings * lax.axis_size("head")
    heading_step = 2.0 * math.pi / heading_total
    speed_step = (speed_high - speed_low) / (speed_count - 1)
    speed_row = np.float32(speed_low) + np.arange(speed_count, dtype=np.float32) * np.float32(
        speed_step
    )
    angles = np.arange(heading_total, dtype=np.float32) * np.float32(heading_step)
    waves = [np.cos(angles), np.sin(angles)]
    bounds = []
    for wave in waves:
        product = wave[:, None] * speed_row[None, :]
        bounds.append((float(product.min()), float(product.max())))
    waves = jnp.asarray(np.stack(waves)[..., None] * np.ones(cross_count, np.float32))

    vmem = pl.BlockSpec(memory_space=pltpu.VMEM)
    tile = (speed_count, cross_count)

    def shape(*dims):
        return jax.ShapeDtypeStruct(dims + tile, jnp.float32)

    field = shape(planes, headings)
    short = rim * headings
    middle = max(short + 1, rim * planes)

    longest = middle + 1
    rows = pltpu.VMEM((planes,) + tile, jnp.float32)
    cells = math.prod(level_set.shape)

    def call(kernel, ins, outs, scratch=(), work=0):
        return pl.pallas_call(
            kernel,
            out_shape=outs,
            in_specs=[vmem] * len(ins),
            out_specs=[vmem] * len(outs),
            scratch_shapes=list(scratch),
            compiler_params=pltpu.CompilerParams(vmem_limit_bytes=16 * 1024 * 1024),
            cost_estimate=pl.CostEstimate(
                flops=work * cells, bytes_accessed=work * cells, transcendentals=0
            ),
        )(*ins)

    wind = jnp.transpose(wind_field, (1, 0, 2))
    many = 16
    groups, lanes = -(-planes * headings // many), many * speed_count
    turned = (groups, cross_count, lanes)
    room = [
        pltpu.VMEM((groups, cross_count + 8, lanes), jnp.float32),
        pltpu.VMEM(turned, jnp.float32),
    ]
    wide_room = room + [pltpu.VMEM(turned, jnp.float32), pltpu.VMEM(level_set.shape, jnp.float32)]
    values = level_set
    size = lax.axis_size("gx")

    def spread(most, reach):
        if size & (size - 1):
            pairs = [(i, (i + reach) % size) for i in range(size)]
        else:
            pairs = [(i, i ^ reach) for i in range(size)]
        return lax.ppermute(most, "gx", pairs)

    (most,) = call(extremes_kernel, [wind], [shape(longest + 2)])
    other = spread(most, 1)
    x_shapes = [shape(longest), shape(longest + 1)]
    x_out, x_last, t_out, t_last = call(opening_kernel, [values], x_shapes + [shape(middle)] * 2)
    far_shapes = [shape(short), shape(rim * planes), shape(middle)]
    for section in (1, 2, 3):
        opening = section == 1
        x_near = trade(x_out, "gx", 0)
        t_near = trade(t_out, "head", 0)
        t_far = trade(t_last, "head", 1, True)
        x_far = trade(x_last, "gx", 1)
        free = functools.partial(free_kernel, opening, speed_step)
        turning = functools.partial(heading_kernel, heading_step)
        if opening:
            (most,) = call(meeting_kernel, [most, other], [shape()])
            other = spread(most, 2)
            ins = [values, wind, waves]
            spun, part, extra, flow = call(
                free, ins, [field] * 3 + [jax.ShapeDtypeStruct(turned, jnp.float32)], wide_room, work=300
            )
            reach = 4
            while reach < size:
                most = jnp.maximum(most, other)
                most, part = lax.optimization_barrier((most, part))
                other = spread(most, reach)
                reach *= 2
            part, x_far = lax.optimization_barrier((part, x_far))
        else:
            if section == 3:
                values, x_near = lax.optimization_barrier((values, x_near))
            spun, part = call(free, [values, flow, pk], [field] * 2, room)
            if section == 2:
                part, x_near = lax.optimization_barrier((part, x_near))
        (part,) = call(turning, [values, spun, part, t_near, t_far], [field], work=1000)
        if opening:
            ins = [values, part, x_near, x_far, wind, waves]
            first = functools.partial(first_kernel, speed_step)
            part, gap = call(first, ins, [field] * 2, [rows])
            closing = functools.partial(closing_kernel, bounds, heading_step, speed_step)
            ins = [values, part, gap, extra, target_mask, target_depth, most, other]
            outs = [field, shape(longest), *far_shapes, shape()]
            values, x_out, x_last, t_out, t_last, pk = call(closing, ins, outs, [rows])
        else:
            more = section == 2
            ins = [level_set, values, part, x_near, wind, waves, target_mask, target_depth, pk]
            outs = [field] + ([shape(longest)] if more else [])
            last = functools.partial(section_kernel, section, (0, planes - rim), speed_step)
            early, *x_next = call(last, ins, outs, [rows, rows])
            ins = ins[:3] + [x_far] + ins[4:] + [early]
            outs = [field] + (far_shapes if more else [])
            last = functools.partial(section_kernel, section, (planes - rim, planes), speed_step)
            values, *far_next = call(last, ins, outs, [rows, rows])
            if more:
                (x_out,), (x_last, t_out, t_last) = x_next, far_next
    return values


def solution(mesh):
    return jax.shard_map(
        local,
        mesh=mesh,
        in_specs=(P("gx", "head", None, None), P(None, "gx", None), P("gx", None), P("gx", None)),
        out_specs=P("gx", "head", None, None),
        check_vma=False,
    )
```
